32 devices in a mesh: dp: 2 (over x), dom: 16 (over z, y, core).
Axes of the slice: x: 2, y: 2, z: 4, core: 2. Of those that a mesh axis runs over, the one named last changes fastest.
Arguments:
- features: bfloat16 [2, 16384, 256], P('dp', 'dom'), may hold values from -6 to 6
- send_order: int32 [16, 1024], P('dom'), may hold values from 0 to 1023, each once within a row
- adj_count: int32 [128], P('dom'), may hold values from 2 to 4, as said below
- adj_target: int32 [128, 4], P('dom'), may hold values from 6 to 17, as said below
- adj_vals: bfloat16 [128, 4, 128, 128], P('dom'), may hold values from -0.3125 to 0.3125
- w_edge: bfloat16 [256, 256], replicated, may hold values from -0.375 to 0.375
- w_node: bfloat16 [512, 256], replicated, may hold values from -0.25 to 0.25
- cotangent: bfloat16 [2, 16384, 256], P('dp', 'dom'), may hold values from -6 to 6
Outputs:
- node_out: bfloat16 [2, 16384, 256], P('dp', 'dom')
- grad_features: bfloat16 [2, 16384, 256], P('dp', 'dom')
- grad_edge: float32 [256, 256], replicated
- grad_node: float32 [512, 256], replicated
The draws below stay inside these ranges and needn't reach their ends.
Inputs may be any that keep to these rules, and one draw needn't show every extreme that they name: Each row of send_order is a permutation of 0 to 1023. `adj_count`: every partition has its own most count, reached by one of its blocks; some partition's most is 4. `adj_target`: targets lie in the own partition's blocks or in the last 2 blocks of the previous partition or the first 2 blocks of the next one; slot 0 of each partition's first column block targets the previous partition, and slot 1 of its last column block targets the next one.
All inputs are finite; a program needn't handle non-finite values.
Results may differ from the reference program's by a relative error of at most 0.009.
Values may be sent and summed in bfloat16 or wider, within the bound.
No kernel may reach another device: no remote copies, remote signals or barrier semaphores. Data moves between devices by JAX's collectives and lax.ppermute only.
A program may use at most 64 MiB of HBM per device.

```python
import jax
import jax.numpy as jnp
from jax import lax

H = 256
NODES_DEV = 1024
NB = 4
RIM = 2
NODES = 16384
BLK = 8
NBLOCKS = 128
PER_PEER = 64
N_DP = 2
N_DOM = 16


def draw_adj_count(key, part):
    key_cap = jax.random.fold_in(key, 11)
    key_top = jax.random.fold_in(key, 12)
    key_cnt = jax.random.fold_in(key, 13)
    caps = jax.random.randint(key_cap, (N_DOM,), 2, NB + 1)
    top = jax.random.randint(key_top, (), 0, N_DOM)
    caps = jnp.where(jnp.arange(N_DOM) == top, NB, caps)
    counts = jax.random.randint(key_cnt, (N_DOM, BLK), 2, caps[:, None] + 1)
    counts = jnp.where(jnp.arange(BLK)[None, :] == 0, caps[:, None], counts)
    return counts.reshape(-1).astype(jnp.int32)


def draw_adj_target(key, part):
    key_reg = jax.random.fold_in(key, 21)
    key_off = jax.random.fold_in(key, 22)
    key_own = jax.random.fold_in(key, 23)
    region = jax.random.randint(key_reg, (NBLOCKS, NB), 0, 6)
    offset = jax.random.randint(key_off, (NBLOCKS, NB), 0, RIM)
    own = jax.random.randint(key_own, (NBLOCKS, NB), BLK, 2 * BLK)
    local = (jnp.arange(NBLOCKS) % BLK)[:, None]
    slot = jnp.arange(NB)[None, :]
    region = jnp.where((local == 0) & (slot == 0), 0, region)
    region = jnp.where((local == BLK - 1) & (slot == 1), 1, region)
    target = jnp.where(region == 0, BLK - RIM + offset, jnp.where(region == 1, 2 * BLK + offset, own))
    return target.astype(jnp.int32)


def block_levels(key, shape, cuts, least, high):
    gain = 1.0
    for position, parts in cuts:
        heights = jax.random.uniform(jax.random.fold_in(jax.random.fold_in(key, 6), position), (parts,), jnp.float32, least / len(cuts), high / len(cuts))
        gain = gain * jnp.repeat(jnp.exp(heights), shape[position] // parts).reshape((-1,) + (1,) * (len(shape) - 1 - position))
    return gain


def bell_draw(stream_key, shape, width, bound, shards=(), kind=jnp.bfloat16):
    gain = block_levels(stream_key, shape, shards, -0.22, 0.18) if shards else 1.0
    entries = jax.random.normal(stream_key, shape, jnp.float32) * width * gain
    return jnp.minimum(jnp.maximum(entries, -bound), bound).astype(kind)


def setup_inputs(seed: int = 0) -> dict:
    keys = jax.random.split(jax.random.key(seed), 9)
    return {
        "features": bell_draw(keys[0], (N_DP, NODES, H), 1.0, 6.0, ((0, 2), (1, 16))),
        "send_order": jax.vmap(lambda own: jax.random.permutation(own, NODES_DEV))(jax.random.split(keys[1], N_DOM)).reshape((N_DOM, NODES_DEV)).astype(jnp.int32),
        "adj_count": draw_adj_count(jax.random.fold_in(keys[8], 71), 0),
        "adj_target": draw_adj_target(jax.random.fold_in(keys[8], 71), 0),
        "adj_vals": bell_draw(keys[4], (NBLOCKS, NB, 128, 128), 384 ** -0.5, 0.3125, ((0, 16),)),
        "w_edge": bell_draw(keys[5], (H, H), H ** -0.5, 0.375),
        "w_node": bell_draw(keys[6], (2 * H, H), (2 * H) ** -0.5, 0.25),
        "cotangent": bell_draw(keys[7], (N_DP, NODES, H), 1.0, 6.0, ((0, 2), (1, 16))),
    }


def dsilu(value):
    sig = jax.nn.sigmoid(value)
    return sig * (1.0 + value * (1.0 - sig))


def relay_index(send_order):
    offsets = (jnp.arange(N_DOM, dtype=jnp.int32) * NODES_DEV)[:, None, None]
    order = send_order.reshape(N_DOM, N_DOM, PER_PEER).astype(jnp.int32) + offsets
    return jnp.transpose(order, (1, 0, 2)).reshape(-1)


def slot_table(targets, counts):
    wins = jnp.arange(3 * BLK, dtype=jnp.int32)
    live = jnp.arange(NB, dtype=jnp.int32)[None, :] < counts[:, None]
    return ((targets[None, :, :] == wins[:, None, None]) & live[None]).astype(jnp.float32)


def reference(features, send_order, adj_count, adj_target, adj_vals, w_edge, w_node, cotangent):
    src = relay_index(send_order)
    vals_r = adj_vals.reshape(N_DOM, BLK, NB, 128, 128)
    tgt_r = adj_target.reshape(N_DOM, BLK, NB)
    cnt_r = adj_count.reshape(N_DOM, BLK)
    scale = 1.0 / (float(N_DP * NODES) ** 0.5)

    def window_fn(args):
        vq, tq, cq, mq = args
        contrib = jnp.einsum('csrk,ckh->csrh', vq.astype(jnp.float32), mq.astype(jnp.float32))
        table = slot_table(tq, cq)
        win = jnp.einsum('wcs,csrh->wrh', table, contrib, precision=lax.Precision.HIGHEST)
        return win.astype(jnp.bfloat16)

    def dmsg_fn(args):
        vq, tq, cq, gq = args
        table = slot_table(tq, cq)
        picked = jnp.einsum('wcs,wrh->csrh', table, gq.astype(jnp.float32), precision=lax.Precision.HIGHEST)
        out = jnp.einsum('csrk,csrh->ckh', vq.astype(jnp.float32), picked)
        return out.astype(jnp.bfloat16)

    def one_sample(args):
        xs, gs = args
        nodes = xs[src]
        pre_edge = jnp.dot(nodes, w_edge, preferred_element_type=jnp.float32)
        message = jax.nn.silu(pre_edge).astype(jnp.bfloat16)
        mr = message.reshape(N_DOM, BLK, 128, H)
        wins = lax.map(window_fn, (vals_r, tgt_r, cnt_r, mr)).astype(jnp.float32)
        agg = wins[:, BLK:2 * BLK] + jnp.roll(wins[:, :BLK], -1, 0) + jnp.roll(wins[:, 2 * BLK:], 1, 0)
        aggregate = agg.astype(jnp.bfloat16).reshape(NODES, H)
        joined = jnp.concatenate([nodes, aggregate], axis=1)
        pre_node = jnp.dot(joined, w_node, preferred_element_type=jnp.float32)
        node_out = (nodes.astype(jnp.float32) + jax.nn.silu(pre_node)).astype(jnp.bfloat16)
        gout = gs.astype(jnp.float32)
        d_node = (gout * dsilu(pre_node)).astype(jnp.bfloat16)
        back = jnp.dot(d_node, w_node.T, preferred_element_type=jnp.float32)
        d_nodes1 = gout + back[:, :H]
        d_agg = back[:, H:].astype(jnp.bfloat16).reshape(N_DOM, BLK, 128, H)
        window_g = jnp.concatenate([jnp.roll(d_agg, 1, 0), d_agg, jnp.roll(d_agg, -1, 0)], axis=1)
        d_message = lax.map(dmsg_fn, (vals_r, tgt_r, cnt_r, window_g)).reshape(NODES, H)
        d_edge = (d_message.astype(jnp.float32) * dsilu(pre_edge)).astype(jnp.bfloat16)
        d_nodes = (d_nodes1 + jnp.dot(d_edge, w_edge.T, preferred_element_type=jnp.float32)).astype(jnp.bfloat16)
        grad_x = jnp.zeros((NODES, H), jnp.bfloat16).at[src].set(d_nodes)
        g_edge = jnp.dot(nodes.T, d_edge, preferred_element_type=jnp.float32)
        g_node = jnp.dot(joined.T, d_node, preferred_element_type=jnp.float32)
        return node_out, grad_x, g_edge, g_node

    outs, grads_x, g_edges, g_nodes = lax.map(one_sample, (features, cotangent))
    return outs, grads_x, jnp.sum(g_edges, axis=0) * scale, jnp.sum(g_nodes, axis=0) * scale
```

```python
import functools
import math

import jax
import jax.numpy as jnp
from jax import lax
from jax.experimental import pallas as pl
from jax.experimental.pallas import tpu as pltpu
from jax.sharding import PartitionSpec as P

ROWS = 128
RIM = 2
VMEM = pl.BlockSpec(memory_space=pltpu.VMEM)
SMEM = pl.BlockSpec(memory_space=pltpu.SMEM)
BF16 = jnp.bfloat16
F32 = jnp.float32


def passed_along(x, axis, by):
    peers = lax.axis_size(axis)
    return lax.ppermute(x, axis, [(i, (i + by) % peers) for i in range(peers)])


def dsilu(value):
    sig = jax.nn.sigmoid(value)
    return sig * (1.0 + value * (1.0 - sig))


def dot(a, b, contract=((1,), (0,))):
    return lax.dot_general(a, b, (contract, ((), ())), preferred_element_type=F32)


def call(body, outs, args, specs, scratch=(), flops=0, nbytes=0):
    return pl.pallas_call(
        body,
        out_shape=outs,
        in_specs=specs,
        out_specs=[VMEM] * len(outs),
        scratch_shapes=list(scratch),
        cost_estimate=pl.CostEstimate(flops=flops, bytes_accessed=nbytes, transcendentals=0),
        compiler_params=pltpu.CompilerParams(vmem_limit_bytes=24 * 1024 * 1024),
    )(*args)


def pick_body(order_ref, feat_ref, out_ref):
    rows = feat_ref.shape[0]
    feat = feat_ref[...]
    lane = lax.broadcasted_iota(jnp.int32, (ROWS, rows), 1).astype(F32)
    for k in range(rows // ROWS):
        mine = slice(k * ROWS, (k + 1) * ROWS)
        row = order_ref[:, mine].astype(F32)
        col = jnp.transpose(jnp.broadcast_to(row, (ROWS, ROWS)))
        wide = jnp.concatenate([col] * (rows // ROWS), axis=1)
        hot = jnp.where(wide == lane, 1.0, 0.0).astype(BF16)
        out_ref[mine, :] = dot(hot, feat).astype(BF16)


def place_body(order_ref, back_ref, out_ref):
    rows = back_ref.shape[0]
    back = back_ref[...]
    order = jnp.broadcast_to(order_ref[...], (ROWS, rows))
    for k in range(rows // ROWS):
        mine = slice(k * ROWS, (k + 1) * ROWS)
        row = lax.broadcasted_iota(jnp.int32, (ROWS, rows), 0) + k * ROWS
        hot = jnp.where(order == row, 1.0, 0.0).astype(BF16)
        out_ref[mine, :] = dot(hot, back).astype(BF16)


def window_body(cnt_ref, tgt_ref, nodes_ref, vals_ref, w_edge_ref, prev_ref, own_ref, next_ref, win):
    blocks, slots = vals_ref.shape[0], vals_ref.shape[1]
    base = blocks - RIM
    trash = blocks + 2 * RIM
    win[...] = jnp.zeros_like(win)
    w_edge = w_edge_ref[...]
    for c in range(blocks):
        pre = dot(nodes_ref[c * ROWS : (c + 1) * ROWS, :], w_edge)
        message = (pre * jax.nn.sigmoid(pre)).astype(BF16)
        contrib = dot(vals_ref[c].reshape(slots * ROWS, ROWS), message)
        for s in range(slots):
            to = jnp.where(s < cnt_ref[c], tgt_ref[c, s] - base, trash)
            win[to] += contrib[s * ROWS : (s + 1) * ROWS, :]
    for b in range(RIM):
        prev_ref[b * ROWS : (b + 1) * ROWS, :] = win[b].astype(BF16)
        next_ref[b * ROWS : (b + 1) * ROWS, :] = win[RIM + blocks + b].astype(BF16)
    for b in range(blocks):
        own_ref[b * ROWS : (b + 1) * ROWS, :] = win[RIM + b].astype(BF16)


def node_body(
    nodes_ref, own_ref, from_prev_ref, from_next_ref, cot_ref, w_node_ref,
    out_ref, agg_ref, d_node_ref, d_nodes1_ref, d_agg_ref,
):
    rows, width = nodes_ref.shape
    w_node = w_node_ref[...]
    step = RIM * ROWS
    for k in range(rows // step):
        mine = slice(k * step, (k + 1) * step)
        agg = own_ref[mine, :].astype(F32)
        if k == 0:
            agg = agg + from_prev_ref[...].astype(F32)
        if k == rows // step - 1:
            agg = agg + from_next_ref[...].astype(F32)
        agg = agg.astype(BF16)
        agg_ref[mine, :] = agg
        nodes = nodes_ref[mine, :]
        pre = dot(nodes, w_node[:width]) + dot(agg, w_node[width:])
        sig = jax.nn.sigmoid(pre)
        out_ref[mine, :] = (nodes.astype(F32) + pre * sig).astype(BF16)
        gout = cot_ref[mine, :].astype(F32)
        d_node = (gout * (sig * (1.0 + pre * (1.0 - sig)))).astype(BF16)
        d_node_ref[mine, :] = d_node
        back = dot(d_node, w_node, ((1,), (1,)))
        d_nodes1_ref[mine, :] = gout + back[:, :width]
        d_agg_ref[mine, :] = back[:, width:].astype(BF16)


def grad_node_body(scale, nodes_ref, agg_ref, d_node_ref, out_ref):
    width = nodes_ref.shape[1]
    d_node = d_node_ref[...]
    out_ref[:width, :] = dot(nodes_ref[...], d_node, ((0,), (0,))) * scale
    out_ref[width:, :] = dot(agg_ref[...], d_node, ((0,), (0,))) * scale


def edge_body(
    cnt_ref, tgt_ref, nodes_ref, vals_ref, w_edge_ref, d_agg_ref, prev_ref, next_ref, d_nodes1_ref,
    d_nodes_ref, d_edge_ref, win,
):
    blocks, slots = vals_ref.shape[0], vals_ref.shape[1]
    base = blocks - RIM
    dead = blocks + 2 * RIM
    for b in range(RIM):
        win[b] = prev_ref[b * ROWS : (b + 1) * ROWS, :]
        win[RIM + blocks + b] = next_ref[b * ROWS : (b + 1) * ROWS, :]
    for b in range(blocks):
        win[RIM + b] = d_agg_ref[b * ROWS : (b + 1) * ROWS, :]
    win[dead] = jnp.zeros(win.shape[1:], BF16)
    w_edge = w_edge_ref[...]
    for c in range(blocks):
        mine = slice(c * ROWS, (c + 1) * ROWS)
        picked = []
        for s in range(slots):
            at = jnp.where(s < cnt_ref[c], tgt_ref[c, s] - base, dead)
            picked.append(win[at])
        picked = jnp.concatenate(picked, axis=0)
        d_message = dot(vals_ref[c].reshape(slots * ROWS, ROWS), picked, ((0,), (0,)))
        pre = dot(nodes_ref[mine, :], w_edge)
        d_edge = (d_message.astype(BF16).astype(F32) * dsilu(pre)).astype(BF16)
        d_edge_ref[mine, :] = d_edge
        d_nodes_ref[mine, :] = (d_nodes1_ref[mine, :] + dot(d_edge, w_edge, ((1,), (1,)))).astype(BF16)


def grad_edge_body(scale, nodes_ref, d_edge_ref, out_ref):
    out_ref[...] = dot(nodes_ref[...], d_edge_ref[...], ((0,), (0,))) * scale


def shards(features, send_order, adj_count, adj_target, adj_vals, w_edge, w_node, cotangent):
    ndom = lax.axis_size("dom")
    rows, width = features.shape[1:]
    per_peer = rows // ndom
    blocks, slots = adj_vals.shape[:2]
    rim = RIM * ROWS
    scale = 1.0 / math.sqrt(float(lax.axis_size("dp") * rows * ndom))
    tall = jax.ShapeDtypeStruct((rows, width), BF16)
    tall_f = jax.ShapeDtypeStruct((rows, width), F32)
    edge = jax.ShapeDtypeStruct((rim, width), BF16)
    unit = rows * width * 2

    (picked,) = call(
        pick_body, [tall], (send_order, features[0]), [VMEM, VMEM], flops=2 * rows * rows * width, nbytes=2 * unit
    )
    nodes = lax.all_to_all(
        picked.reshape(ndom, per_peer, width), "dom", split_axis=0, concat_axis=0, tiled=True
    ).reshape(rows, width)
    send_prev, own, send_next = call(
        window_body,
        [edge, tall, edge],
        (adj_count, adj_target, nodes, adj_vals, w_edge),
        [SMEM, SMEM, VMEM, VMEM, VMEM],
        [pltpu.VMEM((blocks + 2 * RIM + 1, ROWS, width), F32)],
        flops=2 * rows * width * (width + slots * ROWS),
        nbytes=4 * unit,
    )
    from_next = passed_along(send_prev, "dom", -1)
    from_prev = passed_along(send_next, "dom", 1)
    node_out, agg, d_node, d_nodes1, d_agg = call(
        node_body,
        [tall, tall, tall, tall_f, tall],
        (nodes, own, from_prev, from_next, cotangent[0], w_node),
        [VMEM] * 6,
        flops=8 * rows * width * width,
        nbytes=8 * unit,
    )
    prev_rows = passed_along(d_agg[rows - rim :], "dom", 1)
    next_rows = passed_along(d_agg[:rim], "dom", -1)
    (local_node,) = call(
        functools.partial(grad_node_body, scale),
        [jax.ShapeDtypeStruct((2 * width, width), F32)],
        (nodes, agg, d_node),
        [VMEM] * 3,
        flops=4 * rows * width * width,
        nbytes=3 * unit,
    )
    grad_node = lax.psum(local_node, ("dp", "dom"))
    d_nodes, d_edge = call(
        edge_body,
        [tall, tall],
        (adj_count, adj_target, nodes, adj_vals, w_edge, d_agg, prev_rows, next_rows, d_nodes1),
        [SMEM, SMEM] + [VMEM] * 7,
        [pltpu.VMEM((blocks + 2 * RIM + 1, ROWS, width), BF16)],
        flops=2 * rows * width * (2 * width + slots * ROWS),
        nbytes=6 * unit,
    )
    returned = lax.all_to_all(
        d_nodes.reshape(ndom, per_peer, width), "dom", split_axis=0, concat_axis=0, tiled=True
    ).reshape(rows, width)
    (local_edge,) = call(
        functools.partial(grad_edge_body, scale),
        [jax.ShapeDtypeStruct((width, width), F32)],
        (nodes, d_edge),
        [VMEM] * 2,
        flops=2 * rows * width * width,
        nbytes=2 * unit,
    )
    grad_edge = lax.psum(local_edge, ("dp", "dom"))
    (grad_brick,) = call(
        place_body, [tall], (send_order, returned), [VMEM, VMEM], flops=2 * rows * rows * width, nbytes=2 * unit
    )
    return (node_out[None], grad_brick[None], grad_edge, grad_node)


def solution(mesh):
    in_specs = (
        P("dp", "dom", None),
        P("dom", None),
        P("dom"),
        P("dom", None),
        P("dom", None, None, None),
        P(),
        P(),
        P("dp", "dom", None),
    )
    out_specs = (P("dp", "dom", None), P("dp", "dom", None), P(), P())
    return jax.shard_map(shards, mesh=mesh, in_specs=in_specs, out_specs=out_specs, check_vma=False)
```

```python
import functools
import math

import jax
import jax.numpy as jnp
from jax import lax
from jax.experimental import pallas as pl
from jax.experimental.pallas import tpu as pltpu
from jax.sharding import PartitionSpec as P

ROWS = 128
RIM = 2
VMEM = pl.BlockSpec(memory_space=pltpu.VMEM)
SMEM = pl.BlockSpec(memory_space=pltpu.SMEM)
BF16 = jnp.bfloat16
F32 = jnp.float32


def passed_along(x, axis, by):
    peers = lax.axis_size(axis)
    return lax.ppermute(x, axis, [(i, (i + by) % peers) for i in range(peers)])


def dsilu(value):
    sig = jax.nn.sigmoid(value)
    return sig * (1.0 + value * (1.0 - sig))


def dot(a, b, contract=((1,), (0,))):
    return lax.dot_general(a, b, (contract, ((), ())), preferred_element_type=F32)


def call(body, outs, args, specs, scratch=(), flops=0, nbytes=0):
    return pl.pallas_call(
        body,
        out_shape=outs,
        in_specs=specs,
        out_specs=[VMEM] * len(outs),
        scratch_shapes=list(scratch),
        cost_estimate=pl.CostEstimate(flops=flops, bytes_accessed=nbytes, transcendentals=0),
        compiler_params=pltpu.CompilerParams(vmem_limit_bytes=24 * 1024 * 1024),
    )(*args)


def pick_body(order_ref, feat_ref, out_ref):
    rows = feat_ref.shape[0]
    feat = feat_ref[...]
    lane = lax.broadcasted_iota(jnp.int32, (ROWS, rows), 1).astype(F32)
    for k in range(rows // ROWS):
        mine = slice(k * ROWS, (k + 1) * ROWS)
        row = order_ref[:, mine].astype(F32)
        col = jnp.transpose(jnp.broadcast_to(row, (ROWS, ROWS)))
        wide = jnp.concatenate([col] * (rows // ROWS), axis=1)
        hot = jnp.where(wide == lane, 1.0, 0.0).astype(BF16)
        out_ref[mine, :] = dot(hot, feat).astype(BF16)


def place_body(order_ref, back_ref, out_ref):
    rows = back_ref.shape[0]
    back = back_ref[...]
    order = jnp.broadcast_to(order_ref[...], (ROWS, rows))
    for k in range(rows // ROWS):
        mine = slice(k * ROWS, (k + 1) * ROWS)
        row = lax.broadcasted_iota(jnp.int32, (ROWS, rows), 0) + k * ROWS
        hot = jnp.where(order == row, 1.0, 0.0).astype(BF16)
        out_ref[mine, :] = dot(hot, back).astype(BF16)


def window_body(cnt_ref, tgt_ref, nodes_ref, vals_ref, w_edge_ref, prev_ref, own_ref, next_ref, win):
    blocks, slots = vals_ref.shape[0], vals_ref.shape[1]
    base = blocks - RIM
    trash = blocks + 2 * RIM
    win[...] = jnp.zeros_like(win)
    w_edge = w_edge_ref[...]
    for c in range(blocks):
        pre = dot(nodes_ref[c * ROWS : (c + 1) * ROWS, :], w_edge)
        message = (pre * jax.nn.sigmoid(pre)).astype(BF16)
        contrib = dot(vals_ref[c].reshape(slots * ROWS, ROWS), message)
        for s in range(slots):
            to = jnp.where(s < cnt_ref[c], tgt_ref[c, s] - base, trash)
            win[to] += contrib[s * ROWS : (s + 1) * ROWS, :]
    for b in range(RIM):
        prev_ref[b * ROWS : (b + 1) * ROWS, :] = win[b].astype(BF16)
        next_ref[b * ROWS : (b + 1) * ROWS, :] = win[RIM + blocks + b].astype(BF16)
    for b in range(blocks):
        own_ref[b * ROWS : (b + 1) * ROWS, :] = win[RIM + b].astype(BF16)


def node_body(
    nodes_ref, own_ref, from_prev_ref, from_next_ref, cot_ref, w_node_ref,
    out_ref, agg_ref, d_node_ref, d_nodes1_ref, d_agg_ref,
):
    rows, width = nodes_ref.shape
    w_node = w_node_ref[...]
    step = RIM * ROWS
    for k in range(rows // step):
        mine = slice(k * step, (k + 1) * step)
        agg = own_ref[mine, :].astype(F32)
        if k == 0:
            agg = agg + from_prev_ref[...].astype(F32)
        if k == rows // step - 1:
            agg = agg + from_next_ref[...].astype(F32)
        agg = agg.astype(BF16)
        agg_ref[mine, :] = agg
        nodes = nodes_ref[mine, :]
        pre = dot(nodes, w_node[:width]) + dot(agg, w_node[width:])
        sig = jax.nn.sigmoid(pre)
        out_ref[mine, :] = (nodes.astype(F32) + pre * sig).astype(BF16)
        gout = cot_ref[mine, :].astype(F32)
        d_node = (gout * (sig * (1.0 + pre * (1.0 - sig)))).astype(BF16)
        d_node_ref[mine, :] = d_node
        back = dot(d_node, w_node, ((1,), (1,)))
        d_nodes1_ref[mine, :] = gout + back[:, :width]
        d_agg_ref[mine, :] = back[:, width:].astype(BF16)


def grad_node_body(scale, nodes_ref, agg_ref, d_node_ref, out_ref):
    width = nodes_ref.shape[1]
    d_node = d_node_ref[...]
    out_ref[:width, :] = (dot(nodes_ref[...], d_node, ((0,), (0,))) * scale).astype(BF16)
    out_ref[width:, :] = (dot(agg_ref[...], d_node, ((0,), (0,))) * scale).astype(BF16)


def edge_body(
    cnt_ref, tgt_ref, nodes_ref, vals_ref, w_edge_ref, d_agg_ref, prev_ref, next_ref, d_nodes1_ref,
    d_nodes_ref, d_edge_ref, win,
):
    blocks, slots = vals_ref.shape[0], vals_ref.shape[1]
    base = blocks - RIM
    dead = blocks + 2 * RIM
    for b in range(RIM):
        win[b] = prev_ref[b * ROWS : (b + 1) * ROWS, :]
        win[RIM + blocks + b] = next_ref[b * ROWS : (b + 1) * ROWS, :]
    for b in range(blocks):
        win[RIM + b] = d_agg_ref[b * ROWS : (b + 1) * ROWS, :]
    win[dead] = jnp.zeros(win.shape[1:], BF16)
    w_edge = w_edge_ref[...]
    for c in range(blocks):
        mine = slice(c * ROWS, (c + 1) * ROWS)
        picked = []
        for s in range(slots):
            at = jnp.where(s < cnt_ref[c], tgt_ref[c, s] - base, dead)
            picked.append(win[at])
        picked = jnp.concatenate(picked, axis=0)
        d_message = dot(vals_ref[c].reshape(slots * ROWS, ROWS), picked, ((0,), (0,)))
        pre = dot(nodes_ref[mine, :], w_edge)
        d_edge = (d_message.astype(BF16).astype(F32) * dsilu(pre)).astype(BF16)
        d_edge_ref[mine, :] = d_edge
        d_nodes_ref[mine, :] = (d_nodes1_ref[mine, :] + dot(d_edge, w_edge, ((1,), (1,)))).astype(BF16)


def grad_edge_body(scale, nodes_ref, d_edge_ref, out_ref):
    out_ref[...] = (dot(nodes_ref[...], d_edge_ref[...], ((0,), (0,))) * scale).astype(BF16)


def shards(features, send_order, adj_count, adj_target, adj_vals, w_edge, w_node, cotangent):
    ndom = lax.axis_size("dom")
    rows, width = features.shape[1:]
    per_peer = rows // ndom
    blocks, slots = adj_vals.shape[:2]
    rim = RIM * ROWS
    scale = 1.0 / math.sqrt(float(lax.axis_size("dp") * rows * ndom))
    tall = jax.ShapeDtypeStruct((rows, width), BF16)
    tall_f = jax.ShapeDtypeStruct((rows, width), F32)
    edge = jax.ShapeDtypeStruct((rim, width), BF16)
    unit = rows * width * 2

    (picked,) = call(
        pick_body, [tall], (send_order, features[0]), [VMEM, VMEM], flops=2 * rows * rows * width, nbytes=2 * unit
    )
    nodes = lax.all_to_all(
        picked.reshape(ndom, per_peer, width), "dom", split_axis=0, concat_axis=0, tiled=True
    ).reshape(rows, width)
    send_prev, own, send_next = call(
        window_body,
        [edge, tall, edge],
        (adj_count, adj_target, nodes, adj_vals, w_edge),
        [SMEM, SMEM, VMEM, VMEM, VMEM],
        [pltpu.VMEM((blocks + 2 * RIM + 1, ROWS, width), F32)],
        flops=2 * rows * width * (width + slots * ROWS),
        nbytes=4 * unit,
    )
    from_next = passed_along(send_prev, "dom", -1)
    from_prev = passed_along(send_next, "dom", 1)
    node_out, agg, d_node, d_nodes1, d_agg = call(
        node_body,
        [tall, tall, tall, tall_f, tall],
        (nodes, own, from_prev, from_next, cotangent[0], w_node),
        [VMEM] * 6,
        flops=8 * rows * width * width,
        nbytes=8 * unit,
    )
    prev_rows = passed_along(d_agg[rows - rim :], "dom", 1)
    next_rows = passed_along(d_agg[:rim], "dom", -1)
    (local_node,) = call(
        functools.partial(grad_node_body, scale),
        [jax.ShapeDtypeStruct((2 * width, width), BF16)],
        (nodes, agg, d_node),
        [VMEM] * 3,
        flops=4 * rows * width * width,
        nbytes=3 * unit,
    )
    grad_node = lax.psum(local_node, ("dp", "dom"))
    d_nodes, d_edge = call(
        edge_body,
        [tall, tall],
        (adj_count, adj_target, nodes, adj_vals, w_edge, d_agg, prev_rows, next_rows, d_nodes1),
        [SMEM, SMEM] + [VMEM] * 7,
        [pltpu.VMEM((blocks + 2 * RIM + 1, ROWS, width), BF16)],
        flops=2 * rows * width * (2 * width + slots * ROWS),
        nbytes=6 * unit,
    )
    returned = lax.all_to_all(
        d_nodes.reshape(ndom, per_peer, width), "dom", split_axis=0, concat_axis=0, tiled=True
    ).reshape(rows, width)
    (local_edge,) = call(
        functools.partial(grad_edge_body, scale),
        [jax.ShapeDtypeStruct((width, width), BF16)],
        (nodes, d_edge),
        [VMEM] * 2,
        flops=2 * rows * width * width,
        nbytes=2 * unit,
    )
    local_edge, grad_node = lax.optimization_barrier((local_edge, grad_node))
    grad_edge = lax.psum(local_edge, ("dp", "dom"))
    (grad_brick,) = call(
        place_body, [tall], (send_order, returned), [VMEM, VMEM], flops=2 * rows * rows * width, nbytes=2 * unit
    )
    return (node_out[None], grad_brick[None], grad_edge.astype(F32), grad_node.astype(F32))


def solution(mesh):
    in_specs = (
        P("dp", "dom", None),
        P("dom", None),
        P("dom"),
        P("dom", None),
        P("dom", None, None, None),
        P(),
        P(),
        P("dp", "dom", None),
    )
    out_specs = (P("dp", "dom", None), P("dp", "dom", None), P(), P())
    return jax.shard_map(shards, mesh=mesh, in_specs=in_specs, out_specs=out_specs, check_vma=False)
```

```python
import functools
import math

import jax
import jax.numpy as jnp
from jax import lax
from jax.experimental import pallas as pl
from jax.experimental.pallas import tpu as pltpu
from jax.sharding import PartitionSpec as P

ROWS = 128
RIM = 2
VMEM = pl.BlockSpec(memory_space=pltpu.VMEM)
SMEM = pl.BlockSpec(memory_space=pltpu.SMEM)
BF16 = jnp.bfloat16
F32 = jnp.float32


def passed_along(x, axis, by):
    peers = lax.axis_size(axis)
    return lax.ppermute(x, axis, [(i, (i + by) % peers) for i in range(peers)])


def summed_over(x, axis):
    if lax.axis_size(axis) != 2:
        return lax.psum(x.astype(F32), axis).astype(BF16)
    return (x.astype(F32) + passed_along(x, axis, 1).astype(F32)).astype(BF16)


def dsilu(value):
    sig = jax.nn.sigmoid(value)
    return sig * (1.0 + value * (1.0 - sig))


def dot(a, b, contract=((1,), (0,))):
    return lax.dot_general(a, b, (contract, ((), ())), preferred_element_type=F32)


def call(body, outs, args, specs, scratch=(), flops=0, nbytes=0):
    return pl.pallas_call(
        body,
        out_shape=outs,
        in_specs=specs,
        out_specs=[VMEM] * len(outs),
        scratch_shapes=list(scratch),
        cost_estimate=pl.CostEstimate(flops=flops, bytes_accessed=nbytes, transcendentals=0),
        compiler_params=pltpu.CompilerParams(vmem_limit_bytes=24 * 1024 * 1024),
    )(*args)


def pick_body(order_ref, feat_ref, out_ref):
    rows = feat_ref.shape[0]
    feat = feat_ref[...]
    lane = lax.broadcasted_iota(jnp.int32, (ROWS, rows), 1).astype(F32)
    for k in range(rows // ROWS):
        mine = slice(k * ROWS, (k + 1) * ROWS)
        row = order_ref[:, mine].astype(F32)
        col = jnp.transpose(jnp.broadcast_to(row, (ROWS, ROWS)))
        wide = jnp.concatenate([col] * (rows // ROWS), axis=1)
        hot = jnp.where(wide == lane, 1.0, 0.0).astype(BF16)
        out_ref[mine, :] = dot(hot, feat).astype(BF16)


def total_body(back_ref, out_ref):
    share = out_ref.shape[0]
    out_ref[...] = jnp.sum(back_ref[:, back_ref.shape[1] - share :, :].astype(F32), axis=0).astype(BF16)


def place_body(order_ref, back_ref, out_ref):
    rows, width = out_ref.shape
    per_peer = rows // back_ref.shape[0]
    back = back_ref[:, :per_peer, :].reshape(rows, width)
    order = jnp.broadcast_to(order_ref[...], (ROWS, rows))
    for k in range(rows // ROWS):
        mine = slice(k * ROWS, (k + 1) * ROWS)
        row = lax.broadcasted_iota(jnp.int32, (ROWS, rows), 0) + k * ROWS
        hot = jnp.where(order == row, 1.0, 0.0).astype(BF16)
        out_ref[mine, :] = dot(hot, back).astype(BF16)


def window_body(cnt_ref, tgt_ref, nodes_ref, vals_ref, w_edge_ref, prev_ref, own_ref, next_ref, win):
    blocks, slots = vals_ref.shape[0], vals_ref.shape[1]
    base = blocks - RIM
    trash = blocks + 2 * RIM
    win[...] = jnp.zeros_like(win)
    w_edge = w_edge_ref[...]
    for c in range(blocks):
        pre = dot(nodes_ref[c * ROWS : (c + 1) * ROWS, :], w_edge)
        message = (pre * jax.nn.sigmoid(pre)).astype(BF16)
        contrib = dot(vals_ref[c].reshape(slots * ROWS, ROWS), message)
        for s in range(slots):
            to = jnp.where(s < cnt_ref[c], tgt_ref[c, s] - base, trash)
            win[to] += contrib[s * ROWS : (s + 1) * ROWS, :]
    for b in range(RIM):
        prev_ref[b * ROWS : (b + 1) * ROWS, :] = win[b].astype(BF16)
        next_ref[b * ROWS : (b + 1) * ROWS, :] = win[RIM + blocks + b].astype(BF16)
    for b in range(blocks):
        own_ref[b * ROWS : (b + 1) * ROWS, :] = win[RIM + b].astype(BF16)


def node_body(
    nodes_ref, own_ref, from_prev_ref, from_next_ref, cot_ref, w_node_ref,
    out_ref, agg_ref, d_node_ref, d_nodes1_ref, d_agg_ref,
):
    rows, width = nodes_ref.shape
    w_node = w_node_ref[...]
    step = RIM * ROWS
    for k in range(rows // step):
        mine = slice(k * step, (k + 1) * step)
        agg = own_ref[mine, :].astype(F32)
        if k == 0:
            agg = agg + from_prev_ref[...].astype(F32)
        if k == rows // step - 1:
            agg = agg + from_next_ref[...].astype(F32)
        agg = agg.astype(BF16)
        agg_ref[mine, :] = agg
        nodes = nodes_ref[mine, :]
        pre = dot(nodes, w_node[:width]) + dot(agg, w_node[width:])
        sig = jax.nn.sigmoid(pre)
        out_ref[mine, :] = (nodes.astype(F32) + pre * sig).astype(BF16)
        gout = cot_ref[mine, :].astype(F32)
        d_node = (gout * (sig * (1.0 + pre * (1.0 - sig)))).astype(BF16)
        d_node_ref[mine, :] = d_node
        back = dot(d_node, w_node, ((1,), (1,)))
        d_nodes1_ref[mine, :] = gout + back[:, :width]
        d_agg_ref[mine, :] = back[:, width:].astype(BF16)


def grad_node_body(scale, nodes_ref, agg_ref, d_node_ref, out_ref):
    width = nodes_ref.shape[1]
    d_node = d_node_ref[...]
    out_ref[:width, :] = (dot(nodes_ref[...], d_node, ((0,), (0,))) * scale).astype(BF16)
    out_ref[width:, :] = (dot(agg_ref[...], d_node, ((0,), (0,))) * scale).astype(BF16)


def edge_body(
    scale, cnt_ref, tgt_ref, nodes_ref, vals_ref, w_edge_ref, d_agg_ref, prev_ref, next_ref, d_nodes1_ref, g_node_ref,
    back_ref, win, d_edge_ref, grads_ref,
):
    blocks, slots = vals_ref.shape[0], vals_ref.shape[1]
    base = blocks - RIM
    dead = blocks + 2 * RIM
    for b in range(RIM):
        win[b] = prev_ref[b * ROWS : (b + 1) * ROWS, :]
        win[RIM + blocks + b] = next_ref[b * ROWS : (b + 1) * ROWS, :]
    for b in range(blocks):
        win[RIM + b] = d_agg_ref[b * ROWS : (b + 1) * ROWS, :]
    win[dead] = jnp.zeros(win.shape[1:], BF16)
    w_edge = w_edge_ref[...]
    peers = back_ref.shape[0]
    per_peer = nodes_ref.shape[0] // peers
    share = back_ref.shape[1] - per_peer
    for c in range(blocks):
        mine = slice(c * ROWS, (c + 1) * ROWS)
        picked = []
        for s in range(slots):
            at = jnp.where(s < cnt_ref[c], tgt_ref[c, s] - base, dead)
            picked.append(win[at])
        picked = jnp.concatenate(picked, axis=0)
        d_message = dot(vals_ref[c].reshape(slots * ROWS, ROWS), picked, ((0,), (0,)))
        pre = dot(nodes_ref[mine, :], w_edge)
        d_edge = (d_message.astype(BF16).astype(F32) * dsilu(pre)).astype(BF16)
        d_edge_ref[mine, :] = d_edge
        d_nodes = (d_nodes1_ref[mine, :] + dot(d_edge, w_edge, ((1,), (1,)))).astype(BF16)
        for p in range(ROWS // per_peer):
            back_ref[c * (ROWS // per_peer) + p, :per_peer, :] = d_nodes[p * per_peer : (p + 1) * per_peer, :]
    width = w_edge.shape[0]
    grads_ref[:width, :] = (dot(nodes_ref[...], d_edge_ref[...], ((0,), (0,))) * scale).astype(BF16)
    grads_ref[width:, :] = g_node_ref[...]
    for j in range(peers):
        back_ref[j, per_peer:, :] = grads_ref[j * share : (j + 1) * share, :]


def shards(features, send_order, adj_count, adj_target, adj_vals, w_edge, w_node, cotangent):
    ndom = lax.axis_size("dom")
    rows, width = features.shape[1:]
    per_peer = rows // ndom
    blocks, slots = adj_vals.shape[:2]
    rim = RIM * ROWS
    scale = 1.0 / math.sqrt(float(lax.axis_size("dp") * rows * ndom))
    tall = jax.ShapeDtypeStruct((rows, width), BF16)
    tall_f = jax.ShapeDtypeStruct((rows, width), F32)
    edge = jax.ShapeDtypeStruct((rim, width), BF16)
    unit = rows * width * 2

    (picked,) = call(
        pick_body, [tall], (send_order, features[0]), [VMEM, VMEM], flops=2 * rows * rows * width, nbytes=2 * unit
    )
    nodes = lax.all_to_all(
        picked.reshape(ndom, per_peer, width), "dom", split_axis=0, concat_axis=0, tiled=True
    ).reshape(rows, width)
    send_prev, own, send_next = call(
        window_body,
        [edge, tall, edge],
        (adj_count, adj_target, nodes, adj_vals, w_edge),
        [SMEM, SMEM, VMEM, VMEM, VMEM],
        [pltpu.VMEM((blocks + 2 * RIM + 1, ROWS, width), F32)],
        flops=2 * rows * width * (width + slots * ROWS),
        nbytes=4 * unit,
    )
    from_next = passed_along(send_prev, "dom", -1)
    from_prev = passed_along(send_next, "dom", 1)
    node_out, agg, d_node, d_nodes1, d_agg = call(
        node_body,
        [tall, tall, tall, tall_f, tall],
        (nodes, own, from_prev, from_next, cotangent[0], w_node),
        [VMEM] * 6,
        flops=8 * rows * width * width,
        nbytes=8 * unit,
    )
    prev_rows = passed_along(d_agg[rows - rim :], "dom", 1)
    next_rows = passed_along(d_agg[:rim], "dom", -1)
    (local_node,) = call(
        functools.partial(grad_node_body, scale),
        [jax.ShapeDtypeStruct((2 * width, width), BF16)],
        (nodes, agg, d_node),
        [VMEM] * 3,
        flops=4 * rows * width * width,
        nbytes=3 * unit,
    )
    share = 3 * width // ndom
    (back,) = call(
        functools.partial(edge_body, scale),
        [jax.ShapeDtypeStruct((ndom, per_peer + share, width), BF16)],
        (adj_count, adj_target, nodes, adj_vals, w_edge, d_agg, prev_rows, next_rows, d_nodes1, local_node),
        [SMEM, SMEM] + [VMEM] * 8,
        [
            pltpu.VMEM((blocks + 2 * RIM + 1, ROWS, width), BF16),
            pltpu.VMEM((rows, width), BF16),
            pltpu.VMEM((3 * width, width), BF16),
        ],
        flops=2 * rows * width * (3 * width + slots * ROWS),
        nbytes=6 * unit,
    )
    back = lax.all_to_all(back, "dom", split_axis=0, concat_axis=0, tiled=True)
    (part,) = call(total_body, [jax.ShapeDtypeStruct((share, width), BF16)], (back,), [VMEM], nbytes=unit)
    part = summed_over(part, "dp")
    grads = lax.all_to_all(
        jnp.broadcast_to(part[None], (ndom, share, width)), "dom", split_axis=0, concat_axis=0, tiled=True
    )
    (grad_brick,) = call(
        place_body, [tall], (send_order, back), [VMEM, VMEM], flops=2 * rows * rows * width, nbytes=2 * unit
    )
    grads = grads.reshape(ndom * share, width).astype(F32)
    grad_edge, grad_node = grads[:width], grads[width:]
    return (node_out[None], grad_brick[None], grad_edge, grad_node)


def solution(mesh):
    in_specs = (
        P("dp", "dom", None),
        P("dom", None),
        P("dom"),
        P("dom", None),
        P("dom", None, None, None),
        P(),
        P(),
        P("dp", "dom", None),
    )
    out_specs = (P("dp", "dom", None), P("dp", "dom", None), P(), P())
    return jax.shard_map(shards, mesh=mesh, in_specs=in_specs, out_specs=out_specs, check_vma=False)
```

```python
import functools
import math

import jax
import jax.numpy as jnp
from jax import lax
from jax.experimental import pallas as pl
from jax.experimental.pallas import tpu as pltpu
from jax.sharding import PartitionSpec as P

ROWS = 128
RIM = 2
ANY = pl.BlockSpec(memory_space=pl.ANY)
VMEM = pl.BlockSpec(memory_space=pltpu.VMEM)
SMEM = pl.BlockSpec(memory_space=pltpu.SMEM)
BF16 = jnp.bfloat16
F32 = jnp.float32
MIB = 1024 * 1024


def swapped(x, axis, mask):
    peers = lax.axis_size(axis)
    return lax.ppermute(x, axis, [(i, i ^ mask) for i in range(peers)])


def swapped_across(x, axis):
    peers = lax.axis_size(axis)
    return lax.ppermute(x, axis, [(i, (i + 1 if i % 2 else i - 1) % peers) for i in range(peers)])


def dot(a, b, contract=((1,), (0,))):
    return lax.dot_general(a, b, (contract, ((), ())), preferred_element_type=F32)


def shape(*dims, dtype=BF16):
    return jax.ShapeDtypeStruct(dims, dtype)


def call(body, outs, args, specs=None, scratch=(), flops=0, nbytes=0, limit=24 * MIB):
    return pl.pallas_call(
        body,
        out_shape=outs,
        in_specs=specs or [VMEM] * len(args),
        out_specs=[VMEM] * len(outs),
        scratch_shapes=list(scratch),
        cost_estimate=pl.CostEstimate(flops=flops, bytes_accessed=nbytes, transcendentals=0),
        compiler_params=pltpu.CompilerParams(vmem_limit_bytes=limit),
    )(*args)


def pick_body(order_hbm, feat_hbm, out_ref, order_ref, feat_ref, hot_ref, order_sem, feat_sem):
    rows = feat_ref.shape[0]
    load_order = pltpu.make_async_copy(order_hbm, order_ref, order_sem)
    load_feat = pltpu.make_async_copy(feat_hbm, feat_ref, feat_sem)
    load_order.start()
    load_feat.start()
    lane = lax.broadcasted_iota(jnp.int32, (ROWS, rows), 1).astype(F32)
    load_order.wait()
    for k in range(rows // ROWS):
        mine = slice(k * ROWS, (k + 1) * ROWS)
        row = order_ref[:, mine].astype(F32)
        col = jnp.transpose(jnp.broadcast_to(row, (ROWS, ROWS)))
        wide = jnp.concatenate([col] * (rows // ROWS), axis=1)
        hot_ref[mine, :] = jnp.where(wide == lane, 1.0, 0.0).astype(BF16)
    load_feat.wait()
    out_ref[...] = dot(hot_ref[...], feat_ref[...]).astype(BF16)


def place_body(order_ref, back_ref, out_ref):
    rows = back_ref.shape[0]
    back = back_ref[...]
    order = jnp.broadcast_to(order_ref[...], (ROWS, rows))
    for k in range(rows // ROWS):
        mine = slice(k * ROWS, (k + 1) * ROWS)
        row = lax.broadcasted_iota(jnp.int32, (ROWS, rows), 0) + k * ROWS
        hot = jnp.where(order == row, 1.0, 0.0).astype(BF16)
        out_ref[mine, :] = dot(hot, back).astype(BF16)


def window_body(cnt_ref, tgt_ref, nodes_ref, vals_ref, w_edge_ref, near_ref, far_ref, own_ref, win):
    blocks, slots = vals_ref.shape[0], vals_ref.shape[1]
    base = blocks - RIM
    trash = blocks + 2 * RIM
    odd = lax.rem(lax.axis_index("dom"), 2)
    win[...] = jnp.zeros_like(win)
    w_edge = w_edge_ref[...]
    for c in range(blocks):
        pre = dot(nodes_ref[c * ROWS : (c + 1) * ROWS, :], w_edge)
        message = (pre * jax.nn.sigmoid(pre)).astype(BF16)
        contrib = dot(vals_ref[c].reshape(slots * ROWS, ROWS), message)
        for s in range(slots):
            to = jnp.where(s < cnt_ref[c], tgt_ref[c, s] - base, trash)
            win[to] += contrib[s * ROWS : (s + 1) * ROWS, :]
    for b in range(RIM):
        rows = slice(b * ROWS, (b + 1) * ROWS)
        near_ref[rows, :] = win[jnp.where(odd == 1, b, RIM + blocks + b)].astype(BF16)
        far_ref[rows, :] = win[jnp.where(odd == 1, RIM + blocks + b, b)].astype(BF16)
    for b in range(blocks):
        own_ref[b * ROWS : (b + 1) * ROWS, :] = win[RIM + b].astype(BF16)


def node_body(
    nodes_ref, own_ref, near_in_ref, far_in_ref, cot_ref, w_node_ref,
    out_ref, agg_ref, d_node_ref, d_nodes1_ref, d_agg_ref, near_ref, far_ref,
):
    rows, width = nodes_ref.shape
    odd = lax.rem(lax.axis_index("dom"), 2) == 1
    near = near_in_ref[...].astype(F32)
    far = far_in_ref[...].astype(F32)
    w_node = w_node_ref[...]
    step = RIM * ROWS
    last = rows // step - 1
    rims = []
    for k in [0, last] + list(range(1, last)):
        mine = slice(k * step, (k + 1) * step)
        agg = own_ref[mine, :].astype(F32)
        if k == 0:
            agg = agg + jnp.where(odd, near, far)
        if k == last:
            agg = agg + jnp.where(odd, far, near)
        agg = agg.astype(BF16)
        agg_ref[mine, :] = agg
        nodes = nodes_ref[mine, :]
        pre = dot(nodes, w_node[:width]) + dot(agg, w_node[width:])
        sig = jax.nn.sigmoid(pre)
        out_ref[mine, :] = (nodes.astype(F32) + pre * sig).astype(BF16)
        gout = cot_ref[mine, :].astype(F32)
        d_node = (gout * (sig * (1.0 + pre * (1.0 - sig)))).astype(BF16)
        d_node_ref[mine, :] = d_node
        back = dot(d_node, w_node, ((1,), (1,)))
        d_nodes1_ref[mine, :] = gout + back[:, :width]
        d_agg_ref[mine, :] = back[:, width:].astype(BF16)
        rims.append(back[:, width:])
    near_ref[...] = jnp.where(odd, rims[0], rims[1]).astype(BF16)
    far_ref[...] = jnp.where(odd, rims[1], rims[0]).astype(BF16)


def grad_node_body(scale, nodes_ref, agg_ref, d_node_ref, out_ref):
    width = nodes_ref.shape[1]
    d_node = d_node_ref[...]
    out_ref[:width, :] = dot(nodes_ref[...], d_node, ((0,), (0,))) * scale
    out_ref[width:, :] = dot(agg_ref[...], d_node, ((0,), (0,))) * scale


def edge_body(
    scale, cnt_ref, tgt_ref, nodes_ref, vals_ref, w_edge_ref, d_agg_ref, near_ref, far_ref, d_nodes1_ref, g_node_ref,
    back_ref, grads_ref, win, d_edge_ref,
):
    blocks, slots = vals_ref.shape[0], vals_ref.shape[1]
    base = blocks - RIM
    dead = blocks + 2 * RIM
    odd = lax.rem(lax.axis_index("dom"), 2)
    for b in range(RIM):
        rows = slice(b * ROWS, (b + 1) * ROWS)
        win[jnp.where(odd == 1, b, RIM + blocks + b)] = near_ref[rows, :]
        win[jnp.where(odd == 1, RIM + blocks + b, b)] = far_ref[rows, :]
    for b in range(blocks):
        win[RIM + b] = d_agg_ref[b * ROWS : (b + 1) * ROWS, :]
    win[dead] = jnp.zeros(win.shape[1:], BF16)
    w_edge = w_edge_ref[...]
    width = w_edge.shape[0]
    for c in range(blocks):
        mine = slice(c * ROWS, (c + 1) * ROWS)
        picked = []
        for s in range(slots):
            at = jnp.where(s < cnt_ref[c], tgt_ref[c, s] - base, dead)
            picked.append(win[at])
        picked = jnp.concatenate(picked, axis=0)
        d_message = dot(vals_ref[c].reshape(slots * ROWS, ROWS), picked, ((0,), (0,)))
        pre = dot(nodes_ref[mine, :], w_edge)
        sig = jax.nn.sigmoid(pre)
        d_edge = (d_message.astype(BF16).astype(F32) * (sig * (1.0 + pre * (1.0 - sig)))).astype(BF16)
        d_edge_ref[mine, :] = d_edge
        back_ref[mine, :] = (d_nodes1_ref[mine, :] + dot(d_edge, w_edge, ((1,), (1,)))).astype(BF16)
    grads_ref[:width, :] = dot(nodes_ref[...], d_edge_ref[...], ((0,), (0,))) * scale
    grads_ref[width:, :] = g_node_ref[...]


def halves_body(grads_ref, keep_ref, send_ref):
    half = grads_ref.shape[1] // 2
    first = lax.axis_index("dp") == 0
    left = grads_ref[:, :half]
    right = grads_ref[:, half:]
    keep_ref[...] = jnp.where(first, left, right)
    send_ref[...] = jnp.where(first, right, left).astype(BF16)


def place_in(group):
    return lax.rem(lax.axis_index("dom"), 4) if group == 0 else lax.div(lax.axis_index("dom"), 4)


def quarter(index, mask, size):
    return pl.ds(pl.multiple_of((index ^ mask) * size, 16), size)


def split_body(group, *refs):
    keep_ref, recv_refs = refs[0], refs[1 : -5]
    out_ref, send_refs, total = refs[-5], refs[-4:-1], refs[-1]
    value = keep_ref[...]
    for recv in recv_refs:
        value = value + recv[...].astype(F32)
    total[...] = value
    size = total.shape[0] // 4
    at = place_in(group)
    out_ref[...] = total[quarter(at, 0, size), :]
    for k, send in enumerate(send_refs):
        send[...] = total[quarter(at, k + 1, size), :].astype(BF16)


def total_body(*refs):
    value = refs[0][...]
    for recv in refs[1:-1]:
        value = value + recv[...].astype(F32)
    refs[-1][...] = value.astype(BF16)


def join_body(group, *refs):
    size = refs[0].shape[0]
    at = place_in(group)
    for k, piece in enumerate(refs[:4]):
        refs[4][quarter(at, k, size), :] = piece[...]


def finish_body(mine_ref, other_ref, edge_ref, node_ref):
    width = edge_ref.shape[0]
    first = lax.axis_index("dp") == 0
    mine = mine_ref[...].astype(F32)
    other = other_ref[...].astype(F32)
    left = jnp.where(first, mine, other)
    right = jnp.where(first, other, mine)
    half = left.shape[1]
    edge_ref[:, :half] = left[:width]
    edge_ref[:, half:] = right[:width]
    node_ref[:, :half] = left[width:]
    node_ref[:, half:] = right[width:]


def reduced(grads):
    rows, width = grads.shape
    half = width // 2
    masks = [[1, 2, 3], [4, 8, 12]]
    keep, send = call(halves_body, [shape(rows, half, dtype=F32), shape(rows, half)], (grads,))
    recv = [swapped(send, "dp", 1)]
    size = rows
    for group in range(2):
        keep, *send = call(
            functools.partial(split_body, group),
            [shape(size // 4, half, dtype=F32)] + [shape(size // 4, half)] * 3,
            (keep, *recv),
            scratch=[pltpu.VMEM((size, half), F32)],
        )
        size //= 4
        recv = [swapped(piece, "dom", mask) for piece, mask in zip(send, masks[group])]
    (mine,) = call(total_body, [shape(size, half)], (keep, *recv))
    for group in (1, 0):
        recv = [swapped(mine, "dom", mask) for mask in masks[group]]
        size *= 4
        (mine,) = call(functools.partial(join_body, group), [shape(size, half)], (mine, *recv))
    other = swapped(mine, "dp", 1)
    return call(finish_body, [shape(width, width, dtype=F32), shape(rows - width, width, dtype=F32)], (mine, other))


def shards(features, send_order, adj_count, adj_target, adj_vals, w_edge, w_node, cotangent):
    ndp = lax.axis_size("dp")
    ndom = lax.axis_size("dom")
    rows, width = features.shape[1:]
    per_peer = rows // ndom
    blocks, slots = adj_vals.shape[:2]
    rim = RIM * ROWS
    scale = 1.0 / math.sqrt(float(ndp * rows * ndom))
    tall = shape(rows, width)
    tall_f = shape(rows, width, dtype=F32)
    edge = shape(rim, width)
    unit = rows * width * 2

    (picked,) = call(
        pick_body,
        [tall],
        (send_order, features[0]),
        [ANY, ANY],
        [
            pltpu.VMEM((1, rows), jnp.int32),
            pltpu.VMEM((rows, width), BF16),
            pltpu.VMEM((rows, rows), BF16),
            pltpu.SemaphoreType.DMA,
            pltpu.SemaphoreType.DMA,
        ],
        flops=2 * rows * rows * width,
        nbytes=2 * unit,
        limit=56 * MIB,
    )
    nodes = lax.all_to_all(
        picked.reshape(ndom, per_peer, width), "dom", split_axis=0, concat_axis=0, tiled=True
    ).reshape(rows, width)
    near, far, own = call(
        window_body,
        [edge, edge, tall],
        (adj_count, adj_target, nodes, adj_vals, w_edge),
        [SMEM, SMEM, VMEM, VMEM, VMEM],
        [pltpu.VMEM((blocks + 2 * RIM + 1, ROWS, width), F32)],
        flops=2 * rows * width * (width + slots * ROWS),
        nbytes=4 * unit,
    )
    far = swapped_across(far, "dom")
    near = swapped(near, "dom", 1)
    node_out, agg, d_node, d_nodes1, d_agg, near, far = call(
        node_body,
        [tall, tall, tall, tall_f, tall, edge, edge],
        (nodes, own, near, far, cotangent[0], w_node),
        flops=8 * rows * width * width,
        nbytes=8 * unit,
    )
    far = swapped_across(far, "dom")
    near = swapped(near, "dom", 1)
    (local_node,) = call(
        functools.partial(grad_node_body, scale),
        [shape(2 * width, width, dtype=F32)],
        (nodes, agg, d_node),
        flops=4 * rows * width * width,
        nbytes=3 * unit,
    )
    back, grads = call(
        functools.partial(edge_body, scale),
        [tall, shape(3 * width, width, dtype=F32)],
        (adj_count, adj_target, nodes, adj_vals, w_edge, d_agg, near, far, d_nodes1, local_node),
        [SMEM, SMEM] + [VMEM] * 8,
        [pltpu.VMEM((blocks + 2 * RIM + 1, ROWS, width), BF16), pltpu.VMEM((rows, width), BF16)],
        flops=2 * rows * width * (3 * width + slots * ROWS),
        nbytes=6 * unit,
    )
    back = lax.all_to_all(
        back.reshape(ndom, per_peer, width), "dom", split_axis=0, concat_axis=0, tiled=True
    ).reshape(rows, width)
    if ndp == 2 and ndom == 16:
        grad_edge, grad_node = reduced(grads)
    else:
        grads = lax.psum(grads, ("dp", "dom"))
        grad_edge, grad_node = grads[:width], grads[width:]
    (grad_brick,) = call(place_body, [tall], (send_order, back), flops=2 * rows * rows * width, nbytes=2 * unit)
    return (node_out[None], grad_brick[None], grad_edge, grad_node)


def solution(mesh):
    in_specs = (
        P("dp", "dom", None),
        P("dom", None),
        P("dom"),
        P("dom", None),
        P("dom", None, None, None),
        P(),
        P(),
        P("dp", "dom", None),
    )
    out_specs = (P("dp", "dom", None), P("dp", "dom", None), P(), P())
    return jax.shard_map(shards, mesh=mesh, in_specs=in_specs, out_specs=out_specs, check_vma=False)
```

```python
import functools
import math

import jax
import jax.numpy as jnp
from jax import lax
from jax.experimental import pallas as pl
from jax.experimental.pallas import tpu as pltpu
from jax.sharding import PartitionSpec as P

ROWS = 128
RIM = 2
ANY = pl.BlockSpec(memory_space=pl.ANY)
VMEM = pl.BlockSpec(memory_space=pltpu.VMEM)
SMEM = pl.BlockSpec(memory_space=pltpu.SMEM)
BF16 = jnp.bfloat16
F32 = jnp.float32
MIB = 1024 * 1024


def swapped(x, axis, mask):
    peers = lax.axis_size(axis)
    return lax.ppermute(x, axis, [(i, i ^ mask) for i in range(peers)])


def swapped_across(x, axis):
    peers = lax.axis_size(axis)
    return lax.ppermute(x, axis, [(i, (i + 1 if i % 2 else i - 1) % peers) for i in range(peers)])


def dot(a, b, contract=((1,), (0,))):
    return lax.dot_general(a, b, (contract, ((), ())), preferred_element_type=F32)


def shape(*dims, dtype=BF16):
    return jax.ShapeDtypeStruct(dims, dtype)


def call(body, outs, args, specs=None, scratch=(), flops=0, nbytes=0, limit=24 * MIB):
    return pl.pallas_call(
        body,
        out_shape=outs,
        in_specs=specs or [VMEM] * len(args),
        out_specs=[VMEM] * len(outs),
        scratch_shapes=list(scratch),
        cost_estimate=pl.CostEstimate(flops=flops, bytes_accessed=nbytes, transcendentals=0),
        compiler_params=pltpu.CompilerParams(vmem_limit_bytes=limit),
    )(*args)


def pick_body(order_hbm, feat_hbm, out_ref, order_ref, feat_ref, hot_ref, order_sem, feat_sem):
    rows = feat_ref.shape[0]
    load_order = pltpu.make_async_copy(order_hbm, order_ref, order_sem)
    load_feat = pltpu.make_async_copy(feat_hbm, feat_ref, feat_sem)
    load_order.start()
    load_feat.start()
    lane = lax.broadcasted_iota(jnp.int32, (ROWS, rows), 1).astype(F32)
    load_order.wait()
    for k in range(rows // ROWS):
        mine = slice(k * ROWS, (k + 1) * ROWS)
        row = order_ref[:, mine].astype(F32)
        col = jnp.transpose(jnp.broadcast_to(row, (ROWS, ROWS)))
        wide = jnp.concatenate([col] * (rows // ROWS), axis=1)
        hot_ref[mine, :] = jnp.where(wide == lane, 1.0, 0.0).astype(BF16)
    load_feat.wait()
    out_ref[...] = dot(hot_ref[...], feat_ref[...]).astype(BF16)


def place_body(order_ref, back_ref, out_ref):
    rows = back_ref.shape[0]
    back = back_ref[...]
    order = jnp.broadcast_to(order_ref[...], (ROWS, rows))
    for k in range(rows // ROWS):
        mine = slice(k * ROWS, (k + 1) * ROWS)
        row = lax.broadcasted_iota(jnp.int32, (ROWS, rows), 0) + k * ROWS
        hot = jnp.where(order == row, 1.0, 0.0).astype(BF16)
        out_ref[mine, :] = dot(hot, back).astype(BF16)


def window_body(cnt_ref, tgt_ref, nodes_ref, vals_ref, w_edge_ref, near_ref, far_ref, own_ref, win):
    blocks, slots = vals_ref.shape[0], vals_ref.shape[1]
    base = blocks - RIM
    trash = blocks + 2 * RIM
    odd = lax.rem(lax.axis_index("dom"), 2)
    win[...] = jnp.zeros_like(win)
    w_edge = w_edge_ref[...]
    for c in range(blocks):
        pre = dot(nodes_ref[c * ROWS : (c + 1) * ROWS, :], w_edge)
        message = (pre * jax.nn.sigmoid(pre)).astype(BF16)
        contrib = dot(vals_ref[c].reshape(slots * ROWS, ROWS), message)
        for s in range(slots):
            to = jnp.where(s < cnt_ref[c], tgt_ref[c, s] - base, trash)
            win[to] += contrib[s * ROWS : (s + 1) * ROWS, :]
    for b in range(RIM):
        rows = slice(b * ROWS, (b + 1) * ROWS)
        near_ref[rows, :] = win[jnp.where(odd == 1, b, RIM + blocks + b)].astype(BF16)
        far_ref[rows, :] = win[jnp.where(odd == 1, RIM + blocks + b, b)].astype(BF16)
    for b in range(blocks):
        own_ref[b * ROWS : (b + 1) * ROWS, :] = win[RIM + b].astype(BF16)


def node_body(
    nodes_ref, own_ref, near_in_ref, far_in_ref, cot_ref, w_node_ref,
    out_ref, agg_ref, d_node_ref, d_nodes1_ref, d_agg_ref, near_ref, far_ref,
):
    rows, width = nodes_ref.shape
    odd = lax.rem(lax.axis_index("dom"), 2) == 1
    near = near_in_ref[...].astype(F32)
    far = far_in_ref[...].astype(F32)
    w_node = w_node_ref[...]
    step = RIM * ROWS
    last = rows // step - 1
    rims = []
    for k in [0, last] + list(range(1, last)):
        mine = slice(k * step, (k + 1) * step)
        agg = own_ref[mine, :].astype(F32)
        if k == 0:
            agg = agg + jnp.where(odd, near, far)
        if k == last:
            agg = agg + jnp.where(odd, far, near)
        agg = agg.astype(BF16)
        agg_ref[mine, :] = agg
        nodes = nodes_ref[mine, :]
        pre = dot(nodes, w_node[:width]) + dot(agg, w_node[width:])
        sig = jax.nn.sigmoid(pre)
        out_ref[mine, :] = (nodes.astype(F32) + pre * sig).astype(BF16)
        gout = cot_ref[mine, :].astype(F32)
        d_node = (gout * (sig * (1.0 + pre * (1.0 - sig)))).astype(BF16)
        d_node_ref[mine, :] = d_node
        back = dot(d_node, w_node, ((1,), (1,)))
        d_nodes1_ref[mine, :] = gout + back[:, :width]
        d_agg_ref[mine, :] = back[:, width:].astype(BF16)
        rims.append(back[:, width:])
    near_ref[...] = jnp.where(odd, rims[0], rims[1]).astype(BF16)
    far_ref[...] = jnp.where(odd, rims[1], rims[0]).astype(BF16)


def grad_node_body(scale, nodes_ref, agg_ref, d_node_ref, out_ref):
    width = nodes_ref.shape[1]
    d_node = d_node_ref[...]
    out_ref[:width, :] = (dot(nodes_ref[...], d_node, ((0,), (0,))) * scale).astype(BF16)
    out_ref[width:, :] = (dot(agg_ref[...], d_node, ((0,), (0,))) * scale).astype(BF16)


def edge_body(
    scale, cnt_ref, tgt_ref, nodes_ref, vals_ref, w_edge_ref, d_agg_ref, near_ref, far_ref, d_nodes1_ref, g_node_ref,
    back_ref, grads_ref, win, d_edge_ref,
):
    blocks, slots = vals_ref.shape[0], vals_ref.shape[1]
    base = blocks - RIM
    dead = blocks + 2 * RIM
    odd = lax.rem(lax.axis_index("dom"), 2)
    for b in range(RIM):
        rows = slice(b * ROWS, (b + 1) * ROWS)
        win[jnp.where(odd == 1, b, RIM + blocks + b)] = near_ref[rows, :]
        win[jnp.where(odd == 1, RIM + blocks + b, b)] = far_ref[rows, :]
    for b in range(blocks):
        win[RIM + b] = d_agg_ref[b * ROWS : (b + 1) * ROWS, :]
    win[dead] = jnp.zeros(win.shape[1:], BF16)
    w_edge = w_edge_ref[...]
    width = w_edge.shape[0]
    for c in range(blocks):
        mine = slice(c * ROWS, (c + 1) * ROWS)
        picked = []
        for s in range(slots):
            at = jnp.where(s < cnt_ref[c], tgt_ref[c, s] - base, dead)
            picked.append(win[at])
        picked = jnp.concatenate(picked, axis=0)
        d_message = dot(vals_ref[c].reshape(slots * ROWS, ROWS), picked, ((0,), (0,)))
        pre = dot(nodes_ref[mine, :], w_edge)
        sig = jax.nn.sigmoid(pre)
        d_edge = (d_message.astype(BF16).astype(F32) * (sig * (1.0 + pre * (1.0 - sig)))).astype(BF16)
        d_edge_ref[mine, :] = d_edge
        back_ref[mine, :] = (d_nodes1_ref[mine, :] + dot(d_edge, w_edge, ((1,), (1,)))).astype(BF16)
    all_grads = [
        (dot(nodes_ref[...], d_edge_ref[...], ((0,), (0,))) * scale).astype(BF16),
        g_node_ref[...],
    ]
    if len(grads_ref.shape) == 2:
        grads_ref[:width, :], grads_ref[width:, :] = all_grads
        return
    share, lanes = grads_ref.shape[1:]
    peers = 3 * width // share
    all_grads = jnp.concatenate(all_grads, axis=0)
    for p in range(grads_ref.shape[0]):
        row = p % peers * share
        grads_ref[p] = all_grads[row : row + share, p // peers * lanes : (p // peers + 1) * lanes]


def share_body(parts_ref, out_ref):
    total = jnp.sum(parts_ref[...].astype(F32), axis=0).astype(BF16)
    out_ref[...] = jnp.broadcast_to(total[None], out_ref.shape)


def finish_body(parts_ref, edge_ref, node_ref):
    width = edge_ref.shape[0]
    share = parts_ref.shape[1]
    lanes = parts_ref.shape[2]
    peers = (width + node_ref.shape[0]) // share
    for p in range(parts_ref.shape[0]):
        column = slice(p // peers * lanes, (p // peers + 1) * lanes)
        row = p % peers * share
        value = parts_ref[p].astype(F32)
        split = min(max(width - row, 0), share)
        if split > 0:
            edge_ref[row : row + split, column] = value[:split]
        if split < share:
            node_ref[row + split - width : row + share - width, column] = value[split:]


def shards(features, send_order, adj_count, adj_target, adj_vals, w_edge, w_node, cotangent):
    ndp = lax.axis_size("dp")
    ndom = lax.axis_size("dom")
    rows, width = features.shape[1:]
    per_peer = rows // ndom
    blocks, slots = adj_vals.shape[:2]
    rim = RIM * ROWS
    scale = 1.0 / math.sqrt(float(ndp * rows * ndom))
    tall = shape(rows, width)
    tall_f = shape(rows, width, dtype=F32)
    edge = shape(rim, width)
    unit = rows * width * 2
    share = 3 * width // ndom
    tiled = share % 16 == 0 and width // ndp % 128 == 0

    (picked,) = call(
        pick_body,
        [tall],
        (send_order, features[0]),
        [ANY, ANY],
        [
            pltpu.VMEM((1, rows), jnp.int32),
            pltpu.VMEM((rows, width), BF16),
            pltpu.VMEM((rows, rows), BF16),
            pltpu.SemaphoreType.DMA,
            pltpu.SemaphoreType.DMA,
        ],
        flops=2 * rows * rows * width,
        nbytes=2 * unit,
        limit=56 * MIB,
    )
    nodes = lax.all_to_all(
        picked.reshape(ndom, per_peer, width), "dom", split_axis=0, concat_axis=0, tiled=True
    ).reshape(rows, width)
    near, far, own = call(
        window_body,
        [edge, edge, tall],
        (adj_count, adj_target, nodes, adj_vals, w_edge),
        [SMEM, SMEM, VMEM, VMEM, VMEM],
        [pltpu.VMEM((blocks + 2 * RIM + 1, ROWS, width), F32)],
        flops=2 * rows * width * (width + slots * ROWS),
        nbytes=4 * unit,
    )
    far = swapped_across(far, "dom")
    near = swapped(near, "dom", 1)
    node_out, agg, d_node, d_nodes1, d_agg, near, far = call(
        node_body,
        [tall, tall, tall, tall_f, tall, edge, edge],
        (nodes, own, near, far, cotangent[0], w_node),
        flops=8 * rows * width * width,
        nbytes=8 * unit,
    )
    far = swapped_across(far, "dom")
    near = swapped(near, "dom", 1)
    (local_node,) = call(
        functools.partial(grad_node_body, scale),
        [shape(2 * width, width)],
        (nodes, agg, d_node),
        flops=4 * rows * width * width,
        nbytes=3 * unit,
    )
    back, grads = call(
        functools.partial(edge_body, scale),
        [tall, shape(ndp * ndom, share, width // ndp) if tiled else shape(3 * width, width)],
        (adj_count, adj_target, nodes, adj_vals, w_edge, d_agg, near, far, d_nodes1, local_node),
        [SMEM, SMEM] + [VMEM] * 8,
        [pltpu.VMEM((blocks + 2 * RIM + 1, ROWS, width), BF16), pltpu.VMEM((rows, width), BF16)],
        flops=2 * rows * width * (3 * width + slots * ROWS),
        nbytes=6 * unit,
    )
    if tiled:
        parts = lax.all_to_all(grads, ("dp", "dom"), split_axis=0, concat_axis=0, tiled=True)
    back = lax.all_to_all(
        back.reshape(ndom, per_peer, width), "dom", split_axis=0, concat_axis=0, tiled=True
    ).reshape(rows, width)
    if tiled:
        (shared,) = call(share_body, [shape(*parts.shape)], (parts,), nbytes=unit)
        shared = lax.all_to_all(shared, ("dp", "dom"), split_axis=0, concat_axis=0, tiled=True)
        grad_edge, grad_node = call(
            finish_body, [shape(width, width, dtype=F32), shape(2 * width, width, dtype=F32)], (shared,), nbytes=2 * unit
        )
    else:
        grads = lax.psum(grads.astype(F32), ("dp", "dom"))
        grad_edge, grad_node = grads[:width], grads[width:]
    (grad_brick,) = call(place_body, [tall], (send_order, back), flops=2 * rows * rows * width, nbytes=2 * unit)
    return (node_out[None], grad_brick[None], grad_edge, grad_node)


def solution(mesh):
    in_specs = (
        P("dp", "dom", None),
        P("dom", None),
        P("dom"),
        P("dom", None),
        P("dom", None, None, None),
        P(),
        P(),
        P("dp", "dom", None),
    )
    out_specs = (P("dp", "dom", None), P("dp", "dom", None), P(), P())
    return jax.shard_map(shards, mesh=mesh, in_specs=in_specs, out_specs=out_specs, check_vma=False)
```

```python
import functools
import math

import jax
import jax.numpy as jnp
from jax import lax
from jax.experimental import pallas as pl
from jax.experimental.pallas import tpu as pltpu
from jax.sharding import PartitionSpec as P

ROWS = 128
RIM = 2
ANY = pl.BlockSpec(memory_space=pl.ANY)
VMEM = pl.BlockSpec(memory_space=pltpu.VMEM)
SMEM = pl.BlockSpec(memory_space=pltpu.SMEM)
BF16 = jnp.bfloat16
F32 = jnp.float32
MIB = 1024 * 1024


def swapped(x, axis, mask):
    peers = lax.axis_size(axis)
    return lax.ppermute(x, axis, [(i, i ^ mask) for i in range(peers)])


def swapped_across(x, axis):
    peers = lax.axis_size(axis)
    return lax.ppermute(x, axis, [(i, (i + 1 if i % 2 else i - 1) % peers) for i in range(peers)])


def dot(a, b, contract=((1,), (0,))):
    return lax.dot_general(a, b, (contract, ((), ())), preferred_element_type=F32)


def shape(*dims, dtype=BF16):
    return jax.ShapeDtypeStruct(dims, dtype)


def call(body, outs, args, specs=None, scratch=(), flops=0, nbytes=0, limit=24 * MIB):
    return pl.pallas_call(
        body,
        out_shape=outs,
        in_specs=specs or [VMEM] * len(args),
        out_specs=[VMEM] * len(outs),
        scratch_shapes=list(scratch),
        cost_estimate=pl.CostEstimate(flops=flops, bytes_accessed=nbytes, transcendentals=0),
        compiler_params=pltpu.CompilerParams(vmem_limit_bytes=limit),
    )(*args)


def pick_body(order_hbm, feat_hbm, out_ref, order_ref, feat_ref, order_sem, feat_sem):
    rows = feat_ref.shape[0]
    load_order = pltpu.make_async_copy(order_hbm, order_ref, order_sem)
    load_feat = pltpu.make_async_copy(feat_hbm, feat_ref, feat_sem)
    load_order.start()
    load_feat.start()
    load_order.wait()
    load_feat.wait()
    feat = feat_ref[...]
    lane = lax.broadcasted_iota(jnp.int32, (ROWS, rows), 1).astype(F32)
    for k in range(rows // ROWS):
        mine = slice(k * ROWS, (k + 1) * ROWS)
        row = order_ref[:, mine].astype(F32)
        col = jnp.transpose(jnp.broadcast_to(row, (ROWS, ROWS)))
        wide = jnp.concatenate([col] * (rows // ROWS), axis=1)
        hot = jnp.where(wide == lane, 1.0, 0.0).astype(BF16)
        out_ref[mine, :] = dot(hot, feat).astype(BF16)


def build_body(cnt_ref, tgt_ref, vals_ref, a_ref, at_ref):
    blocks, slots = vals_ref.shape[:2]
    spare = blocks + 2 * RIM
    a_ref[...] = jnp.zeros_like(a_ref)
    at_ref[...] = jnp.zeros_like(at_ref)
    for c in range(blocks):
        mine = slice(c * ROWS, (c + 1) * ROWS)
        for s in range(slots):
            w = tgt_ref[c, s]
            at = jnp.where(w < blocks, w + RIM, jnp.where(w < 2 * blocks, w - blocks, w - blocks + RIM))
            at = jnp.where(s < cnt_ref[c], at, spare)
            value = vals_ref[c, s].astype(F32)
            a_ref[at, :, mine] = (a_ref[at, :, mine].astype(F32) + value).astype(BF16)
            lanes = pl.ds(pl.multiple_of(at * ROWS, ROWS), ROWS)
            at_ref[mine, lanes] = (at_ref[mine, lanes].astype(F32) + jnp.transpose(value)).astype(BF16)


def chosen(first, second):
    odd = lax.rem(lax.axis_index("dom"), 2) == 1
    return jnp.where(odd, first, second), jnp.where(odd, second, first)


def message_body(nodes_ref, a_ref, w_edge_ref, near_ref, far_ref, msg_ref):
    rows = nodes_ref.shape[0]
    rim = RIM * ROWS
    for k in range(rows // rim):
        mine = slice(k * rim, (k + 1) * rim)
        pre = dot(nodes_ref[mine, :], w_edge_ref[...])
        msg_ref[mine, :] = (pre * jax.nn.sigmoid(pre)).astype(BF16)
    blocks = rows // ROWS
    sums = dot(a_ref[blocks : blocks + 2 * RIM].reshape(2 * rim, rows), msg_ref[...])
    near, far = chosen(sums[:rim], sums[rim:])
    near_ref[...] = near.astype(BF16)
    far_ref[...] = far.astype(BF16)


def node_step(nodes, agg, gout, w_node):
    width = nodes.shape[1]
    pre = dot(nodes, w_node[:width]) + dot(agg, w_node[width:])
    sig = jax.nn.sigmoid(pre)
    out = (nodes.astype(F32) + pre * sig).astype(BF16)
    gout = gout.astype(F32)
    d_node = (gout * (sig * (1.0 + pre * (1.0 - sig)))).astype(BF16)
    back = dot(d_node, w_node, ((1,), (1,)))
    return out, d_node, gout + back[:, :width], back[:, width:].astype(BF16)


def own_body(
    nodes_ref, msg_ref, a_ref, cot_ref, w_node_ref,
    own_ref, out_ref, agg_ref, d_node_ref, d_nodes1_ref, d_agg_ref,
):
    rows, width = nodes_ref.shape
    rim = RIM * ROWS
    msg = msg_ref[...]
    for k in range(rows // rim):
        mine = slice(k * rim, (k + 1) * rim)
        window = dot(a_ref[k * RIM : (k + 1) * RIM].reshape(rim, rows), msg).astype(BF16)
        if k == 0:
            own_ref[:rim, :] = window
        elif k == rows // rim - 1:
            own_ref[rim:, :] = window
        else:
            here = slice((k - 1) * rim, k * rim)
            agg_ref[here, :] = window
            out, d_node, d_nodes1, d_agg = node_step(nodes_ref[mine, :], window, cot_ref[mine, :], w_node_ref[...])
            out_ref[here, :] = out
            d_node_ref[here, :] = d_node
            d_nodes1_ref[here, :] = d_nodes1
            d_agg_ref[here, :] = d_agg


def rim_body(
    nodes_ref, own_ref, near_in_ref, far_in_ref, cot_ref, w_node_ref,
    near_ref, far_ref, out_ref, agg_ref, d_node_ref, d_nodes1_ref, d_agg_ref,
):
    rows = nodes_ref.shape[0]
    rim = RIM * ROWS
    arrived = chosen(near_in_ref[...].astype(F32), far_in_ref[...].astype(F32))
    rims = []
    for k in range(2):
        mine = slice(k * (rows - rim), k * (rows - rim) + rim)
        here = slice(k * rim, (k + 1) * rim)
        agg = (own_ref[here, :].astype(F32) + arrived[k]).astype(BF16)
        agg_ref[here, :] = agg
        out, d_node, d_nodes1, d_agg = node_step(nodes_ref[mine, :], agg, cot_ref[mine, :], w_node_ref[...])
        out_ref[here, :] = out
        d_node_ref[here, :] = d_node
        d_nodes1_ref[here, :] = d_nodes1
        d_agg_ref[here, :] = d_agg
        rims.append(d_agg)
    near_ref[...], far_ref[...] = chosen(rims[0], rims[1])


def in_order(mid_ref, rim_ref):
    rim = RIM * ROWS
    return jnp.concatenate([rim_ref[:rim, :], mid_ref[...], rim_ref[rim:, :]], axis=0)


def grad_node_body(scale, nodes_ref, agg_mid_ref, agg_rim_ref, d_node_mid_ref, d_node_rim_ref, *out_refs):
    width = nodes_ref.shape[1]
    d_node = in_order(d_node_mid_ref, d_node_rim_ref)
    agg = in_order(agg_mid_ref, agg_rim_ref)
    first = lax.axis_index("dp") == 0
    for k, left in enumerate((nodes_ref[...], agg)):
        mine = slice(k * width, (k + 1) * width)
        grad = dot(left, d_node, ((0,), (0,))) * scale
        if len(out_refs) == 1:
            out_refs[0][mine, :] = grad.astype(BF16)
            continue
        half = width // 2
        out_refs[0][mine, :] = jnp.where(first, grad[:, :half], grad[:, half:])
        out_refs[1][mine, :] = jnp.where(first, grad[:, half:], grad[:, :half]).astype(BF16)


def behind_body(
    nodes_ref, at_ref, w_edge_ref, out_mid_ref, out_rim_ref, d_agg_mid_ref, d_agg_rim_ref,
    out_ref, d_msg_ref, slope_ref,
):
    rows = nodes_ref.shape[0]
    rim = RIM * ROWS
    out_ref[...] = in_order(out_mid_ref, out_rim_ref)
    d_agg = in_order(d_agg_mid_ref, d_agg_rim_ref)
    for k in range(rows // rim):
        mine = slice(k * rim, (k + 1) * rim)
        d_msg_ref[mine, :] = dot(at_ref[mine, :rows], d_agg)
        pre = dot(nodes_ref[mine, :], w_edge_ref[...])
        sig = jax.nn.sigmoid(pre)
        slope_ref[mine, :] = sig * (1.0 + pre * (1.0 - sig))


def edge_body(
    scale, tiled, nodes_ref, at_ref, near_ref, far_ref, d_msg_ref, slope_ref, mid_ref, rim_ref, w_edge_ref, *refs
):
    back_ref, d_edge_ref = refs[-2 if tiled else -3], refs[-1]
    rows, width = nodes_ref.shape
    rim = RIM * ROWS
    peers = back_ref.shape[0]
    per_peer = rows // peers
    prev, after = chosen(near_ref[...], far_ref[...])
    rims = jnp.concatenate([prev, after], axis=0)
    w_edge = w_edge_ref[...]
    for k in range(rows // rim):
        mine = slice(k * rim, (k + 1) * rim)
        d_msg = d_msg_ref[mine, :] + dot(at_ref[mine, rows : rows + 2 * rim], rims)
        d_edge = (d_msg.astype(BF16).astype(F32) * slope_ref[mine, :]).astype(BF16)
        d_edge_ref[mine, :] = d_edge
        if k == 0:
            d_nodes1 = rim_ref[:rim, :]
        elif k == rows // rim - 1:
            d_nodes1 = rim_ref[rim:, :]
        else:
            d_nodes1 = mid_ref[(k - 1) * rim : k * rim, :]
        d_nodes = (d_nodes1 + dot(d_edge, w_edge, ((1,), (1,)))).astype(BF16)
        for p in range(rim // per_peer):
            back_ref[k * (rim // per_peer) + p, :per_peer, :] = d_nodes[p * per_peer : (p + 1) * per_peer, :]
    g_edge = (dot(nodes_ref[...], d_edge_ref[...], ((0,), (0,))) * scale).astype(BF16)
    if not tiled:
        refs[-2][...] = g_edge
        return
    keep_ref, recv_ref = refs[:2]
    g_node = (keep_ref[...] + recv_ref[...].astype(F32)).astype(BF16)
    share = width // peers
    half = width // 2
    for p in range(peers):
        back_ref[p, per_peer : per_peer + share, :] = g_edge[p * share : (p + 1) * share, :]
        row = 2 * p * share
        back_ref[p, per_peer + share :, :half] = g_node[row : row + share, :]
        back_ref[p, per_peer + share :, half:] = g_node[row + share : row + 2 * share, :]


def share_body(back_ref, out_ref):
    share = out_ref.shape[1]
    total = jnp.sum(back_ref[:, back_ref.shape[1] - share :, :].astype(F32), axis=0).astype(BF16)
    out_ref[...] = jnp.broadcast_to(total[None], out_ref.shape)


def finish_body(parts_ref, edge_ref, node_ref):
    share = parts_ref.shape[1] // 2
    half = parts_ref.shape[2] // 2
    peers = parts_ref.shape[0] // 2
    for p in range(peers):
        one, two = parts_ref[p].astype(F32), parts_ref[peers + p].astype(F32)
        edge_ref[p * share : (p + 1) * share, :] = one[:share] + two[:share]
        row = 2 * p * share
        for k, part in enumerate((one[share:], two[share:])):
            lanes = slice(k * half, (k + 1) * half)
            node_ref[row : row + share, lanes] = part[:, :half]
            node_ref[row + share : row + 2 * share, lanes] = part[:, half:]


def place_body(order_ref, back_ref, out_ref):
    rows, width = out_ref.shape
    per_peer = rows // back_ref.shape[0]
    back = back_ref[:, :per_peer, :].reshape(rows, width)
    order = jnp.broadcast_to(order_ref[...], (ROWS, rows))
    for k in range(rows // ROWS):
        mine = slice(k * ROWS, (k + 1) * ROWS)
        row = lax.broadcasted_iota(jnp.int32, (ROWS, rows), 0) + k * ROWS
        hot = jnp.where(order == row, 1.0, 0.0).astype(BF16)
        out_ref[mine, :] = dot(hot, back).astype(BF16)


def shards(features, send_order, adj_count, adj_target, adj_vals, w_edge, w_node, cotangent):
    ndp = lax.axis_size("dp")
    ndom = lax.axis_size("dom")
    rows, width = features.shape[1:]
    per_peer = rows // ndom
    blocks, slots = adj_vals.shape[:2]
    rim = RIM * ROWS
    scale = 1.0 / math.sqrt(float(ndp * rows * ndom))
    tall = shape(rows, width)
    tall_f = shape(rows, width, dtype=F32)
    edge = shape(rim, width)
    rims = shape(2 * rim, width)
    mid = shape(rows - 2 * rim, width)
    unit = rows * width * 2
    square = 2 * rows * width * width
    share = width // ndom
    tiled = ndp == 2 and share % 16 == 0

    (picked,) = call(
        pick_body,
        [tall],
        (send_order, features[0]),
        [ANY, ANY],
        [
            pltpu.VMEM((1, rows), jnp.int32),
            pltpu.VMEM((rows, width), BF16),
            pltpu.SemaphoreType.DMA,
            pltpu.SemaphoreType.DMA,
        ],
        flops=2 * rows * rows * width,
        nbytes=2 * unit,
        limit=56 * MIB,
    )
    nodes = lax.all_to_all(
        picked.reshape(ndom, per_peer, width), "dom", split_axis=0, concat_axis=0, tiled=True
    ).reshape(rows, width)
    spots = blocks + 2 * RIM + 1
    adj, adj_t = call(
        build_body,
        [shape(spots, ROWS, rows), shape(rows, spots * ROWS)],
        (adj_count, adj_target, adj_vals),
        [SMEM, SMEM, VMEM],
        nbytes=16 * unit,
    )
    near, far, msg = call(
        message_body, [edge, edge, tall], (nodes, adj, w_edge), flops=square + 4 * rim * rows * width, nbytes=4 * unit
    )
    far = swapped_across(far, "dom")
    near = swapped(near, "dom", 1)
    cot = cotangent[0]
    own, out_mid, agg_mid, d_node_mid, d_nodes1_mid, d_agg_mid = call(
        own_body,
        [rims, mid, mid, mid, shape(*mid.shape, dtype=F32), mid],
        (nodes, msg, adj, cot, w_node),
        flops=2 * rows * rows * width + 2 * square,
        nbytes=8 * unit,
    )
    near, far, out_rim, agg_rim, d_node_rim, d_nodes1_rim, d_agg_rim = call(
        rim_body,
        [edge, edge, rims, rims, rims, shape(*rims.shape, dtype=F32), rims],
        (nodes, own, near, far, cot, w_node),
        flops=2 * square,
        nbytes=4 * unit,
    )
    far = swapped_across(far, "dom")
    near = swapped(near, "dom", 1)
    halves = [shape(2 * width, width // 2, dtype=F32), shape(2 * width, width // 2)]
    node_parts = call(
        functools.partial(grad_node_body, scale),
        halves if tiled else [shape(2 * width, width)],
        (nodes, agg_mid, agg_rim, d_node_mid, d_node_rim),
        flops=2 * square,
        nbytes=3 * unit,
    )
    if tiled:
        node_parts = (node_parts[0], swapped(node_parts[1], "dp", 1))
    node_out, d_msg, slope = call(
        behind_body,
        [tall, tall_f, tall_f],
        (nodes, adj_t, w_edge, out_mid, out_rim, d_agg_mid, d_agg_rim),
        flops=2 * rows * rows * width + square,
        nbytes=8 * unit,
    )
    back, *g_edge = call(
        functools.partial(edge_body, scale, tiled),
        [shape(ndom, per_peer + 2 * share, width)] if tiled else [shape(ndom, per_peer, width), shape(width, width)],
        (nodes, adj_t, near, far, d_msg, slope, d_nodes1_mid, d_nodes1_rim, w_edge, *(node_parts if tiled else ())),
        scratch=[pltpu.VMEM((rows, width), BF16)],
        flops=2 * square + 4 * rim * rows * width,
        nbytes=8 * unit,
    )
    back = lax.all_to_all(back, "dom", split_axis=0, concat_axis=0, tiled=True)
    if tiled:
        (shared,) = call(share_body, [shape(ndp * ndom, 2 * share, width)], (back,), nbytes=unit)
        shared = lax.all_to_all(shared, ("dp", "dom"), split_axis=0, concat_axis=0, tiled=True)
        grad_edge, grad_node = call(
            finish_body, [shape(width, width, dtype=F32), shape(2 * width, width, dtype=F32)], (shared,), nbytes=2 * unit
        )
    else:
        grad_edge = lax.psum(g_edge[0].astype(F32), ("dp", "dom"))
        grad_node = lax.psum(node_parts[0].astype(F32), ("dp", "dom"))
    (grad_brick,) = call(place_body, [tall], (send_order, back), flops=2 * rows * rows * width, nbytes=2 * unit)
    return (node_out[None], grad_brick[None], grad_edge, grad_node)


def solution(mesh):
    in_specs = (
        P("dp", "dom", None),
        P("dom", None),
        P("dom"),
        P("dom", None),
        P("dom", None, None, None),
        P(),
        P(),
        P("dp", "dom", None),
    )
    out_specs = (P("dp", "dom", None), P("dp", "dom", None), P(), P())
    return jax.shard_map(shards, mesh=mesh, in_specs=in_specs, out_specs=out_specs, check_vma=False)
```

```python
import functools
import math

import jax
import jax.numpy as jnp
from jax import lax
from jax.experimental import pallas as pl
from jax.experimental.pallas import tpu as pltpu
from jax.sharding import PartitionSpec as P

ROWS = 128
RIM = 2
ANY = pl.BlockSpec(memory_space=pl.ANY)
VMEM = pl.BlockSpec(memory_space=pltpu.VMEM)
SMEM = pl.BlockSpec(memory_space=pltpu.SMEM)
BF16 = jnp.bfloat16
F32 = jnp.float32
MIB = 1024 * 1024


def swapped(x, axis, mask):
    peers = lax.axis_size(axis)
    return lax.ppermute(x, axis, [(i, i ^ mask) for i in range(peers)])


def swapped_across(x, axis):
    peers = lax.axis_size(axis)
    return lax.ppermute(x, axis, [(i, (i + 1 if i % 2 else i - 1) % peers) for i in range(peers)])


def dot(a, b, contract=((1,), (0,))):
    return lax.dot_general(a, b, (contract, ((), ())), preferred_element_type=F32)


def shape(*dims, dtype=BF16):
    return jax.ShapeDtypeStruct(dims, dtype)


def call(body, outs, args, specs=None, scratch=(), flops=0, nbytes=0, limit=24 * MIB):
    return pl.pallas_call(
        body,
        out_shape=outs,
        in_specs=specs or [VMEM] * len(args),
        out_specs=[VMEM] * len(outs),
        scratch_shapes=list(scratch),
        cost_estimate=pl.CostEstimate(flops=flops, bytes_accessed=nbytes, transcendentals=0),
        compiler_params=pltpu.CompilerParams(vmem_limit_bytes=limit),
    )(*args)


def pick_body(order_hbm, feat_hbm, out_ref, order_ref, feat_ref, hot_ref, order_sem, feat_sem):
    rows = feat_ref.shape[0]
    early = hot_ref.shape[0] // ROWS
    load_order = pltpu.make_async_copy(order_hbm, order_ref, order_sem)
    load_feat = pltpu.make_async_copy(feat_hbm, feat_ref, feat_sem)
    load_order.start()
    load_feat.start()
    lane = lax.broadcasted_iota(jnp.int32, (ROWS, rows), 1).astype(F32)
    load_order.wait()

    def hot_rows(k):
        row = order_ref[:, k * ROWS : (k + 1) * ROWS].astype(F32)
        col = jnp.transpose(jnp.broadcast_to(row, (ROWS, ROWS)))
        wide = jnp.concatenate([col] * (rows // ROWS), axis=1)
        return jnp.where(wide == lane, 1.0, 0.0).astype(BF16)

    for k in range(early):
        hot_ref[k * ROWS : (k + 1) * ROWS, :] = hot_rows(k)
    load_feat.wait()
    feat = feat_ref[...]
    for k in range(rows // ROWS):
        mine = slice(k * ROWS, (k + 1) * ROWS)
        hot = hot_ref[mine, :] if k < early else hot_rows(k)
        out_ref[mine, :] = dot(hot, feat).astype(BF16)


def build_body(cnt_ref, tgt_ref, vals_ref, own_ref, rim_ref, at_ref, a_ref):
    blocks, slots = vals_ref.shape[:2]
    spare = blocks + 2 * RIM
    a_ref[...] = jnp.zeros_like(a_ref)
    at_ref[...] = jnp.zeros_like(at_ref)
    for c in range(blocks):
        mine = slice(c * ROWS, (c + 1) * ROWS)
        for s in range(slots):
            w = tgt_ref[c, s]
            at = jnp.where(w < blocks, w + RIM, jnp.where(w < 2 * blocks, w - blocks, w - blocks + RIM))
            at = jnp.where(s < cnt_ref[c], at, spare)
            value = vals_ref[c, s].astype(F32)
            a_ref[at, :, mine] = (a_ref[at, :, mine].astype(F32) + value).astype(BF16)
            lanes = pl.ds(pl.multiple_of(at * ROWS, ROWS), ROWS)
            at_ref[mine, lanes] = (at_ref[mine, lanes].astype(F32) + jnp.transpose(value)).astype(BF16)
    own_ref[...] = a_ref[:blocks]
    rim_ref[...] = a_ref[blocks:spare]


def chosen(first, second):
    odd = lax.rem(lax.axis_index("dom"), 2) == 1
    return jnp.where(odd, first, second), jnp.where(odd, second, first)


def message_body(nodes_ref, a_hbm, w_edge_ref, near_ref, far_ref, msg_ref, a_ref, a_sem):
    rows = nodes_ref.shape[0]
    rim = RIM * ROWS
    load = pltpu.make_async_copy(a_hbm, a_ref, a_sem)
    load.start()
    for k in range(rows // rim):
        mine = slice(k * rim, (k + 1) * rim)
        pre = dot(nodes_ref[mine, :], w_edge_ref[...])
        msg_ref[mine, :] = (pre * jax.nn.sigmoid(pre)).astype(BF16)
    load.wait()
    sums = dot(a_ref[...].reshape(2 * rim, rows), msg_ref[...])
    near, far = chosen(sums[:rim], sums[rim:])
    near_ref[...] = near.astype(BF16)
    far_ref[...] = far.astype(BF16)


def node_step(nodes, agg, gout, w_node):
    width = nodes.shape[1]
    pre = dot(nodes, w_node[:width]) + dot(agg, w_node[width:])
    sig = jax.nn.sigmoid(pre)
    out = (nodes.astype(F32) + pre * sig).astype(BF16)
    gout = gout.astype(F32)
    d_node = (gout * (sig * (1.0 + pre * (1.0 - sig)))).astype(BF16)
    back = dot(d_node, w_node, ((1,), (1,)))
    return out, d_node, gout + back[:, :width], back[:, width:].astype(BF16)


def own_body(
    nodes_ref, msg_ref, a_ref, cot_ref, w_node_ref,
    own_ref, out_ref, agg_ref, d_node_ref, d_nodes1_ref, d_agg_ref,
):
    rows, width = nodes_ref.shape
    rim = RIM * ROWS
    msg = msg_ref[...]
    for k in range(rows // rim):
        mine = slice(k * rim, (k + 1) * rim)
        window = dot(a_ref[k * RIM : (k + 1) * RIM].reshape(rim, rows), msg).astype(BF16)
        if k == 0:
            own_ref[:rim, :] = window
        elif k == rows // rim - 1:
            own_ref[rim:, :] = window
        else:
            here = slice((k - 1) * rim, k * rim)
            agg_ref[here, :] = window
            out, d_node, d_nodes1, d_agg = node_step(nodes_ref[mine, :], window, cot_ref[mine, :], w_node_ref[...])
            out_ref[here, :] = out
            d_node_ref[here, :] = d_node
            d_nodes1_ref[here, :] = d_nodes1
            d_agg_ref[here, :] = d_agg


def rim_body(
    nodes_ref, own_ref, near_in_ref, far_in_ref, cot_ref, w_node_ref,
    near_ref, far_ref, out_ref, agg_ref, d_node_ref, d_nodes1_ref, d_agg_ref,
):
    rows = nodes_ref.shape[0]
    rim = RIM * ROWS
    arrived = chosen(near_in_ref[...].astype(F32), far_in_ref[...].astype(F32))
    rims = []
    for k in range(2):
        mine = slice(k * (rows - rim), k * (rows - rim) + rim)
        here = slice(k * rim, (k + 1) * rim)
        agg = (own_ref[here, :].astype(F32) + arrived[k]).astype(BF16)
        agg_ref[here, :] = agg
        out, d_node, d_nodes1, d_agg = node_step(nodes_ref[mine, :], agg, cot_ref[mine, :], w_node_ref[...])
        out_ref[here, :] = out
        d_node_ref[here, :] = d_node
        d_nodes1_ref[here, :] = d_nodes1
        d_agg_ref[here, :] = d_agg
        rims.append(d_agg)
    near_ref[...], far_ref[...] = chosen(rims[0], rims[1])


def in_order(mid_ref, rim_ref):
    rim = RIM * ROWS
    return jnp.concatenate([rim_ref[:rim, :], mid_ref[...], rim_ref[rim:, :]], axis=0)


def grad_node_body(scale, nodes_ref, agg_mid_ref, agg_rim_ref, d_node_mid_ref, d_node_rim_ref, *out_refs):
    width = nodes_ref.shape[1]
    d_node = in_order(d_node_mid_ref, d_node_rim_ref)
    agg = in_order(agg_mid_ref, agg_rim_ref)
    first = lax.axis_index("dp") == 0
    for k, left in enumerate((nodes_ref[...], agg)):
        mine = slice(k * width, (k + 1) * width)
        grad = dot(left, d_node, ((0,), (0,))) * scale
        if len(out_refs) == 1:
            out_refs[0][mine, :] = grad.astype(BF16)
            continue
        half = width // 2
        out_refs[0][mine, :] = jnp.where(first, grad[:, :half], grad[:, half:])
        out_refs[1][mine, :] = jnp.where(first, grad[:, half:], grad[:, :half]).astype(BF16)


def behind_body(
    nodes_ref, at_ref, w_edge_ref, out_mid_ref, out_rim_ref, d_agg_mid_ref, d_agg_rim_ref,
    out_ref, d_msg_ref, slope_ref,
):
    rows = nodes_ref.shape[0]
    rim = RIM * ROWS
    out_ref[...] = in_order(out_mid_ref, out_rim_ref)
    d_agg = in_order(d_agg_mid_ref, d_agg_rim_ref)
    for k in range(rows // rim):
        mine = slice(k * rim, (k + 1) * rim)
        d_msg_ref[mine, :] = dot(at_ref[mine, :rows], d_agg)
        pre = dot(nodes_ref[mine, :], w_edge_ref[...])
        sig = jax.nn.sigmoid(pre)
        slope_ref[mine, :] = sig * (1.0 + pre * (1.0 - sig))


def edge_body(
    scale, tiled, nodes_ref, at_ref, near_ref, far_ref, d_msg_ref, slope_ref, mid_ref, rim_ref, w_edge_ref, *refs
):
    back_ref, d_edge_ref = refs[-2 if tiled else -3], refs[-1]
    rows, width = nodes_ref.shape
    rim = RIM * ROWS
    peers = back_ref.shape[0]
    per_peer = rows // peers
    prev, after = chosen(near_ref[...], far_ref[...])
    rims = jnp.concatenate([prev, after], axis=0)
    w_edge = w_edge_ref[...]
    for k in range(rows // rim):
        mine = slice(k * rim, (k + 1) * rim)
        d_msg = d_msg_ref[mine, :] + dot(at_ref[mine, rows : rows + 2 * rim], rims)
        d_edge = (d_msg.astype(BF16).astype(F32) * slope_ref[mine, :]).astype(BF16)
        d_edge_ref[mine, :] = d_edge
        if k == 0:
            d_nodes1 = rim_ref[:rim, :]
        elif k == rows // rim - 1:
            d_nodes1 = rim_ref[rim:, :]
        else:
            d_nodes1 = mid_ref[(k - 1) * rim : k * rim, :]
        d_nodes = (d_nodes1 + dot(d_edge, w_edge, ((1,), (1,)))).astype(BF16)
        for p in range(rim // per_peer):
            back_ref[k * (rim // per_peer) + p, :per_peer, :] = d_nodes[p * per_peer : (p + 1) * per_peer, :]
    g_edge = (dot(nodes_ref[...], d_edge_ref[...], ((0,), (0,))) * scale).astype(BF16)
    if not tiled:
        refs[-2][...] = g_edge
        return
    share = width // peers
    for p in range(peers):
        back_ref[p, per_peer : per_peer + share, :] = g_edge[p * share : (p + 1) * share, :]


def add_node_body(keep_ref, recv_ref, back_ref, out_ref, part_ref, sem):
    g_node = (keep_ref[...] + recv_ref[...].astype(F32)).astype(BF16)
    peers, share, width = part_ref.shape
    half = width // 2
    for p in range(peers):
        row = 2 * p * share
        part_ref[p, :, :half] = g_node[row : row + share, :]
        part_ref[p, :, half:] = g_node[row + share : row + 2 * share, :]
    put = pltpu.make_async_copy(part_ref, out_ref.at[:, pl.ds(out_ref.shape[1] - share, share), :], sem)
    put.start()
    put.wait()


def share_body(back_ref, out_ref):
    share = out_ref.shape[1]
    total = jnp.sum(back_ref[:, back_ref.shape[1] - share :, :].astype(F32), axis=0).astype(BF16)
    out_ref[...] = jnp.broadcast_to(total[None], out_ref.shape)


def finish_body(mine_ref, other_ref, edge_ref, node_ref):
    share = mine_ref.shape[1] // 2
    half = mine_ref.shape[2] // 2
    chips = mine_ref.shape[0] // 2
    for c in range(chips):
        for core, (one, two) in enumerate(
            zip(chosen(other_ref[c], mine_ref[c]), chosen(other_ref[chips + c], mine_ref[chips + c]))
        ):
            one, two = one.astype(F32), two.astype(F32)
            p = 2 * c + core
            edge_ref[p * share : (p + 1) * share, :] = one[:share] + two[:share]
            row = 2 * p * share
            for k, part in enumerate((one[share:], two[share:])):
                lanes = slice(k * half, (k + 1) * half)
                node_ref[row : row + share, lanes] = part[:, :half]
                node_ref[row + share : row + 2 * share, lanes] = part[:, half:]


def place_body(order_ref, back_ref, out_ref):
    rows, width = out_ref.shape
    per_peer = rows // back_ref.shape[0]
    back = back_ref[:, :per_peer, :].reshape(rows, width)
    order = jnp.broadcast_to(order_ref[...], (ROWS, rows))
    for k in range(rows // ROWS):
        mine = slice(k * ROWS, (k + 1) * ROWS)
        row = lax.broadcasted_iota(jnp.int32, (ROWS, rows), 0) + k * ROWS
        hot = jnp.where(order == row, 1.0, 0.0).astype(BF16)
        out_ref[mine, :] = dot(hot, back).astype(BF16)


def shards(features, send_order, adj_count, adj_target, adj_vals, w_edge, w_node, cotangent):
    ndp = lax.axis_size("dp")
    ndom = lax.axis_size("dom")
    rows, width = features.shape[1:]
    per_peer = rows // ndom
    blocks, slots = adj_vals.shape[:2]
    rim = RIM * ROWS
    scale = 1.0 / math.sqrt(float(ndp * rows * ndom))
    tall = shape(rows, width)
    tall_f = shape(rows, width, dtype=F32)
    edge = shape(rim, width)
    rims = shape(2 * rim, width)
    mid = shape(rows - 2 * rim, width)
    unit = rows * width * 2
    square = 2 * rows * width * width
    share = width // ndom
    tiled = ndp == 2 and share % 16 == 0

    (picked,) = call(
        pick_body,
        [tall],
        (send_order, features[0]),
        [ANY, ANY],
        [
            pltpu.VMEM((1, rows), jnp.int32),
            pltpu.VMEM((rows, width), BF16),
            pltpu.VMEM((2 * ROWS, rows), BF16),
            pltpu.SemaphoreType.DMA,
            pltpu.SemaphoreType.DMA,
        ],
        flops=2 * rows * rows * width,
        nbytes=2 * unit,
        limit=56 * MIB,
    )
    nodes = lax.all_to_all(
        picked.reshape(ndom, per_peer, width), "dom", split_axis=0, concat_axis=0, tiled=True
    ).reshape(rows, width)
    spots = blocks + 2 * RIM + 1
    adj, adj_rim, adj_t = call(
        build_body,
        [shape(blocks, ROWS, rows), shape(2 * RIM, ROWS, rows), shape(rows, spots * ROWS)],
        (adj_count, adj_target, adj_vals),
        [SMEM, SMEM, VMEM],
        [pltpu.VMEM((spots, ROWS, rows), BF16)],
        nbytes=16 * unit,
    )
    near, far, msg = call(
        message_body,
        [edge, edge, tall],
        (nodes, adj_rim, w_edge),
        [VMEM, ANY, VMEM],
        [pltpu.VMEM((2 * RIM, ROWS, rows), BF16), pltpu.SemaphoreType.DMA],
        flops=square + 4 * rim * rows * width,
        nbytes=4 * unit,
    )
    far = swapped_across(far, "dom")
    near = swapped(near, "dom", 1)
    cot = cotangent[0]
    own, out_mid, agg_mid, d_node_mid, d_nodes1_mid, d_agg_mid = call(
        own_body,
        [rims, mid, mid, mid, shape(*mid.shape, dtype=F32), mid],
        (nodes, msg, adj, cot, w_node),
        flops=2 * rows * rows * width + 2 * square,
        nbytes=8 * unit,
    )
    near, far, out_rim, agg_rim, d_node_rim, d_nodes1_rim, d_agg_rim = call(
        rim_body,
        [edge, edge, rims, rims, rims, shape(*rims.shape, dtype=F32), rims],
        (nodes, own, near, far, cot, w_node),
        flops=2 * square,
        nbytes=4 * unit,
    )
    far = swapped_across(far, "dom")
    near = swapped(near, "dom", 1)
    halves = [shape(2 * width, width // 2, dtype=F32), shape(2 * width, width // 2)]
    node_parts = call(
        functools.partial(grad_node_body, scale),
        halves if tiled else [shape(2 * width, width)],
        (nodes, agg_mid, agg_rim, d_node_mid, d_node_rim),
        flops=2 * square,
        nbytes=3 * unit,
    )
    if tiled:
        node_parts = (node_parts[0], swapped(node_parts[1], "dp", 1))
    node_out, d_msg, slope = call(
        behind_body,
        [tall, tall_f, tall_f],
        (nodes, adj_t, w_edge, out_mid, out_rim, d_agg_mid, d_agg_rim),
        flops=2 * rows * rows * width + square,
        nbytes=8 * unit,
    )
    back, *g_edge = call(
        functools.partial(edge_body, scale, tiled),
        [shape(ndom, per_peer + 2 * share, width)] if tiled else [shape(ndom, per_peer, width), shape(width, width)],
        (nodes, adj_t, near, far, d_msg, slope, d_nodes1_mid, d_nodes1_rim, w_edge),
        scratch=[pltpu.VMEM((rows, width), BF16)],
        flops=2 * square + 4 * rim * rows * width,
        nbytes=8 * unit,
    )
    if tiled:
        back = pl.pallas_call(
            add_node_body,
            out_shape=shape(*back.shape),
            in_specs=[VMEM, VMEM, ANY],
            out_specs=ANY,
            scratch_shapes=[pltpu.VMEM((ndom, share, width), BF16), pltpu.SemaphoreType.DMA],
            input_output_aliases={2: 0},
            compiler_params=pltpu.CompilerParams(vmem_limit_bytes=24 * MIB),
        )(*node_parts, back)
    back = lax.all_to_all(back, "dom", split_axis=0, concat_axis=0, tiled=True)
    if tiled:
        chips = ndp * ndom // 2
        same_core = [[2 * chip + core for chip in range(chips)] for core in range(2)]
        (shared,) = call(share_body, [shape(chips, 2 * share, width)], (back,), nbytes=unit)
        shared = lax.all_to_all(
            shared, ("dp", "dom"), split_axis=0, concat_axis=0, tiled=True, axis_index_groups=same_core
        )
        grad_edge, grad_node = call(
            finish_body,
            [shape(width, width, dtype=F32), shape(2 * width, width, dtype=F32)],
            (shared, swapped(shared, "dom", 1)),
            nbytes=2 * unit,
        )
    else:
        grad_edge = lax.psum(g_edge[0].astype(F32), ("dp", "dom"))
        grad_node = lax.psum(node_parts[0].astype(F32), ("dp", "dom"))
    (grad_brick,) = call(place_body, [tall], (send_order, back), flops=2 * rows * rows * width, nbytes=2 * unit)
    return (node_out[None], grad_brick[None], grad_edge, grad_node)


def solution(mesh):
    in_specs = (
        P("dp", "dom", None),
        P("dom", None),
        P("dom"),
        P("dom", None),
        P("dom", None, None, None),
        P(),
        P(),
        P("dp", "dom", None),
    )
    out_specs = (P("dp", "dom", None), P("dp", "dom", None), P(), P())
    return jax.shard_map(shards, mesh=mesh, in_specs=in_specs, out_specs=out_specs, check_vma=False)
```

```python
import functools
import math

import jax
import jax.numpy as jnp
from jax import lax
from jax.experimental import pallas as pl
from jax.experimental.pallas import tpu as pltpu
from jax.sharding import PartitionSpec as P

ROWS = 128
RIM = 2
ANY = pl.BlockSpec(memory_space=pl.ANY)
VMEM = pl.BlockSpec(memory_space=pltpu.VMEM)
SMEM = pl.BlockSpec(memory_space=pltpu.SMEM)
BF16 = jnp.bfloat16
F32 = jnp.float32
MIB = 1024 * 1024


def swapped(x, axis, mask):
    peers = lax.axis_size(axis)
    return lax.ppermute(x, axis, [(i, i ^ mask) for i in range(peers)])


def swapped_across(x, axis):
    peers = lax.axis_size(axis)
    return lax.ppermute(x, axis, [(i, (i + 1 if i % 2 else i - 1) % peers) for i in range(peers)])


def dot(a, b, contract=((1,), (0,))):
    return lax.dot_general(a, b, (contract, ((), ())), preferred_element_type=F32)


def shape(*dims, dtype=BF16):
    return jax.ShapeDtypeStruct(dims, dtype)


def call(body, outs, args, specs=None, scratch=(), flops=0, nbytes=0, limit=24 * MIB):
    return pl.pallas_call(
        body,
        out_shape=outs,
        in_specs=specs or [VMEM] * len(args),
        out_specs=[VMEM] * len(outs),
        scratch_shapes=list(scratch),
        cost_estimate=pl.CostEstimate(flops=flops, bytes_accessed=nbytes, transcendentals=0),
        compiler_params=pltpu.CompilerParams(vmem_limit_bytes=limit),
    )(*args)


def pick_body(order_hbm, feat_hbm, out_ref, order_ref, feat_ref, hot_ref, order_sem, feat_sem):
    rows = feat_ref.shape[0]
    early = hot_ref.shape[0] // ROWS
    load_order = pltpu.make_async_copy(order_hbm, order_ref, order_sem)
    load_feat = pltpu.make_async_copy(feat_hbm, feat_ref, feat_sem)
    load_order.start()
    load_feat.start()
    lane = lax.broadcasted_iota(jnp.int32, (ROWS, rows), 1).astype(F32)
    load_order.wait()

    def hot_rows(k):
        row = order_ref[:, k * ROWS : (k + 1) * ROWS].astype(F32)
        col = jnp.transpose(jnp.broadcast_to(row, (ROWS, ROWS)))
        wide = jnp.concatenate([col] * (rows // ROWS), axis=1)
        return jnp.where(wide == lane, 1.0, 0.0).astype(BF16)

    for k in range(early):
        hot_ref[k * ROWS : (k + 1) * ROWS, :] = hot_rows(k)
    load_feat.wait()
    feat = feat_ref[...]
    for k in range(rows // ROWS):
        mine = slice(k * ROWS, (k + 1) * ROWS)
        hot = hot_ref[mine, :] if k < early else hot_rows(k)
        out_ref[mine, :] = dot(hot, feat).astype(BF16)


def build_body(cnt_ref, tgt_ref, vals_ref, own_ref, rim_ref, at_ref, a_ref):
    blocks, slots = vals_ref.shape[:2]
    spare = blocks + 2 * RIM
    a_ref[...] = jnp.zeros_like(a_ref)
    at_ref[...] = jnp.zeros_like(at_ref)
    for c in range(blocks):
        mine = slice(c * ROWS, (c + 1) * ROWS)
        for s in range(slots):
            w = tgt_ref[c, s]
            at = jnp.where(w < blocks, w + RIM, jnp.where(w < 2 * blocks, w - blocks, w - blocks + RIM))
            at = jnp.where(s < cnt_ref[c], at, spare)
            value = vals_ref[c, s].astype(F32)
            a_ref[at, :, mine] = (a_ref[at, :, mine].astype(F32) + value).astype(BF16)
            lanes = pl.ds(pl.multiple_of(at * ROWS, ROWS), ROWS)
            at_ref[mine, lanes] = (at_ref[mine, lanes].astype(F32) + jnp.transpose(value)).astype(BF16)
    own_ref[...] = a_ref[:blocks]
    rim_ref[...] = a_ref[blocks:spare]


def chosen(first, second):
    odd = lax.rem(lax.axis_index("dom"), 2) == 1
    return jnp.where(odd, first, second), jnp.where(odd, second, first)


def message_body(nodes_ref, a_hbm, w_edge_ref, near_ref, far_ref, msg_ref, a_ref, a_sem):
    rows = nodes_ref.shape[0]
    rim = RIM * ROWS
    load = pltpu.make_async_copy(a_hbm, a_ref, a_sem)
    load.start()
    for k in range(rows // rim):
        mine = slice(k * rim, (k + 1) * rim)
        pre = dot(nodes_ref[mine, :], w_edge_ref[...])
        msg_ref[mine, :] = (pre * jax.nn.sigmoid(pre)).astype(BF16)
    load.wait()
    sums = dot(a_ref[...].reshape(2 * rim, rows), msg_ref[...])
    near, far = chosen(sums[:rim], sums[rim:])
    near_ref[...] = near.astype(BF16)
    far_ref[...] = far.astype(BF16)


def node_step(nodes, agg, gout, w_node):
    width = nodes.shape[1]
    pre = dot(nodes, w_node[:width]) + dot(agg, w_node[width:])
    sig = jax.nn.sigmoid(pre)
    out = (nodes.astype(F32) + pre * sig).astype(BF16)
    gout = gout.astype(F32)
    d_node = (gout * (sig * (1.0 + pre * (1.0 - sig)))).astype(BF16)
    back = dot(d_node, w_node, ((1,), (1,)))
    return out, d_node, gout + back[:, :width], back[:, width:].astype(BF16)


def own_body(
    nodes_ref, msg_ref, a_hbm, cot_ref, w_node_ref,
    own_ref, out_ref, agg_ref, d_node_ref, d_nodes1_ref, d_agg_ref, a_ref, a_sems,
):
    rows, width = nodes_ref.shape
    rim = RIM * ROWS
    msg = msg_ref[...]
    loads = []
    for k in range(rows // rim):
        part = pl.ds(k * RIM, RIM)
        loads.append(pltpu.make_async_copy(a_hbm.at[part], a_ref.at[part], a_sems.at[k]))
        loads[k].start()
    for k in range(rows // rim):
        mine = slice(k * rim, (k + 1) * rim)
        loads[k].wait()
        window = dot(a_ref[k * RIM : (k + 1) * RIM].reshape(rim, rows), msg).astype(BF16)
        if k == 0:
            own_ref[:rim, :] = window
        elif k == rows // rim - 1:
            own_ref[rim:, :] = window
        else:
            here = slice((k - 1) * rim, k * rim)
            agg_ref[here, :] = window
            out, d_node, d_nodes1, d_agg = node_step(nodes_ref[mine, :], window, cot_ref[mine, :], w_node_ref[...])
            out_ref[here, :] = out
            d_node_ref[here, :] = d_node
            d_nodes1_ref[here, :] = d_nodes1
            d_agg_ref[here, :] = d_agg


def rim_body(
    nodes_ref, own_ref, near_in_ref, far_in_ref, cot_ref, w_node_ref,
    near_ref, far_ref, out_ref, agg_ref, d_node_ref, d_nodes1_ref, d_agg_ref,
):
    rows = nodes_ref.shape[0]
    rim = RIM * ROWS
    arrived = chosen(near_in_ref[...].astype(F32), far_in_ref[...].astype(F32))
    rims = []
    for k in range(2):
        mine = slice(k * (rows - rim), k * (rows - rim) + rim)
        here = slice(k * rim, (k + 1) * rim)
        agg = (own_ref[here, :].astype(F32) + arrived[k]).astype(BF16)
        agg_ref[here, :] = agg
        out, d_node, d_nodes1, d_agg = node_step(nodes_ref[mine, :], agg, cot_ref[mine, :], w_node_ref[...])
        out_ref[here, :] = out
        d_node_ref[here, :] = d_node
        d_nodes1_ref[here, :] = d_nodes1
        d_agg_ref[here, :] = d_agg
        rims.append(d_agg)
    near_ref[...], far_ref[...] = chosen(rims[0], rims[1])


def in_order(mid_ref, rim_ref):
    rim = RIM * ROWS
    return jnp.concatenate([rim_ref[:rim, :], mid_ref[...], rim_ref[rim:, :]], axis=0)


def grad_node_body(scale, nodes_ref, agg_mid_ref, agg_rim_ref, d_node_mid_ref, d_node_rim_ref, *out_refs):
    width = nodes_ref.shape[1]
    d_node = in_order(d_node_mid_ref, d_node_rim_ref)
    agg = in_order(agg_mid_ref, agg_rim_ref)
    for k, left in enumerate((nodes_ref[...], agg)):
        put_halves(dot(left, d_node, ((0,), (0,))) * scale, out_refs, slice(k * width, (k + 1) * width))


def behind_body(
    nodes_ref, at_ref, w_edge_ref, out_mid_ref, out_rim_ref, d_agg_mid_ref, d_agg_rim_ref,
    out_ref, d_msg_ref, slope_ref,
):
    rows = nodes_ref.shape[0]
    rim = RIM * ROWS
    out_ref[...] = in_order(out_mid_ref, out_rim_ref)
    d_agg = in_order(d_agg_mid_ref, d_agg_rim_ref)
    for k in range(rows // rim):
        mine = slice(k * rim, (k + 1) * rim)
        d_msg_ref[mine, :] = dot(at_ref[mine, :rows], d_agg)
        pre = dot(nodes_ref[mine, :], w_edge_ref[...])
        sig = jax.nn.sigmoid(pre)
        slope_ref[mine, :] = sig * (1.0 + pre * (1.0 - sig))


def edge_body(
    scale, nodes_ref, at_ref, near_ref, far_ref, d_msg_ref, slope_ref, mid_ref, rim_ref, w_edge_ref,
    back_ref, *refs,
):
    d_edge_ref = refs[-1]
    rows, width = nodes_ref.shape
    rim = RIM * ROWS
    prev, after = chosen(near_ref[...], far_ref[...])
    rims = jnp.concatenate([prev, after], axis=0)
    w_edge = w_edge_ref[...]
    for k in range(rows // rim):
        mine = slice(k * rim, (k + 1) * rim)
        d_msg = d_msg_ref[mine, :] + dot(at_ref[mine, rows : rows + 2 * rim], rims)
        d_edge = (d_msg.astype(BF16).astype(F32) * slope_ref[mine, :]).astype(BF16)
        d_edge_ref[mine, :] = d_edge
        if k == 0:
            d_nodes1 = rim_ref[:rim, :]
        elif k == rows // rim - 1:
            d_nodes1 = rim_ref[rim:, :]
        else:
            d_nodes1 = mid_ref[(k - 1) * rim : k * rim, :]
        back_ref[mine, :] = (d_nodes1 + dot(d_edge, w_edge, ((1,), (1,)))).astype(BF16)
    put_halves(dot(nodes_ref[...], d_edge_ref[...], ((0,), (0,))) * scale, refs[:-1])


def put_halves(grad, refs, rows=slice(None)):
    if len(refs) == 1:
        refs[0][rows, :] = grad.astype(BF16)
        return
    first = lax.axis_index("dp") == 0
    half = grad.shape[1] // 2
    refs[0][rows, :] = jnp.where(first, grad[:, :half], grad[:, half:])
    refs[1][rows, :] = jnp.where(first, grad[:, half:], grad[:, :half]).astype(BF16)


def bit_of(mask):
    return lax.rem(lax.div(lax.axis_index("dom"), mask), 2)


def cut_rows(total_ref, mask, keep_ref, send_ref):
    size = keep_ref.shape[0]
    bit = bit_of(mask)
    keep_ref[...] = total_ref[pl.ds(pl.multiple_of(bit * size, 16), size), :]
    send_ref[...] = total_ref[pl.ds(pl.multiple_of((1 - bit) * size, 16), size), :].astype(BF16)


def first_cut_body(mask, edge_ref, edge_in_ref, node_ref, node_in_ref, keep_ref, send_ref, total_ref):
    width = edge_ref.shape[0]
    total_ref[:width, :] = edge_ref[...] + edge_in_ref[...].astype(F32)
    total_ref[width:, :] = node_ref[...] + node_in_ref[...].astype(F32)
    cut_rows(total_ref, mask, keep_ref, send_ref)


def next_cut_body(mask, mine_ref, in_ref, keep_ref, send_ref, total_ref):
    total_ref[...] = mine_ref[...] + in_ref[...].astype(F32)
    cut_rows(total_ref, mask, keep_ref, send_ref)


def sum_body(mine_ref, in_ref, out_ref):
    out_ref[...] = (mine_ref[...].astype(F32) + in_ref[...].astype(F32)).astype(BF16)


def join_lanes_body(mine_ref, in_ref, out_ref):
    half = mine_ref.shape[1]
    first = lax.axis_index("dp") == 0
    mine, other = mine_ref[...], in_ref[...]
    out_ref[:, :half] = jnp.where(first, mine, other)
    out_ref[:, half:] = jnp.where(first, other, mine)


def join_rows_body(mask, mine_ref, in_ref, out_ref):
    size = mine_ref.shape[0]
    low = bit_of(mask) == 0
    mine, other = mine_ref[...], in_ref[...]
    out_ref[:size, :] = jnp.where(low, mine, other)
    out_ref[size:, :] = jnp.where(low, other, mine)


def finish_body(mask, mine_ref, in_ref, edge_ref, node_ref):
    size = mine_ref.shape[0]
    width = edge_ref.shape[0]
    low = bit_of(mask) == 0
    mine, other = mine_ref[...].astype(F32), in_ref[...].astype(F32)
    upper = jnp.where(low, mine, other)
    edge_ref[...] = upper[:width]
    node_ref[: size - width, :] = upper[width:]
    node_ref[size - width :, :] = jnp.where(low, other, mine)


def reduced(edge_part, node_part, back):
    core, along_y, along_z, along_zz = 1, 2, 4, 8
    rows = edge_part[0].shape[0] + node_part[0].shape[0]
    half = edge_part[0].shape[1]

    def cut(body, mask, args, size):
        return call(
            functools.partial(body, mask),
            [shape(size // 2, half, dtype=F32), shape(size // 2, half)],
            args,
            scratch=[pltpu.VMEM((size, half), F32)],
        )

    edge_in = swapped(edge_part[1], "dp", 1)
    keep, send = cut(first_cut_body, core, (edge_part[0], edge_in, *node_part), rows)
    keep, send = cut(next_cut_body, along_y, (keep, swapped(send, "dom", core)), rows // 2)
    (mine,) = call(sum_body, [shape(rows // 4, half)], (keep, swapped(send, "dom", along_y)))
    for mask in (along_z, along_zz):
        (mine,) = call(sum_body, [shape(rows // 4, half)], (mine, swapped(mine, "dom", mask)))
    (mine,) = call(join_lanes_body, [shape(rows // 4, 2 * half)], (mine, swapped(mine, "dp", 1)))
    mine, back = lax.optimization_barrier((mine, back))
    (mine,) = call(
        functools.partial(join_rows_body, along_y),
        [shape(rows // 2, 2 * half)],
        (mine, swapped(mine, "dom", along_y)),
    )
    edge, node = (shape(part[0].shape[0], 2 * half, dtype=F32) for part in (edge_part, node_part))
    return *call(functools.partial(finish_body, core), [edge, node], (mine, swapped(mine, "dom", core))), back


def place_body(order_ref, back_ref, out_ref):
    rows = back_ref.shape[0]
    back = back_ref[...]
    order = jnp.broadcast_to(order_ref[...], (ROWS, rows))
    for k in range(rows // ROWS):
        mine = slice(k * ROWS, (k + 1) * ROWS)
        row = lax.broadcasted_iota(jnp.int32, (ROWS, rows), 0) + k * ROWS
        hot = jnp.where(order == row, 1.0, 0.0).astype(BF16)
        out_ref[mine, :] = dot(hot, back).astype(BF16)


def shards(features, send_order, adj_count, adj_target, adj_vals, w_edge, w_node, cotangent):
    ndp = lax.axis_size("dp")
    ndom = lax.axis_size("dom")
    rows, width = features.shape[1:]
    per_peer = rows // ndom
    blocks, slots = adj_vals.shape[:2]
    rim = RIM * ROWS
    scale = 1.0 / math.sqrt(float(ndp * rows * ndom))
    tall = shape(rows, width)
    tall_f = shape(rows, width, dtype=F32)
    edge = shape(rim, width)
    rims = shape(2 * rim, width)
    mid = shape(rows - 2 * rim, width)
    unit = rows * width * 2
    square = 2 * rows * width * width

    (picked,) = call(
        pick_body,
        [tall],
        (send_order, features[0]),
        [ANY, ANY],
        [
            pltpu.VMEM((1, rows), jnp.int32),
            pltpu.VMEM((rows, width), BF16),
            pltpu.VMEM((2 * ROWS, rows), BF16),
            pltpu.SemaphoreType.DMA,
            pltpu.SemaphoreType.DMA,
        ],
        flops=2 * rows * rows * width,
        nbytes=2 * unit,
        limit=56 * MIB,
    )
    nodes = lax.all_to_all(
        picked.reshape(ndom, per_peer, width), "dom", split_axis=0, concat_axis=0, tiled=True
    ).reshape(rows, width)
    spots = blocks + 2 * RIM + 1
    adj, adj_rim, adj_t = call(
        build_body,
        [shape(blocks, ROWS, rows), shape(2 * RIM, ROWS, rows), shape(rows, spots * ROWS)],
        (adj_count, adj_target, adj_vals),
        [SMEM, SMEM, VMEM],
        [pltpu.VMEM((spots, ROWS, rows), BF16)],
        nbytes=16 * unit,
    )
    near, far, msg = call(
        message_body,
        [edge, edge, tall],
        (nodes, adj_rim, w_edge),
        [VMEM, ANY, VMEM],
        [pltpu.VMEM((2 * RIM, ROWS, rows), BF16), pltpu.SemaphoreType.DMA],
        flops=square + 4 * rim * rows * width,
        nbytes=4 * unit,
    )
    far = swapped_across(far, "dom")
    near = swapped(near, "dom", 1)
    cot = cotangent[0]
    own, out_mid, agg_mid, d_node_mid, d_nodes1_mid, d_agg_mid = call(
        own_body,
        [rims, mid, mid, mid, shape(*mid.shape, dtype=F32), mid],
        (nodes, msg, adj, cot, w_node),
        [VMEM, VMEM, ANY, VMEM, VMEM],
        [pltpu.VMEM((blocks, ROWS, rows), BF16), pltpu.SemaphoreType.DMA((rows // rim,))],
        flops=2 * rows * rows * width + 2 * square,
        nbytes=8 * unit,
    )
    near, far, out_rim, agg_rim, d_node_rim, d_nodes1_rim, d_agg_rim = call(
        rim_body,
        [edge, edge, rims, rims, rims, shape(*rims.shape, dtype=F32), rims],
        (nodes, own, near, far, cot, w_node),
        flops=2 * square,
        nbytes=4 * unit,
    )
    far = swapped_across(far, "dom")
    near = swapped(near, "dom", 1)
    tiled = ndp == 2 and ndom == 16

    def halves(size):
        if not tiled:
            return [shape(size, width)]
        return [shape(size, width // 2, dtype=F32), shape(size, width // 2)]

    node_part = call(
        functools.partial(grad_node_body, scale),
        halves(2 * width),
        (nodes, agg_mid, agg_rim, d_node_mid, d_node_rim),
        flops=2 * square,
        nbytes=3 * unit,
    )
    if tiled:
        node_part = (node_part[0], swapped(node_part[1], "dp", 1))
    node_out, d_msg, slope = call(
        behind_body,
        [tall, tall_f, tall_f],
        (nodes, adj_t, w_edge, out_mid, out_rim, d_agg_mid, d_agg_rim),
        flops=2 * rows * rows * width + square,
        nbytes=8 * unit,
    )
    back, *edge_part = call(
        functools.partial(edge_body, scale),
        [tall, *halves(width)],
        (nodes, adj_t, near, far, d_msg, slope, d_nodes1_mid, d_nodes1_rim, w_edge),
        scratch=[pltpu.VMEM((rows, width), BF16)],
        flops=2 * square + 4 * rim * rows * width,
        nbytes=8 * unit,
    )
    back = lax.all_to_all(
        back.reshape(ndom, per_peer, width), "dom", split_axis=0, concat_axis=0, tiled=True
    ).reshape(rows, width)
    if tiled:
        grad_edge, grad_node, back = reduced(edge_part, node_part, back)
    else:
        grad_edge, grad_node = (lax.psum(part[0].astype(F32), ("dp", "dom")) for part in (edge_part, node_part))
    (grad_brick,) = call(place_body, [tall], (send_order, back), flops=2 * rows * rows * width, nbytes=2 * unit)
    return (node_out[None], grad_brick[None], grad_edge, grad_node)


def solution(mesh):
    in_specs = (
        P("dp", "dom", None),
        P("dom", None),
        P("dom"),
        P("dom", None),
        P("dom", None, None, None),
        P(),
        P(),
        P("dp", "dom", None),
    )
    out_specs = (P("dp", "dom", None), P("dp", "dom", None), P(), P())
    return jax.shard_map(shards, mesh=mesh, in_specs=in_specs, out_specs=out_specs, check_vma=False)
```

```python
import functools
import math

import jax
import jax.numpy as jnp
from jax import lax
from jax.experimental import pallas as pl
from jax.experimental.pallas import tpu as pltpu
from jax.sharding import PartitionSpec as P

ROWS = 128
RIM = 2
ANY = pl.BlockSpec(memory_space=pl.ANY)
VMEM = pl.BlockSpec(memory_space=pltpu.VMEM)
SMEM = pl.BlockSpec(memory_space=pltpu.SMEM)
BF16 = jnp.bfloat16
F32 = jnp.float32
MIB = 1024 * 1024
CORE, ALONG_Y, ALONG_Z = 1, 2, 4


def swapped(x, axis, mask):
    peers = lax.axis_size(axis)
    return lax.ppermute(x, axis, [(i, i ^ mask) for i in range(peers)])


def swapped_across(x, axis):
    peers = lax.axis_size(axis)
    return lax.ppermute(x, axis, [(i, (i + 1 if i % 2 else i - 1) % peers) for i in range(peers)])


def dot(a, b, contract=((1,), (0,))):
    return lax.dot_general(a, b, (contract, ((), ())), preferred_element_type=F32)


def shape(*dims, dtype=BF16):
    return jax.ShapeDtypeStruct(dims, dtype)


def call(body, outs, args, specs=None, scratch=(), flops=0, nbytes=0, limit=24 * MIB):
    return pl.pallas_call(
        body,
        out_shape=outs,
        in_specs=specs or [VMEM] * len(args),
        out_specs=[VMEM] * len(outs),
        scratch_shapes=list(scratch),
        cost_estimate=pl.CostEstimate(flops=flops, bytes_accessed=nbytes, transcendentals=0),
        compiler_params=pltpu.CompilerParams(vmem_limit_bytes=limit),
    )(*args)


def pick_body(order_hbm, feat_hbm, out_ref, order_ref, feat_ref, hot_ref, order_sem, feat_sem):
    rows = feat_ref.shape[0]
    early = hot_ref.shape[0] // ROWS
    load_order = pltpu.make_async_copy(order_hbm, order_ref, order_sem)
    load_feat = pltpu.make_async_copy(feat_hbm, feat_ref, feat_sem)
    load_order.start()
    load_feat.start()
    lane = lax.broadcasted_iota(jnp.int32, (ROWS, rows), 1).astype(F32)
    load_order.wait()

    def hot_rows(k):
        row = order_ref[:, k * ROWS : (k + 1) * ROWS].astype(F32)
        col = jnp.transpose(jnp.broadcast_to(row, (ROWS, ROWS)))
        wide = jnp.concatenate([col] * (rows // ROWS), axis=1)
        return jnp.where(wide == lane, 1.0, 0.0).astype(BF16)

    for k in range(early):
        hot_ref[k * ROWS : (k + 1) * ROWS, :] = hot_rows(k)
    load_feat.wait()
    feat = feat_ref[...]
    for k in range(rows // ROWS):
        mine = slice(k * ROWS, (k + 1) * ROWS)
        hot = hot_ref[mine, :] if k < early else hot_rows(k)
        out_ref[mine, :] = dot(hot, feat).astype(BF16)


def build_body(cnt_ref, tgt_ref, vals_ref, own_ref, rim_ref, at_ref, a_ref):
    blocks, slots = vals_ref.shape[:2]
    spare = blocks + 2 * RIM
    a_ref[...] = jnp.zeros_like(a_ref)
    at_ref[...] = jnp.zeros_like(at_ref)
    for c in range(blocks):
        mine = slice(c * ROWS, (c + 1) * ROWS)
        for s in range(slots):
            w = tgt_ref[c, s]
            at = jnp.where(w < blocks, w + RIM, jnp.where(w < 2 * blocks, w - blocks, w - blocks + RIM))
            at = jnp.where(s < cnt_ref[c], at, spare)
            value = vals_ref[c, s].astype(F32)
            a_ref[at, :, mine] = (a_ref[at, :, mine].astype(F32) + value).astype(BF16)
            lanes = pl.ds(pl.multiple_of(at * ROWS, ROWS), ROWS)
            at_ref[mine, lanes] = (at_ref[mine, lanes].astype(F32) + jnp.transpose(value)).astype(BF16)
    own_ref[...] = a_ref[:blocks]
    rim_ref[...] = a_ref[blocks:spare]


def chosen(first, second):
    odd = lax.rem(lax.axis_index("dom"), 2) == 1
    return jnp.where(odd, first, second), jnp.where(odd, second, first)


def message_body(nodes_ref, a_hbm, w_edge_ref, near_ref, far_ref, msg_ref, a_ref, a_sem):
    rows = nodes_ref.shape[0]
    rim = RIM * ROWS
    load = pltpu.make_async_copy(a_hbm, a_ref, a_sem)
    load.start()
    for k in range(rows // rim):
        mine = slice(k * rim, (k + 1) * rim)
        pre = dot(nodes_ref[mine, :], w_edge_ref[...])
        msg_ref[mine, :] = (pre * jax.nn.sigmoid(pre)).astype(BF16)
    load.wait()
    sums = dot(a_ref[...].reshape(2 * rim, rows), msg_ref[...])
    near, far = chosen(sums[:rim], sums[rim:])
    near_ref[...] = near.astype(BF16)
    far_ref[...] = far.astype(BF16)


def node_step(nodes, agg, gout, w_node):
    width = nodes.shape[1]
    pre = dot(nodes, w_node[:width]) + dot(agg, w_node[width:])
    sig = jax.nn.sigmoid(pre)
    out = (nodes.astype(F32) + pre * sig).astype(BF16)
    gout = gout.astype(F32)
    d_node = (gout * (sig * (1.0 + pre * (1.0 - sig)))).astype(BF16)
    back = dot(d_node, w_node, ((1,), (1,)))
    return out, d_node, gout + back[:, :width], back[:, width:].astype(BF16)


def own_body(
    nodes_ref, msg_ref, a_hbm, cot_ref, w_node_ref,
    own_ref, out_ref, agg_ref, d_node_ref, d_nodes1_ref, d_agg_ref, a_ref, a_sems,
):
    rows, width = nodes_ref.shape
    rim = RIM * ROWS
    msg = msg_ref[...]
    loads = []
    for k in range(rows // rim):
        part = pl.ds(k * RIM, RIM)
        loads.append(pltpu.make_async_copy(a_hbm.at[part], a_ref.at[part], a_sems.at[k]))
        loads[k].start()
    for k in range(rows // rim):
        mine = slice(k * rim, (k + 1) * rim)
        loads[k].wait()
        window = dot(a_ref[k * RIM : (k + 1) * RIM].reshape(rim, rows), msg).astype(BF16)
        if k == 0:
            own_ref[:rim, :] = window
        elif k == rows // rim - 1:
            own_ref[rim:, :] = window
        else:
            here = slice((k - 1) * rim, k * rim)
            agg_ref[here, :] = window
            out, d_node, d_nodes1, d_agg = node_step(nodes_ref[mine, :], window, cot_ref[mine, :], w_node_ref[...])
            out_ref[here, :] = out
            d_node_ref[here, :] = d_node
            d_nodes1_ref[here, :] = d_nodes1
            d_agg_ref[here, :] = d_agg


def rim_body(
    nodes_ref, own_ref, near_in_ref, far_in_ref, cot_ref, w_node_ref,
    near_ref, far_ref, out_ref, agg_ref, d_node_ref, d_nodes1_ref, d_agg_ref,
):
    rows = nodes_ref.shape[0]
    rim = RIM * ROWS
    arrived = chosen(near_in_ref[...].astype(F32), far_in_ref[...].astype(F32))
    rims = []
    for k in range(2):
        mine = slice(k * (rows - rim), k * (rows - rim) + rim)
        here = slice(k * rim, (k + 1) * rim)
        agg = (own_ref[here, :].astype(F32) + arrived[k]).astype(BF16)
        agg_ref[here, :] = agg
        out, d_node, d_nodes1, d_agg = node_step(nodes_ref[mine, :], agg, cot_ref[mine, :], w_node_ref[...])
        out_ref[here, :] = out
        d_node_ref[here, :] = d_node
        d_nodes1_ref[here, :] = d_nodes1
        d_agg_ref[here, :] = d_agg
        rims.append(d_agg)
    near_ref[...], far_ref[...] = chosen(rims[0], rims[1])


def in_order(mid_ref, rim_ref):
    rim = RIM * ROWS
    return jnp.concatenate([rim_ref[:rim, :], mid_ref[...], rim_ref[rim:, :]], axis=0)


def grad_node_body(scale, nodes_ref, agg_mid_ref, agg_rim_ref, d_node_mid_ref, d_node_rim_ref, *out_refs):
    width = nodes_ref.shape[1]
    d_node = in_order(d_node_mid_ref, d_node_rim_ref)
    agg = in_order(agg_mid_ref, agg_rim_ref)
    first = lax.axis_index("dp") == 0
    for k, left in enumerate((nodes_ref[...], agg)):
        mine = slice(k * width, (k + 1) * width)
        grad = dot(left, d_node, ((0,), (0,))) * scale
        if len(out_refs) == 1:
            out_refs[0][mine, :] = grad
            continue
        half = width // 2
        out_refs[0][mine, :] = jnp.where(first, grad[:, :half], grad[:, half:])
        out_refs[1][mine, :] = jnp.where(first, grad[:, half:], grad[:, :half]).astype(BF16)


def behind_body(
    nodes_ref, at_ref, w_edge_ref, out_mid_ref, out_rim_ref, d_agg_mid_ref, d_agg_rim_ref,
    out_ref, d_msg_ref, slope_ref,
):
    rows = nodes_ref.shape[0]
    rim = RIM * ROWS
    out_ref[...] = in_order(out_mid_ref, out_rim_ref)
    d_agg = in_order(d_agg_mid_ref, d_agg_rim_ref)
    for k in range(rows // rim):
        mine = slice(k * rim, (k + 1) * rim)
        d_msg_ref[mine, :] = dot(at_ref[mine, :rows], d_agg)
        pre = dot(nodes_ref[mine, :], w_edge_ref[...])
        sig = jax.nn.sigmoid(pre)
        slope_ref[mine, :] = sig * (1.0 + pre * (1.0 - sig))


def edge_body(
    scale, nodes_ref, at_ref, near_ref, far_ref, d_msg_ref, slope_ref, mid_ref, rim_ref, w_edge_ref,
    back_ref, g_edge_ref, d_edge_ref,
):
    rows, width = nodes_ref.shape
    rim = RIM * ROWS
    prev, after = chosen(near_ref[...], far_ref[...])
    rims = jnp.concatenate([prev, after], axis=0)
    w_edge = w_edge_ref[...]
    for k in range(rows // rim):
        mine = slice(k * rim, (k + 1) * rim)
        d_msg = d_msg_ref[mine, :] + dot(at_ref[mine, rows : rows + 2 * rim], rims)
        d_edge = (d_msg.astype(BF16).astype(F32) * slope_ref[mine, :]).astype(BF16)
        d_edge_ref[mine, :] = d_edge
        if k == 0:
            d_nodes1 = rim_ref[:rim, :]
        elif k == rows // rim - 1:
            d_nodes1 = rim_ref[rim:, :]
        else:
            d_nodes1 = mid_ref[(k - 1) * rim : k * rim, :]
        back_ref[mine, :] = (d_nodes1 + dot(d_edge, w_edge, ((1,), (1,)))).astype(BF16)
    g_edge_ref[...] = dot(nodes_ref[...], d_edge_ref[...], ((0,), (0,))) * scale


def bit_of(mask):
    return lax.rem(lax.div(lax.axis_index("dom"), mask), 2)


def cut_rows(total_ref, mask, keep_ref, send_ref):
    size = keep_ref.shape[0]
    bit = bit_of(mask)
    keep_ref[...] = total_ref[pl.ds(pl.multiple_of(bit * size, 16), size), :]
    send_ref[...] = total_ref[pl.ds(pl.multiple_of((1 - bit) * size, 16), size), :].astype(BF16)


def first_cut_body(mask, edge_ref, node_ref, node_in_ref, keep_ref, send_ref, total_ref):
    half = node_ref.shape[1]
    few, more = edge_ref.shape[0] // 4, node_ref.shape[0] // 4
    for q in range(4):
        row = q * (2 * few + more)
        mine = slice(q * more, (q + 1) * more)
        total_ref[row : row + more, :] = node_ref[mine, :] + node_in_ref[mine, :].astype(F32)
        row += more
        mine = slice(q * few, (q + 1) * few)
        total_ref[row : row + few, :] = edge_ref[mine, :half]
        total_ref[row + few : row + 2 * few, :] = edge_ref[mine, half:]
    cut_rows(total_ref, mask, keep_ref, send_ref)


def next_cut_body(mask, mine_ref, in_ref, keep_ref, send_ref, total_ref):
    total_ref[...] = mine_ref[...] + in_ref[...].astype(F32)
    cut_rows(total_ref, mask, keep_ref, send_ref)


def sum_body(mine_ref, in_ref, out_ref):
    out_ref[...] = (mine_ref[...].astype(F32) + in_ref[...].astype(F32)).astype(BF16)


def join_lanes_body(mine_ref, in_ref, out_ref):
    size, half = mine_ref.shape
    more = size // 2
    few = more // 2
    first = lax.axis_index("dp") == 0
    mine, other = mine_ref[:more, :], in_ref[:more, :]
    out_ref[few:, :half] = jnp.where(first, mine, other)
    out_ref[few:, half:] = jnp.where(first, other, mine)
    total = (mine_ref[more:, :].astype(F32) + in_ref[more:, :].astype(F32)).astype(BF16)
    out_ref[:few, :half] = total[:few]
    out_ref[:few, half:] = total[few:]


def join_rows_body(mask, mine_ref, in_ref, out_ref):
    size = mine_ref.shape[0]
    low = bit_of(mask) == 0
    mine, other = mine_ref[...], in_ref[...]
    out_ref[:size, :] = jnp.where(low, mine, other)
    out_ref[size:, :] = jnp.where(low, other, mine)


def finish_body(mask, mine_ref, in_ref, edge_ref, node_ref):
    few, more = edge_ref.shape[0] // 4, node_ref.shape[0] // 4
    low = bit_of(mask) == 0
    mine, other = mine_ref[...].astype(F32), in_ref[...].astype(F32)
    for side, value in enumerate((jnp.where(low, mine, other), jnp.where(low, other, mine))):
        for part in range(2):
            q = 2 * side + part
            row = part * (few + more)
            edge_ref[q * few : (q + 1) * few, :] = value[row : row + few]
            node_ref[q * more : (q + 1) * more, :] = value[row + few : row + few + more]


def cut_before(edge_part, node_part):
    half = node_part[0].shape[1]
    size = node_part[0].shape[0] + 2 * edge_part.shape[0]

    def cut(body, mask, args, size):
        return call(
            functools.partial(body, mask),
            [shape(size // 2, half, dtype=F32), shape(size // 2, half)],
            args,
            scratch=[pltpu.VMEM((size, half), F32)],
        )

    keep, send = cut(first_cut_body, CORE, (edge_part, *node_part), size)
    return cut(next_cut_body, ALONG_Y, (keep, swapped(send, "dom", CORE)), size // 2)


def reduced(keep, send, back, width):
    quarter, half = keep.shape
    few = width // 4
    (mine,) = call(sum_body, [shape(quarter, half)], (keep, swapped(send, "dom", ALONG_Y)))
    for mask in (ALONG_Z, 2 * ALONG_Z):
        (mine,) = call(sum_body, [shape(quarter, half)], (mine, swapped(mine, "dom", mask)))
    (mine,) = call(join_lanes_body, [shape(3 * few, width)], (mine, swapped(mine, "dp", 1)))
    mine, back = lax.optimization_barrier((mine, back))
    (mine,) = call(
        functools.partial(join_rows_body, ALONG_Y), [shape(6 * few, width)], (mine, swapped(mine, "dom", ALONG_Y))
    )
    grad_edge, grad_node = call(
        functools.partial(finish_body, CORE),
        [shape(width, width, dtype=F32), shape(2 * width, width, dtype=F32)],
        (mine, swapped(mine, "dom", CORE)),
    )
    return grad_edge, grad_node, back


def place_body(order_ref, back_ref, out_ref):
    rows = back_ref.shape[0]
    back = back_ref[...]
    order = jnp.broadcast_to(order_ref[...], (ROWS, rows))
    for k in range(rows // ROWS):
        mine = slice(k * ROWS, (k + 1) * ROWS)
        row = lax.broadcasted_iota(jnp.int32, (ROWS, rows), 0) + k * ROWS
        hot = jnp.where(order == row, 1.0, 0.0).astype(BF16)
        out_ref[mine, :] = dot(hot, back).astype(BF16)


def shards(features, send_order, adj_count, adj_target, adj_vals, w_edge, w_node, cotangent):
    ndp = lax.axis_size("dp")
    ndom = lax.axis_size("dom")
    rows, width = features.shape[1:]
    per_peer = rows // ndom
    blocks, slots = adj_vals.shape[:2]
    rim = RIM * ROWS
    scale = 1.0 / math.sqrt(float(ndp * rows * ndom))
    tall = shape(rows, width)
    tall_f = shape(rows, width, dtype=F32)
    edge = shape(rim, width)
    rims = shape(2 * rim, width)
    mid = shape(rows - 2 * rim, width)
    unit = rows * width * 2
    square = 2 * rows * width * width

    (picked,) = call(
        pick_body,
        [tall],
        (send_order, features[0]),
        [ANY, ANY],
        [
            pltpu.VMEM((1, rows), jnp.int32),
            pltpu.VMEM((rows, width), BF16),
            pltpu.VMEM((2 * ROWS, rows), BF16),
            pltpu.SemaphoreType.DMA,
            pltpu.SemaphoreType.DMA,
        ],
        flops=2 * rows * rows * width,
        nbytes=2 * unit,
        limit=56 * MIB,
    )
    nodes = lax.all_to_all(
        picked.reshape(ndom, per_peer, width), "dom", split_axis=0, concat_axis=0, tiled=True
    ).reshape(rows, width)
    spots = blocks + 2 * RIM + 1
    adj, adj_rim, adj_t = call(
        build_body,
        [shape(blocks, ROWS, rows), shape(2 * RIM, ROWS, rows), shape(rows, spots * ROWS)],
        (adj_count, adj_target, adj_vals),
        [SMEM, SMEM, VMEM],
        [pltpu.VMEM((spots, ROWS, rows), BF16)],
        nbytes=16 * unit,
    )
    near, far, msg = call(
        message_body,
        [edge, edge, tall],
        (nodes, adj_rim, w_edge),
        [VMEM, ANY, VMEM],
        [pltpu.VMEM((2 * RIM, ROWS, rows), BF16), pltpu.SemaphoreType.DMA],
        flops=square + 4 * rim * rows * width,
        nbytes=4 * unit,
    )
    far = swapped_across(far, "dom")
    near = swapped(near, "dom", 1)
    cot = cotangent[0]
    own, out_mid, agg_mid, d_node_mid, d_nodes1_mid, d_agg_mid = call(
        own_body,
        [rims, mid, mid, mid, shape(*mid.shape, dtype=F32), mid],
        (nodes, msg, adj, cot, w_node),
        [VMEM, VMEM, ANY, VMEM, VMEM],
        [pltpu.VMEM((blocks, ROWS, rows), BF16), pltpu.SemaphoreType.DMA((rows // rim,))],
        flops=2 * rows * rows * width + 2 * square,
        nbytes=8 * unit,
    )
    near, far, out_rim, agg_rim, d_node_rim, d_nodes1_rim, d_agg_rim = call(
        rim_body,
        [edge, edge, rims, rims, rims, shape(*rims.shape, dtype=F32), rims],
        (nodes, own, near, far, cot, w_node),
        flops=2 * square,
        nbytes=4 * unit,
    )
    far = swapped_across(far, "dom")
    near = swapped(near, "dom", 1)
    tiled = ndp == 2 and ndom == 16

    node_part = call(
        functools.partial(grad_node_body, scale),
        [shape(2 * width, width // 2, dtype=F32), shape(2 * width, width // 2)]
        if tiled
        else [shape(2 * width, width, dtype=F32)],
        (nodes, agg_mid, agg_rim, d_node_mid, d_node_rim),
        flops=2 * square,
        nbytes=3 * unit,
    )
    if tiled:
        node_part = (node_part[0], swapped(node_part[1], "dp", 1))
    node_out, d_msg, slope = call(
        behind_body,
        [tall, tall_f, tall_f],
        (nodes, adj_t, w_edge, out_mid, out_rim, d_agg_mid, d_agg_rim),
        flops=2 * rows * rows * width + square,
        nbytes=8 * unit,
    )
    back, edge_part = call(
        functools.partial(edge_body, scale),
        [tall, shape(width, width, dtype=F32)],
        (nodes, adj_t, near, far, d_msg, slope, d_nodes1_mid, d_nodes1_rim, w_edge),
        scratch=[pltpu.VMEM((rows, width), BF16)],
        flops=2 * square + 4 * rim * rows * width,
        nbytes=8 * unit,
    )
    if tiled:
        keep, send = cut_before(edge_part, node_part)
        back, send = lax.optimization_barrier((back, send))
    back = lax.all_to_all(
        back.reshape(ndom, per_peer, width), "dom", split_axis=0, concat_axis=0, tiled=True
    ).reshape(rows, width)
    if tiled:
        grad_edge, grad_node, back = reduced(keep, send, back, width)
    else:
        grad_edge, grad_node = (lax.psum(part, ("dp", "dom")) for part in (edge_part, node_part[0]))
    (grad_brick,) = call(place_body, [tall], (send_order, back), flops=2 * rows * rows * width, nbytes=2 * unit)
    return (node_out[None], grad_brick[None], grad_edge, grad_node)


def solution(mesh):
    in_specs = (
        P("dp", "dom", None),
        P("dom", None),
        P("dom"),
        P("dom", None),
        P("dom", None, None, None),
        P(),
        P(),
        P("dp", "dom", None),
    )
    out_specs = (P("dp", "dom", None), P("dp", "dom", None), P(), P())
    return jax.shard_map(shards, mesh=mesh, in_specs=in_specs, out_specs=out_specs, check_vma=False)
```

```python
import functools
import math

import jax
import jax.numpy as jnp
from jax import lax
from jax.experimental import pallas as pl
from jax.experimental.pallas import tpu as pltpu
from jax.sharding import PartitionSpec as P

ROWS = 128
RIM = 2
ANY = pl.BlockSpec(memory_space=pl.ANY)
VMEM = pl.BlockSpec(memory_space=pltpu.VMEM)
SMEM = pl.BlockSpec(memory_space=pltpu.SMEM)
BF16 = jnp.bfloat16
F32 = jnp.float32
MIB = 1024 * 1024
CORE, ALONG_Y, ALONG_Z = 1, 2, 4


def swapped(x, axis, mask):
    peers = lax.axis_size(axis)
    return lax.ppermute(x, axis, [(i, i ^ mask) for i in range(peers)])


def swapped_across(x, axis):
    peers = lax.axis_size(axis)
    return lax.ppermute(x, axis, [(i, (i + 1 if i % 2 else i - 1) % peers) for i in range(peers)])


def dot(a, b, contract=((1,), (0,))):
    return lax.dot_general(a, b, (contract, ((), ())), preferred_element_type=F32)


def shape(*dims, dtype=BF16):
    return jax.ShapeDtypeStruct(dims, dtype)


def call(body, outs, args, specs=None, scratch=(), flops=0, nbytes=0, limit=24 * MIB):
    return pl.pallas_call(
        body,
        out_shape=outs,
        in_specs=specs or [VMEM] * len(args),
        out_specs=[VMEM] * len(outs),
        scratch_shapes=list(scratch),
        cost_estimate=pl.CostEstimate(flops=flops, bytes_accessed=nbytes, transcendentals=0),
        compiler_params=pltpu.CompilerParams(vmem_limit_bytes=limit),
    )(*args)


def pick_body(order_hbm, feat_hbm, out_ref, order_ref, feat_ref, hot_ref, order_sem, feat_sem):
    rows = feat_ref.shape[0]
    early = hot_ref.shape[0] // ROWS
    load_order = pltpu.make_async_copy(order_hbm, order_ref, order_sem)
    load_feat = pltpu.make_async_copy(feat_hbm, feat_ref, feat_sem)
    load_order.start()
    load_feat.start()
    lane = lax.broadcasted_iota(jnp.int32, (ROWS, rows), 1).astype(F32)
    load_order.wait()

    def hot_rows(k):
        row = order_ref[:, k * ROWS : (k + 1) * ROWS].astype(F32)
        col = jnp.transpose(jnp.broadcast_to(row, (ROWS, ROWS)))
        wide = jnp.concatenate([col] * (rows // ROWS), axis=1)
        return jnp.where(wide == lane, 1.0, 0.0).astype(BF16)

    for k in range(early):
        hot_ref[k * ROWS : (k + 1) * ROWS, :] = hot_rows(k)
    load_feat.wait()
    feat = feat_ref[...]
    for k in range(rows // ROWS):
        mine = slice(k * ROWS, (k + 1) * ROWS)
        hot = hot_ref[mine, :] if k < early else hot_rows(k)
        out_ref[mine, :] = dot(hot, feat).astype(BF16)


def build_body(cnt_ref, tgt_ref, vals_ref, own_ref, rim_ref, at_ref, a_ref):
    blocks, slots = vals_ref.shape[:2]
    spare = blocks + 2 * RIM
    a_ref[...] = jnp.zeros_like(a_ref)
    at_ref[...] = jnp.zeros_like(at_ref)
    for c in range(blocks):
        mine = slice(c * ROWS, (c + 1) * ROWS)
        for s in range(slots):
            w = tgt_ref[c, s]
            at = jnp.where(w < blocks, w + RIM, jnp.where(w < 2 * blocks, w - blocks, w - blocks + RIM))
            at = jnp.where(s < cnt_ref[c], at, spare)
            value = vals_ref[c, s].astype(F32)
            a_ref[at, :, mine] = (a_ref[at, :, mine].astype(F32) + value).astype(BF16)
            lanes = pl.ds(pl.multiple_of(at * ROWS, ROWS), ROWS)
            at_ref[mine, lanes] = (at_ref[mine, lanes].astype(F32) + jnp.transpose(value)).astype(BF16)
    own_ref[...] = a_ref[:blocks]
    rim_ref[...] = a_ref[blocks:spare]


def chosen(first, second):
    odd = lax.rem(lax.axis_index("dom"), 2) == 1
    return jnp.where(odd, first, second), jnp.where(odd, second, first)


def message_body(nodes_ref, a_hbm, w_edge_ref, near_ref, far_ref, msg_ref, a_ref, a_sem):
    rows = nodes_ref.shape[0]
    rim = RIM * ROWS
    load = pltpu.make_async_copy(a_hbm, a_ref, a_sem)
    load.start()
    for k in range(rows // rim):
        mine = slice(k * rim, (k + 1) * rim)
        pre = dot(nodes_ref[mine, :], w_edge_ref[...])
        msg_ref[mine, :] = (pre * jax.nn.sigmoid(pre)).astype(BF16)
    load.wait()
    sums = dot(a_ref[...].reshape(2 * rim, rows), msg_ref[...])
    near, far = chosen(sums[:rim], sums[rim:])
    near_ref[...] = near.astype(BF16)
    far_ref[...] = far.astype(BF16)


def node_step(nodes, agg, gout, w_node):
    width = nodes.shape[1]
    pre = dot(nodes, w_node[:width]) + dot(agg, w_node[width:])
    sig = jax.nn.sigmoid(pre)
    out = (nodes.astype(F32) + pre * sig).astype(BF16)
    gout = gout.astype(F32)
    d_node = (gout * (sig * (1.0 + pre * (1.0 - sig)))).astype(BF16)
    back = dot(d_node, w_node, ((1,), (1,)))
    return out, d_node, gout + back[:, :width], back[:, width:].astype(BF16)


def own_body(
    nodes_ref, msg_ref, a_hbm, cot_ref, w_node_ref,
    own_ref, out_ref, agg_ref, d_node_ref, d_nodes1_ref, d_agg_ref, a_ref, a_sems,
):
    rows, width = nodes_ref.shape
    rim = RIM * ROWS
    msg = msg_ref[...]
    loads = []
    for k in range(rows // rim):
        part = pl.ds(k * RIM, RIM)
        loads.append(pltpu.make_async_copy(a_hbm.at[part], a_ref.at[part], a_sems.at[k]))
        loads[k].start()
    for k in range(rows // rim):
        mine = slice(k * rim, (k + 1) * rim)
        loads[k].wait()
        window = dot(a_ref[k * RIM : (k + 1) * RIM].reshape(rim, rows), msg).astype(BF16)
        if k == 0:
            own_ref[:rim, :] = window
        elif k == rows // rim - 1:
            own_ref[rim:, :] = window
        else:
            here = slice((k - 1) * rim, k * rim)
            agg_ref[here, :] = window
            out, d_node, d_nodes1, d_agg = node_step(nodes_ref[mine, :], window, cot_ref[mine, :], w_node_ref[...])
            out_ref[here, :] = out
            d_node_ref[here, :] = d_node
            d_nodes1_ref[here, :] = d_nodes1
            d_agg_ref[here, :] = d_agg


def rim_body(
    nodes_ref, own_ref, near_in_ref, far_in_ref, cot_ref, w_node_ref,
    near_ref, far_ref, out_ref, agg_ref, d_node_ref, d_nodes1_ref, d_agg_ref,
):
    rows = nodes_ref.shape[0]
    rim = RIM * ROWS
    arrived = chosen(near_in_ref[...].astype(F32), far_in_ref[...].astype(F32))
    rims = []
    for k in range(2):
        mine = slice(k * (rows - rim), k * (rows - rim) + rim)
        here = slice(k * rim, (k + 1) * rim)
        agg = (own_ref[here, :].astype(F32) + arrived[k]).astype(BF16)
        agg_ref[here, :] = agg
        out, d_node, d_nodes1, d_agg = node_step(nodes_ref[mine, :], agg, cot_ref[mine, :], w_node_ref[...])
        out_ref[here, :] = out
        d_node_ref[here, :] = d_node
        d_nodes1_ref[here, :] = d_nodes1
        d_agg_ref[here, :] = d_agg
        rims.append(d_agg)
    near_ref[...], far_ref[...] = chosen(rims[0], rims[1])


def in_order(mid_ref, rim_ref):
    rim = RIM * ROWS
    return jnp.concatenate([rim_ref[:rim, :], mid_ref[...], rim_ref[rim:, :]], axis=0)


def grad_node_body(scale, nodes_ref, agg_mid_ref, agg_rim_ref, d_node_mid_ref, d_node_rim_ref, *out_refs):
    width = nodes_ref.shape[1]
    d_node = in_order(d_node_mid_ref, d_node_rim_ref)
    agg = in_order(agg_mid_ref, agg_rim_ref)
    first = lax.axis_index("dp") == 0
    for k, left in enumerate((nodes_ref[...], agg)):
        mine = slice(k * width, (k + 1) * width)
        grad = dot(left, d_node, ((0,), (0,))) * scale
        if len(out_refs) == 1:
            out_refs[0][mine, :] = grad
            continue
        half = width // 2
        out_refs[0][mine, :] = jnp.where(first, grad[:, :half], grad[:, half:])
        out_refs[1][mine, :] = jnp.where(first, grad[:, half:], grad[:, :half]).astype(BF16)


def behind_body(
    nodes_ref, at_ref, w_edge_ref, out_mid_ref, out_rim_ref, d_agg_mid_ref, d_agg_rim_ref,
    out_ref, d_msg_ref, slope_ref,
):
    rows = nodes_ref.shape[0]
    rim = RIM * ROWS
    out_ref[...] = in_order(out_mid_ref, out_rim_ref)
    d_agg = in_order(d_agg_mid_ref, d_agg_rim_ref)
    for k in range(rows // rim):
        mine = slice(k * rim, (k + 1) * rim)
        d_msg_ref[mine, :] = dot(at_ref[mine, :rows], d_agg)
        pre = dot(nodes_ref[mine, :], w_edge_ref[...])
        sig = jax.nn.sigmoid(pre)
        slope_ref[mine, :] = sig * (1.0 + pre * (1.0 - sig))


def edge_body(
    scale, nodes_ref, at_ref, near_ref, far_ref, d_msg_ref, slope_ref, mid_ref, rim_ref, w_edge_ref,
    back_ref, g_edge_ref, d_edge_ref,
):
    rows, width = nodes_ref.shape
    rim = RIM * ROWS
    prev, after = chosen(near_ref[...], far_ref[...])
    rims = jnp.concatenate([prev, after], axis=0)
    w_edge = w_edge_ref[...]
    for k in range(rows // rim):
        mine = slice(k * rim, (k + 1) * rim)
        d_msg = d_msg_ref[mine, :] + dot(at_ref[mine, rows : rows + 2 * rim], rims)
        d_edge = (d_msg.astype(BF16).astype(F32) * slope_ref[mine, :]).astype(BF16)
        d_edge_ref[mine, :] = d_edge
        if k == 0:
            d_nodes1 = rim_ref[:rim, :]
        elif k == rows // rim - 1:
            d_nodes1 = rim_ref[rim:, :]
        else:
            d_nodes1 = mid_ref[(k - 1) * rim : k * rim, :]
        back_ref[mine, :] = (d_nodes1 + dot(d_edge, w_edge, ((1,), (1,)))).astype(BF16)
    g_edge_ref[...] = dot(nodes_ref[...], d_edge_ref[...], ((0,), (0,))) * scale


def bit_of(mask):
    return lax.rem(lax.div(lax.axis_index("dom"), mask), 2)


def cut_rows(total_ref, mask, keep_ref, send_ref):
    size = keep_ref.shape[0]
    bit = bit_of(mask)
    keep_ref[...] = total_ref[pl.ds(pl.multiple_of(bit * size, 16), size), :]
    send_ref[...] = total_ref[pl.ds(pl.multiple_of((1 - bit) * size, 16), size), :].astype(BF16)


def first_cut_body(mask, edge_ref, node_ref, node_in_ref, keep_ref, send_ref, total_ref):
    half = node_ref.shape[1]
    few, more = edge_ref.shape[0] // 4, node_ref.shape[0] // 4
    for q in range(4):
        row = q * (2 * few + more)
        mine = slice(q * more, (q + 1) * more)
        total_ref[row : row + more, :] = node_ref[mine, :] + node_in_ref[mine, :].astype(F32)
        row += more
        mine = slice(q * few, (q + 1) * few)
        total_ref[row : row + few, :] = edge_ref[mine, :half]
        total_ref[row + few : row + 2 * few, :] = edge_ref[mine, half:]
    cut_rows(total_ref, mask, keep_ref, send_ref)


def next_cut_body(mask, mine_ref, in_ref, keep_ref, send_ref, total_ref):
    total_ref[...] = mine_ref[...] + in_ref[...].astype(F32)
    cut_rows(total_ref, mask, keep_ref, send_ref)


def sum_body(mine_ref, in_ref, out_ref):
    out_ref[...] = (mine_ref[...].astype(F32) + in_ref[...].astype(F32)).astype(BF16)


def join_body(mask, mine_ref, dp_ref, y_ref, both_ref, out_ref):
    size, half = mine_ref.shape
    more = size // 2
    few = more // 2
    first = lax.axis_index("dp") == 0
    low = bit_of(mask) == 0
    mine = [ref[...] for ref in (mine_ref, dp_ref)]
    other = [ref[...] for ref in (y_ref, both_ref)]
    for side in range(2):
        a, b = (jnp.where(low, x, y) if side == 0 else jnp.where(low, y, x) for x, y in zip(mine, other))
        row = side * (few + more)
        total = (a[more:].astype(F32) + b[more:].astype(F32)).astype(BF16)
        out_ref[row : row + few, :half] = total[:few]
        out_ref[row : row + few, half:] = total[few:]
        row += few
        out_ref[row : row + more, :half] = jnp.where(first, a[:more], b[:more])
        out_ref[row : row + more, half:] = jnp.where(first, b[:more], a[:more])


def finish_body(mask, mine_ref, in_ref, edge_ref, node_ref):
    few, more = edge_ref.shape[0] // 4, node_ref.shape[0] // 4
    low = bit_of(mask) == 0
    mine, other = mine_ref[...].astype(F32), in_ref[...].astype(F32)
    for side, value in enumerate((jnp.where(low, mine, other), jnp.where(low, other, mine))):
        for part in range(2):
            q = 2 * side + part
            row = part * (few + more)
            edge_ref[q * few : (q + 1) * few, :] = value[row : row + few]
            node_ref[q * more : (q + 1) * more, :] = value[row + few : row + few + more]


def swapped_both(x, mask):
    peers = lax.axis_size("dom")
    total = 2 * peers
    return lax.ppermute(x, ("dp", "dom"), [(i, (i + peers) % total ^ mask) for i in range(total)])


def cut_and_summed(edge_part, node_part):
    half = node_part[0].shape[1]
    size = node_part[0].shape[0] + 2 * edge_part.shape[0]

    def cut(body, mask, args, size):
        return call(
            functools.partial(body, mask),
            [shape(size // 2, half, dtype=F32), shape(size // 2, half)],
            args,
            scratch=[pltpu.VMEM((size, half), F32)],
        )

    keep, send = cut(first_cut_body, CORE, (edge_part, *node_part), size)
    keep, send = cut(next_cut_body, ALONG_Y, (keep, swapped(send, "dom", CORE)), size // 2)
    out = [shape(*send.shape)]
    (mine,) = call(sum_body, out, (keep, swapped(send, "dom", ALONG_Y)))
    return call(sum_body, out, (mine, swapped(mine, "dom", ALONG_Z)))[0]


def joined(mine, back, width):
    (mine,) = call(sum_body, [shape(*mine.shape)], (mine, swapped(mine, "dom", 2 * ALONG_Z)))
    (mine,) = call(
        functools.partial(join_body, ALONG_Y),
        [shape(6 * (width // 4), width)],
        (mine, swapped(mine, "dp", 1), swapped(mine, "dom", ALONG_Y), swapped_both(mine, ALONG_Y)),
    )
    mine, back = lax.optimization_barrier((mine, back))
    grad_edge, grad_node = call(
        functools.partial(finish_body, CORE),
        [shape(width, width, dtype=F32), shape(2 * width, width, dtype=F32)],
        (mine, swapped(mine, "dom", CORE)),
    )
    return grad_edge, grad_node, back


def place_body(order_ref, back_ref, out_ref):
    rows = back_ref.shape[0]
    back = back_ref[...]
    order = jnp.broadcast_to(order_ref[...], (ROWS, rows))
    for k in range(rows // ROWS):
        mine = slice(k * ROWS, (k + 1) * ROWS)
        row = lax.broadcasted_iota(jnp.int32, (ROWS, rows), 0) + k * ROWS
        hot = jnp.where(order == row, 1.0, 0.0).astype(BF16)
        out_ref[mine, :] = dot(hot, back).astype(BF16)


def shards(features, send_order, adj_count, adj_target, adj_vals, w_edge, w_node, cotangent):
    ndp = lax.axis_size("dp")
    ndom = lax.axis_size("dom")
    rows, width = features.shape[1:]
    per_peer = rows // ndom
    blocks, slots = adj_vals.shape[:2]
    rim = RIM * ROWS
    scale = 1.0 / math.sqrt(float(ndp * rows * ndom))
    tall = shape(rows, width)
    tall_f = shape(rows, width, dtype=F32)
    edge = shape(rim, width)
    rims = shape(2 * rim, width)
    mid = shape(rows - 2 * rim, width)
    unit = rows * width * 2
    square = 2 * rows * width * width

    (picked,) = call(
        pick_body,
        [tall],
        (send_order, features[0]),
        [ANY, ANY],
        [
            pltpu.VMEM((1, rows), jnp.int32),
            pltpu.VMEM((rows, width), BF16),
            pltpu.VMEM((2 * ROWS, rows), BF16),
            pltpu.SemaphoreType.DMA,
            pltpu.SemaphoreType.DMA,
        ],
        flops=2 * rows * rows * width,
        nbytes=2 * unit,
        limit=56 * MIB,
    )
    nodes = lax.all_to_all(
        picked.reshape(ndom, per_peer, width), "dom", split_axis=0, concat_axis=0, tiled=True
    ).reshape(rows, width)
    spots = blocks + 2 * RIM + 1
    adj, adj_rim, adj_t = call(
        build_body,
        [shape(blocks, ROWS, rows), shape(2 * RIM, ROWS, rows), shape(rows, spots * ROWS)],
        (adj_count, adj_target, adj_vals),
        [SMEM, SMEM, VMEM],
        [pltpu.VMEM((spots, ROWS, rows), BF16)],
        nbytes=16 * unit,
    )
    near, far, msg = call(
        message_body,
        [edge, edge, tall],
        (nodes, adj_rim, w_edge),
        [VMEM, ANY, VMEM],
        [pltpu.VMEM((2 * RIM, ROWS, rows), BF16), pltpu.SemaphoreType.DMA],
        flops=square + 4 * rim * rows * width,
        nbytes=4 * unit,
    )
    far = swapped_across(far, "dom")
    near = swapped(near, "dom", 1)
    cot = cotangent[0]
    own, out_mid, agg_mid, d_node_mid, d_nodes1_mid, d_agg_mid = call(
        own_body,
        [rims, mid, mid, mid, shape(*mid.shape, dtype=F32), mid],
        (nodes, msg, adj, cot, w_node),
        [VMEM, VMEM, ANY, VMEM, VMEM],
        [pltpu.VMEM((blocks, ROWS, rows), BF16), pltpu.SemaphoreType.DMA((rows // rim,))],
        flops=2 * rows * rows * width + 2 * square,
        nbytes=8 * unit,
    )
    near, far, out_rim, agg_rim, d_node_rim, d_nodes1_rim, d_agg_rim = call(
        rim_body,
        [edge, edge, rims, rims, rims, shape(*rims.shape, dtype=F32), rims],
        (nodes, own, near, far, cot, w_node),
        flops=2 * square,
        nbytes=4 * unit,
    )
    far = swapped_across(far, "dom")
    near = swapped(near, "dom", 1)
    tiled = ndp == 2 and ndom == 16

    node_part = call(
        functools.partial(grad_node_body, scale),
        [shape(2 * width, width // 2, dtype=F32), shape(2 * width, width // 2)]
        if tiled
        else [shape(2 * width, width, dtype=F32)],
        (nodes, agg_mid, agg_rim, d_node_mid, d_node_rim),
        flops=2 * square,
        nbytes=3 * unit,
    )
    if tiled:
        node_part = (node_part[0], swapped(node_part[1], "dp", 1))
    node_out, d_msg, slope = call(
        behind_body,
        [tall, tall_f, tall_f],
        (nodes, adj_t, w_edge, out_mid, out_rim, d_agg_mid, d_agg_rim),
        flops=2 * rows * rows * width + square,
        nbytes=8 * unit,
    )
    back, edge_part = call(
        functools.partial(edge_body, scale),
        [tall, shape(width, width, dtype=F32)],
        (nodes, adj_t, near, far, d_msg, slope, d_nodes1_mid, d_nodes1_rim, w_edge),
        scratch=[pltpu.VMEM((rows, width), BF16)],
        flops=2 * square + 4 * rim * rows * width,
        nbytes=8 * unit,
    )
    if tiled:
        mine = cut_and_summed(edge_part, node_part)
        back, mine = lax.optimization_barrier((back, mine))
    back = lax.all_to_all(
        back.reshape(ndom, per_peer, width), "dom", split_axis=0, concat_axis=0, tiled=True
    ).reshape(rows, width)
    if tiled:
        grad_edge, grad_node, back = joined(mine, back, width)
    else:
        grad_edge, grad_node = (lax.psum(part, ("dp", "dom")) for part in (edge_part, node_part[0]))
    (grad_brick,) = call(place_body, [tall], (send_order, back), flops=2 * rows * rows * width, nbytes=2 * unit)
    return (node_out[None], grad_brick[None], grad_edge, grad_node)


def solution(mesh):
    in_specs = (
        P("dp", "dom", None),
        P("dom", None),
        P("dom"),
        P("dom", None),
        P("dom", None, None, None),
        P(),
        P(),
        P("dp", "dom", None),
    )
    out_specs = (P("dp", "dom", None), P("dp", "dom", None), P(), P())
    return jax.shard_map(shards, mesh=mesh, in_specs=in_specs, out_specs=out_specs, check_vma=False)
```

```python
import functools
import math

import jax
import jax.numpy as jnp
from jax import lax
from jax.experimental import pallas as pl
from jax.experimental.pallas import tpu as pltpu
from jax.sharding import PartitionSpec as P

ROWS = 128
RIM = 2
ANY = pl.BlockSpec(memory_space=pl.ANY)
VMEM = pl.BlockSpec(memory_space=pltpu.VMEM)
SMEM = pl.BlockSpec(memory_space=pltpu.SMEM)
BF16 = jnp.bfloat16
F32 = jnp.float32
MIB = 1024 * 1024
STORE = 24 * MIB
CORE, ALONG_Y, ALONG_Z = 1, 2, 4


def swapped(x, axis, mask):
    peers = lax.axis_size(axis)
    return lax.ppermute(x, axis, [(i, i ^ mask) for i in range(peers)])


def swapped_across(x, axis):
    peers = lax.axis_size(axis)
    return lax.ppermute(x, axis, [(i, (i + 1 if i % 2 else i - 1) % peers) for i in range(peers)])


def dot(a, b, contract=((1,), (0,))):
    return lax.dot_general(a, b, (contract, ((), ())), preferred_element_type=F32)


def shape(*dims, dtype=BF16):
    return jax.ShapeDtypeStruct(dims, dtype)


def call(body, outs, args, specs=None, scratch=(), flops=0, nbytes=0, limit=24 * MIB, out_specs=None):
    return pl.pallas_call(
        body,
        out_shape=outs,
        in_specs=specs or [VMEM] * len(args),
        out_specs=out_specs or [VMEM] * len(outs),
        scratch_shapes=list(scratch),
        cost_estimate=pl.CostEstimate(flops=flops, bytes_accessed=nbytes, transcendentals=0),
        compiler_params=pltpu.CompilerParams(vmem_limit_bytes=limit),
    )(*args)


def pick_body(order_hbm, feat_hbm, out_ref, order_ref, feat_ref, hot_ref, order_sem, feat_sem):
    rows = feat_ref.shape[0]
    early = hot_ref.shape[0] // ROWS
    load_order = pltpu.make_async_copy(order_hbm, order_ref, order_sem)
    load_feat = pltpu.make_async_copy(feat_hbm, feat_ref, feat_sem)
    load_order.start()
    load_feat.start()
    lane = lax.broadcasted_iota(jnp.int32, (ROWS, rows), 1).astype(F32)
    load_order.wait()

    def hot_rows(k):
        row = order_ref[:, k * ROWS : (k + 1) * ROWS].astype(F32)
        col = jnp.transpose(jnp.broadcast_to(row, (ROWS, ROWS)))
        wide = jnp.concatenate([col] * (rows // ROWS), axis=1)
        return jnp.where(wide == lane, 1.0, 0.0).astype(BF16)

    for k in range(early):
        hot_ref[k * ROWS : (k + 1) * ROWS, :] = hot_rows(k)
    load_feat.wait()
    feat = feat_ref[...]
    for k in range(rows // ROWS):
        mine = slice(k * ROWS, (k + 1) * ROWS)
        hot = hot_ref[mine, :] if k < early else hot_rows(k)
        out_ref[mine, :] = dot(hot, feat).astype(BF16)


def build_body(cnt_ref, tgt_ref, vals_ref, own_ref, at_ref, rim_hbm, a_ref, sem):
    blocks, slots = vals_ref.shape[:2]
    spare = blocks + 2 * RIM
    a_ref[...] = jnp.zeros_like(a_ref)
    at_ref[...] = jnp.zeros_like(at_ref)
    for c in range(blocks):
        mine = slice(c * ROWS, (c + 1) * ROWS)
        for s in range(slots):
            w = tgt_ref[c, s]
            at = jnp.where(w < blocks, w + RIM, jnp.where(w < 2 * blocks, w - blocks, w - blocks + RIM))
            at = jnp.where(s < cnt_ref[c], at, spare)
            value = vals_ref[c, s].astype(F32)
            a_ref[at, :, mine] = (a_ref[at, :, mine].astype(F32) + value).astype(BF16)
            lanes = pl.ds(pl.multiple_of(at * ROWS, ROWS), ROWS)
            at_ref[mine, lanes] = (at_ref[mine, lanes].astype(F32) + jnp.transpose(value)).astype(BF16)
    put = pltpu.make_async_copy(a_ref.at[pl.ds(blocks, 2 * RIM)], rim_hbm.at[pl.ds(0, 2 * RIM)], sem)
    put.start()
    own_ref[...] = a_ref[:blocks]
    put.wait()


def chosen(first, second):
    odd = lax.rem(lax.axis_index("dom"), 2) == 1
    return jnp.where(odd, first, second), jnp.where(odd, second, first)


def message_body(nodes_ref, a_hbm, w_edge_ref, near_ref, far_ref, msg_ref, a_ref, a_sems):
    rows = nodes_ref.shape[0]
    rim = RIM * ROWS
    loads = [pltpu.make_async_copy(a_hbm.at[b], a_ref.at[b], a_sems.at[b]) for b in range(2 * RIM)]
    for load in loads:
        load.start()
    for k in range(rows // rim):
        mine = slice(k * rim, (k + 1) * rim)
        pre = dot(nodes_ref[mine, :], w_edge_ref[...])
        msg_ref[mine, :] = (pre * jax.nn.sigmoid(pre)).astype(BF16)
    for load in loads:
        load.wait()
    sums = dot(a_ref[...].reshape(2 * rim, rows), msg_ref[...])
    near, far = chosen(sums[:rim], sums[rim:])
    near_ref[...] = near.astype(BF16)
    far_ref[...] = far.astype(BF16)


def node_step(nodes, agg, gout, w_node):
    width = nodes.shape[1]
    pre = dot(nodes, w_node[:width]) + dot(agg, w_node[width:])
    sig = jax.nn.sigmoid(pre)
    out = (nodes.astype(F32) + pre * sig).astype(BF16)
    gout = gout.astype(F32)
    d_node = (gout * (sig * (1.0 + pre * (1.0 - sig)))).astype(BF16)
    back = dot(d_node, w_node, ((1,), (1,)))
    return out, d_node, gout + back[:, :width], back[:, width:].astype(BF16)


def own_body(
    nodes_ref, msg_ref, a_hbm, cot_ref, w_node_ref,
    own_ref, out_ref, agg_ref, d_node_ref, d_nodes1_ref, d_agg_ref, a_ref, a_sems,
):
    rows, width = nodes_ref.shape
    rim = RIM * ROWS
    msg = msg_ref[...]
    loads = []
    for k in range(rows // rim):
        part = pl.ds(k * RIM, RIM)
        loads.append(pltpu.make_async_copy(a_hbm.at[part], a_ref.at[part], a_sems.at[k]))
        loads[k].start()
    for k in range(rows // rim):
        mine = slice(k * rim, (k + 1) * rim)
        loads[k].wait()
        window = dot(a_ref[k * RIM : (k + 1) * RIM].reshape(rim, rows), msg).astype(BF16)
        if k == 0:
            own_ref[:rim, :] = window
        elif k == rows // rim - 1:
            own_ref[rim:, :] = window
        else:
            here = slice((k - 1) * rim, k * rim)
            agg_ref[here, :] = window
            out, d_node, d_nodes1, d_agg = node_step(nodes_ref[mine, :], window, cot_ref[mine, :], w_node_ref[...])
            out_ref[here, :] = out
            d_node_ref[here, :] = d_node
            d_nodes1_ref[here, :] = d_nodes1
            d_agg_ref[here, :] = d_agg


def rim_body(
    nodes_ref, own_ref, near_in_ref, far_in_ref, cot_ref, w_node_ref,
    near_ref, far_ref, out_ref, agg_ref, d_node_ref, d_nodes1_ref, d_agg_ref,
):
    rows = nodes_ref.shape[0]
    rim = RIM * ROWS
    arrived = chosen(near_in_ref[...].astype(F32), far_in_ref[...].astype(F32))
    rims = []
    for k in range(2):
        mine = slice(k * (rows - rim), k * (rows - rim) + rim)
        here = slice(k * rim, (k + 1) * rim)
        agg = (own_ref[here, :].astype(F32) + arrived[k]).astype(BF16)
        agg_ref[here, :] = agg
        out, d_node, d_nodes1, d_agg = node_step(nodes_ref[mine, :], agg, cot_ref[mine, :], w_node_ref[...])
        out_ref[here, :] = out
        d_node_ref[here, :] = d_node
        d_nodes1_ref[here, :] = d_nodes1
        d_agg_ref[here, :] = d_agg
        rims.append(d_agg)
    near_ref[...], far_ref[...] = chosen(rims[0], rims[1])


def in_order(mid_ref, rim_ref):
    rim = RIM * ROWS
    return jnp.concatenate([rim_ref[:rim, :], mid_ref[...], rim_ref[rim:, :]], axis=0)


def grad_node_body(scale, nodes_ref, agg_mid_ref, agg_rim_ref, d_node_mid_ref, d_node_rim_ref, *out_refs):
    width = nodes_ref.shape[1]
    d_node = in_order(d_node_mid_ref, d_node_rim_ref)
    agg = in_order(agg_mid_ref, agg_rim_ref)
    first = lax.axis_index("dp") == 0
    for k, left in enumerate((nodes_ref[...], agg)):
        mine = slice(k * width, (k + 1) * width)
        grad = dot(left, d_node, ((0,), (0,))) * scale
        if len(out_refs) == 1:
            out_refs[0][mine, :] = grad
            continue
        half = width // 2
        out_refs[0][mine, :] = jnp.where(first, grad[:, :half], grad[:, half:])
        out_refs[1][mine, :] = jnp.where(first, grad[:, half:], grad[:, :half]).astype(BF16)


def behind_body(
    nodes_ref, at_ref, w_edge_ref, out_mid_ref, out_rim_ref, d_agg_mid_ref, d_agg_rim_ref,
    out_ref, d_msg_ref, slope_ref,
):
    rows = nodes_ref.shape[0]
    rim = RIM * ROWS
    out_ref[...] = in_order(out_mid_ref, out_rim_ref)
    d_agg = in_order(d_agg_mid_ref, d_agg_rim_ref)
    for k in range(rows // rim):
        mine = slice(k * rim, (k + 1) * rim)
        d_msg_ref[mine, :] = dot(at_ref[mine, :rows], d_agg)
        pre = dot(nodes_ref[mine, :], w_edge_ref[...])
        sig = jax.nn.sigmoid(pre)
        slope_ref[mine, :] = sig * (1.0 + pre * (1.0 - sig))


def edge_body(
    scale, nodes_ref, at_ref, near_ref, far_ref, d_msg_ref, slope_ref, mid_ref, rim_ref, w_edge_ref,
    back_ref, g_edge_ref, d_edge_ref,
):
    rows, width = nodes_ref.shape
    rim = RIM * ROWS
    prev, after = chosen(near_ref[...], far_ref[...])
    rims = jnp.concatenate([prev, after], axis=0)
    w_edge = w_edge_ref[...]
    for k in range(rows // rim):
        mine = slice(k * rim, (k + 1) * rim)
        d_msg = d_msg_ref[mine, :] + dot(at_ref[mine, rows : rows + 2 * rim], rims)
        d_edge = (d_msg.astype(BF16).astype(F32) * slope_ref[mine, :]).astype(BF16)
        d_edge_ref[mine, :] = d_edge
        if k == 0:
            d_nodes1 = rim_ref[:rim, :]
        elif k == rows // rim - 1:
            d_nodes1 = rim_ref[rim:, :]
        else:
            d_nodes1 = mid_ref[(k - 1) * rim : k * rim, :]
        back_ref[mine, :] = (d_nodes1 + dot(d_edge, w_edge, ((1,), (1,)))).astype(BF16)
    g_edge_ref[...] = dot(nodes_ref[...], d_edge_ref[...], ((0,), (0,))) * scale


def bit_of(mask):
    return lax.rem(lax.div(lax.axis_index("dom"), mask), 2)


def cut_body(edge_ref, node_ref, node_in_ref, keep_ref, *refs):
    send_refs, total_ref = refs[:-1], refs[-1]
    size, half = keep_ref.shape
    few, more = edge_ref.shape[0] // 4, node_ref.shape[0] // 4
    for q in range(4):
        row = q * size
        mine = slice(q * more, (q + 1) * more)
        total_ref[row : row + more, :] = node_ref[mine, :] + node_in_ref[mine, :].astype(F32)
        row += more
        mine = slice(q * few, (q + 1) * few)
        total_ref[row : row + few, :] = edge_ref[mine, :half]
        total_ref[row + few : row + 2 * few, :] = edge_ref[mine, half:]
    core, side = bit_of(CORE), bit_of(ALONG_Y)

    def piece(core, side):
        return total_ref[pl.ds(pl.multiple_of((2 * core + side) * size, 16), size), :]

    keep_ref[...] = piece(core, side)
    for ref, (c, y) in zip(send_refs, ((1 - core, side), (core, 1 - side), (1 - core, 1 - side))):
        ref[...] = piece(c, y).astype(BF16)


def sum_all_body(keep_ref, *refs):
    total = keep_ref[...]
    for ref in refs[:-1]:
        total = total + ref[...].astype(F32)
    refs[-1][...] = total.astype(BF16)


def sum_body(mine_ref, in_ref, out_ref):
    out_ref[...] = (mine_ref[...].astype(F32) + in_ref[...].astype(F32)).astype(BF16)


def join_body(mask, mine_ref, dp_ref, y_ref, both_ref, out_ref):
    size, half = mine_ref.shape
    more = size // 2
    few = more // 2
    first = lax.axis_index("dp") == 0
    low = bit_of(mask) == 0
    mine = [ref[...] for ref in (mine_ref, dp_ref)]
    other = [ref[...] for ref in (y_ref, both_ref)]
    for side in range(2):
        a, b = (jnp.where(low, x, y) if side == 0 else jnp.where(low, y, x) for x, y in zip(mine, other))
        row = side * (few + more)
        total = (a[more:].astype(F32) + b[more:].astype(F32)).astype(BF16)
        out_ref[row : row + few, :half] = total[:few]
        out_ref[row : row + few, half:] = total[few:]
        row += few
        out_ref[row : row + more, :half] = jnp.where(first, a[:more], b[:more])
        out_ref[row : row + more, half:] = jnp.where(first, b[:more], a[:more])


def finish_body(mask, mine_ref, in_ref, edge_ref, node_ref):
    few, more = edge_ref.shape[0] // 4, node_ref.shape[0] // 4
    low = bit_of(mask) == 0
    mine, other = mine_ref[...].astype(F32), in_ref[...].astype(F32)
    for side, value in enumerate((jnp.where(low, mine, other), jnp.where(low, other, mine))):
        for part in range(2):
            q = 2 * side + part
            row = part * (few + more)
            edge_ref[q * few : (q + 1) * few, :] = value[row : row + few]
            node_ref[q * more : (q + 1) * more, :] = value[row + few : row + few + more]


def swapped_both(x, mask):
    peers = lax.axis_size("dom")
    total = 2 * peers
    return lax.ppermute(x, ("dp", "dom"), [(i, (i + peers) % total ^ mask) for i in range(total)])


def cut_grads(edge_part, node_part):
    half = node_part[0].shape[1]
    size = node_part[0].shape[0] + 2 * edge_part.shape[0]
    piece = shape(size // 4, half)
    keep, *send = call(
        cut_body,
        [shape(size // 4, half, dtype=F32), piece, piece, piece],
        (edge_part, *node_part),
        scratch=[pltpu.VMEM((size, half), F32)],
    )
    masks = (CORE, ALONG_Y, CORE | ALONG_Y)
    return keep, [swapped(part, "dom", mask) for part, mask in zip(send, masks)]


def joined(keep, parts, back, width, stage):
    out = [shape(*keep.shape)]
    (mine,) = call(sum_all_body, out, (keep, *parts), nbytes=stage)
    for mask in (ALONG_Z, 2 * ALONG_Z):
        (mine,) = call(sum_body, out, (mine, swapped(mine, "dom", mask)), nbytes=stage)
    (mine,) = call(
        functools.partial(join_body, ALONG_Y),
        [shape(6 * (width // 4), width)],
        (mine, swapped(mine, "dp", 1), swapped(mine, "dom", ALONG_Y), swapped_both(mine, ALONG_Y)),
        nbytes=stage,
    )
    mine, back = lax.optimization_barrier((mine, back))
    grad_edge, grad_node = call(
        functools.partial(finish_body, CORE),
        [shape(width, width, dtype=F32), shape(2 * width, width, dtype=F32)],
        (mine, swapped(mine, "dom", CORE)),
        nbytes=stage,
    )
    return grad_edge, grad_node, back


def place_body(order_ref, back_ref, out_ref):
    rows = back_ref.shape[0]
    back = back_ref[...]
    order = jnp.broadcast_to(order_ref[...], (ROWS, rows))
    for k in range(rows // ROWS):
        mine = slice(k * ROWS, (k + 1) * ROWS)
        row = lax.broadcasted_iota(jnp.int32, (ROWS, rows), 0) + k * ROWS
        hot = jnp.where(order == row, 1.0, 0.0).astype(BF16)
        out_ref[mine, :] = dot(hot, back).astype(BF16)


def shards(features, send_order, adj_count, adj_target, adj_vals, w_edge, w_node, cotangent):
    ndp = lax.axis_size("dp")
    ndom = lax.axis_size("dom")
    rows, width = features.shape[1:]
    per_peer = rows // ndom
    blocks, slots = adj_vals.shape[:2]
    rim = RIM * ROWS
    scale = 1.0 / math.sqrt(float(ndp * rows * ndom))
    tall = shape(rows, width)
    tall_f = shape(rows, width, dtype=F32)
    edge = shape(rim, width)
    rims = shape(2 * rim, width)
    mid = shape(rows - 2 * rim, width)
    unit = rows * width * 2
    square = 2 * rows * width * width

    (picked,) = call(
        pick_body,
        [tall],
        (send_order, features[0]),
        [ANY, ANY],
        [
            pltpu.VMEM((1, rows), jnp.int32),
            pltpu.VMEM((rows, width), BF16),
            pltpu.VMEM((2 * ROWS, rows), BF16),
            pltpu.SemaphoreType.DMA,
            pltpu.SemaphoreType.DMA,
        ],
        flops=2 * rows * rows * width,
        nbytes=2 * unit,
        limit=56 * MIB,
    )
    nodes = lax.all_to_all(
        picked.reshape(ndom, per_peer, width), "dom", split_axis=0, concat_axis=0, tiled=True
    ).reshape(rows, width)
    spots = blocks + 2 * RIM + 1
    adj, adj_t, adj_rim = call(
        build_body,
        [shape(blocks, ROWS, rows), shape(rows, spots * ROWS), shape(STORE // (2 * ROWS * rows), ROWS, rows)],
        (adj_count, adj_target, adj_vals),
        [SMEM, SMEM, VMEM],
        [pltpu.VMEM((spots, ROWS, rows), BF16), pltpu.SemaphoreType.DMA],
        nbytes=16 * unit,
        out_specs=[VMEM, VMEM, ANY],
        limit=40 * MIB,
    )
    near, far, msg = call(
        message_body,
        [edge, edge, tall],
        (nodes, adj_rim, w_edge),
        [VMEM, ANY, VMEM],
        [pltpu.VMEM((2 * RIM, ROWS, rows), BF16), pltpu.SemaphoreType.DMA((2 * RIM,))],
        flops=square + 4 * rim * rows * width,
        nbytes=4 * unit,
        limit=40 * MIB,
    )
    far = swapped_across(far, "dom")
    near = swapped(near, "dom", 1)
    cot = cotangent[0]
    own, out_mid, agg_mid, d_node_mid, d_nodes1_mid, d_agg_mid = call(
        own_body,
        [rims, mid, mid, mid, shape(*mid.shape, dtype=F32), mid],
        (nodes, msg, adj, cot, w_node),
        [VMEM, VMEM, ANY, VMEM, VMEM],
        [pltpu.VMEM((blocks, ROWS, rows), BF16), pltpu.SemaphoreType.DMA((rows // rim,))],
        flops=2 * rows * rows * width + 2 * square,
        nbytes=8 * unit,
    )
    near, far, out_rim, agg_rim, d_node_rim, d_nodes1_rim, d_agg_rim = call(
        rim_body,
        [edge, edge, rims, rims, rims, shape(*rims.shape, dtype=F32), rims],
        (nodes, own, near, far, cot, w_node),
        flops=2 * square,
        nbytes=4 * unit,
    )
    far = swapped_across(far, "dom")
    near = swapped(near, "dom", 1)
    tiled = ndp == 2 and ndom == 16

    node_part = call(
        functools.partial(grad_node_body, scale),
        [shape(2 * width, width // 2, dtype=F32), shape(2 * width, width // 2)]
        if tiled
        else [shape(2 * width, width, dtype=F32)],
        (nodes, agg_mid, agg_rim, d_node_mid, d_node_rim),
        flops=2 * square,
        nbytes=3 * unit,
    )
    if tiled:
        node_part = (node_part[0], swapped(node_part[1], "dp", 1))
    node_out, d_msg, slope = call(
        behind_body,
        [tall, tall_f, tall_f],
        (nodes, adj_t, w_edge, out_mid, out_rim, d_agg_mid, d_agg_rim),
        flops=2 * rows * rows * width + square,
        nbytes=8 * unit,
    )
    back, edge_part = call(
        functools.partial(edge_body, scale),
        [tall, shape(width, width, dtype=F32)],
        (nodes, adj_t, near, far, d_msg, slope, d_nodes1_mid, d_nodes1_rim, w_edge),
        scratch=[pltpu.VMEM((rows, width), BF16)],
        flops=2 * square + 4 * rim * rows * width,
        nbytes=8 * unit,
    )
    if tiled:
        keep, parts = cut_grads(edge_part, node_part)
    back = lax.all_to_all(
        back.reshape(ndom, per_peer, width), "dom", split_axis=0, concat_axis=0, tiled=True
    ).reshape(rows, width)
    if tiled:
        grad_edge, grad_node, back = joined(keep, parts, back, width, 32 * unit)
    else:
        grad_edge, grad_node = (lax.psum(part, ("dp", "dom")) for part in (edge_part, node_part[0]))
    (grad_brick,) = call(place_body, [tall], (send_order, back), flops=2 * rows * rows * width, nbytes=2 * unit)
    return (node_out[None], grad_brick[None], grad_edge, grad_node)


def solution(mesh):
    in_specs = (
        P("dp", "dom", None),
        P("dom", None),
        P("dom"),
        P("dom", None),
        P("dom", None, None, None),
        P(),
        P(),
        P("dp", "dom", None),
    )
    out_specs = (P("dp", "dom", None), P("dp", "dom", None), P(), P())
    return jax.shard_map(shards, mesh=mesh, in_specs=in_specs, out_specs=out_specs, check_vma=False)
```

```python
import functools
import math

import jax
import jax.numpy as jnp
from jax import lax
from jax.experimental import pallas as pl
from jax.experimental.pallas import tpu as pltpu
from jax.sharding import PartitionSpec as P

ROWS = 128
RIM = 2
ANY = pl.BlockSpec(memory_space=pl.ANY)
VMEM = pl.BlockSpec(memory_space=pltpu.VMEM)
SMEM = pl.BlockSpec(memory_space=pltpu.SMEM)
BF16 = jnp.bfloat16
F32 = jnp.float32
MIB = 1024 * 1024
STORE = 24 * MIB
CORE, ALONG_Y, ALONG_Z = 1, 2, 4


def swapped(x, axis, mask):
    peers = lax.axis_size(axis)
    return lax.ppermute(x, axis, [(i, i ^ mask) for i in range(peers)])


def swapped_across(x, axis):
    peers = lax.axis_size(axis)
    return lax.ppermute(x, axis, [(i, (i + 1 if i % 2 else i - 1) % peers) for i in range(peers)])


def dot(a, b, contract=((1,), (0,))):
    return lax.dot_general(a, b, (contract, ((), ())), preferred_element_type=F32)


def shape(*dims, dtype=BF16):
    return jax.ShapeDtypeStruct(dims, dtype)


def call(body, outs, args, specs=None, scratch=(), flops=0, nbytes=0, limit=24 * MIB, out_specs=None):
    return pl.pallas_call(
        body,
        out_shape=outs,
        in_specs=specs or [VMEM] * len(args),
        out_specs=out_specs or [VMEM] * len(outs),
        scratch_shapes=list(scratch),
        cost_estimate=pl.CostEstimate(flops=flops, bytes_accessed=nbytes, transcendentals=0),
        compiler_params=pltpu.CompilerParams(vmem_limit_bytes=limit),
    )(*args)


def pick_body(order_hbm, feat_hbm, out_ref, order_ref, feat_ref, hot_ref, order_sem, feat_sem):
    rows = feat_ref.shape[0]
    early = hot_ref.shape[0] // ROWS
    load_order = pltpu.make_async_copy(order_hbm, order_ref, order_sem)
    load_feat = pltpu.make_async_copy(feat_hbm, feat_ref, feat_sem)
    load_order.start()
    load_feat.start()
    lane = lax.broadcasted_iota(jnp.int32, (ROWS, rows), 1).astype(F32)
    load_order.wait()

    def hot_rows(k):
        row = order_ref[:, k * ROWS : (k + 1) * ROWS].astype(F32)
        col = jnp.transpose(jnp.broadcast_to(row, (ROWS, ROWS)))
        wide = jnp.concatenate([col] * (rows // ROWS), axis=1)
        return jnp.where(wide == lane, 1.0, 0.0).astype(BF16)

    for k in range(early):
        hot_ref[k * ROWS : (k + 1) * ROWS, :] = hot_rows(k)
    load_feat.wait()
    feat = feat_ref[...]
    for k in range(rows // ROWS):
        mine = slice(k * ROWS, (k + 1) * ROWS)
        hot = hot_ref[mine, :] if k < early else hot_rows(k)
        out_ref[mine, :] = dot(hot, feat).astype(BF16)


def build_body(cnt_ref, tgt_ref, vals_ref, rim_ref, at_ref, own_hbm, a_ref, sem):
    blocks, slots = vals_ref.shape[:2]
    spare = blocks + 2 * RIM
    a_ref[...] = jnp.zeros_like(a_ref)
    at_ref[...] = jnp.zeros_like(at_ref)
    for c in range(blocks):
        mine = slice(c * ROWS, (c + 1) * ROWS)
        for s in range(slots):
            w = tgt_ref[c, s]
            at = jnp.where(w < blocks, w + RIM, jnp.where(w < 2 * blocks, w - blocks, w - blocks + RIM))
            at = jnp.where(s < cnt_ref[c], at, spare)
            value = vals_ref[c, s].astype(F32)
            a_ref[at, :, mine] = (a_ref[at, :, mine].astype(F32) + value).astype(BF16)
            lanes = pl.ds(pl.multiple_of(at * ROWS, ROWS), ROWS)
            at_ref[mine, lanes] = (at_ref[mine, lanes].astype(F32) + jnp.transpose(value)).astype(BF16)
    put = pltpu.make_async_copy(a_ref.at[pl.ds(0, blocks)], own_hbm.at[pl.ds(0, blocks)], sem)
    put.start()
    rim_ref[...] = a_ref[blocks:spare]
    put.wait()


def chosen(first, second):
    odd = lax.rem(lax.axis_index("dom"), 2) == 1
    return jnp.where(odd, first, second), jnp.where(odd, second, first)


def message_body(nodes_ref, a_ref, w_edge_ref, near_ref, far_ref, msg_ref):
    rows = nodes_ref.shape[0]
    rim = RIM * ROWS
    for k in range(rows // rim):
        mine = slice(k * rim, (k + 1) * rim)
        pre = dot(nodes_ref[mine, :], w_edge_ref[...])
        msg_ref[mine, :] = (pre * jax.nn.sigmoid(pre)).astype(BF16)
    sums = dot(a_ref[...].reshape(2 * rim, rows), msg_ref[...])
    near, far = chosen(sums[:rim], sums[rim:])
    near_ref[...] = near.astype(BF16)
    far_ref[...] = far.astype(BF16)


def node_step(nodes, agg, gout, w_node):
    width = nodes.shape[1]
    pre = dot(nodes, w_node[:width]) + dot(agg, w_node[width:])
    sig = jax.nn.sigmoid(pre)
    out = (nodes.astype(F32) + pre * sig).astype(BF16)
    gout = gout.astype(F32)
    d_node = (gout * (sig * (1.0 + pre * (1.0 - sig)))).astype(BF16)
    back = dot(d_node, w_node, ((1,), (1,)))
    return out, d_node, gout + back[:, :width], back[:, width:].astype(BF16)


def own_body(
    nodes_ref, msg_ref, a_hbm, cot_ref, w_node_ref,
    own_ref, out_ref, agg_ref, d_node_ref, d_nodes1_ref, d_agg_ref, a_ref, a_sems,
):
    rows, width = nodes_ref.shape
    rim = RIM * ROWS
    msg = msg_ref[...]
    loads = []
    for k in range(rows // rim):
        part = pl.ds(k * RIM, RIM)
        loads.append(pltpu.make_async_copy(a_hbm.at[part], a_ref.at[part], a_sems.at[k]))
        loads[k].start()
    for k in range(rows // rim):
        mine = slice(k * rim, (k + 1) * rim)
        loads[k].wait()
        window = dot(a_ref[k * RIM : (k + 1) * RIM].reshape(rim, rows), msg).astype(BF16)
        if k == 0:
            own_ref[:rim, :] = window
        elif k == rows // rim - 1:
            own_ref[rim:, :] = window
        else:
            here = slice((k - 1) * rim, k * rim)
            agg_ref[here, :] = window
            out, d_node, d_nodes1, d_agg = node_step(nodes_ref[mine, :], window, cot_ref[mine, :], w_node_ref[...])
            out_ref[here, :] = out
            d_node_ref[here, :] = d_node
            d_nodes1_ref[here, :] = d_nodes1
            d_agg_ref[here, :] = d_agg


def rim_body(
    nodes_ref, own_ref, near_in_ref, far_in_ref, cot_ref, w_node_ref,
    near_ref, far_ref, out_ref, agg_ref, d_node_ref, d_nodes1_ref, d_agg_ref,
):
    rows = nodes_ref.shape[0]
    rim = RIM * ROWS
    arrived = chosen(near_in_ref[...].astype(F32), far_in_ref[...].astype(F32))
    rims = []
    for k in range(2):
        mine = slice(k * (rows - rim), k * (rows - rim) + rim)
        here = slice(k * rim, (k + 1) * rim)
        agg = (own_ref[here, :].astype(F32) + arrived[k]).astype(BF16)
        agg_ref[here, :] = agg
        out, d_node, d_nodes1, d_agg = node_step(nodes_ref[mine, :], agg, cot_ref[mine, :], w_node_ref[...])
        out_ref[here, :] = out
        d_node_ref[here, :] = d_node
        d_nodes1_ref[here, :] = d_nodes1
        d_agg_ref[here, :] = d_agg
        rims.append(d_agg)
    near_ref[...], far_ref[...] = chosen(rims[0], rims[1])


def in_order(mid_ref, rim_ref):
    rim = RIM * ROWS
    return jnp.concatenate([rim_ref[:rim, :], mid_ref[...], rim_ref[rim:, :]], axis=0)


def grad_node_body(scale, nodes_ref, agg_mid_ref, agg_rim_ref, d_node_mid_ref, d_node_rim_ref, *out_refs):
    width = nodes_ref.shape[1]
    d_node = in_order(d_node_mid_ref, d_node_rim_ref)
    agg = in_order(agg_mid_ref, agg_rim_ref)
    first = lax.axis_index("dp") == 0
    for k, left in enumerate((nodes_ref[...], agg)):
        mine = slice(k * width, (k + 1) * width)
        grad = dot(left, d_node, ((0,), (0,))) * scale
        if len(out_refs) == 1:
            out_refs[0][mine, :] = grad
            continue
        half = width // 2
        out_refs[0][mine, :] = jnp.where(first, grad[:, :half], grad[:, half:])
        out_refs[1][mine, :] = jnp.where(first, grad[:, half:], grad[:, :half]).astype(BF16)


def behind_body(
    nodes_ref, at_ref, w_edge_ref, out_mid_ref, out_rim_ref, d_agg_mid_ref, d_agg_rim_ref,
    out_ref, d_msg_ref, slope_ref,
):
    rows = nodes_ref.shape[0]
    rim = RIM * ROWS
    out_ref[...] = in_order(out_mid_ref, out_rim_ref)
    d_agg = in_order(d_agg_mid_ref, d_agg_rim_ref)
    for k in range(rows // rim):
        mine = slice(k * rim, (k + 1) * rim)
        d_msg_ref[mine, :] = dot(at_ref[mine, :rows], d_agg)
        pre = dot(nodes_ref[mine, :], w_edge_ref[...])
        sig = jax.nn.sigmoid(pre)
        slope_ref[mine, :] = sig * (1.0 + pre * (1.0 - sig))


def edge_body(
    scale, nodes_ref, at_ref, near_ref, far_ref, d_msg_ref, slope_ref, mid_ref, rim_ref, w_edge_ref,
    back_ref, g_edge_ref, d_edge_ref,
):
    rows, width = nodes_ref.shape
    rim = RIM * ROWS
    prev, after = chosen(near_ref[...], far_ref[...])
    rims = jnp.concatenate([prev, after], axis=0)
    w_edge = w_edge_ref[...]
    for k in range(rows // rim):
        mine = slice(k * rim, (k + 1) * rim)
        d_msg = d_msg_ref[mine, :] + dot(at_ref[mine, rows : rows + 2 * rim], rims)
        d_edge = (d_msg.astype(BF16).astype(F32) * slope_ref[mine, :]).astype(BF16)
        d_edge_ref[mine, :] = d_edge
        if k == 0:
            d_nodes1 = rim_ref[:rim, :]
        elif k == rows // rim - 1:
            d_nodes1 = rim_ref[rim:, :]
        else:
            d_nodes1 = mid_ref[(k - 1) * rim : k * rim, :]
        back_ref[mine, :] = (d_nodes1 + dot(d_edge, w_edge, ((1,), (1,)))).astype(BF16)
    g_edge_ref[...] = dot(nodes_ref[...], d_edge_ref[...], ((0,), (0,))) * scale


def bit_of(mask):
    return lax.rem(lax.div(lax.axis_index("dom"), mask), 2)


def cut_body(edge_ref, node_ref, node_in_ref, keep_ref, *refs):
    send_refs, total_ref = refs[:-1], refs[-1]
    size, half = keep_ref.shape
    few, more = edge_ref.shape[0] // 4, node_ref.shape[0] // 4
    for q in range(4):
        row = q * size
        mine = slice(q * more, (q + 1) * more)
        total_ref[row : row + more, :] = node_ref[mine, :] + node_in_ref[mine, :].astype(F32)
        row += more
        mine = slice(q * few, (q + 1) * few)
        total_ref[row : row + few, :] = edge_ref[mine, :half]
        total_ref[row + few : row + 2 * few, :] = edge_ref[mine, half:]
    core, side = bit_of(CORE), bit_of(ALONG_Y)

    def piece(core, side):
        return total_ref[pl.ds(pl.multiple_of((2 * core + side) * size, 16), size), :]

    keep_ref[...] = piece(core, side)
    for ref, (c, y) in zip(send_refs, ((1 - core, side), (core, 1 - side), (1 - core, 1 - side))):
        ref[...] = piece(c, y).astype(BF16)


def sum_all_body(keep_ref, *refs):
    total = keep_ref[...]
    for ref in refs[:-1]:
        total = total + ref[...].astype(F32)
    refs[-1][...] = total.astype(BF16)


def sum_body(mine_ref, in_ref, out_ref):
    out_ref[...] = (mine_ref[...].astype(F32) + in_ref[...].astype(F32)).astype(BF16)


def join_body(mask, mine_ref, dp_ref, y_ref, both_ref, out_ref):
    size, half = mine_ref.shape
    more = size // 2
    few = more // 2
    first = lax.axis_index("dp") == 0
    low = bit_of(mask) == 0
    mine = [ref[...] for ref in (mine_ref, dp_ref)]
    other = [ref[...] for ref in (y_ref, both_ref)]
    for side in range(2):
        a, b = (jnp.where(low, x, y) if side == 0 else jnp.where(low, y, x) for x, y in zip(mine, other))
        row = side * (few + more)
        total = (a[more:].astype(F32) + b[more:].astype(F32)).astype(BF16)
        out_ref[row : row + few, :half] = total[:few]
        out_ref[row : row + few, half:] = total[few:]
        row += few
        out_ref[row : row + more, :half] = jnp.where(first, a[:more], b[:more])
        out_ref[row : row + more, half:] = jnp.where(first, b[:more], a[:more])


def finish_body(own, *refs):
    part_ref = refs[0]
    edge_hbm, node_hbm, edge_ref, node_ref, sems = refs[-5:]
    few, more = edge_ref.shape[0] // 2, node_ref.shape[0] // 2
    for k in range(2):
        row = k * (few + more)
        edge_ref[k * few : (k + 1) * few, :] = part_ref[row : row + few, :].astype(F32)
        node_ref[k * more : (k + 1) * more, :] = part_ref[row + few : row + few + more, :].astype(F32)
    side = bit_of(CORE) if own else 1 - bit_of(CORE)
    puts = []
    for k, (ref, hbm) in enumerate(((edge_ref, edge_hbm), (node_ref, node_hbm))):
        size = ref.shape[0]
        to = hbm.at[pl.ds(pl.multiple_of(side * size, 8), size), :]
        puts.append(pltpu.make_async_copy(ref, to, sems.at[k]))
        puts[k].start()
    for put in puts:
        put.wait()


def finished(own, part, grads, width):
    outs = [shape(width, width, dtype=F32), shape(2 * width, width, dtype=F32)]
    return pl.pallas_call(
        functools.partial(finish_body, own),
        out_shape=outs,
        in_specs=[VMEM] + [ANY] * len(grads),
        out_specs=[ANY, ANY],
        scratch_shapes=[
            pltpu.VMEM((width // 2, width), F32),
            pltpu.VMEM((width, width), F32),
            pltpu.SemaphoreType.DMA((2,)),
        ],
        input_output_aliases={1: 0, 2: 1} if grads else {},
        cost_estimate=pl.CostEstimate(flops=0, bytes_accessed=3 * width * width * 4, transcendentals=0),
        compiler_params=pltpu.CompilerParams(vmem_limit_bytes=24 * MIB),
    )(part, *grads)


def swapped_both(x, mask):
    peers = lax.axis_size("dom")
    total = 2 * peers
    return lax.ppermute(x, ("dp", "dom"), [(i, (i + peers) % total ^ mask) for i in range(total)])


def cut_grads(edge_part, node_part):
    half = node_part[0].shape[1]
    size = node_part[0].shape[0] + 2 * edge_part.shape[0]
    piece = shape(size // 4, half)
    keep, *send = call(
        cut_body,
        [shape(size // 4, half, dtype=F32), piece, piece, piece],
        (edge_part, *node_part),
        scratch=[pltpu.VMEM((size, half), F32)],
    )
    masks = (CORE, ALONG_Y, CORE | ALONG_Y)
    return keep, [swapped(part, "dom", mask) for part, mask in zip(send, masks)]


def joined(keep, parts, width, stage):
    out = [shape(*keep.shape)]
    (mine,) = call(sum_all_body, out, (keep, *parts), nbytes=stage)
    for mask in (ALONG_Z, 2 * ALONG_Z):
        (mine,) = call(sum_body, out, (mine, swapped(mine, "dom", mask)), nbytes=stage)
    (mine,) = call(
        functools.partial(join_body, ALONG_Y),
        [shape(6 * (width // 4), width)],
        (mine, swapped(mine, "dp", 1), swapped(mine, "dom", ALONG_Y), swapped_both(mine, ALONG_Y)),
        nbytes=stage,
    )
    return mine


def ended(mine, grad_brick, width):
    mine, grad_brick = lax.optimization_barrier((mine, grad_brick))
    other = swapped(mine, "dom", CORE)
    grads = finished(True, mine, (), width)
    return *finished(False, other, grads, width), grad_brick


def place_body(order_ref, back_ref, out_ref):
    rows = back_ref.shape[0]
    back = back_ref[...]
    order = jnp.broadcast_to(order_ref[...], (ROWS, rows))
    for k in range(rows // ROWS):
        mine = slice(k * ROWS, (k + 1) * ROWS)
        row = lax.broadcasted_iota(jnp.int32, (ROWS, rows), 0) + k * ROWS
        hot = jnp.where(order == row, 1.0, 0.0).astype(BF16)
        out_ref[mine, :] = dot(hot, back).astype(BF16)


def shards(features, send_order, adj_count, adj_target, adj_vals, w_edge, w_node, cotangent):
    ndp = lax.axis_size("dp")
    ndom = lax.axis_size("dom")
    rows, width = features.shape[1:]
    per_peer = rows // ndom
    blocks, slots = adj_vals.shape[:2]
    rim = RIM * ROWS
    scale = 1.0 / math.sqrt(float(ndp * rows * ndom))
    tall = shape(rows, width)
    tall_f = shape(rows, width, dtype=F32)
    edge = shape(rim, width)
    rims = shape(2 * rim, width)
    mid = shape(rows - 2 * rim, width)
    unit = rows * width * 2
    square = 2 * rows * width * width

    (picked,) = call(
        pick_body,
        [tall],
        (send_order, features[0]),
        [ANY, ANY],
        [
            pltpu.VMEM((1, rows), jnp.int32),
            pltpu.VMEM((rows, width), BF16),
            pltpu.VMEM((2 * ROWS, rows), BF16),
            pltpu.SemaphoreType.DMA,
            pltpu.SemaphoreType.DMA,
        ],
        flops=2 * rows * rows * width,
        nbytes=2 * unit,
        limit=56 * MIB,
    )
    nodes = lax.all_to_all(
        picked.reshape(ndom, per_peer, width), "dom", split_axis=0, concat_axis=0, tiled=True
    ).reshape(rows, width)
    spots = blocks + 2 * RIM + 1
    adj_rim, adj_t, adj = call(
        build_body,
        [shape(2 * RIM, ROWS, rows), shape(rows, spots * ROWS), shape(STORE // (2 * ROWS * rows), ROWS, rows)],
        (adj_count, adj_target, adj_vals),
        [SMEM, SMEM, VMEM],
        [pltpu.VMEM((spots, ROWS, rows), BF16), pltpu.SemaphoreType.DMA],
        nbytes=16 * unit,
        out_specs=[VMEM, VMEM, ANY],
        limit=40 * MIB,
    )
    near, far, msg = call(
        message_body,
        [edge, edge, tall],
        (nodes, adj_rim, w_edge),
        flops=square + 4 * rim * rows * width,
        nbytes=4 * unit,
    )
    far = swapped_across(far, "dom")
    near = swapped(near, "dom", 1)
    cot = cotangent[0]
    own, out_mid, agg_mid, d_node_mid, d_nodes1_mid, d_agg_mid = call(
        own_body,
        [rims, mid, mid, mid, shape(*mid.shape, dtype=F32), mid],
        (nodes, msg, adj, cot, w_node),
        [VMEM, VMEM, ANY, VMEM, VMEM],
        [pltpu.VMEM((blocks, ROWS, rows), BF16), pltpu.SemaphoreType.DMA((rows // rim,))],
        flops=2 * rows * rows * width + 2 * square,
        nbytes=8 * unit,
        limit=40 * MIB,
    )
    near, far, out_rim, agg_rim, d_node_rim, d_nodes1_rim, d_agg_rim = call(
        rim_body,
        [edge, edge, rims, rims, rims, shape(*rims.shape, dtype=F32), rims],
        (nodes, own, near, far, cot, w_node),
        flops=2 * square,
        nbytes=4 * unit,
    )
    far = swapped_across(far, "dom")
    near = swapped(near, "dom", 1)
    tiled = ndp == 2 and ndom == 16

    node_part = call(
        functools.partial(grad_node_body, scale),
        [shape(2 * width, width // 2, dtype=F32), shape(2 * width, width // 2)]
        if tiled
        else [shape(2 * width, width, dtype=F32)],
        (nodes, agg_mid, agg_rim, d_node_mid, d_node_rim),
        flops=2 * square,
        nbytes=3 * unit,
    )
    if tiled:
        node_part = (node_part[0], swapped(node_part[1], "dp", 1))
    node_out, d_msg, slope = call(
        behind_body,
        [tall, tall_f, tall_f],
        (nodes, adj_t, w_edge, out_mid, out_rim, d_agg_mid, d_agg_rim),
        flops=2 * rows * rows * width + square,
        nbytes=8 * unit,
    )
    back, edge_part = call(
        functools.partial(edge_body, scale),
        [tall, shape(width, width, dtype=F32)],
        (nodes, adj_t, near, far, d_msg, slope, d_nodes1_mid, d_nodes1_rim, w_edge),
        scratch=[pltpu.VMEM((rows, width), BF16)],
        flops=2 * square + 4 * rim * rows * width,
        nbytes=8 * unit,
    )
    if tiled:
        back, node_in = lax.optimization_barrier((back, node_part[1]))
        keep, parts = cut_grads(edge_part, (node_part[0], node_in))
    back = lax.all_to_all(
        back.reshape(ndom, per_peer, width), "dom", split_axis=0, concat_axis=0, tiled=True
    ).reshape(rows, width)
    if tiled:
        mine = joined(keep, parts, width, 32 * unit)
    else:
        grad_edge, grad_node = (lax.psum(part, ("dp", "dom")) for part in (edge_part, node_part[0]))
    (grad_brick,) = call(place_body, [tall], (send_order, back), flops=2 * rows * rows * width, nbytes=2 * unit)
    if tiled:
        grad_edge, grad_node, grad_brick = ended(mine, grad_brick, width)
    return (node_out[None], grad_brick[None], grad_edge, grad_node)


def solution(mesh):
    in_specs = (
        P("dp", "dom", None),
        P("dom", None),
        P("dom"),
        P("dom", None),
        P("dom", None, None, None),
        P(),
        P(),
        P("dp", "dom", None),
    )
    out_specs = (P("dp", "dom", None), P("dp", "dom", None), P(), P())
    return jax.shard_map(shards, mesh=mesh, in_specs=in_specs, out_specs=out_specs, check_vma=False)
```

```python
import functools
import math

import jax
import jax.numpy as jnp
from jax import lax
from jax.experimental import pallas as pl
from jax.experimental.pallas import tpu as pltpu
from jax.sharding import PartitionSpec as P

ROWS = 128
RIM = 2
ANY = pl.BlockSpec(memory_space=pl.ANY)
VMEM = pl.BlockSpec(memory_space=pltpu.VMEM)
SMEM = pl.BlockSpec(memory_space=pltpu.SMEM)
BF16 = jnp.bfloat16
F32 = jnp.float32
MIB = 1024 * 1024
CORE, ALONG_Y, ALONG_Z = 1, 2, 4


def swapped(x, axis, mask):
    peers = lax.axis_size(axis)
    return lax.ppermute(x, axis, [(i, i ^ mask) for i in range(peers)])


def swapped_across(x, axis):
    peers = lax.axis_size(axis)
    return lax.ppermute(x, axis, [(i, (i + 1 if i % 2 else i - 1) % peers) for i in range(peers)])


def dot(a, b, contract=((1,), (0,))):
    return lax.dot_general(a, b, (contract, ((), ())), preferred_element_type=F32)


def shape(*dims, dtype=BF16):
    return jax.ShapeDtypeStruct(dims, dtype)


def call(body, outs, args, specs=None, scratch=(), flops=0, nbytes=0, limit=24 * MIB, out_specs=None):
    return pl.pallas_call(
        body,
        out_shape=outs,
        in_specs=specs or [VMEM] * len(args),
        out_specs=out_specs or [VMEM] * len(outs),
        scratch_shapes=list(scratch),
        cost_estimate=pl.CostEstimate(flops=flops, bytes_accessed=nbytes, transcendentals=0),
        compiler_params=pltpu.CompilerParams(vmem_limit_bytes=limit),
    )(*args)


def pick_body(order_hbm, feat_hbm, out_hbm, order_ref, feat_ref, hot_ref, out_ref, order_sem, feat_sem, out_sems):
    rows = feat_ref.shape[0]
    early = hot_ref.shape[0] // ROWS
    load_order = pltpu.make_async_copy(order_hbm, order_ref, order_sem)
    load_feat = pltpu.make_async_copy(feat_hbm, feat_ref, feat_sem)
    load_order.start()
    load_feat.start()
    lane = lax.broadcasted_iota(jnp.int32, (ROWS, rows), 1).astype(F32)
    load_order.wait()

    def hot_rows(k):
        row = order_ref[:, k * ROWS : (k + 1) * ROWS].astype(F32)
        col = jnp.transpose(jnp.broadcast_to(row, (ROWS, ROWS)))
        wide = jnp.concatenate([col] * (rows // ROWS), axis=1)
        return jnp.where(wide == lane, 1.0, 0.0).astype(BF16)

    for k in range(early):
        hot_ref[k * ROWS : (k + 1) * ROWS, :] = hot_rows(k)
    load_feat.wait()
    feat = feat_ref[...]
    puts = []
    for k in range(rows // ROWS):
        mine = slice(k * ROWS, (k + 1) * ROWS)
        hot = hot_ref[mine, :] if k < early else hot_rows(k)
        out_ref[mine, :] = dot(hot, feat).astype(BF16)
        puts.append(pltpu.make_async_copy(out_ref.at[pl.ds(k * ROWS, ROWS)], out_hbm.at[pl.ds(k * ROWS, ROWS)], out_sems.at[k]))
        puts[k].start()
    for put in puts:
        put.wait()


def build_body(cnt_ref, tgt_ref, vals_ref, own_ref, rim_ref, at_ref, a_ref):
    blocks, slots = vals_ref.shape[:2]
    spare = blocks + 2 * RIM
    a_ref[...] = jnp.zeros_like(a_ref)
    at_ref[...] = jnp.zeros_like(at_ref)
    for c in range(blocks):
        mine = slice(c * ROWS, (c + 1) * ROWS)
        for s in range(slots):
            w = tgt_ref[c, s]
            at = jnp.where(w < blocks, w + RIM, jnp.where(w < 2 * blocks, w - blocks, w - blocks + RIM))
            at = jnp.where(s < cnt_ref[c], at, spare)
            value = vals_ref[c, s].astype(F32)
            a_ref[at, :, mine] = (a_ref[at, :, mine].astype(F32) + value).astype(BF16)
            lanes = pl.ds(pl.multiple_of(at * ROWS, ROWS), ROWS)
            at_ref[mine, lanes] = (at_ref[mine, lanes].astype(F32) + jnp.transpose(value)).astype(BF16)
    own_ref[...] = a_ref[:blocks]
    rim_ref[...] = a_ref[blocks:spare]


def chosen(first, second):
    odd = lax.rem(lax.axis_index("dom"), 2) == 1
    return jnp.where(odd, first, second), jnp.where(odd, second, first)


def message_body(nodes_ref, a_ref, w_edge_ref, near_ref, far_ref, msg_ref):
    rows = nodes_ref.shape[0]
    rim = RIM * ROWS
    for k in range(rows // rim):
        mine = slice(k * rim, (k + 1) * rim)
        pre = dot(nodes_ref[mine, :], w_edge_ref[...])
        msg_ref[mine, :] = (pre * jax.nn.sigmoid(pre)).astype(BF16)
    sums = dot(a_ref[...].reshape(2 * rim, rows), msg_ref[...])
    near, far = chosen(sums[:rim], sums[rim:])
    near_ref[...] = near.astype(BF16)
    far_ref[...] = far.astype(BF16)


def node_step(nodes, agg, gout, w_node):
    width = nodes.shape[1]
    pre = dot(nodes, w_node[:width]) + dot(agg, w_node[width:])
    sig = jax.nn.sigmoid(pre)
    out = (nodes.astype(F32) + pre * sig).astype(BF16)
    gout = gout.astype(F32)
    d_node = (gout * (sig * (1.0 + pre * (1.0 - sig)))).astype(BF16)
    back = dot(d_node, w_node, ((1,), (1,)))
    return out, d_node, gout + back[:, :width], back[:, width:].astype(BF16)


def own_body(
    nodes_ref, msg_ref, a_hbm, cot_ref, w_node_ref,
    own_ref, out_ref, agg_ref, d_node_ref, d_nodes1_ref, d_agg_ref, a_ref, a_sems,
):
    rows, width = nodes_ref.shape
    rim = RIM * ROWS
    msg = msg_ref[...]
    loads = []
    for k in range(rows // rim):
        part = pl.ds(k * RIM, RIM)
        loads.append(pltpu.make_async_copy(a_hbm.at[part], a_ref.at[part], a_sems.at[k]))
        loads[k].start()
    for k in range(rows // rim):
        mine = slice(k * rim, (k + 1) * rim)
        loads[k].wait()
        window = dot(a_ref[k * RIM : (k + 1) * RIM].reshape(rim, rows), msg).astype(BF16)
        if k == 0:
            own_ref[:rim, :] = window
        elif k == rows // rim - 1:
            own_ref[rim:, :] = window
        else:
            here = slice((k - 1) * rim, k * rim)
            agg_ref[here, :] = window
            out, d_node, d_nodes1, d_agg = node_step(nodes_ref[mine, :], window, cot_ref[mine, :], w_node_ref[...])
            out_ref[here, :] = out
            d_node_ref[here, :] = d_node
            d_nodes1_ref[here, :] = d_nodes1
            d_agg_ref[here, :] = d_agg


def rim_body(
    nodes_ref, own_ref, near_in_ref, far_in_ref, cot_ref, w_node_ref,
    near_ref, far_ref, out_ref, agg_ref, d_node_ref, d_nodes1_ref, d_agg_ref,
):
    rows = nodes_ref.shape[0]
    rim = RIM * ROWS
    arrived = chosen(near_in_ref[...].astype(F32), far_in_ref[...].astype(F32))
    rims = []
    for k in range(2):
        mine = slice(k * (rows - rim), k * (rows - rim) + rim)
        here = slice(k * rim, (k + 1) * rim)
        agg = (own_ref[here, :].astype(F32) + arrived[k]).astype(BF16)
        agg_ref[here, :] = agg
        out, d_node, d_nodes1, d_agg = node_step(nodes_ref[mine, :], agg, cot_ref[mine, :], w_node_ref[...])
        out_ref[here, :] = out
        d_node_ref[here, :] = d_node
        d_nodes1_ref[here, :] = d_nodes1
        d_agg_ref[here, :] = d_agg
        rims.append(d_agg)
    near_ref[...], far_ref[...] = chosen(rims[0], rims[1])


def in_order(mid_ref, rim_ref):
    rim = RIM * ROWS
    return jnp.concatenate([rim_ref[:rim, :], mid_ref[...], rim_ref[rim:, :]], axis=0)


def grad_node_body(scale, nodes_ref, agg_mid_ref, agg_rim_ref, d_node_mid_ref, d_node_rim_ref, *out_refs):
    width = nodes_ref.shape[1]
    d_node = in_order(d_node_mid_ref, d_node_rim_ref)
    agg = in_order(agg_mid_ref, agg_rim_ref)
    first = lax.axis_index("dp") == 0
    for k, left in enumerate((nodes_ref[...], agg)):
        mine = slice(k * width, (k + 1) * width)
        grad = dot(left, d_node, ((0,), (0,))) * scale
        if len(out_refs) == 1:
            out_refs[0][mine, :] = grad
            continue
        half = width // 2
        out_refs[0][mine, :] = jnp.where(first, grad[:, :half], grad[:, half:])
        out_refs[1][mine, :] = jnp.where(first, grad[:, half:], grad[:, :half]).astype(BF16)


def behind_body(
    nodes_ref, at_ref, w_edge_ref, out_mid_ref, out_rim_ref, d_agg_mid_ref, d_agg_rim_ref,
    out_ref, d_msg_ref, slope_ref,
):
    rows = nodes_ref.shape[0]
    rim = RIM * ROWS
    out_ref[...] = in_order(out_mid_ref, out_rim_ref)
    d_agg = in_order(d_agg_mid_ref, d_agg_rim_ref)
    for k in range(rows // rim):
        mine = slice(k * rim, (k + 1) * rim)
        d_msg_ref[mine, :] = dot(at_ref[mine, :rows], d_agg)
        pre = dot(nodes_ref[mine, :], w_edge_ref[...])
        sig = jax.nn.sigmoid(pre)
        slope_ref[mine, :] = sig * (1.0 + pre * (1.0 - sig))


def edge_body(
    scale, nodes_ref, at_ref, near_ref, far_ref, d_msg_ref, slope_ref, mid_ref, rim_ref, w_edge_ref,
    back_hbm, g_edge_ref, d_edge_ref, back_ref, sems,
):
    rows, width = nodes_ref.shape
    rim = RIM * ROWS
    prev, after = chosen(near_ref[...], far_ref[...])
    rims = jnp.concatenate([prev, after], axis=0)
    w_edge = w_edge_ref[...]
    puts = []
    for k in range(rows // rim):
        mine = slice(k * rim, (k + 1) * rim)
        d_msg = d_msg_ref[mine, :] + dot(at_ref[mine, rows : rows + 2 * rim], rims)
        d_edge = (d_msg.astype(BF16).astype(F32) * slope_ref[mine, :]).astype(BF16)
        d_edge_ref[mine, :] = d_edge
        if k == 0:
            d_nodes1 = rim_ref[:rim, :]
        elif k == rows // rim - 1:
            d_nodes1 = rim_ref[rim:, :]
        else:
            d_nodes1 = mid_ref[(k - 1) * rim : k * rim, :]
        back_ref[mine, :] = (d_nodes1 + dot(d_edge, w_edge, ((1,), (1,)))).astype(BF16)
        part = pl.ds(k * rim, rim)
        puts.append(pltpu.make_async_copy(back_ref.at[part], back_hbm.at[part], sems.at[k]))
        puts[k].start()
    g_edge_ref[...] = dot(nodes_ref[...], d_edge_ref[...], ((0,), (0,))) * scale
    for put in puts:
        put.wait()


def bit_of(mask):
    return lax.rem(lax.div(lax.axis_index("dom"), mask), 2)


def cut_rows(total_ref, mask, keep_ref, send_ref):
    size = keep_ref.shape[0]
    bit = bit_of(mask)
    keep_ref[...] = total_ref[pl.ds(pl.multiple_of(bit * size, 16), size), :]
    send_ref[...] = total_ref[pl.ds(pl.multiple_of((1 - bit) * size, 16), size), :].astype(BF16)


def first_cut_body(mask, edge_ref, node_ref, node_in_ref, keep_ref, send_ref, total_ref):
    half = node_ref.shape[1]
    few, more = edge_ref.shape[0] // 4, node_ref.shape[0] // 4
    for q in range(4):
        row = q * (2 * few + more)
        mine = slice(q * more, (q + 1) * more)
        total_ref[row : row + more, :] = node_ref[mine, :] + node_in_ref[mine, :].astype(F32)
        row += more
        mine = slice(q * few, (q + 1) * few)
        total_ref[row : row + few, :] = edge_ref[mine, :half]
        total_ref[row + few : row + 2 * few, :] = edge_ref[mine, half:]
    cut_rows(total_ref, mask, keep_ref, send_ref)


def next_cut_body(mask, mine_ref, in_ref, keep_ref, send_ref, total_ref):
    total_ref[...] = mine_ref[...] + in_ref[...].astype(F32)
    cut_rows(total_ref, mask, keep_ref, send_ref)


def sum_body(mine_ref, in_ref, out_ref):
    out_ref[...] = (mine_ref[...].astype(F32) + in_ref[...].astype(F32)).astype(BF16)


def join_body(mask, mine_ref, dp_ref, y_ref, both_ref, out_ref):
    size, half = mine_ref.shape
    more = size // 2
    few = more // 2
    first = lax.axis_index("dp") == 0
    low = bit_of(mask) == 0
    mine = [ref[...] for ref in (mine_ref, dp_ref)]
    other = [ref[...] for ref in (y_ref, both_ref)]
    for side in range(2):
        a, b = (jnp.where(low, x, y) if side == 0 else jnp.where(low, y, x) for x, y in zip(mine, other))
        row = side * (few + more)
        total = (a[more:].astype(F32) + b[more:].astype(F32)).astype(BF16)
        out_ref[row : row + few, :half] = total[:few]
        out_ref[row : row + few, half:] = total[few:]
        row += few
        out_ref[row : row + more, :half] = jnp.where(first, a[:more], b[:more])
        out_ref[row : row + more, half:] = jnp.where(first, b[:more], a[:more])


def finish_body(own, *refs):
    part_ref = refs[0]
    edge_hbm, node_hbm, edge_ref, node_ref, sems = refs[-5:]
    few, more = edge_ref.shape[0] // 2, node_ref.shape[0] // 2
    for k in range(2):
        row = k * (few + more)
        edge_ref[k * few : (k + 1) * few, :] = part_ref[row : row + few, :].astype(F32)
        node_ref[k * more : (k + 1) * more, :] = part_ref[row + few : row + few + more, :].astype(F32)
    side = bit_of(CORE) if own else 1 - bit_of(CORE)
    puts = []
    for k, (ref, hbm) in enumerate(((edge_ref, edge_hbm), (node_ref, node_hbm))):
        size = ref.shape[0]
        to = hbm.at[pl.ds(pl.multiple_of(side * size, 8), size), :]
        puts.append(pltpu.make_async_copy(ref, to, sems.at[k]))
        puts[k].start()
    for put in puts:
        put.wait()


def finished(own, part, grads, width):
    outs = [shape(width, width, dtype=F32), shape(2 * width, width, dtype=F32)]
    return pl.pallas_call(
        functools.partial(finish_body, own),
        out_shape=outs,
        in_specs=[VMEM] + [ANY] * len(grads),
        out_specs=[ANY, ANY],
        scratch_shapes=[
            pltpu.VMEM((width // 2, width), F32),
            pltpu.VMEM((width, width), F32),
            pltpu.SemaphoreType.DMA((2,)),
        ],
        input_output_aliases={1: 0, 2: 1} if grads else {},
        cost_estimate=pl.CostEstimate(flops=0, bytes_accessed=3 * width * width * 4, transcendentals=0),
        compiler_params=pltpu.CompilerParams(vmem_limit_bytes=24 * MIB),
    )(part, *grads)


def swapped_both(x, mask):
    peers = lax.axis_size("dom")
    total = 2 * peers
    return lax.ppermute(x, ("dp", "dom"), [(i, (i + peers) % total ^ mask) for i in range(total)])


def cut_grads(edge_part, node_part):
    half = node_part[0].shape[1]
    size = node_part[0].shape[0] + 2 * edge_part.shape[0]

    def cut(body, mask, args, size):
        return call(
            functools.partial(body, mask),
            [shape(size // 2, half, dtype=F32), shape(size // 2, half)],
            args,
            scratch=[pltpu.VMEM((size, half), F32)],
        )

    keep, send = cut(first_cut_body, CORE, (edge_part, *node_part), size)
    return cut(next_cut_body, ALONG_Y, (keep, swapped(send, "dom", CORE)), size // 2)


def joined(keep, send, back, send_order, width):
    out = [shape(*send.shape)]
    (mine,) = call(sum_body, out, (keep, swapped(send, "dom", ALONG_Y)))
    for mask in (ALONG_Z, 2 * ALONG_Z):
        (mine,) = call(sum_body, out, (mine, swapped(mine, "dom", mask)))
    others = swapped(mine, "dp", 1), swapped(mine, "dom", ALONG_Y), swapped_both(mine, ALONG_Y)
    grad_brick = placed(send_order, back)
    mine, grad_brick = lax.optimization_barrier((mine, grad_brick))
    (mine,) = call(functools.partial(join_body, ALONG_Y), [shape(6 * (width // 4), width)], (mine, *others))
    grads = finished(True, mine, (), width)
    return *finished(False, swapped(mine, "dom", CORE), grads, width), grad_brick


def placed(send_order, back):
    rows, width = back.shape
    return call(
        place_body,
        [shape(rows, width)],
        (send_order, back),
        flops=2 * rows * rows * width,
        nbytes=4 * rows * width,
    )[0]


def place_body(order_ref, back_ref, out_ref):
    rows = back_ref.shape[0]
    back = back_ref[...]
    order = jnp.broadcast_to(order_ref[...], (ROWS, rows))
    for k in range(rows // ROWS):
        mine = slice(k * ROWS, (k + 1) * ROWS)
        row = lax.broadcasted_iota(jnp.int32, (ROWS, rows), 0) + k * ROWS
        hot = jnp.where(order == row, 1.0, 0.0).astype(BF16)
        out_ref[mine, :] = dot(hot, back).astype(BF16)


def shards(features, send_order, adj_count, adj_target, adj_vals, w_edge, w_node, cotangent):
    ndp = lax.axis_size("dp")
    ndom = lax.axis_size("dom")
    rows, width = features.shape[1:]
    per_peer = rows // ndom
    blocks, slots = adj_vals.shape[:2]
    rim = RIM * ROWS
    scale = 1.0 / math.sqrt(float(ndp * rows * ndom))
    tall = shape(rows, width)
    tall_f = shape(rows, width, dtype=F32)
    edge = shape(rim, width)
    rims = shape(2 * rim, width)
    mid = shape(rows - 2 * rim, width)
    unit = rows * width * 2
    square = 2 * rows * width * width

    (picked,) = call(
        pick_body,
        [tall],
        (send_order, features[0]),
        [ANY, ANY],
        [
            pltpu.VMEM((1, rows), jnp.int32),
            pltpu.VMEM((rows, width), BF16),
            pltpu.VMEM((2 * ROWS, rows), BF16),
            pltpu.VMEM((rows, width), BF16),
            pltpu.SemaphoreType.DMA,
            pltpu.SemaphoreType.DMA,
            pltpu.SemaphoreType.DMA((blocks,)),
        ],
        flops=2 * rows * rows * width,
        nbytes=2 * unit,
        out_specs=[ANY],
        limit=56 * MIB,
    )
    nodes = lax.all_to_all(
        picked.reshape(ndom, per_peer, width), "dom", split_axis=0, concat_axis=0, tiled=True
    ).reshape(rows, width)
    spots = blocks + 2 * RIM + 1
    adj, adj_rim, adj_t = call(
        build_body,
        [shape(blocks, ROWS, rows), shape(2 * RIM, ROWS, rows), shape(rows, spots * ROWS)],
        (adj_count, adj_target, adj_vals),
        [SMEM, SMEM, VMEM],
        [pltpu.VMEM((spots, ROWS, rows), BF16)],
        nbytes=16 * unit,
    )
    near, far, msg = call(
        message_body,
        [edge, edge, tall],
        (nodes, adj_rim, w_edge),
        flops=square + 4 * rim * rows * width,
        nbytes=4 * unit,
    )
    far = swapped_across(far, "dom")
    near = swapped(near, "dom", 1)
    cot = cotangent[0]
    own, out_mid, agg_mid, d_node_mid, d_nodes1_mid, d_agg_mid = call(
        own_body,
        [rims, mid, mid, mid, shape(*mid.shape, dtype=F32), mid],
        (nodes, msg, adj, cot, w_node),
        [VMEM, VMEM, ANY, VMEM, VMEM],
        [pltpu.VMEM((blocks, ROWS, rows), BF16), pltpu.SemaphoreType.DMA((rows // rim,))],
        flops=2 * rows * rows * width + 2 * square,
        nbytes=8 * unit,
    )
    near, far, out_rim, agg_rim, d_node_rim, d_nodes1_rim, d_agg_rim = call(
        rim_body,
        [edge, edge, rims, rims, rims, shape(*rims.shape, dtype=F32), rims],
        (nodes, own, near, far, cot, w_node),
        flops=2 * square,
        nbytes=4 * unit,
    )
    far = swapped_across(far, "dom")
    near = swapped(near, "dom", 1)
    tiled = ndp == 2 and ndom == 16

    node_part = call(
        functools.partial(grad_node_body, scale),
        [shape(2 * width, width // 2, dtype=F32), shape(2 * width, width // 2)]
        if tiled
        else [shape(2 * width, width, dtype=F32)],
        (nodes, agg_mid, agg_rim, d_node_mid, d_node_rim),
        flops=2 * square,
        nbytes=3 * unit,
    )
    if tiled:
        node_part = (node_part[0], swapped(node_part[1], "dp", 1))
    node_out, d_msg, slope = call(
        behind_body,
        [tall, tall_f, tall_f],
        (nodes, adj_t, w_edge, out_mid, out_rim, d_agg_mid, d_agg_rim),
        flops=2 * rows * rows * width + square,
        nbytes=8 * unit,
    )
    back, edge_part = call(
        functools.partial(edge_body, scale),
        [tall, shape(width, width, dtype=F32)],
        (nodes, adj_t, near, far, d_msg, slope, d_nodes1_mid, d_nodes1_rim, w_edge),
        scratch=[
            pltpu.VMEM((rows, width), BF16),
            pltpu.VMEM((rows, width), BF16),
            pltpu.SemaphoreType.DMA((rows // rim,)),
        ],
        out_specs=[ANY, VMEM],
        flops=2 * square + 4 * rim * rows * width,
        nbytes=8 * unit,
    )
    if tiled:
        keep, send = cut_grads(edge_part, node_part)
        back, send = lax.optimization_barrier((back, send))
    back = lax.all_to_all(
        back.reshape(ndom, per_peer, width), "dom", split_axis=0, concat_axis=0, tiled=True
    ).reshape(rows, width)
    if tiled:
        grad_edge, grad_node, grad_brick = joined(keep, send, back, send_order, width)
    else:
        grad_edge, grad_node = (lax.psum(part, ("dp", "dom")) for part in (edge_part, node_part[0]))
        grad_brick = placed(send_order, back)
    return (node_out[None], grad_brick[None], grad_edge, grad_node)


def solution(mesh):
    in_specs = (
        P("dp", "dom", None),
        P("dom", None),
        P("dom"),
        P("dom", None),
        P("dom", None, None, None),
        P(),
        P(),
        P("dp", "dom", None),
    )
    out_specs = (P("dp", "dom", None), P("dp", "dom", None), P(), P())
    return jax.shard_map(shards, mesh=mesh, in_specs=in_specs, out_specs=out_specs, check_vma=False)
```

```python
import functools
import math

import jax
import jax.numpy as jnp
from jax import lax
from jax.experimental import pallas as pl
from jax.experimental.pallas import tpu as pltpu
from jax.sharding import PartitionSpec as P

ROWS = 128
RIM = 2
ANY = pl.BlockSpec(memory_space=pl.ANY)
VMEM = pl.BlockSpec(memory_space=pltpu.VMEM)
SMEM = pl.BlockSpec(memory_space=pltpu.SMEM)
BF16 = jnp.bfloat16
F32 = jnp.float32
MIB = 1024 * 1024
CORE, ALONG_Y, ALONG_Z = 1, 2, 4


def swapped(x, axis, mask):
    peers = lax.axis_size(axis)
    return lax.ppermute(x, axis, [(i, i ^ mask) for i in range(peers)])


def swapped_across(x, axis):
    peers = lax.axis_size(axis)
    return lax.ppermute(x, axis, [(i, (i + 1 if i % 2 else i - 1) % peers) for i in range(peers)])


def dot(a, b, contract=((1,), (0,))):
    return lax.dot_general(a, b, (contract, ((), ())), preferred_element_type=F32)


def shape(*dims, dtype=BF16):
    return jax.ShapeDtypeStruct(dims, dtype)


def call(body, outs, args, specs=None, scratch=(), flops=0, nbytes=0, limit=24 * MIB, out_specs=None):
    return pl.pallas_call(
        body,
        out_shape=outs,
        in_specs=specs or [VMEM] * len(args),
        out_specs=out_specs or [VMEM] * len(outs),
        scratch_shapes=list(scratch),
        cost_estimate=pl.CostEstimate(flops=flops, bytes_accessed=nbytes, transcendentals=0),
        compiler_params=pltpu.CompilerParams(vmem_limit_bytes=limit),
    )(*args)


def pick_body(order_hbm, feat_hbm, out_hbm, order_ref, feat_ref, hot_ref, out_ref, order_sem, feat_sem, out_sems):
    rows = feat_ref.shape[0]
    early = hot_ref.shape[0] // ROWS
    load_order = pltpu.make_async_copy(order_hbm, order_ref, order_sem)
    load_feat = pltpu.make_async_copy(feat_hbm, feat_ref, feat_sem)
    load_order.start()
    load_feat.start()
    lane = lax.broadcasted_iota(jnp.int32, (ROWS, ROWS), 1).astype(F32)
    zero = jnp.zeros((ROWS, ROWS), BF16)
    load_order.wait()

    def column(row):
        return jnp.transpose(jnp.broadcast_to(row.astype(F32), (ROWS, ROWS)))

    def hot_rows(k):
        row = order_ref[:, k * ROWS : (k + 1) * ROWS]
        high = column(row // ROWS).astype(BF16)
        low = jnp.where(column(row % ROWS) == lane, 1.0, 0.0).astype(BF16)
        return jnp.concatenate([jnp.where(high == b, low, zero) for b in range(rows // ROWS)], axis=1)

    for k in range(early):
        hot_ref[k * ROWS : (k + 1) * ROWS, :] = hot_rows(k)
    load_feat.wait()
    feat = feat_ref[...]
    puts = []
    for k in range(rows // ROWS):
        mine = slice(k * ROWS, (k + 1) * ROWS)
        hot = hot_ref[mine, :] if k < early else hot_rows(k)
        out_ref[mine, :] = dot(hot, feat).astype(BF16)
        puts.append(pltpu.make_async_copy(out_ref.at[pl.ds(k * ROWS, ROWS)], out_hbm.at[pl.ds(k * ROWS, ROWS)], out_sems.at[k]))
        puts[k].start()
    for put in puts:
        put.wait()


def build_body(cnt_ref, tgt_ref, vals_ref, own_ref, rim_ref, at_ref, a_ref):
    blocks, slots = vals_ref.shape[:2]
    spare = blocks + 2 * RIM
    a_ref[...] = jnp.zeros_like(a_ref)
    at_ref[...] = jnp.zeros_like(at_ref)
    for c in range(blocks):
        mine = slice(c * ROWS, (c + 1) * ROWS)
        for s in range(slots):
            w = tgt_ref[c, s]
            at = jnp.where(w < blocks, w + RIM, jnp.where(w < 2 * blocks, w - blocks, w - blocks + RIM))
            at = jnp.where(s < cnt_ref[c], at, spare)
            value = vals_ref[c, s].astype(F32)
            a_ref[at, :, mine] = (a_ref[at, :, mine].astype(F32) + value).astype(BF16)
            lanes = pl.ds(pl.multiple_of(at * ROWS, ROWS), ROWS)
            at_ref[mine, lanes] = (at_ref[mine, lanes].astype(F32) + jnp.transpose(value)).astype(BF16)
    own_ref[...] = a_ref[:blocks]
    rim_ref[...] = a_ref[blocks:spare]


def chosen(first, second):
    odd = lax.rem(lax.axis_index("dom"), 2) == 1
    return jnp.where(odd, first, second), jnp.where(odd, second, first)


def message_body(nodes_ref, a_ref, w_edge_ref, near_ref, far_ref, msg_ref):
    rows = nodes_ref.shape[0]
    rim = RIM * ROWS
    for k in range(rows // rim):
        mine = slice(k * rim, (k + 1) * rim)
        pre = dot(nodes_ref[mine, :], w_edge_ref[...])
        msg_ref[mine, :] = (pre * jax.nn.sigmoid(pre)).astype(BF16)
    sums = dot(a_ref[...].reshape(2 * rim, rows), msg_ref[...])
    near, far = chosen(sums[:rim], sums[rim:])
    near_ref[...] = near.astype(BF16)
    far_ref[...] = far.astype(BF16)


def node_step(nodes, agg, gout, w_node):
    width = nodes.shape[1]
    pre = dot(nodes, w_node[:width]) + dot(agg, w_node[width:])
    sig = jax.nn.sigmoid(pre)
    out = (nodes.astype(F32) + pre * sig).astype(BF16)
    gout = gout.astype(F32)
    d_node = (gout * (sig * (1.0 + pre * (1.0 - sig)))).astype(BF16)
    back = dot(d_node, w_node, ((1,), (1,)))
    return out, d_node, gout + back[:, :width], back[:, width:].astype(BF16)


def own_body(
    nodes_ref, msg_ref, a_hbm, cot_ref, w_node_ref,
    own_ref, out_ref, agg_ref, d_node_ref, d_nodes1_ref, d_agg_ref, a_ref, a_sems,
):
    rows, width = nodes_ref.shape
    rim = RIM * ROWS
    msg = msg_ref[...]
    loads = []
    for k in range(rows // rim):
        part = pl.ds(k * RIM, RIM)
        loads.append(pltpu.make_async_copy(a_hbm.at[part], a_ref.at[part], a_sems.at[k]))
        loads[k].start()
    for k in range(rows // rim):
        mine = slice(k * rim, (k + 1) * rim)
        loads[k].wait()
        window = dot(a_ref[k * RIM : (k + 1) * RIM].reshape(rim, rows), msg).astype(BF16)
        if k == 0:
            own_ref[:rim, :] = window
        elif k == rows // rim - 1:
            own_ref[rim:, :] = window
        else:
            here = slice((k - 1) * rim, k * rim)
            agg_ref[here, :] = window
            out, d_node, d_nodes1, d_agg = node_step(nodes_ref[mine, :], window, cot_ref[mine, :], w_node_ref[...])
            out_ref[here, :] = out
            d_node_ref[here, :] = d_node
            d_nodes1_ref[here, :] = d_nodes1
            d_agg_ref[here, :] = d_agg


def rim_body(
    nodes_ref, own_ref, near_in_ref, far_in_ref, cot_ref, w_node_ref,
    near_ref, far_ref, out_ref, agg_ref, d_node_ref, d_nodes1_ref, d_agg_ref,
):
    rows = nodes_ref.shape[0]
    rim = RIM * ROWS
    arrived = chosen(near_in_ref[...].astype(F32), far_in_ref[...].astype(F32))
    rims = []
    for k in range(2):
        mine = slice(k * (rows - rim), k * (rows - rim) + rim)
        here = slice(k * rim, (k + 1) * rim)
        agg = (own_ref[here, :].astype(F32) + arrived[k]).astype(BF16)
        agg_ref[here, :] = agg
        out, d_node, d_nodes1, d_agg = node_step(nodes_ref[mine, :], agg, cot_ref[mine, :], w_node_ref[...])
        out_ref[here, :] = out
        d_node_ref[here, :] = d_node
        d_nodes1_ref[here, :] = d_nodes1
        d_agg_ref[here, :] = d_agg
        rims.append(d_agg)
    near_ref[...], far_ref[...] = chosen(rims[0], rims[1])


def in_order(mid_ref, rim_ref):
    rim = RIM * ROWS
    return jnp.concatenate([rim_ref[:rim, :], mid_ref[...], rim_ref[rim:, :]], axis=0)


def grad_node_body(scale, nodes_ref, agg_mid_ref, agg_rim_ref, d_node_mid_ref, d_node_rim_ref, *out_refs):
    width = nodes_ref.shape[1]
    d_node = in_order(d_node_mid_ref, d_node_rim_ref)
    agg = in_order(agg_mid_ref, agg_rim_ref)
    first = lax.axis_index("dp") == 0
    for k, left in enumerate((nodes_ref[...], agg)):
        mine = slice(k * width, (k + 1) * width)
        grad = dot(left, d_node, ((0,), (0,))) * scale
        if len(out_refs) == 1:
            out_refs[0][mine, :] = grad
            continue
        half = width // 2
        out_refs[0][mine, :] = jnp.where(first, grad[:, :half], grad[:, half:])
        out_refs[1][mine, :] = jnp.where(first, grad[:, half:], grad[:, :half]).astype(BF16)


def behind_body(
    nodes_ref, at_ref, w_edge_ref, out_mid_ref, out_rim_ref, d_agg_mid_ref, d_agg_rim_ref,
    out_ref, d_msg_ref, slope_ref,
):
    rows = nodes_ref.shape[0]
    rim = RIM * ROWS
    out_ref[...] = in_order(out_mid_ref, out_rim_ref)
    d_agg = in_order(d_agg_mid_ref, d_agg_rim_ref)
    for k in range(rows // rim):
        mine = slice(k * rim, (k + 1) * rim)
        d_msg_ref[mine, :] = dot(at_ref[mine, :rows], d_agg)
        pre = dot(nodes_ref[mine, :], w_edge_ref[...])
        sig = jax.nn.sigmoid(pre)
        slope_ref[mine, :] = sig * (1.0 + pre * (1.0 - sig))


def edge_body(
    scale, nodes_ref, at_ref, near_ref, far_ref, d_msg_ref, slope_ref, mid_ref, rim_ref, w_edge_ref,
    back_hbm, g_edge_ref, d_edge_ref, back_ref, sems,
):
    rows, width = nodes_ref.shape
    rim = RIM * ROWS
    prev, after = chosen(near_ref[...], far_ref[...])
    rims = jnp.concatenate([prev, after], axis=0)
    w_edge = w_edge_ref[...]
    puts = []
    for k in range(rows // rim):
        mine = slice(k * rim, (k + 1) * rim)
        d_msg = d_msg_ref[mine, :] + dot(at_ref[mine, rows : rows + 2 * rim], rims)
        d_edge = (d_msg.astype(BF16).astype(F32) * slope_ref[mine, :]).astype(BF16)
        d_edge_ref[mine, :] = d_edge
        if k == 0:
            d_nodes1 = rim_ref[:rim, :]
        elif k == rows // rim - 1:
            d_nodes1 = rim_ref[rim:, :]
        else:
            d_nodes1 = mid_ref[(k - 1) * rim : k * rim, :]
        back_ref[mine, :] = (d_nodes1 + dot(d_edge, w_edge, ((1,), (1,)))).astype(BF16)
        part = pl.ds(k * rim, rim)
        puts.append(pltpu.make_async_copy(back_ref.at[part], back_hbm.at[part], sems.at[k]))
        puts[k].start()
    g_edge_ref[...] = dot(nodes_ref[...], d_edge_ref[...], ((0,), (0,))) * scale
    for put in puts:
        put.wait()


def bit_of(mask):
    return lax.rem(lax.div(lax.axis_index("dom"), mask), 2)


def cut_rows(total_ref, mask, keep_ref, send_ref):
    size = keep_ref.shape[0]
    bit = bit_of(mask)
    keep_ref[...] = total_ref[pl.ds(pl.multiple_of(bit * size, 16), size), :]
    send_ref[...] = total_ref[pl.ds(pl.multiple_of((1 - bit) * size, 16), size), :].astype(BF16)


def first_cut_body(mask, edge_ref, node_ref, node_in_ref, keep_ref, send_ref, total_ref):
    half = node_ref.shape[1]
    few, more = edge_ref.shape[0] // 4, node_ref.shape[0] // 4
    for q in range(4):
        row = q * (2 * few + more)
        mine = slice(q * more, (q + 1) * more)
        total_ref[row : row + more, :] = node_ref[mine, :] + node_in_ref[mine, :].astype(F32)
        row += more
        mine = slice(q * few, (q + 1) * few)
        total_ref[row : row + few, :] = edge_ref[mine, :half]
        total_ref[row + few : row + 2 * few, :] = edge_ref[mine, half:]
    cut_rows(total_ref, mask, keep_ref, send_ref)


def next_cut_body(mask, mine_ref, in_ref, keep_ref, send_ref, total_ref):
    total_ref[...] = mine_ref[...] + in_ref[...].astype(F32)
    cut_rows(total_ref, mask, keep_ref, send_ref)


def sum_body(mine_ref, in_ref, out_ref):
    out_ref[...] = (mine_ref[...].astype(F32) + in_ref[...].astype(F32)).astype(BF16)


def join_body(mask, mine_ref, dp_ref, y_ref, both_ref, out_ref):
    size, half = mine_ref.shape
    more = size // 2
    few = more // 2
    first = lax.axis_index("dp") == 0
    low = bit_of(mask) == 0
    mine = [ref[...] for ref in (mine_ref, dp_ref)]
    other = [ref[...] for ref in (y_ref, both_ref)]
    for side in range(2):
        a, b = (jnp.where(low, x, y) if side == 0 else jnp.where(low, y, x) for x, y in zip(mine, other))
        row = side * (few + more)
        total = (a[more:].astype(F32) + b[more:].astype(F32)).astype(BF16)
        out_ref[row : row + few, :half] = total[:few]
        out_ref[row : row + few, half:] = total[few:]
        row += few
        out_ref[row : row + more, :half] = jnp.where(first, a[:more], b[:more])
        out_ref[row : row + more, half:] = jnp.where(first, b[:more], a[:more])


def finish_body(own, *refs):
    part_ref = refs[0]
    edge_hbm, node_hbm, edge_ref, node_ref, sems = refs[-5:]
    few, more = edge_ref.shape[0] // 2, node_ref.shape[0] // 2
    for k in range(2):
        row = k * (few + more)
        edge_ref[k * few : (k + 1) * few, :] = part_ref[row : row + few, :].astype(F32)
        node_ref[k * more : (k + 1) * more, :] = part_ref[row + few : row + few + more, :].astype(F32)
    side = bit_of(CORE) if own else 1 - bit_of(CORE)
    puts = []
    for k, (ref, hbm) in enumerate(((edge_ref, edge_hbm), (node_ref, node_hbm))):
        size = ref.shape[0]
        to = hbm.at[pl.ds(pl.multiple_of(side * size, 8), size), :]
        puts.append(pltpu.make_async_copy(ref, to, sems.at[k]))
        puts[k].start()
    for put in puts:
        put.wait()


def finished(own, part, grads, width):
    outs = [shape(width, width, dtype=F32), shape(2 * width, width, dtype=F32)]
    return pl.pallas_call(
        functools.partial(finish_body, own),
        out_shape=outs,
        in_specs=[VMEM] + [ANY] * len(grads),
        out_specs=[ANY, ANY],
        scratch_shapes=[
            pltpu.VMEM((width // 2, width), F32),
            pltpu.VMEM((width, width), F32),
            pltpu.SemaphoreType.DMA((2,)),
        ],
        input_output_aliases={1: 0, 2: 1} if grads else {},
        cost_estimate=pl.CostEstimate(flops=0, bytes_accessed=3 * width * width * 4, transcendentals=0),
        compiler_params=pltpu.CompilerParams(vmem_limit_bytes=24 * MIB),
    )(part, *grads)


def swapped_both(x, mask):
    peers = lax.axis_size("dom")
    total = 2 * peers
    return lax.ppermute(x, ("dp", "dom"), [(i, (i + peers) % total ^ mask) for i in range(total)])


def cut_grads(edge_part, node_part):
    half = node_part[0].shape[1]
    size = node_part[0].shape[0] + 2 * edge_part.shape[0]

    def cut(body, mask, args, size):
        return call(
            functools.partial(body, mask),
            [shape(size // 2, half, dtype=F32), shape(size // 2, half)],
            args,
            scratch=[pltpu.VMEM((size, half), F32)],
        )

    keep, send = cut(first_cut_body, CORE, (edge_part, *node_part), size)
    return cut(next_cut_body, ALONG_Y, (keep, swapped(send, "dom", CORE)), size // 2)


def joined(keep, send, back, send_order, width):
    out = [shape(*send.shape)]
    (mine,) = call(sum_body, out, (keep, swapped(send, "dom", ALONG_Y)))
    for mask in (ALONG_Z, 2 * ALONG_Z):
        (mine,) = call(sum_body, out, (mine, swapped(mine, "dom", mask)))
    others = swapped(mine, "dp", 1), swapped(mine, "dom", ALONG_Y), swapped_both(mine, ALONG_Y)
    grad_brick = placed(send_order, back)
    mine, grad_brick = lax.optimization_barrier((mine, grad_brick))
    (mine,) = call(functools.partial(join_body, ALONG_Y), [shape(6 * (width // 4), width)], (mine, *others))
    grads = finished(True, mine, (), width)
    return *finished(False, swapped(mine, "dom", CORE), grads, width), grad_brick


def placed(send_order, back):
    rows, width = back.shape
    return call(
        place_body,
        [shape(rows, width)],
        (send_order, back),
        flops=2 * rows * rows * width,
        nbytes=4 * rows * width,
    )[0]


def place_body(order_ref, back_ref, out_ref):
    rows = back_ref.shape[0]
    back = back_ref[...]
    order = order_ref[...]
    high = jnp.broadcast_to((order // ROWS).astype(F32), (ROWS, rows)).astype(BF16)
    row = lax.broadcasted_iota(jnp.int32, (ROWS, rows), 0)
    low = jnp.where(jnp.broadcast_to(order % ROWS, (ROWS, rows)) == row, 1.0, 0.0).astype(BF16)
    zero = jnp.zeros((ROWS, rows), BF16)
    for k in range(rows // ROWS):
        mine = slice(k * ROWS, (k + 1) * ROWS)
        hot = jnp.where(high == k, low, zero)
        out_ref[mine, :] = dot(hot, back).astype(BF16)


def shards(features, send_order, adj_count, adj_target, adj_vals, w_edge, w_node, cotangent):
    ndp = lax.axis_size("dp")
    ndom = lax.axis_size("dom")
    rows, width = features.shape[1:]
    per_peer = rows // ndom
    blocks, slots = adj_vals.shape[:2]
    rim = RIM * ROWS
    scale = 1.0 / math.sqrt(float(ndp * rows * ndom))
    tall = shape(rows, width)
    tall_f = shape(rows, width, dtype=F32)
    edge = shape(rim, width)
    rims = shape(2 * rim, width)
    mid = shape(rows - 2 * rim, width)
    unit = rows * width * 2
    square = 2 * rows * width * width

    (picked,) = call(
        pick_body,
        [tall],
        (send_order, features[0]),
        [ANY, ANY],
        [
            pltpu.VMEM((1, rows), jnp.int32),
            pltpu.VMEM((rows, width), BF16),
            pltpu.VMEM((2 * ROWS, rows), BF16),
            pltpu.VMEM((rows, width), BF16),
            pltpu.SemaphoreType.DMA,
            pltpu.SemaphoreType.DMA,
            pltpu.SemaphoreType.DMA((blocks,)),
        ],
        flops=2 * rows * rows * width,
        nbytes=2 * unit,
        out_specs=[ANY],
        limit=56 * MIB,
    )
    nodes = lax.all_to_all(
        picked.reshape(ndom, per_peer, width), "dom", split_axis=0, concat_axis=0, tiled=True
    ).reshape(rows, width)
    spots = blocks + 2 * RIM + 1
    adj, adj_rim, adj_t = call(
        build_body,
        [shape(blocks, ROWS, rows), shape(2 * RIM, ROWS, rows), shape(rows, spots * ROWS)],
        (adj_count, adj_target, adj_vals),
        [SMEM, SMEM, VMEM],
        [pltpu.VMEM((spots, ROWS, rows), BF16)],
        nbytes=16 * unit,
    )
    near, far, msg = call(
        message_body,
        [edge, edge, tall],
        (nodes, adj_rim, w_edge),
        flops=square + 4 * rim * rows * width,
        nbytes=4 * unit,
    )
    far = swapped_across(far, "dom")
    near = swapped(near, "dom", 1)
    cot = cotangent[0]
    own, out_mid, agg_mid, d_node_mid, d_nodes1_mid, d_agg_mid = call(
        own_body,
        [rims, mid, mid, mid, shape(*mid.shape, dtype=F32), mid],
        (nodes, msg, adj, cot, w_node),
        [VMEM, VMEM, ANY, VMEM, VMEM],
        [pltpu.VMEM((blocks, ROWS, rows), BF16), pltpu.SemaphoreType.DMA((rows // rim,))],
        flops=2 * rows * rows * width + 2 * square,
        nbytes=8 * unit,
    )
    near, far, out_rim, agg_rim, d_node_rim, d_nodes1_rim, d_agg_rim = call(
        rim_body,
        [edge, edge, rims, rims, rims, shape(*rims.shape, dtype=F32), rims],
        (nodes, own, near, far, cot, w_node),
        flops=2 * square,
        nbytes=4 * unit,
    )
    far = swapped_across(far, "dom")
    near = swapped(near, "dom", 1)
    tiled = ndp == 2 and ndom == 16

    node_part = call(
        functools.partial(grad_node_body, scale),
        [shape(2 * width, width // 2, dtype=F32), shape(2 * width, width // 2)]
        if tiled
        else [shape(2 * width, width, dtype=F32)],
        (nodes, agg_mid, agg_rim, d_node_mid, d_node_rim),
        flops=2 * square,
        nbytes=3 * unit,
    )
    if tiled:
        node_part = (node_part[0], swapped(node_part[1], "dp", 1))
    node_out, d_msg, slope = call(
        behind_body,
        [tall, tall_f, tall_f],
        (nodes, adj_t, w_edge, out_mid, out_rim, d_agg_mid, d_agg_rim),
        flops=2 * rows * rows * width + square,
        nbytes=8 * unit,
    )
    back, edge_part = call(
        functools.partial(edge_body, scale),
        [tall, shape(width, width, dtype=F32)],
        (nodes, adj_t, near, far, d_msg, slope, d_nodes1_mid, d_nodes1_rim, w_edge),
        scratch=[
            pltpu.VMEM((rows, width), BF16),
            pltpu.VMEM((rows, width), BF16),
            pltpu.SemaphoreType.DMA((rows // rim,)),
        ],
        out_specs=[ANY, VMEM],
        flops=2 * square + 4 * rim * rows * width,
        nbytes=8 * unit,
    )
    if tiled:
        back, node_in = lax.optimization_barrier((back, node_part[1]))
        keep, send = cut_grads(edge_part, (node_part[0], node_in))
    back = lax.all_to_all(
        back.reshape(ndom, per_peer, width), "dom", split_axis=0, concat_axis=0, tiled=True
    ).reshape(rows, width)
    if tiled:
        grad_edge, grad_node, grad_brick = joined(keep, send, back, send_order, width)
    else:
        grad_edge, grad_node = (lax.psum(part, ("dp", "dom")) for part in (edge_part, node_part[0]))
        grad_brick = placed(send_order, back)
    return (node_out[None], grad_brick[None], grad_edge, grad_node)


def solution(mesh):
    in_specs = (
        P("dp", "dom", None),
        P("dom", None),
        P("dom"),
        P("dom", None),
        P("dom", None, None, None),
        P(),
        P(),
        P("dp", "dom", None),
    )
    out_specs = (P("dp", "dom", None), P("dp", "dom", None), P(), P())
    return jax.shard_map(shards, mesh=mesh, in_specs=in_specs, out_specs=out_specs, check_vma=False)
```

```python
import functools
import math

import jax
import jax.numpy as jnp
from jax import lax
from jax.experimental import pallas as pl
from jax.experimental.pallas import tpu as pltpu
from jax.sharding import PartitionSpec as P

ROWS = 128
RIM = 2
TALL = 4
ANY = pl.BlockSpec(memory_space=pl.ANY)
VMEM = pl.BlockSpec(memory_space=pltpu.VMEM)
SMEM = pl.BlockSpec(memory_space=pltpu.SMEM)
BF16 = jnp.bfloat16
F32 = jnp.float32
MIB = 1024 * 1024
CORE, ALONG_Y, ALONG_Z = 1, 2, 4


def swapped(x, axis, mask):
    peers = lax.axis_size(axis)
    return lax.ppermute(x, axis, [(i, i ^ mask) for i in range(peers)])


def swapped_across(x, axis):
    peers = lax.axis_size(axis)
    return lax.ppermute(x, axis, [(i, (i + 1 if i % 2 else i - 1) % peers) for i in range(peers)])


def dot(a, b, contract=((1,), (0,))):
    return lax.dot_general(a, b, (contract, ((), ())), preferred_element_type=F32)


def shape(*dims, dtype=BF16):
    return jax.ShapeDtypeStruct(dims, dtype)


def call(body, outs, args, specs=None, scratch=(), flops=0, nbytes=0, limit=24 * MIB, out_specs=None):
    return pl.pallas_call(
        body,
        out_shape=outs,
        in_specs=specs or [VMEM] * len(args),
        out_specs=out_specs or [VMEM] * len(outs),
        scratch_shapes=list(scratch),
        cost_estimate=pl.CostEstimate(flops=flops, bytes_accessed=nbytes, transcendentals=0),
        compiler_params=pltpu.CompilerParams(vmem_limit_bytes=limit),
    )(*args)


def pick_body(order_hbm, feat_hbm, out_hbm, order_ref, feat_ref, hot_ref, out_ref, order_sem, feat_sem, out_sems):
    rows = feat_ref.shape[0]
    load_order = pltpu.make_async_copy(order_hbm, order_ref, order_sem)
    load_feat = pltpu.make_async_copy(feat_hbm, feat_ref, feat_sem)
    load_order.start()
    load_feat.start()
    lane = lax.broadcasted_iota(jnp.int32, (ROWS, ROWS), 1).astype(F32)
    zero = jnp.zeros((ROWS, ROWS), BF16)
    load_order.wait()

    def column(row):
        return jnp.transpose(jnp.broadcast_to(row.astype(F32), (ROWS, ROWS)))

    def hot_rows(k):
        row = order_ref[:, k * ROWS : (k + 1) * ROWS]
        high = column(row // ROWS).astype(BF16)
        low = jnp.where(column(row % ROWS) == lane, 1.0, 0.0).astype(BF16)
        return jnp.concatenate([jnp.where(high == b, low, zero) for b in range(rows // ROWS)], axis=1)

    def build(k):
        for b in range(k * TALL, (k + 1) * TALL):
            hot_ref[b * ROWS : (b + 1) * ROWS, :] = hot_rows(b)

    size = TALL * ROWS
    build(0)
    load_feat.wait()
    feat = feat_ref[...]
    puts = []
    for k in range(rows // size):
        if k > 0:
            build(k)
        mine = slice(k * size, (k + 1) * size)
        out_ref[mine, :] = dot(hot_ref[mine, :], feat).astype(BF16)
        part = pl.ds(k * size, size)
        puts.append(pltpu.make_async_copy(out_ref.at[part], out_hbm.at[part], out_sems.at[k]))
        puts[k].start()
    for put in puts:
        put.wait()


def build_body(cnt_ref, tgt_ref, vals_ref, rim_ref, both_ref, a_ref):
    blocks, slots = vals_ref.shape[:2]
    spare = blocks + 2 * RIM
    a_ref[...] = jnp.zeros_like(a_ref)
    both_ref[...] = jnp.zeros_like(both_ref)
    for c in range(blocks):
        mine = slice(c * ROWS, (c + 1) * ROWS)
        for s in range(slots):
            w = tgt_ref[c, s]
            at = jnp.where(w < blocks, w + RIM, jnp.where(w < 2 * blocks, w - blocks, w - blocks + RIM))
            at = jnp.where(s < cnt_ref[c], at, spare)
            value = vals_ref[c, s].astype(F32)
            a_ref[at, :, mine] = (a_ref[at, :, mine].astype(F32) + value).astype(BF16)
            lanes = pl.ds(pl.multiple_of(at * ROWS, ROWS), ROWS)
            both_ref[mine, lanes] = (both_ref[mine, lanes].astype(F32) + jnp.transpose(value)).astype(BF16)
    rim_ref[...] = a_ref[blocks:spare]
    both_ref[:, (spare + 1) * ROWS :] = a_ref[:blocks].reshape(blocks * ROWS, blocks * ROWS)


def chosen(first, second):
    odd = lax.rem(lax.axis_index("dom"), 2) == 1
    return jnp.where(odd, first, second), jnp.where(odd, second, first)


def message_body(nodes_ref, a_ref, w_edge_ref, near_ref, far_ref, msg_ref):
    rows = nodes_ref.shape[0]
    rim = RIM * ROWS
    pre = dot(nodes_ref[...], w_edge_ref[...])
    msg_ref[...] = (pre * jax.nn.sigmoid(pre)).astype(BF16)
    sums = dot(a_ref[...].reshape(2 * rim, rows), msg_ref[...])
    near, far = chosen(sums[:rim], sums[rim:])
    near_ref[...] = near.astype(BF16)
    far_ref[...] = far.astype(BF16)


def node_step(nodes, agg, gout, w_node):
    width = nodes.shape[1]
    pre = dot(nodes, w_node[:width]) + dot(agg, w_node[width:])
    sig = jax.nn.sigmoid(pre)
    out = (nodes.astype(F32) + pre * sig).astype(BF16)
    gout = gout.astype(F32)
    d_node = (gout * (sig * (1.0 + pre * (1.0 - sig)))).astype(BF16)
    back = dot(d_node, w_node, ((1,), (1,)))
    return out, d_node, gout + back[:, :width], back[:, width:].astype(BF16)


def own_body(
    nodes_ref, msg_ref, adj_ref, cot_ref, w_node_ref,
    own_ref, out_ref, agg_ref, d_node_ref, d_nodes1_ref, d_agg_ref,
):
    rows, width = nodes_ref.shape
    rim = RIM * ROWS
    msg = msg_ref[...]
    first = adj_ref.shape[1] - rows
    for k in range(rows // rim):
        mine = slice(k * rim, (k + 1) * rim)
        window = dot(adj_ref[mine, first:], msg).astype(BF16)
        if k == 0:
            own_ref[:rim, :] = window
        elif k == rows // rim - 1:
            own_ref[rim:, :] = window
        else:
            here = slice((k - 1) * rim, k * rim)
            agg_ref[here, :] = window
            out, d_node, d_nodes1, d_agg = node_step(nodes_ref[mine, :], window, cot_ref[mine, :], w_node_ref[...])
            out_ref[here, :] = out
            d_node_ref[here, :] = d_node
            d_nodes1_ref[here, :] = d_nodes1
            d_agg_ref[here, :] = d_agg


def rim_body(
    nodes_ref, own_ref, near_in_ref, far_in_ref, cot_ref, w_node_ref,
    near_ref, far_ref, out_ref, agg_ref, d_node_ref, d_nodes1_ref, d_agg_ref,
):
    rows = nodes_ref.shape[0]
    rim = RIM * ROWS
    arrived = jnp.concatenate(chosen(near_in_ref[...].astype(F32), far_in_ref[...].astype(F32)), axis=0)

    def ends(ref):
        return jnp.concatenate([ref[:rim, :], ref[rows - rim :, :]], axis=0)

    agg = (own_ref[...].astype(F32) + arrived).astype(BF16)
    agg_ref[...] = agg
    out, d_node, d_nodes1, d_agg = node_step(ends(nodes_ref), agg, ends(cot_ref), w_node_ref[...])
    out_ref[...] = out
    d_node_ref[...] = d_node
    d_nodes1_ref[...] = d_nodes1
    d_agg_ref[...] = d_agg
    near_ref[...], far_ref[...] = chosen(d_agg[:rim], d_agg[rim:])


def in_order(mid_ref, rim_ref):
    rim = RIM * ROWS
    return jnp.concatenate([rim_ref[:rim, :], mid_ref[...], rim_ref[rim:, :]], axis=0)


def grad_node_body(scale, nodes_ref, agg_mid_ref, agg_rim_ref, d_node_mid_ref, d_node_rim_ref, *out_refs):
    width = nodes_ref.shape[1]
    d_node = in_order(d_node_mid_ref, d_node_rim_ref)
    agg = in_order(agg_mid_ref, agg_rim_ref)
    first = lax.axis_index("dp") == 0
    for k, left in enumerate((nodes_ref[...], agg)):
        mine = slice(k * width, (k + 1) * width)
        grad = dot(left, d_node, ((0,), (0,))) * scale
        if len(out_refs) == 1:
            out_refs[0][mine, :] = grad
            continue
        half = width // 2
        out_refs[0][mine, :] = jnp.where(first, grad[:, :half], grad[:, half:])
        out_refs[1][mine, :] = jnp.where(first, grad[:, half:], grad[:, :half]).astype(BF16)


def behind_body(
    nodes_ref, at_ref, w_edge_ref, out_mid_ref, out_rim_ref, d_agg_mid_ref, d_agg_rim_ref,
    out_ref, d_msg_ref, slope_ref,
):
    rows = nodes_ref.shape[0]
    rim = RIM * ROWS
    out_ref[...] = in_order(out_mid_ref, out_rim_ref)
    d_agg = in_order(d_agg_mid_ref, d_agg_rim_ref)
    for k in range(rows // rim):
        mine = slice(k * rim, (k + 1) * rim)
        d_msg_ref[mine, :] = dot(at_ref[mine, :rows], d_agg)
        pre = dot(nodes_ref[mine, :], w_edge_ref[...])
        sig = jax.nn.sigmoid(pre)
        slope_ref[mine, :] = sig * (1.0 + pre * (1.0 - sig))


def edge_body(
    scale, nodes_ref, at_ref, near_ref, far_ref, d_msg_ref, slope_ref, mid_ref, rim_ref, w_edge_ref,
    back_hbm, g_edge_ref, d_edge_ref, back_ref, sem,
):
    rows, width = nodes_ref.shape
    rim = RIM * ROWS
    prev, after = chosen(near_ref[...], far_ref[...])
    rims = jnp.concatenate([prev, after], axis=0)
    w_edge = w_edge_ref[...]
    d_msg = d_msg_ref[...] + dot(at_ref[:, rows : rows + 2 * rim], rims)
    d_edge = (d_msg.astype(BF16).astype(F32) * slope_ref[...]).astype(BF16)
    d_edge_ref[...] = d_edge
    d_nodes = in_order(mid_ref, rim_ref) + dot(d_edge, w_edge, ((1,), (1,)))
    back_ref[...] = d_nodes.astype(BF16)
    put = pltpu.make_async_copy(back_ref, back_hbm, sem)
    put.start()
    g_edge_ref[...] = dot(nodes_ref[...], d_edge_ref[...], ((0,), (0,))) * scale
    put.wait()


def bit_of(mask):
    return lax.rem(lax.div(lax.axis_index("dom"), mask), 2)


def cut_rows(total_ref, mask, keep_ref, send_ref):
    size = keep_ref.shape[0]
    bit = bit_of(mask)
    keep_ref[...] = total_ref[pl.ds(pl.multiple_of(bit * size, 16), size), :]
    send_ref[...] = total_ref[pl.ds(pl.multiple_of((1 - bit) * size, 16), size), :].astype(BF16)


def first_cut_body(mask, edge_ref, node_ref, node_in_ref, keep_ref, send_ref, total_ref):
    half = node_ref.shape[1]
    few, more = edge_ref.shape[0] // 4, node_ref.shape[0] // 4
    for q in range(4):
        row = q * (2 * few + more)
        mine = slice(q * more, (q + 1) * more)
        total_ref[row : row + more, :] = node_ref[mine, :] + node_in_ref[mine, :].astype(F32)
        row += more
        mine = slice(q * few, (q + 1) * few)
        total_ref[row : row + few, :] = edge_ref[mine, :half]
        total_ref[row + few : row + 2 * few, :] = edge_ref[mine, half:]
    cut_rows(total_ref, mask, keep_ref, send_ref)


def next_cut_body(mask, mine_ref, in_ref, keep_ref, send_ref, total_ref):
    total_ref[...] = mine_ref[...] + in_ref[...].astype(F32)
    cut_rows(total_ref, mask, keep_ref, send_ref)


def sum_body(mine_ref, in_ref, out_ref):
    out_ref[...] = (mine_ref[...].astype(F32) + in_ref[...].astype(F32)).astype(BF16)


def join_body(mask, mine_ref, dp_ref, y_ref, both_ref, out_ref):
    size, half = mine_ref.shape
    more = size // 2
    few = more // 2
    first = lax.axis_index("dp") == 0
    low = bit_of(mask) == 0
    mine = [ref[...] for ref in (mine_ref, dp_ref)]
    other = [ref[...] for ref in (y_ref, both_ref)]
    for side in range(2):
        a, b = (jnp.where(low, x, y) if side == 0 else jnp.where(low, y, x) for x, y in zip(mine, other))
        row = side * (few + more)
        total = (a[more:].astype(F32) + b[more:].astype(F32)).astype(BF16)
        out_ref[row : row + few, :half] = total[:few]
        out_ref[row : row + few, half:] = total[few:]
        row += few
        out_ref[row : row + more, :half] = jnp.where(first, a[:more], b[:more])
        out_ref[row : row + more, half:] = jnp.where(first, b[:more], a[:more])


def finish_body(own, *refs):
    part_ref = refs[0]
    edge_hbm, node_hbm, edge_ref, node_ref, sems = refs[-5:]
    few, more = edge_ref.shape[0] // 2, node_ref.shape[0] // 2
    for k in range(2):
        row = k * (few + more)
        edge_ref[k * few : (k + 1) * few, :] = part_ref[row : row + few, :].astype(F32)
        node_ref[k * more : (k + 1) * more, :] = part_ref[row + few : row + few + more, :].astype(F32)
    side = bit_of(CORE) if own else 1 - bit_of(CORE)
    puts = []
    for k, (ref, hbm) in enumerate(((edge_ref, edge_hbm), (node_ref, node_hbm))):
        size = ref.shape[0]
        to = hbm.at[pl.ds(pl.multiple_of(side * size, 8), size), :]
        puts.append(pltpu.make_async_copy(ref, to, sems.at[k]))
        puts[k].start()
    for put in puts:
        put.wait()


def finished(own, part, grads, width):
    outs = [shape(width, width, dtype=F32), shape(2 * width, width, dtype=F32)]
    return pl.pallas_call(
        functools.partial(finish_body, own),
        out_shape=outs,
        in_specs=[VMEM] + [ANY] * len(grads),
        out_specs=[ANY, ANY],
        scratch_shapes=[
            pltpu.VMEM((width // 2, width), F32),
            pltpu.VMEM((width, width), F32),
            pltpu.SemaphoreType.DMA((2,)),
        ],
        input_output_aliases={1: 0, 2: 1} if grads else {},
        cost_estimate=pl.CostEstimate(flops=0, bytes_accessed=3 * width * width * 4, transcendentals=0),
        compiler_params=pltpu.CompilerParams(vmem_limit_bytes=24 * MIB),
    )(part, *grads)


def swapped_both(x, mask):
    peers = lax.axis_size("dom")
    total = 2 * peers
    return lax.ppermute(x, ("dp", "dom"), [(i, (i + peers) % total ^ mask) for i in range(total)])


def cut_grads(edge_part, node_part):
    half = node_part[0].shape[1]
    size = node_part[0].shape[0] + 2 * edge_part.shape[0]

    def cut(body, mask, args, size):
        return call(
            functools.partial(body, mask),
            [shape(size // 2, half, dtype=F32), shape(size // 2, half)],
            args,
            scratch=[pltpu.VMEM((size, half), F32)],
        )

    keep, send = cut(first_cut_body, CORE, (edge_part, *node_part), size)
    return cut(next_cut_body, ALONG_Y, (keep, swapped(send, "dom", CORE)), size // 2)


def joined(keep, send, back, send_order, width):
    out = [shape(*send.shape)]
    (mine,) = call(sum_body, out, (keep, swapped(send, "dom", ALONG_Y)))
    for mask in (ALONG_Z, 2 * ALONG_Z):
        (mine,) = call(sum_body, out, (mine, swapped(mine, "dom", mask)))
    others = swapped(mine, "dp", 1), swapped(mine, "dom", ALONG_Y), swapped_both(mine, ALONG_Y)
    grad_brick = placed(send_order, back)
    mine, grad_brick = lax.optimization_barrier((mine, grad_brick))
    (mine,) = call(functools.partial(join_body, ALONG_Y), [shape(6 * (width // 4), width)], (mine, *others))
    grads = finished(True, mine, (), width)
    return *finished(False, swapped(mine, "dom", CORE), grads, width), grad_brick


def placed(send_order, back):
    rows, width = back.shape
    return call(
        place_body,
        [shape(rows, width)],
        (send_order, back),
        flops=2 * rows * rows * width,
        nbytes=4 * rows * width,
    )[0]


def place_body(order_ref, back_ref, out_ref):
    rows = back_ref.shape[0]
    back = back_ref[...]
    order = order_ref[...]
    high = jnp.broadcast_to((order // ROWS).astype(F32), (ROWS, rows)).astype(BF16)
    row = lax.broadcasted_iota(jnp.int32, (ROWS, rows), 0)
    low = jnp.where(jnp.broadcast_to(order % ROWS, (ROWS, rows)) == row, 1.0, 0.0).astype(BF16)
    zero = jnp.zeros((ROWS, rows), BF16)
    size = TALL * ROWS
    for k in range(rows // size):
        mine = slice(k * size, (k + 1) * size)
        hot = [jnp.where(high == b, low, zero) for b in range(k * TALL, (k + 1) * TALL)]
        out_ref[mine, :] = dot(jnp.concatenate(hot, axis=0), back).astype(BF16)


def shards(features, send_order, adj_count, adjarget, adj_vals, w_edge, w_node, cotangent):
    ndp = lax.axis_size("dp")
    ndom = lax.axis_size("dom")
    rows, width = features.shape[1:]
    per_peer = rows // ndom
    blocks, slots = adj_vals.shape[:2]
    rim = RIM * ROWS
    scale = 1.0 / math.sqrt(float(ndp * rows * ndom))
    tall = shape(rows, width)
    tall_f = shape(rows, width, dtype=F32)
    edge = shape(rim, width)
    rims = shape(2 * rim, width)
    mid = shape(rows - 2 * rim, width)
    unit = rows * width * 2
    square = 2 * rows * width * width

    (picked,) = call(
        pick_body,
        [tall],
        (send_order, features[0]),
        [ANY, ANY],
        [
            pltpu.VMEM((1, rows), jnp.int32),
            pltpu.VMEM((rows, width), BF16),
            pltpu.VMEM((rows, rows), BF16),
            pltpu.VMEM((rows, width), BF16),
            pltpu.SemaphoreType.DMA,
            pltpu.SemaphoreType.DMA,
            pltpu.SemaphoreType.DMA((blocks // TALL,)),
        ],
        flops=2 * rows * rows * width,
        nbytes=2 * unit,
        out_specs=[ANY],
        limit=56 * MIB,
    )
    nodes = lax.all_to_all(
        picked.reshape(ndom, per_peer, width), "dom", split_axis=0, concat_axis=0, tiled=True
    ).reshape(rows, width)
    spots = blocks + 2 * RIM + 1
    adj_rim, adj = call(
        build_body,
        [shape(2 * RIM, ROWS, rows), shape(rows, spots * ROWS + rows)],
        (adj_count, adjarget, adj_vals),
        [SMEM, SMEM, VMEM],
        [pltpu.VMEM((spots, ROWS, rows), BF16)],
        nbytes=16 * unit,
    )
    near, far, msg = call(
        message_body,
        [edge, edge, tall],
        (nodes, adj_rim, w_edge),
        flops=square + 4 * rim * rows * width,
        nbytes=4 * unit,
    )
    far = swapped_across(far, "dom")
    near = swapped(near, "dom", 1)
    cot = cotangent[0]
    own, out_mid, agg_mid, d_node_mid, d_nodes1_mid, d_agg_mid = call(
        own_body,
        [rims, mid, mid, mid, shape(*mid.shape, dtype=F32), mid],
        (nodes, msg, adj, cot, w_node),
        flops=2 * rows * rows * width + 2 * square,
        nbytes=8 * unit,
    )
    near, far, out_rim, agg_rim, d_node_rim, d_nodes1_rim, d_agg_rim = call(
        rim_body,
        [edge, edge, rims, rims, rims, shape(*rims.shape, dtype=F32), rims],
        (nodes, own, near, far, cot, w_node),
        flops=2 * square,
        nbytes=4 * unit,
    )
    far = swapped_across(far, "dom")
    near = swapped(near, "dom", 1)
    tiled = ndp == 2 and ndom == 16

    node_part = call(
        functools.partial(grad_node_body, scale),
        [shape(2 * width, width // 2, dtype=F32), shape(2 * width, width // 2)]
        if tiled
        else [shape(2 * width, width, dtype=F32)],
        (nodes, agg_mid, agg_rim, d_node_mid, d_node_rim),
        flops=2 * square,
        nbytes=3 * unit,
    )
    if tiled:
        node_part = (node_part[0], swapped(node_part[1], "dp", 1))
    node_out, d_msg, slope = call(
        behind_body,
        [tall, tall_f, tall_f],
        (nodes, adj, w_edge, out_mid, out_rim, d_agg_mid, d_agg_rim),
        flops=2 * rows * rows * width + square,
        nbytes=8 * unit,
    )
    back, edge_part = call(
        functools.partial(edge_body, scale),
        [tall, shape(width, width, dtype=F32)],
        (nodes, adj, near, far, d_msg, slope, d_nodes1_mid, d_nodes1_rim, w_edge),
        scratch=[
            pltpu.VMEM((rows, width), BF16),
            pltpu.VMEM((rows, width), BF16),
            pltpu.SemaphoreType.DMA,
        ],
        out_specs=[ANY, VMEM],
        flops=2 * square + 4 * rim * rows * width,
        nbytes=8 * unit,
    )
    if tiled:
        back, node_in = lax.optimization_barrier((back, node_part[1]))
        keep, send = cut_grads(edge_part, (node_part[0], node_in))
    back = lax.all_to_all(
        back.reshape(ndom, per_peer, width), "dom", split_axis=0, concat_axis=0, tiled=True
    ).reshape(rows, width)
    if tiled:
        grad_edge, grad_node, grad_brick = joined(keep, send, back, send_order, width)
    else:
        grad_edge, grad_node = (lax.psum(part, ("dp", "dom")) for part in (edge_part, node_part[0]))
        grad_brick = placed(send_order, back)
    return (node_out[None], grad_brick[None], grad_edge, grad_node)


def solution(mesh):
    in_specs = (
        P("dp", "dom", None),
        P("dom", None),
        P("dom"),
        P("dom", None),
        P("dom", None, None, None),
        P(),
        P(),
        P("dp", "dom", None),
    )
    out_specs = (P("dp", "dom", None), P("dp", "dom", None), P(), P())
    return jax.shard_map(shards, mesh=mesh, in_specs=in_specs, out_specs=out_specs, check_vma=False)
```

```python
import functools
import math

import jax
import jax.numpy as jnp
from jax import lax
from jax.experimental import pallas as pl
from jax.experimental.pallas import tpu as pltpu
from jax.sharding import PartitionSpec as P

ROWS = 128
RIM = 2
ANY = pl.BlockSpec(memory_space=pl.ANY)
VMEM = pl.BlockSpec(memory_space=pltpu.VMEM)
SMEM = pl.BlockSpec(memory_space=pltpu.SMEM)
BF16 = jnp.bfloat16
F32 = jnp.float32
MIB = 1024 * 1024
CORE, ALONG_Y, ALONG_Z = 1, 2, 4


def swapped(x, axis, mask):
    peers = lax.axis_size(axis)
    return lax.ppermute(x, axis, [(i, i ^ mask) for i in range(peers)])


def swapped_across(x, axis):
    peers = lax.axis_size(axis)
    return lax.ppermute(x, axis, [(i, (i + 1 if i % 2 else i - 1) % peers) for i in range(peers)])


def dot(a, b, contract=((1,), (0,))):
    return lax.dot_general(a, b, (contract, ((), ())), preferred_element_type=F32)


def shape(*dims, dtype=BF16):
    return jax.ShapeDtypeStruct(dims, dtype)


def call(body, outs, args, specs=None, scratch=(), flops=0, nbytes=0, limit=24 * MIB, out_specs=None):
    return pl.pallas_call(
        body,
        out_shape=outs,
        in_specs=specs or [VMEM] * len(args),
        out_specs=out_specs or [VMEM] * len(outs),
        scratch_shapes=list(scratch),
        cost_estimate=pl.CostEstimate(flops=flops, bytes_accessed=nbytes, transcendentals=0),
        compiler_params=pltpu.CompilerParams(vmem_limit_bytes=limit),
    )(*args)


def pick_body(order_hbm, feat_hbm, out_hbm, order_ref, feat_ref, hot_ref, out_ref, order_sem, feat_sem, out_sems):
    rows = feat_ref.shape[0]
    early = hot_ref.shape[0] // ROWS
    load_order = pltpu.make_async_copy(order_hbm, order_ref, order_sem)
    load_feat = pltpu.make_async_copy(feat_hbm, feat_ref, feat_sem)
    load_order.start()
    load_feat.start()
    lane = lax.broadcasted_iota(jnp.int32, (ROWS, ROWS), 1).astype(F32)
    zero = jnp.zeros((ROWS, ROWS), BF16)
    load_order.wait()

    def column(row):
        return jnp.transpose(jnp.broadcast_to(row.astype(F32), (ROWS, ROWS)))

    def hot_rows(k):
        row = order_ref[:, k * ROWS : (k + 1) * ROWS]
        high = column(row // ROWS).astype(BF16)
        low = jnp.where(column(row % ROWS) == lane, 1.0, 0.0).astype(BF16)
        return jnp.concatenate([jnp.where(high == b, low, zero) for b in range(rows // ROWS)], axis=1)

    for k in range(early):
        hot_ref[k * ROWS : (k + 1) * ROWS, :] = hot_rows(k)
    load_feat.wait()
    feat = feat_ref[...]
    puts = []
    for k in range(rows // ROWS):
        mine = slice(k * ROWS, (k + 1) * ROWS)
        hot = hot_ref[mine, :] if k < early else hot_rows(k)
        out_ref[mine, :] = dot(hot, feat).astype(BF16)
        puts.append(pltpu.make_async_copy(out_ref.at[pl.ds(k * ROWS, ROWS)], out_hbm.at[pl.ds(k * ROWS, ROWS)], out_sems.at[k]))
        puts[k].start()
    for put in puts:
        put.wait()


def build_body(cnt_ref, tgt_ref, vals_ref, w_edge_ref, rim_ref, both_ref, a_ref):
    blocks, slots = vals_ref.shape[:2]
    spare = blocks + 2 * RIM
    a_ref[...] = jnp.zeros_like(a_ref)
    both_ref[...] = jnp.zeros_like(both_ref)
    for c in range(blocks):
        mine = slice(c * ROWS, (c + 1) * ROWS)
        for s in range(slots):
            w = tgt_ref[c, s]
            at = jnp.where(w < blocks, w + RIM, jnp.where(w < 2 * blocks, w - blocks, w - blocks + RIM))
            at = jnp.where(s < cnt_ref[c], at, spare)
            value = vals_ref[c, s].astype(F32)
            a_ref[at, :, mine] = (a_ref[at, :, mine].astype(F32) + value).astype(BF16)
            lanes = pl.ds(pl.multiple_of(at * ROWS, ROWS), ROWS)
            both_ref[mine, lanes] = (both_ref[mine, lanes].astype(F32) + jnp.transpose(value)).astype(BF16)
    width = w_edge_ref.shape[0]
    rim_ref[: 2 * RIM * ROWS, :] = a_ref[blocks:spare].reshape(2 * RIM * ROWS, blocks * ROWS)
    rim_ref[2 * RIM * ROWS :, :width] = w_edge_ref[...]
    both_ref[:, (spare + 1) * ROWS :] = a_ref[:blocks].reshape(blocks * ROWS, blocks * ROWS)


def chosen(first, second):
    odd = lax.rem(lax.axis_index("dom"), 2) == 1
    return jnp.where(odd, first, second), jnp.where(odd, second, first)


def message_body(nodes_ref, a_ref, near_ref, far_ref, msg_ref):
    rows, width = nodes_ref.shape
    rim = RIM * ROWS
    w_edge = a_ref[2 * rim :, :width]
    for k in range(rows // rim):
        mine = slice(k * rim, (k + 1) * rim)
        pre = dot(nodes_ref[mine, :], w_edge)
        msg_ref[mine, :] = (pre * jax.nn.sigmoid(pre)).astype(BF16)
    sums = dot(a_ref[: 2 * rim, :], msg_ref[...])
    near, far = chosen(sums[:rim], sums[rim:])
    near_ref[...] = near.astype(BF16)
    far_ref[...] = far.astype(BF16)


def node_step(nodes, agg, gout, w_node):
    width = nodes.shape[1]
    pre = dot(nodes, w_node[:width]) + dot(agg, w_node[width:])
    sig = jax.nn.sigmoid(pre)
    out = (nodes.astype(F32) + pre * sig).astype(BF16)
    gout = gout.astype(F32)
    d_node = (gout * (sig * (1.0 + pre * (1.0 - sig)))).astype(BF16)
    back = dot(d_node, w_node, ((1,), (1,)))
    return out, d_node, gout + back[:, :width], back[:, width:].astype(BF16)


def own_body(
    nodes_ref, msg_ref, adj_ref, cot_ref, w_node_ref,
    own_ref, out_ref, agg_ref, d_node_ref, d_nodes1_ref, d_agg_ref,
):
    rows, width = nodes_ref.shape
    rim = RIM * ROWS
    msg = msg_ref[...]
    first = adj_ref.shape[1] - rows
    for k in range(rows // rim):
        mine = slice(k * rim, (k + 1) * rim)
        window = dot(adj_ref[mine, first:], msg).astype(BF16)
        if k == 0:
            own_ref[:rim, :] = window
        elif k == rows // rim - 1:
            own_ref[rim:, :] = window
        else:
            here = slice((k - 1) * rim, k * rim)
            agg_ref[here, :] = window
            out, d_node, d_nodes1, d_agg = node_step(nodes_ref[mine, :], window, cot_ref[mine, :], w_node_ref[...])
            out_ref[here, :] = out
            d_node_ref[here, :] = d_node
            d_nodes1_ref[here, :] = d_nodes1
            d_agg_ref[here, :] = d_agg


def rim_body(
    nodes_ref, own_ref, near_in_ref, far_in_ref, cot_ref, w_node_ref,
    near_ref, far_ref, out_ref, agg_ref, d_node_ref, d_nodes1_ref, d_agg_ref,
):
    rows = nodes_ref.shape[0]
    rim = RIM * ROWS
    arrived = chosen(near_in_ref[...].astype(F32), far_in_ref[...].astype(F32))
    rims = []
    for k in range(2):
        mine = slice(k * (rows - rim), k * (rows - rim) + rim)
        here = slice(k * rim, (k + 1) * rim)
        agg = (own_ref[here, :].astype(F32) + arrived[k]).astype(BF16)
        agg_ref[here, :] = agg
        out, d_node, d_nodes1, d_agg = node_step(nodes_ref[mine, :], agg, cot_ref[mine, :], w_node_ref[...])
        out_ref[here, :] = out
        d_node_ref[here, :] = d_node
        d_nodes1_ref[here, :] = d_nodes1
        d_agg_ref[here, :] = d_agg
        rims.append(d_agg)
    near_ref[...], far_ref[...] = chosen(rims[0], rims[1])


def in_order(mid_ref, rim_ref):
    rim = RIM * ROWS
    return jnp.concatenate([rim_ref[:rim, :], mid_ref[...], rim_ref[rim:, :]], axis=0)


def grad_node_body(scale, nodes_ref, agg_mid_ref, agg_rim_ref, d_node_mid_ref, d_node_rim_ref, *out_refs):
    width = nodes_ref.shape[1]
    d_node = in_order(d_node_mid_ref, d_node_rim_ref)
    agg = in_order(agg_mid_ref, agg_rim_ref)
    first = lax.axis_index("dp") == 0
    for k, left in enumerate((nodes_ref[...], agg)):
        mine = slice(k * width, (k + 1) * width)
        grad = dot(left, d_node, ((0,), (0,))) * scale
        if len(out_refs) == 1:
            out_refs[0][mine, :] = grad
            continue
        half = width // 2
        out_refs[0][mine, :] = jnp.where(first, grad[:, :half], grad[:, half:])
        out_refs[1][mine, :] = jnp.where(first, grad[:, half:], grad[:, :half]).astype(BF16)


def behind_body(
    nodes_ref, at_ref, w_edge_ref, out_mid_ref, out_rim_ref, d_agg_mid_ref, d_agg_rim_ref,
    out_ref, d_msg_ref, slope_ref,
):
    rows = nodes_ref.shape[0]
    rim = RIM * ROWS
    out_ref[...] = in_order(out_mid_ref, out_rim_ref)
    d_agg = in_order(d_agg_mid_ref, d_agg_rim_ref)
    for k in range(rows // rim):
        mine = slice(k * rim, (k + 1) * rim)
        d_msg_ref[mine, :] = dot(at_ref[mine, :rows], d_agg)
        pre = dot(nodes_ref[mine, :], w_edge_ref[...])
        sig = jax.nn.sigmoid(pre)
        slope_ref[mine, :] = sig * (1.0 + pre * (1.0 - sig))


def edge_body(
    scale, nodes_ref, at_ref, near_ref, far_ref, d_msg_ref, slope_ref, mid_ref, rim_ref, w_edge_ref,
    back_hbm, g_edge_ref, d_edge_ref, back_ref, sems,
):
    rows, width = nodes_ref.shape
    rim = RIM * ROWS
    prev, after = chosen(near_ref[...], far_ref[...])
    rims = jnp.concatenate([prev, after], axis=0)
    w_edge = w_edge_ref[...]
    puts = []
    for k in range(rows // rim):
        mine = slice(k * rim, (k + 1) * rim)
        d_msg = d_msg_ref[mine, :] + dot(at_ref[mine, rows : rows + 2 * rim], rims)
        d_edge = (d_msg.astype(BF16).astype(F32) * slope_ref[mine, :]).astype(BF16)
        d_edge_ref[mine, :] = d_edge
        if k == 0:
            d_nodes1 = rim_ref[:rim, :]
        elif k == rows // rim - 1:
            d_nodes1 = rim_ref[rim:, :]
        else:
            d_nodes1 = mid_ref[(k - 1) * rim : k * rim, :]
        back_ref[mine, :] = (d_nodes1 + dot(d_edge, w_edge, ((1,), (1,)))).astype(BF16)
        part = pl.ds(k * rim, rim)
        puts.append(pltpu.make_async_copy(back_ref.at[part], back_hbm.at[part], sems.at[k]))
        puts[k].start()
    g_edge_ref[...] = dot(nodes_ref[...], d_edge_ref[...], ((0,), (0,))) * scale
    for put in puts:
        put.wait()


def bit_of(mask):
    return lax.rem(lax.div(lax.axis_index("dom"), mask), 2)


def cut_rows(total_ref, mask, keep_ref, send_ref):
    size = keep_ref.shape[0]
    bit = bit_of(mask)
    keep_ref[...] = total_ref[pl.ds(pl.multiple_of(bit * size, 16), size), :]
    send_ref[...] = total_ref[pl.ds(pl.multiple_of((1 - bit) * size, 16), size), :].astype(BF16)


def first_cut_body(mask, edge_ref, node_ref, node_in_ref, keep_ref, send_ref, total_ref):
    half = node_ref.shape[1]
    few, more = edge_ref.shape[0] // 4, node_ref.shape[0] // 4
    for q in range(4):
        row = q * (2 * few + more)
        mine = slice(q * more, (q + 1) * more)
        total_ref[row : row + more, :] = node_ref[mine, :] + node_in_ref[mine, :].astype(F32)
        row += more
        mine = slice(q * few, (q + 1) * few)
        total_ref[row : row + few, :] = edge_ref[mine, :half]
        total_ref[row + few : row + 2 * few, :] = edge_ref[mine, half:]
    cut_rows(total_ref, mask, keep_ref, send_ref)


def next_cut_body(mask, mine_ref, in_ref, keep_ref, send_ref, total_ref):
    total_ref[...] = mine_ref[...] + in_ref[...].astype(F32)
    cut_rows(total_ref, mask, keep_ref, send_ref)


def sum_body(mine_ref, in_ref, out_ref):
    out_ref[...] = (mine_ref[...].astype(F32) + in_ref[...].astype(F32)).astype(BF16)


def join_body(mask, mine_ref, dp_ref, y_ref, both_ref, out_ref):
    size, half = mine_ref.shape
    more = size // 2
    few = more // 2
    first = lax.axis_index("dp") == 0
    low = bit_of(mask) == 0
    mine = [ref[...] for ref in (mine_ref, dp_ref)]
    other = [ref[...] for ref in (y_ref, both_ref)]
    for side in range(2):
        a, b = (jnp.where(low, x, y) if side == 0 else jnp.where(low, y, x) for x, y in zip(mine, other))
        row = side * (few + more)
        total = (a[more:].astype(F32) + b[more:].astype(F32)).astype(BF16)
        out_ref[row : row + few, :half] = total[:few]
        out_ref[row : row + few, half:] = total[few:]
        row += few
        out_ref[row : row + more, :half] = jnp.where(first, a[:more], b[:more])
        out_ref[row : row + more, half:] = jnp.where(first, b[:more], a[:more])


def finish_body(own, *refs):
    part_ref = refs[0]
    edge_hbm, node_hbm, edge_ref, node_ref, sems = refs[-5:]
    few, more = edge_ref.shape[0] // 2, node_ref.shape[0] // 2
    for k in range(2):
        row = k * (few + more)
        edge_ref[k * few : (k + 1) * few, :] = part_ref[row : row + few, :].astype(F32)
        node_ref[k * more : (k + 1) * more, :] = part_ref[row + few : row + few + more, :].astype(F32)
    side = bit_of(CORE) if own else 1 - bit_of(CORE)
    puts = []
    for k, (ref, hbm) in enumerate(((edge_ref, edge_hbm), (node_ref, node_hbm))):
        size = ref.shape[0]
        to = hbm.at[pl.ds(pl.multiple_of(side * size, 8), size), :]
        puts.append(pltpu.make_async_copy(ref, to, sems.at[k]))
        puts[k].start()
    for put in puts:
        put.wait()


def finished(own, part, grads, width):
    outs = [shape(width, width, dtype=F32), shape(2 * width, width, dtype=F32)]
    return pl.pallas_call(
        functools.partial(finish_body, own),
        out_shape=outs,
        in_specs=[VMEM] + [ANY] * len(grads),
        out_specs=[ANY, ANY],
        scratch_shapes=[
            pltpu.VMEM((width // 2, width), F32),
            pltpu.VMEM((width, width), F32),
            pltpu.SemaphoreType.DMA((2,)),
        ],
        input_output_aliases={1: 0, 2: 1} if grads else {},
        cost_estimate=pl.CostEstimate(flops=0, bytes_accessed=3 * width * width * 4, transcendentals=0),
        compiler_params=pltpu.CompilerParams(vmem_limit_bytes=24 * MIB),
    )(part, *grads)


def swapped_both(x, mask):
    peers = lax.axis_size("dom")
    total = 2 * peers
    return lax.ppermute(x, ("dp", "dom"), [(i, (i + peers) % total ^ mask) for i in range(total)])


def cut_grads(edge_part, node_part):
    half = node_part[0].shape[1]
    size = node_part[0].shape[0] + 2 * edge_part.shape[0]

    def cut(body, mask, args, size):
        return call(
            functools.partial(body, mask),
            [shape(size // 2, half, dtype=F32), shape(size // 2, half)],
            args,
            scratch=[pltpu.VMEM((size, half), F32)],
        )

    keep, send = cut(first_cut_body, CORE, (edge_part, *node_part), size)
    return cut(next_cut_body, ALONG_Y, (keep, swapped(send, "dom", CORE)), size // 2)


def joined(keep, send, back, send_order, width):
    out = [shape(*send.shape)]
    (mine,) = call(sum_body, out, (keep, swapped(send, "dom", ALONG_Y)))
    for mask in (ALONG_Z, 2 * ALONG_Z):
        (mine,) = call(sum_body, out, (mine, swapped(mine, "dom", mask)))
    others = swapped(mine, "dp", 1), swapped(mine, "dom", ALONG_Y), swapped_both(mine, ALONG_Y)
    grad_brick = placed(send_order, back)
    mine, grad_brick = lax.optimization_barrier((mine, grad_brick))
    (mine,) = call(functools.partial(join_body, ALONG_Y), [shape(6 * (width // 4), width)], (mine, *others))
    grads = finished(True, mine, (), width)
    return *finished(False, swapped(mine, "dom", CORE), grads, width), grad_brick


def placed(send_order, back):
    rows, width = back.shape
    return call(
        place_body,
        [shape(rows, width)],
        (send_order, back),
        flops=2 * rows * rows * width,
        nbytes=4 * rows * width,
    )[0]


def place_body(order_ref, back_ref, out_ref):
    rows = back_ref.shape[0]
    back = back_ref[...]
    order = order_ref[...]
    high = jnp.broadcast_to((order // ROWS).astype(F32), (ROWS, rows)).astype(BF16)
    row = lax.broadcasted_iota(jnp.int32, (ROWS, rows), 0)
    low = jnp.where(jnp.broadcast_to(order % ROWS, (ROWS, rows)) == row, 1.0, 0.0).astype(BF16)
    zero = jnp.zeros((ROWS, rows), BF16)
    for k in range(rows // ROWS):
        mine = slice(k * ROWS, (k + 1) * ROWS)
        hot = jnp.where(high == k, low, zero)
        out_ref[mine, :] = dot(hot, back).astype(BF16)


def shards(features, send_order, adj_count, adj_target, adj_vals, w_edge, w_node, cotangent):
    ndp = lax.axis_size("dp")
    ndom = lax.axis_size("dom")
    rows, width = features.shape[1:]
    per_peer = rows // ndom
    blocks, slots = adj_vals.shape[:2]
    rim = RIM * ROWS
    scale = 1.0 / math.sqrt(float(ndp * rows * ndom))
    tall = shape(rows, width)
    tall_f = shape(rows, width, dtype=F32)
    edge = shape(rim, width)
    rims = shape(2 * rim, width)
    mid = shape(rows - 2 * rim, width)
    unit = rows * width * 2
    square = 2 * rows * width * width

    (picked,) = call(
        pick_body,
        [tall],
        (send_order, features[0]),
        [ANY, ANY],
        [
            pltpu.VMEM((1, rows), jnp.int32),
            pltpu.VMEM((rows, width), BF16),
            pltpu.VMEM((2 * ROWS, rows), BF16),
            pltpu.VMEM((rows, width), BF16),
            pltpu.SemaphoreType.DMA,
            pltpu.SemaphoreType.DMA,
            pltpu.SemaphoreType.DMA((blocks,)),
        ],
        flops=2 * rows * rows * width,
        nbytes=2 * unit,
        out_specs=[ANY],
        limit=56 * MIB,
    )
    nodes = lax.all_to_all(
        picked.reshape(ndom, per_peer, width), "dom", split_axis=0, concat_axis=0, tiled=True
    ).reshape(rows, width)
    spots = blocks + 2 * RIM + 1
    adj_rim, adj = call(
        build_body,
        [shape(2 * rim + width, rows), shape(rows, spots * ROWS + rows)],
        (adj_count, adj_target, adj_vals, w_edge),
        [SMEM, SMEM, VMEM, VMEM],
        [pltpu.VMEM((spots, ROWS, rows), BF16)],
        nbytes=16 * unit,
    )
    near, far, msg = call(
        message_body, [edge, edge, tall], (nodes, adj_rim), flops=square + 4 * rim * rows * width, nbytes=4 * unit
    )
    far = swapped_across(far, "dom")
    near = swapped(near, "dom", 1)
    cot = cotangent[0]
    own, out_mid, agg_mid, d_node_mid, d_nodes1_mid, d_agg_mid = call(
        own_body,
        [rims, mid, mid, mid, shape(*mid.shape, dtype=F32), mid],
        (nodes, msg, adj, cot, w_node),
        flops=2 * rows * rows * width + 2 * square,
        nbytes=8 * unit,
    )
    near, far, out_rim, agg_rim, d_node_rim, d_nodes1_rim, d_agg_rim = call(
        rim_body,
        [edge, edge, rims, rims, rims, shape(*rims.shape, dtype=F32), rims],
        (nodes, own, near, far, cot, w_node),
        flops=2 * square,
        nbytes=4 * unit,
    )
    far = swapped_across(far, "dom")
    near = swapped(near, "dom", 1)
    tiled = ndp == 2 and ndom == 16

    node_part = call(
        functools.partial(grad_node_body, scale),
        [shape(2 * width, width // 2, dtype=F32), shape(2 * width, width // 2)]
        if tiled
        else [shape(2 * width, width, dtype=F32)],
        (nodes, agg_mid, agg_rim, d_node_mid, d_node_rim),
        flops=2 * square,
        nbytes=3 * unit,
    )
    if tiled:
        node_part = (node_part[0], swapped(node_part[1], "dp", 1))
    node_out, d_msg, slope = call(
        behind_body,
        [tall, tall_f, tall_f],
        (nodes, adj, w_edge, out_mid, out_rim, d_agg_mid, d_agg_rim),
        flops=2 * rows * rows * width + square,
        nbytes=8 * unit,
    )
    back, edge_part = call(
        functools.partial(edge_body, scale),
        [tall, shape(width, width, dtype=F32)],
        (nodes, adj, near, far, d_msg, slope, d_nodes1_mid, d_nodes1_rim, w_edge),
        scratch=[
            pltpu.VMEM((rows, width), BF16),
            pltpu.VMEM((rows, width), BF16),
            pltpu.SemaphoreType.DMA((rows // rim,)),
        ],
        out_specs=[ANY, VMEM],
        flops=2 * square + 4 * rim * rows * width,
        nbytes=8 * unit,
    )
    if tiled:
        back, node_in = lax.optimization_barrier((back, node_part[1]))
        keep, send = cut_grads(edge_part, (node_part[0], node_in))
    back = lax.all_to_all(
        back.reshape(ndom, per_peer, width), "dom", split_axis=0, concat_axis=0, tiled=True
    ).reshape(rows, width)
    if tiled:
        grad_edge, grad_node, grad_brick = joined(keep, send, back, send_order, width)
    else:
        grad_edge, grad_node = (lax.psum(part, ("dp", "dom")) for part in (edge_part, node_part[0]))
        grad_brick = placed(send_order, back)
    return (node_out[None], grad_brick[None], grad_edge, grad_node)


def solution(mesh):
    in_specs = (
        P("dp", "dom", None),
        P("dom", None),
        P("dom"),
        P("dom", None),
        P("dom", None, None, None),
        P(),
        P(),
        P("dp", "dom", None),
    )
    out_specs = (P("dp", "dom", None), P("dp", "dom", None), P(), P())
    return jax.shard_map(shards, mesh=mesh, in_specs=in_specs, out_specs=out_specs, check_vma=False)
```

```python
import functools
import math

import jax
import jax.numpy as jnp
from jax import lax
from jax.experimental import pallas as pl
from jax.experimental.pallas import tpu as pltpu
from jax.sharding import PartitionSpec as P

ROWS = 128
RIM = 2
ANY = pl.BlockSpec(memory_space=pl.ANY)
VMEM = pl.BlockSpec(memory_space=pltpu.VMEM)
SMEM = pl.BlockSpec(memory_space=pltpu.SMEM)
BF16 = jnp.bfloat16
F32 = jnp.float32
MIB = 1024 * 1024
CORE, ALONG_Y, ALONG_Z = 1, 2, 4


def swapped(x, axis, mask):
    peers = lax.axis_size(axis)
    return lax.ppermute(x, axis, [(i, i ^ mask) for i in range(peers)])


def swapped_across(x, axis):
    peers = lax.axis_size(axis)
    return lax.ppermute(x, axis, [(i, (i + 1 if i % 2 else i - 1) % peers) for i in range(peers)])


def dot(a, b, contract=((1,), (0,))):
    return lax.dot_general(a, b, (contract, ((), ())), preferred_element_type=F32)


def shape(*dims, dtype=BF16):
    return jax.ShapeDtypeStruct(dims, dtype)


def call(body, outs, args, specs=None, scratch=(), flops=0, nbytes=0, limit=24 * MIB, out_specs=None):
    return pl.pallas_call(
        body,
        out_shape=outs,
        in_specs=specs or [VMEM] * len(args),
        out_specs=out_specs or [VMEM] * len(outs),
        scratch_shapes=list(scratch),
        cost_estimate=pl.CostEstimate(flops=flops, bytes_accessed=nbytes, transcendentals=0),
        compiler_params=pltpu.CompilerParams(vmem_limit_bytes=limit),
    )(*args)


def pick_body(order_hbm, feat_hbm, out_hbm, order_ref, feat_ref, hot_ref, out_ref, order_sem, feat_sem, out_sems):
    rows = feat_ref.shape[0]
    early = hot_ref.shape[0] // ROWS
    load_order = pltpu.make_async_copy(order_hbm, order_ref, order_sem)
    load_feat = pltpu.make_async_copy(feat_hbm, feat_ref, feat_sem)
    load_order.start()
    load_feat.start()
    lane = lax.broadcasted_iota(jnp.int32, (ROWS, ROWS), 1).astype(F32)
    zero = jnp.zeros((ROWS, ROWS), BF16)
    load_order.wait()

    def column(row):
        return jnp.transpose(jnp.broadcast_to(row.astype(F32), (ROWS, ROWS)))

    def hot_rows(k):
        row = order_ref[:, k * ROWS : (k + 1) * ROWS]
        high = column(row // ROWS).astype(BF16)
        low = jnp.where(column(row % ROWS) == lane, 1.0, 0.0).astype(BF16)
        return jnp.concatenate([jnp.where(high == b, low, zero) for b in range(rows // ROWS)], axis=1)

    for k in range(early):
        hot_ref[k * ROWS : (k + 1) * ROWS, :] = hot_rows(k)
    load_feat.wait()
    feat = feat_ref[...]
    puts = []
    for k in range(rows // ROWS):
        mine = slice(k * ROWS, (k + 1) * ROWS)
        hot = hot_ref[mine, :] if k < early else hot_rows(k)
        out_ref[mine, :] = dot(hot, feat).astype(BF16)
        puts.append(pltpu.make_async_copy(out_ref.at[pl.ds(k * ROWS, ROWS)], out_hbm.at[pl.ds(k * ROWS, ROWS)], out_sems.at[k]))
        puts[k].start()
    for put in puts:
        put.wait()


def build_body(cnt_ref, tgt_ref, vals_ref, w_edge_ref, rim_ref, both_ref, a_ref):
    blocks, slots = vals_ref.shape[:2]
    spare = blocks + 2 * RIM
    a_ref[...] = jnp.zeros_like(a_ref)
    both_ref[...] = jnp.zeros_like(both_ref)
    for c in range(blocks):
        mine = slice(c * ROWS, (c + 1) * ROWS)
        for s in range(slots):
            w = tgt_ref[c, s]
            at = jnp.where(w < blocks, w + RIM, jnp.where(w < 2 * blocks, w - blocks, w - blocks + RIM))
            at = jnp.where(s < cnt_ref[c], at, spare)
            value = vals_ref[c, s].astype(F32)
            a_ref[at, :, mine] = (a_ref[at, :, mine].astype(F32) + value).astype(BF16)
            lanes = pl.ds(pl.multiple_of(at * ROWS, ROWS), ROWS)
            both_ref[mine, lanes] = (both_ref[mine, lanes].astype(F32) + jnp.transpose(value)).astype(BF16)
    width = w_edge_ref.shape[0]
    rim_ref[: 2 * RIM * ROWS, :] = a_ref[blocks:spare].reshape(2 * RIM * ROWS, blocks * ROWS)
    rim_ref[2 * RIM * ROWS :, :width] = w_edge_ref[...]
    both_ref[:, (spare + 1) * ROWS :] = a_ref[:blocks].reshape(blocks * ROWS, blocks * ROWS)


def chosen(first, second):
    odd = lax.rem(lax.axis_index("dom"), 2) == 1
    return jnp.where(odd, first, second), jnp.where(odd, second, first)


def message_body(nodes_ref, a_ref, near_ref, far_ref, msg_ref):
    rows, width = nodes_ref.shape
    rim = RIM * ROWS
    w_edge = a_ref[2 * rim :, :width]
    for k in range(rows // rim):
        mine = slice(k * rim, (k + 1) * rim)
        pre = dot(nodes_ref[mine, :], w_edge)
        msg_ref[mine, :] = (pre * jax.nn.sigmoid(pre)).astype(BF16)
    sums = dot(a_ref[: 2 * rim, :], msg_ref[...])
    near, far = chosen(sums[:rim], sums[rim:])
    near_ref[...] = near.astype(BF16)
    far_ref[...] = far.astype(BF16)


def node_step(nodes, agg, gout, w_node):
    width = nodes.shape[1]
    pre = dot(nodes, w_node[:width]) + dot(agg, w_node[width:])
    sig = jax.nn.sigmoid(pre)
    out = (nodes.astype(F32) + pre * sig).astype(BF16)
    gout = gout.astype(F32)
    d_node = (gout * (sig * (1.0 + pre * (1.0 - sig)))).astype(BF16)
    back = dot(d_node, w_node, ((1,), (1,)))
    return out, d_node, gout + back[:, :width], back[:, width:].astype(BF16)


def own_body(
    nodes_ref, msg_ref, adj_ref, cot_ref, w_node_ref,
    own_ref, out_ref, agg_ref, d_node_ref, d_nodes1_ref, d_agg_ref,
):
    rows, width = nodes_ref.shape
    rim = RIM * ROWS
    msg = msg_ref[...]
    first = adj_ref.shape[1] - rows
    for k in range(rows // rim):
        mine = slice(k * rim, (k + 1) * rim)
        window = dot(adj_ref[mine, first:], msg).astype(BF16)
        if k == 0:
            own_ref[:rim, :] = window
        elif k == rows // rim - 1:
            own_ref[rim:, :] = window
        else:
            here = slice((k - 1) * rim, k * rim)
            agg_ref[here, :] = window
            out, d_node, d_nodes1, d_agg = node_step(nodes_ref[mine, :], window, cot_ref[mine, :], w_node_ref[...])
            out_ref[here, :] = out
            d_node_ref[here, :] = d_node
            d_nodes1_ref[here, :] = d_nodes1
            d_agg_ref[here, :] = d_agg


def rim_body(
    nodes_ref, own_ref, near_in_ref, far_in_ref, cot_ref, w_node_ref,
    near_ref, far_ref, out_ref, agg_ref, d_node_ref, d_nodes1_ref, d_agg_ref,
):
    rows = nodes_ref.shape[0]
    rim = RIM * ROWS
    arrived = chosen(near_in_ref[...].astype(F32), far_in_ref[...].astype(F32))
    rims = []
    for k in range(2):
        mine = slice(k * (rows - rim), k * (rows - rim) + rim)
        here = slice(k * rim, (k + 1) * rim)
        agg = (own_ref[here, :].astype(F32) + arrived[k]).astype(BF16)
        agg_ref[here, :] = agg
        out, d_node, d_nodes1, d_agg = node_step(nodes_ref[mine, :], agg, cot_ref[mine, :], w_node_ref[...])
        out_ref[here, :] = out
        d_node_ref[here, :] = d_node
        d_nodes1_ref[here, :] = d_nodes1
        d_agg_ref[here, :] = d_agg
        rims.append(d_agg)
    near_ref[...], far_ref[...] = chosen(rims[0], rims[1])


def in_order(mid_ref, rim_ref):
    rim = RIM * ROWS
    return jnp.concatenate([rim_ref[:rim, :], mid_ref[...], rim_ref[rim:, :]], axis=0)


def grad_node_body(scale, nodes_ref, agg_mid_ref, agg_rim_ref, d_node_mid_ref, d_node_rim_ref, *out_refs):
    width = nodes_ref.shape[1]
    d_node = in_order(d_node_mid_ref, d_node_rim_ref)
    agg = in_order(agg_mid_ref, agg_rim_ref)
    first = lax.axis_index("dp") == 0
    for k, left in enumerate((nodes_ref[...], agg)):
        mine = slice(k * width, (k + 1) * width)
        grad = dot(left, d_node, ((0,), (0,))) * scale
        if len(out_refs) == 1:
            out_refs[0][mine, :] = grad
            continue
        half = width // 2
        out_refs[0][mine, :] = jnp.where(first, grad[:, :half], grad[:, half:])
        out_refs[1][mine, :] = jnp.where(first, grad[:, half:], grad[:, :half]).astype(BF16)


def behind_body(
    nodes_ref, at_ref, w_edge_ref, out_mid_ref, out_rim_ref, d_agg_mid_ref, d_agg_rim_ref,
    out_ref, d_msg_ref, slope_ref,
):
    rows = nodes_ref.shape[0]
    rim = RIM * ROWS
    out_ref[...] = in_order(out_mid_ref, out_rim_ref)
    d_agg = in_order(d_agg_mid_ref, d_agg_rim_ref)
    for k in range(rows // rim):
        mine = slice(k * rim, (k + 1) * rim)
        d_msg_ref[mine, :] = dot(at_ref[mine, :rows], d_agg)
        pre = dot(nodes_ref[mine, :], w_edge_ref[...])
        sig = jax.nn.sigmoid(pre)
        slope_ref[mine, :] = sig * (1.0 + pre * (1.0 - sig))


def edge_body(
    at_ref, near_ref, far_ref, d_msg_ref, slope_ref, mid_ref, rim_ref, w_edge_ref,
    back_hbm, d_edge_ref, back_ref, sems,
):
    rows, width = back_ref.shape
    rim = RIM * ROWS
    prev, after = chosen(near_ref[...], far_ref[...])
    rims = jnp.concatenate([prev, after], axis=0)
    w_edge = w_edge_ref[...]
    puts = []
    for k in range(rows // rim):
        mine = slice(k * rim, (k + 1) * rim)
        d_msg = d_msg_ref[mine, :] + dot(at_ref[mine, rows : rows + 2 * rim], rims)
        d_edge = (d_msg.astype(BF16).astype(F32) * slope_ref[mine, :]).astype(BF16)
        d_edge_ref[mine, :] = d_edge
        if k == 0:
            d_nodes1 = rim_ref[:rim, :]
        elif k == rows // rim - 1:
            d_nodes1 = rim_ref[rim:, :]
        else:
            d_nodes1 = mid_ref[(k - 1) * rim : k * rim, :]
        back_ref[mine, :] = (d_nodes1 + dot(d_edge, w_edge, ((1,), (1,)))).astype(BF16)
        part = pl.ds(k * rim, rim)
        puts.append(pltpu.make_async_copy(back_ref.at[part], back_hbm.at[part], sems.at[k]))
        puts[k].start()
    for put in puts:
        put.wait()


def bit_of(mask):
    return lax.rem(lax.div(lax.axis_index("dom"), mask), 2)


def cut_rows(total_ref, mask, keep_ref, send_ref):
    size = keep_ref.shape[0]
    bit = bit_of(mask)
    keep_ref[...] = total_ref[pl.ds(pl.multiple_of(bit * size, 16), size), :]
    send_ref[...] = total_ref[pl.ds(pl.multiple_of((1 - bit) * size, 16), size), :].astype(BF16)


def grad_edge_body(scale, nodes_ref, d_edge_ref, out_ref):
    out_ref[...] = dot(nodes_ref[...], d_edge_ref[...], ((0,), (0,))) * scale


def first_cut_body(scale, mask, nodes_ref, d_edge_ref, node_ref, node_in_ref, keep_ref, send_ref, total_ref, edge_ref):
    half = node_ref.shape[1]
    few, more = edge_ref.shape[0] // 4, node_ref.shape[0] // 4
    grad_edge_body(scale, nodes_ref, d_edge_ref, edge_ref)
    for q in range(4):
        row = q * (2 * few + more)
        mine = slice(q * more, (q + 1) * more)
        total_ref[row : row + more, :] = node_ref[mine, :] + node_in_ref[mine, :].astype(F32)
        row += more
        mine = slice(q * few, (q + 1) * few)
        total_ref[row : row + few, :] = edge_ref[mine, :half]
        total_ref[row + few : row + 2 * few, :] = edge_ref[mine, half:]
    cut_rows(total_ref, mask, keep_ref, send_ref)


def next_cut_body(mask, mine_ref, in_ref, keep_ref, send_ref, total_ref):
    total_ref[...] = mine_ref[...] + in_ref[...].astype(F32)
    cut_rows(total_ref, mask, keep_ref, send_ref)


def sum_body(mine_ref, in_ref, out_ref):
    out_ref[...] = (mine_ref[...].astype(F32) + in_ref[...].astype(F32)).astype(BF16)


def join_body(mask, mine_ref, dp_ref, y_ref, both_ref, out_ref):
    size, half = mine_ref.shape
    more = size // 2
    few = more // 2
    first = lax.axis_index("dp") == 0
    low = bit_of(mask) == 0
    mine = [ref[...] for ref in (mine_ref, dp_ref)]
    other = [ref[...] for ref in (y_ref, both_ref)]
    for side in range(2):
        a, b = (jnp.where(low, x, y) if side == 0 else jnp.where(low, y, x) for x, y in zip(mine, other))
        row = side * (few + more)
        total = (a[more:].astype(F32) + b[more:].astype(F32)).astype(BF16)
        out_ref[row : row + few, :half] = total[:few]
        out_ref[row : row + few, half:] = total[few:]
        row += few
        out_ref[row : row + more, :half] = jnp.where(first, a[:more], b[:more])
        out_ref[row : row + more, half:] = jnp.where(first, b[:more], a[:more])


def finish_body(own, *refs):
    part_ref = refs[0]
    edge_hbm, node_hbm, edge_ref, node_ref, sems = refs[-5:]
    few, more = edge_ref.shape[0] // 2, node_ref.shape[0] // 2
    for k in range(2):
        row = k * (few + more)
        edge_ref[k * few : (k + 1) * few, :] = part_ref[row : row + few, :].astype(F32)
        node_ref[k * more : (k + 1) * more, :] = part_ref[row + few : row + few + more, :].astype(F32)
    side = bit_of(CORE) if own else 1 - bit_of(CORE)
    puts = []
    for k, (ref, hbm) in enumerate(((edge_ref, edge_hbm), (node_ref, node_hbm))):
        size = ref.shape[0]
        to = hbm.at[pl.ds(pl.multiple_of(side * size, 8), size), :]
        puts.append(pltpu.make_async_copy(ref, to, sems.at[k]))
        puts[k].start()
    for put in puts:
        put.wait()


def finished(own, part, grads, width):
    outs = [shape(width, width, dtype=F32), shape(2 * width, width, dtype=F32)]
    return pl.pallas_call(
        functools.partial(finish_body, own),
        out_shape=outs,
        in_specs=[VMEM] + [ANY] * len(grads),
        out_specs=[ANY, ANY],
        scratch_shapes=[
            pltpu.VMEM((width // 2, width), F32),
            pltpu.VMEM((width, width), F32),
            pltpu.SemaphoreType.DMA((2,)),
        ],
        input_output_aliases={1: 0, 2: 1} if grads else {},
        cost_estimate=pl.CostEstimate(flops=0, bytes_accessed=3 * width * width * 4, transcendentals=0),
        compiler_params=pltpu.CompilerParams(vmem_limit_bytes=24 * MIB),
    )(part, *grads)


def swapped_both(x, mask):
    peers = lax.axis_size("dom")
    total = 2 * peers
    return lax.ppermute(x, ("dp", "dom"), [(i, (i + peers) % total ^ mask) for i in range(total)])


def cut_grads(scale, nodes, d_edge, node_part):
    width = nodes.shape[1]
    half = width // 2
    size = node_part[0].shape[0] + 2 * width

    def cut(body, args, size, *scratch):
        return call(
            body,
            [shape(size // 2, half, dtype=F32), shape(size // 2, half)],
            args,
            scratch=[pltpu.VMEM((size, half), F32), *scratch],
        )

    first = functools.partial(first_cut_body, scale, CORE)
    keep, send = cut(first, (nodes, d_edge, *node_part), size, pltpu.VMEM((width, width), F32))
    return cut(functools.partial(next_cut_body, ALONG_Y), (keep, swapped(send, "dom", CORE)), size // 2)


def joined(keep, send, back, send_order, width):
    out = [shape(*send.shape)]
    (mine,) = call(sum_body, out, (keep, swapped(send, "dom", ALONG_Y)))
    for mask in (ALONG_Z, 2 * ALONG_Z):
        (mine,) = call(sum_body, out, (mine, swapped(mine, "dom", mask)))
    others = swapped(mine, "dp", 1), swapped(mine, "dom", ALONG_Y), swapped_both(mine, ALONG_Y)
    grad_brick = placed(send_order, back)
    mine, grad_brick = lax.optimization_barrier((mine, grad_brick))
    (mine,) = call(functools.partial(join_body, ALONG_Y), [shape(6 * (width // 4), width)], (mine, *others))
    grads = finished(True, mine, (), width)
    return *finished(False, swapped(mine, "dom", CORE), grads, width), grad_brick


def placed(send_order, back):
    rows, width = back.shape
    return call(
        place_body,
        [shape(rows, width)],
        (send_order, back),
        flops=2 * rows * rows * width,
        nbytes=4 * rows * width,
    )[0]


def place_body(order_ref, back_ref, out_ref):
    rows = back_ref.shape[0]
    back = back_ref[...]
    order = order_ref[...]
    high = jnp.broadcast_to((order // ROWS).astype(F32), (ROWS, rows)).astype(BF16)
    row = lax.broadcasted_iota(jnp.int32, (ROWS, rows), 0)
    low = jnp.where(jnp.broadcast_to(order % ROWS, (ROWS, rows)) == row, 1.0, 0.0).astype(BF16)
    zero = jnp.zeros((ROWS, rows), BF16)
    for k in range(rows // ROWS):
        mine = slice(k * ROWS, (k + 1) * ROWS)
        hot = jnp.where(high == k, low, zero)
        out_ref[mine, :] = dot(hot, back).astype(BF16)


def shards(features, send_order, adj_count, adj_target, adj_vals, w_edge, w_node, cotangent):
    ndp = lax.axis_size("dp")
    ndom = lax.axis_size("dom")
    rows, width = features.shape[1:]
    per_peer = rows // ndom
    blocks, slots = adj_vals.shape[:2]
    rim = RIM * ROWS
    scale = 1.0 / math.sqrt(float(ndp * rows * ndom))
    tall = shape(rows, width)
    tall_f = shape(rows, width, dtype=F32)
    edge = shape(rim, width)
    rims = shape(2 * rim, width)
    mid = shape(rows - 2 * rim, width)
    unit = rows * width * 2
    square = 2 * rows * width * width

    (picked,) = call(
        pick_body,
        [tall],
        (send_order, features[0]),
        [ANY, ANY],
        [
            pltpu.VMEM((1, rows), jnp.int32),
            pltpu.VMEM((rows, width), BF16),
            pltpu.VMEM((rows // 2, rows), BF16),
            pltpu.VMEM((rows, width), BF16),
            pltpu.SemaphoreType.DMA,
            pltpu.SemaphoreType.DMA,
            pltpu.SemaphoreType.DMA((blocks,)),
        ],
        flops=2 * rows * rows * width,
        nbytes=2 * unit,
        out_specs=[ANY],
        limit=56 * MIB,
    )
    nodes = lax.all_to_all(
        picked.reshape(ndom, per_peer, width), "dom", split_axis=0, concat_axis=0, tiled=True
    ).reshape(rows, width)
    spots = blocks + 2 * RIM + 1
    adj_rim, adj = call(
        build_body,
        [shape(2 * rim + width, rows), shape(rows, spots * ROWS + rows)],
        (adj_count, adj_target, adj_vals, w_edge),
        [SMEM, SMEM, VMEM, VMEM],
        [pltpu.VMEM((spots, ROWS, rows), BF16)],
        nbytes=16 * unit,
    )
    near, far, msg = call(
        message_body, [edge, edge, tall], (nodes, adj_rim), flops=square + 4 * rim * rows * width, nbytes=4 * unit
    )
    far = swapped_across(far, "dom")
    near = swapped(near, "dom", 1)
    cot = cotangent[0]
    own, out_mid, agg_mid, d_node_mid, d_nodes1_mid, d_agg_mid = call(
        own_body,
        [rims, mid, mid, mid, shape(*mid.shape, dtype=F32), mid],
        (nodes, msg, adj, cot, w_node),
        flops=2 * rows * rows * width + 2 * square,
        nbytes=8 * unit,
    )
    near, far, out_rim, agg_rim, d_node_rim, d_nodes1_rim, d_agg_rim = call(
        rim_body,
        [edge, edge, rims, rims, rims, shape(*rims.shape, dtype=F32), rims],
        (nodes, own, near, far, cot, w_node),
        flops=2 * square,
        nbytes=4 * unit,
    )
    far = swapped_across(far, "dom")
    near = swapped(near, "dom", 1)
    tiled = ndp == 2 and ndom == 16

    node_part = call(
        functools.partial(grad_node_body, scale),
        [shape(2 * width, width // 2, dtype=F32), shape(2 * width, width // 2)]
        if tiled
        else [shape(2 * width, width, dtype=F32)],
        (nodes, agg_mid, agg_rim, d_node_mid, d_node_rim),
        flops=2 * square,
        nbytes=3 * unit,
    )
    if tiled:
        node_part = (node_part[0], swapped(node_part[1], "dp", 1))
    node_out, d_msg, slope = call(
        behind_body,
        [tall, tall_f, tall_f],
        (nodes, adj, w_edge, out_mid, out_rim, d_agg_mid, d_agg_rim),
        flops=2 * rows * rows * width + square,
        nbytes=8 * unit,
    )
    back, d_edge = call(
        edge_body,
        [tall, tall],
        (adj, near, far, d_msg, slope, d_nodes1_mid, d_nodes1_rim, w_edge),
        scratch=[pltpu.VMEM((rows, width), BF16), pltpu.SemaphoreType.DMA((rows // rim,))],
        out_specs=[ANY, VMEM],
        flops=2 * square + 4 * rim * rows * width,
        nbytes=8 * unit,
    )
    if tiled:
        back, node_in = lax.optimization_barrier((back, node_part[1]))
        keep, send = cut_grads(scale, nodes, d_edge, (node_part[0], node_in))
    back = lax.all_to_all(
        back.reshape(ndom, per_peer, width), "dom", split_axis=0, concat_axis=0, tiled=True
    ).reshape(rows, width)
    if tiled:
        grad_edge, grad_node, grad_brick = joined(keep, send, back, send_order, width)
    else:
        (edge_part,) = call(
            functools.partial(grad_edge_body, scale), [shape(width, width, dtype=F32)], (nodes, d_edge), flops=square
        )
        grad_edge, grad_node = (lax.psum(part, ("dp", "dom")) for part in (edge_part, node_part[0]))
        grad_brick = placed(send_order, back)
    return (node_out[None], grad_brick[None], grad_edge, grad_node)


def solution(mesh):
    in_specs = (
        P("dp", "dom", None),
        P("dom", None),
        P("dom"),
        P("dom", None),
        P("dom", None, None, None),
        P(),
        P(),
        P("dp", "dom", None),
    )
    out_specs = (P("dp", "dom", None), P("dp", "dom", None), P(), P())
    return jax.shard_map(shards, mesh=mesh, in_specs=in_specs, out_specs=out_specs, check_vma=False)
```

```python
import functools
import math

import jax
import jax.numpy as jnp
from jax import lax
from jax.experimental import pallas as pl
from jax.experimental.pallas import tpu as pltpu
from jax.sharding import PartitionSpec as P

ROWS = 128
RIM = 2
ANY = pl.BlockSpec(memory_space=pl.ANY)
VMEM = pl.BlockSpec(memory_space=pltpu.VMEM)
SMEM = pl.BlockSpec(memory_space=pltpu.SMEM)
BF16 = jnp.bfloat16
F32 = jnp.float32
MIB = 1024 * 1024
CORE, ALONG_Y, ALONG_Z = 1, 2, 4


def swapped(x, axis, mask):
    peers = lax.axis_size(axis)
    return lax.ppermute(x, axis, [(i, i ^ mask) for i in range(peers)])


def swapped_across(x, axis):
    peers = lax.axis_size(axis)
    return lax.ppermute(x, axis, [(i, (i + 1 if i % 2 else i - 1) % peers) for i in range(peers)])


def dot(a, b, contract=((1,), (0,))):
    return lax.dot_general(a, b, (contract, ((), ())), preferred_element_type=F32)


def shape(*dims, dtype=BF16):
    return jax.ShapeDtypeStruct(dims, dtype)


def call(body, outs, args, specs=None, scratch=(), flops=0, nbytes=0, limit=24 * MIB, out_specs=None):
    return pl.pallas_call(
        body,
        out_shape=outs,
        in_specs=specs or [VMEM] * len(args),
        out_specs=out_specs or [VMEM] * len(outs),
        scratch_shapes=list(scratch),
        cost_estimate=pl.CostEstimate(flops=flops, bytes_accessed=nbytes, transcendentals=0),
        compiler_params=pltpu.CompilerParams(vmem_limit_bytes=limit),
    )(*args)


def pick_body(order_hbm, feat_hbm, out_hbm, order_ref, feat_ref, hot_ref, out_ref, order_sem, feat_sem, out_sems):
    rows = feat_ref.shape[0]
    early = hot_ref.shape[0] // ROWS
    load_order = pltpu.make_async_copy(order_hbm, order_ref, order_sem)
    load_feat = pltpu.make_async_copy(feat_hbm, feat_ref, feat_sem)
    load_order.start()
    load_feat.start()
    lane = lax.broadcasted_iota(jnp.int32, (ROWS, ROWS), 1).astype(F32)
    zero = jnp.zeros((ROWS, ROWS), BF16)
    load_order.wait()

    def column(row):
        return jnp.transpose(jnp.broadcast_to(row.astype(F32), (ROWS, ROWS)))

    def hot_rows(k):
        row = order_ref[:, k * ROWS : (k + 1) * ROWS]
        high = column(row // ROWS).astype(BF16)
        low = jnp.where(column(row % ROWS) == lane, 1.0, 0.0).astype(BF16)
        return jnp.concatenate([jnp.where(high == b, low, zero) for b in range(rows // ROWS)], axis=1)

    for k in range(early):
        hot_ref[k * ROWS : (k + 1) * ROWS, :] = hot_rows(k)
    load_feat.wait()
    feat = feat_ref[...]
    puts = []
    for k in range(rows // ROWS):
        mine = slice(k * ROWS, (k + 1) * ROWS)
        hot = hot_ref[mine, :] if k < early else hot_rows(k)
        out_ref[mine, :] = dot(hot, feat).astype(BF16)
        puts.append(pltpu.make_async_copy(out_ref.at[pl.ds(k * ROWS, ROWS)], out_hbm.at[pl.ds(k * ROWS, ROWS)], out_sems.at[k]))
        puts[k].start()
    for put in puts:
        put.wait()


def build_body(cnt_ref, tgt_ref, vals_ref, w_edge_ref, rim_ref, both_ref, a_ref):
    blocks, slots = vals_ref.shape[:2]
    spare = blocks + 2 * RIM
    a_ref[...] = jnp.zeros_like(a_ref)
    both_ref[...] = jnp.zeros_like(both_ref)
    for c in range(blocks):
        mine = slice(c * ROWS, (c + 1) * ROWS)
        for s in range(slots):
            w = tgt_ref[c, s]
            at = jnp.where(w < blocks, w + RIM, jnp.where(w < 2 * blocks, w - blocks, w - blocks + RIM))
            at = jnp.where(s < cnt_ref[c], at, spare)
            value = vals_ref[c, s].astype(F32)
            a_ref[at, :, mine] = (a_ref[at, :, mine].astype(F32) + value).astype(BF16)
            lanes = pl.ds(pl.multiple_of(at * ROWS, ROWS), ROWS)
            both_ref[mine, lanes] = (both_ref[mine, lanes].astype(F32) + jnp.transpose(value)).astype(BF16)
    width = w_edge_ref.shape[0]
    rim_ref[: 2 * RIM * ROWS, :] = a_ref[blocks:spare].reshape(2 * RIM * ROWS, blocks * ROWS)
    rim_ref[2 * RIM * ROWS :, :width] = w_edge_ref[...]
    both_ref[:, (spare + 1) * ROWS :] = a_ref[:blocks].reshape(blocks * ROWS, blocks * ROWS)


def chosen(first, second):
    odd = lax.rem(lax.axis_index("dom"), 2) == 1
    return jnp.where(odd, first, second), jnp.where(odd, second, first)


def message_body(nodes_ref, a_ref, far_ref, msg_ref):
    rows, width = nodes_ref.shape
    rim = RIM * ROWS
    w_edge = a_ref[2 * rim :, :width]
    for k in range(rows // rim):
        mine = slice(k * rim, (k + 1) * rim)
        pre = dot(nodes_ref[mine, :], w_edge)
        msg_ref[mine, :] = (pre * jax.nn.sigmoid(pre)).astype(BF16)
    far_ref[...] = dot(a_ref[end_of(True, rim), :], msg_ref[...]).astype(BF16)


def end_of(far, start):
    odd = lax.rem(lax.axis_index("dom"), 2)
    return pl.ds(pl.multiple_of((odd if far else 1 - odd) * start, ROWS), RIM * ROWS)


def near_body(a_ref, msg_ref, near_ref):
    near_ref[...] = dot(a_ref[end_of(False, RIM * ROWS), :], msg_ref[...]).astype(BF16)


def node_step(nodes, agg, gout, w_node):
    width = nodes.shape[1]
    pre = dot(nodes, w_node[:width]) + dot(agg, w_node[width:])
    sig = jax.nn.sigmoid(pre)
    out = (nodes.astype(F32) + pre * sig).astype(BF16)
    gout = gout.astype(F32)
    d_node = (gout * (sig * (1.0 + pre * (1.0 - sig)))).astype(BF16)
    back = dot(d_node, w_node, ((1,), (1,)))
    return out, d_node, gout + back[:, :width], back[:, width:].astype(BF16)


def own_body(
    nodes_ref, msg_ref, adj_ref, cot_ref, w_node_ref,
    own_ref, out_ref, agg_ref, d_node_ref, d_nodes1_ref, d_agg_ref,
):
    rows, width = nodes_ref.shape
    rim = RIM * ROWS
    msg = msg_ref[...]
    first = adj_ref.shape[1] - rows
    for k in range(rows // rim):
        mine = slice(k * rim, (k + 1) * rim)
        window = dot(adj_ref[mine, first:], msg).astype(BF16)
        if k == 0:
            own_ref[:rim, :] = window
        elif k == rows // rim - 1:
            own_ref[rim:, :] = window
        else:
            here = slice((k - 1) * rim, k * rim)
            agg_ref[here, :] = window
            out, d_node, d_nodes1, d_agg = node_step(nodes_ref[mine, :], window, cot_ref[mine, :], w_node_ref[...])
            out_ref[here, :] = out
            d_node_ref[here, :] = d_node
            d_nodes1_ref[here, :] = d_nodes1
            d_agg_ref[here, :] = d_agg


def rim_body(
    far, nodes_ref, own_ref, in_ref, cot_ref, w_node_ref,
    out_ref, agg_ref, d_node_ref, d_nodes1_ref, d_agg_ref,
):
    rim = RIM * ROWS
    mine = end_of(far, nodes_ref.shape[0] - rim)
    agg = (own_ref[end_of(far, rim), :].astype(F32) + in_ref[...].astype(F32)).astype(BF16)
    agg_ref[...] = agg
    out, d_node, d_nodes1, d_agg = node_step(nodes_ref[mine, :], agg, cot_ref[mine, :], w_node_ref[...])
    out_ref[...] = out
    d_node_ref[...] = d_node
    d_nodes1_ref[...] = d_nodes1
    d_agg_ref[...] = d_agg


def in_order(mid_ref, near_ref, far_ref):
    first, last = chosen(near_ref[...], far_ref[...])
    return jnp.concatenate([first, mid_ref[...], last], axis=0)


def grad_node_body(scale, nodes_ref, *refs):
    width = nodes_ref.shape[1]
    out_refs = refs[6:]
    agg = in_order(*refs[:3])
    d_node = in_order(*refs[3:6])
    first = lax.axis_index("dp") == 0
    for k, left in enumerate((nodes_ref[...], agg)):
        mine = slice(k * width, (k + 1) * width)
        grad = dot(left, d_node, ((0,), (0,))) * scale
        if len(out_refs) == 1:
            out_refs[0][mine, :] = grad
            continue
        half = width // 2
        out_refs[0][mine, :] = jnp.where(first, grad[:, :half], grad[:, half:])
        out_refs[1][mine, :] = jnp.where(first, grad[:, half:], grad[:, :half]).astype(BF16)


def behind_body(
    nodes_ref, at_ref, w_edge_ref, out_mid_ref, out_near_ref, out_far_ref,
    d_agg_mid_ref, d_agg_near_ref, d_agg_far_ref, out_ref, d_msg_ref, slope_ref,
):
    rows = nodes_ref.shape[0]
    rim = RIM * ROWS
    out_ref[...] = in_order(out_mid_ref, out_near_ref, out_far_ref)
    d_agg = in_order(d_agg_mid_ref, d_agg_near_ref, d_agg_far_ref)
    for k in range(rows // rim):
        mine = slice(k * rim, (k + 1) * rim)
        d_msg_ref[mine, :] = dot(at_ref[mine, :rows], d_agg)
        pre = dot(nodes_ref[mine, :], w_edge_ref[...])
        sig = jax.nn.sigmoid(pre)
        slope_ref[mine, :] = sig * (1.0 + pre * (1.0 - sig))


def edge_body(
    scale, nodes_ref, at_ref, near_ref, far_ref, d_msg_ref, slope_ref, mid_ref, near1_ref, far1_ref, w_edge_ref,
    back_hbm, g_edge_ref, d_edge_ref, back_ref, sems,
):
    rows, width = nodes_ref.shape
    rim = RIM * ROWS
    prev, after = chosen(near_ref[...], far_ref[...])
    rims = jnp.concatenate([prev, after], axis=0)
    ends = chosen(near1_ref[...], far1_ref[...])
    w_edge = w_edge_ref[...]
    puts = []
    for k in range(rows // rim):
        mine = slice(k * rim, (k + 1) * rim)
        d_msg = d_msg_ref[mine, :] + dot(at_ref[mine, rows : rows + 2 * rim], rims)
        d_edge = (d_msg.astype(BF16).astype(F32) * slope_ref[mine, :]).astype(BF16)
        d_edge_ref[mine, :] = d_edge
        if k == 0:
            d_nodes1 = ends[0]
        elif k == rows // rim - 1:
            d_nodes1 = ends[1]
        else:
            d_nodes1 = mid_ref[(k - 1) * rim : k * rim, :]
        back_ref[mine, :] = (d_nodes1 + dot(d_edge, w_edge, ((1,), (1,)))).astype(BF16)
        part = pl.ds(k * rim, rim)
        puts.append(pltpu.make_async_copy(back_ref.at[part], back_hbm.at[part], sems.at[k]))
        puts[k].start()
    g_edge_ref[...] = dot(nodes_ref[...], d_edge_ref[...], ((0,), (0,))) * scale
    for put in puts:
        put.wait()


def bit_of(mask):
    return lax.rem(lax.div(lax.axis_index("dom"), mask), 2)


def cut_rows(total_ref, mask, keep_ref, send_ref):
    size = keep_ref.shape[0]
    bit = bit_of(mask)
    keep_ref[...] = total_ref[pl.ds(pl.multiple_of(bit * size, 16), size), :]
    send_ref[...] = total_ref[pl.ds(pl.multiple_of((1 - bit) * size, 16), size), :].astype(BF16)


def first_cut_body(mask, edge_ref, node_ref, node_in_ref, keep_ref, send_ref, total_ref):
    half = node_ref.shape[1]
    few, more = edge_ref.shape[0] // 4, node_ref.shape[0] // 4
    for q in range(4):
        row = q * (2 * few + more)
        mine = slice(q * more, (q + 1) * more)
        total_ref[row : row + more, :] = node_ref[mine, :] + node_in_ref[mine, :].astype(F32)
        row += more
        mine = slice(q * few, (q + 1) * few)
        total_ref[row : row + few, :] = edge_ref[mine, :half]
        total_ref[row + few : row + 2 * few, :] = edge_ref[mine, half:]
    cut_rows(total_ref, mask, keep_ref, send_ref)


def next_cut_body(mask, mine_ref, in_ref, keep_ref, send_ref, total_ref):
    total_ref[...] = mine_ref[...] + in_ref[...].astype(F32)
    cut_rows(total_ref, mask, keep_ref, send_ref)


def sum_body(mine_ref, in_ref, out_ref):
    out_ref[...] = (mine_ref[...].astype(F32) + in_ref[...].astype(F32)).astype(BF16)


def join_body(mask, mine_ref, dp_ref, y_ref, both_ref, out_ref):
    size, half = mine_ref.shape
    more = size // 2
    few = more // 2
    first = lax.axis_index("dp") == 0
    low = bit_of(mask) == 0
    mine = [ref[...] for ref in (mine_ref, dp_ref)]
    other = [ref[...] for ref in (y_ref, both_ref)]
    for side in range(2):
        a, b = (jnp.where(low, x, y) if side == 0 else jnp.where(low, y, x) for x, y in zip(mine, other))
        row = side * (few + more)
        total = (a[more:].astype(F32) + b[more:].astype(F32)).astype(BF16)
        out_ref[row : row + few, :half] = total[:few]
        out_ref[row : row + few, half:] = total[few:]
        row += few
        out_ref[row : row + more, :half] = jnp.where(first, a[:more], b[:more])
        out_ref[row : row + more, half:] = jnp.where(first, b[:more], a[:more])


def finish_body(own, *refs):
    part_ref = refs[0]
    edge_hbm, node_hbm, edge_ref, node_ref, sems = refs[-5:]
    few, more = edge_ref.shape[0] // 2, node_ref.shape[0] // 2
    for k in range(2):
        row = k * (few + more)
        edge_ref[k * few : (k + 1) * few, :] = part_ref[row : row + few, :].astype(F32)
        node_ref[k * more : (k + 1) * more, :] = part_ref[row + few : row + few + more, :].astype(F32)
    side = bit_of(CORE) if own else 1 - bit_of(CORE)
    puts = []
    for k, (ref, hbm) in enumerate(((edge_ref, edge_hbm), (node_ref, node_hbm))):
        size = ref.shape[0]
        to = hbm.at[pl.ds(pl.multiple_of(side * size, 8), size), :]
        puts.append(pltpu.make_async_copy(ref, to, sems.at[k]))
        puts[k].start()
    for put in puts:
        put.wait()


def finished(own, part, grads, width):
    outs = [shape(width, width, dtype=F32), shape(2 * width, width, dtype=F32)]
    return pl.pallas_call(
        functools.partial(finish_body, own),
        out_shape=outs,
        in_specs=[VMEM] + [ANY] * len(grads),
        out_specs=[ANY, ANY],
        scratch_shapes=[
            pltpu.VMEM((width // 2, width), F32),
            pltpu.VMEM((width, width), F32),
            pltpu.SemaphoreType.DMA((2,)),
        ],
        input_output_aliases={1: 0, 2: 1} if grads else {},
        cost_estimate=pl.CostEstimate(flops=0, bytes_accessed=3 * width * width * 4, transcendentals=0),
        compiler_params=pltpu.CompilerParams(vmem_limit_bytes=24 * MIB),
    )(part, *grads)


def swapped_both(x, mask):
    peers = lax.axis_size("dom")
    total = 2 * peers
    return lax.ppermute(x, ("dp", "dom"), [(i, (i + peers) % total ^ mask) for i in range(total)])


def cut_grads(edge_part, node_part):
    half = node_part[0].shape[1]
    size = node_part[0].shape[0] + 2 * edge_part.shape[0]

    def cut(body, mask, args, size):
        return call(
            functools.partial(body, mask),
            [shape(size // 2, half, dtype=F32), shape(size // 2, half)],
            args,
            scratch=[pltpu.VMEM((size, half), F32)],
        )

    keep, send = cut(first_cut_body, CORE, (edge_part, *node_part), size)
    return cut(next_cut_body, ALONG_Y, (keep, swapped(send, "dom", CORE)), size // 2)


def joined(keep, send, back, send_order, width):
    out = [shape(*send.shape)]
    (mine,) = call(sum_body, out, (keep, swapped(send, "dom", ALONG_Y)))
    for mask in (ALONG_Z, 2 * ALONG_Z):
        (mine,) = call(sum_body, out, (mine, swapped(mine, "dom", mask)))
    others = swapped(mine, "dp", 1), swapped(mine, "dom", ALONG_Y), swapped_both(mine, ALONG_Y)
    grad_brick = placed(send_order, back)
    mine, grad_brick = lax.optimization_barrier((mine, grad_brick))
    (mine,) = call(functools.partial(join_body, ALONG_Y), [shape(6 * (width // 4), width)], (mine, *others))
    grads = finished(True, mine, (), width)
    return *finished(False, swapped(mine, "dom", CORE), grads, width), grad_brick


def placed(send_order, back):
    rows, width = back.shape
    return call(
        place_body,
        [shape(rows, width)],
        (send_order, back),
        flops=2 * rows * rows * width,
        nbytes=4 * rows * width,
    )[0]


def place_body(order_ref, back_ref, out_ref):
    rows = back_ref.shape[0]
    back = back_ref[...]
    order = order_ref[...]
    high = jnp.broadcast_to((order // ROWS).astype(F32), (ROWS, rows)).astype(BF16)
    row = lax.broadcasted_iota(jnp.int32, (ROWS, rows), 0)
    low = jnp.where(jnp.broadcast_to(order % ROWS, (ROWS, rows)) == row, 1.0, 0.0).astype(BF16)
    zero = jnp.zeros((ROWS, rows), BF16)
    for k in range(rows // ROWS):
        mine = slice(k * ROWS, (k + 1) * ROWS)
        hot = jnp.where(high == k, low, zero)
        out_ref[mine, :] = dot(hot, back).astype(BF16)


def shards(features, send_order, adj_count, adj_target, adj_vals, w_edge, w_node, cotangent):
    ndp = lax.axis_size("dp")
    ndom = lax.axis_size("dom")
    rows, width = features.shape[1:]
    per_peer = rows // ndom
    blocks, slots = adj_vals.shape[:2]
    rim = RIM * ROWS
    scale = 1.0 / math.sqrt(float(ndp * rows * ndom))
    tall = shape(rows, width)
    tall_f = shape(rows, width, dtype=F32)
    edge = shape(rim, width)
    rims = shape(2 * rim, width)
    mid = shape(rows - 2 * rim, width)
    unit = rows * width * 2
    square = 2 * rows * width * width

    (picked,) = call(
        pick_body,
        [tall],
        (send_order, features[0]),
        [ANY, ANY],
        [
            pltpu.VMEM((1, rows), jnp.int32),
            pltpu.VMEM((rows, width), BF16),
            pltpu.VMEM((2 * ROWS, rows), BF16),
            pltpu.VMEM((rows, width), BF16),
            pltpu.SemaphoreType.DMA,
            pltpu.SemaphoreType.DMA,
            pltpu.SemaphoreType.DMA((blocks,)),
        ],
        flops=2 * rows * rows * width,
        nbytes=2 * unit,
        out_specs=[ANY],
        limit=56 * MIB,
    )
    nodes = lax.all_to_all(
        picked.reshape(ndom, per_peer, width), "dom", split_axis=0, concat_axis=0, tiled=True
    ).reshape(rows, width)
    spots = blocks + 2 * RIM + 1
    adj_rim, adj = call(
        build_body,
        [shape(2 * rim + width, rows), shape(rows, spots * ROWS + rows)],
        (adj_count, adj_target, adj_vals, w_edge),
        [SMEM, SMEM, VMEM, VMEM],
        [pltpu.VMEM((spots, ROWS, rows), BF16)],
        nbytes=16 * unit,
    )
    far, msg = call(
        message_body, [edge, tall], (nodes, adj_rim), flops=square + 2 * rim * rows * width, nbytes=4 * unit
    )
    far = swapped_across(far, "dom")
    (near,) = call(near_body, [edge], (adj_rim, msg), flops=2 * rim * rows * width, nbytes=unit)
    near = swapped(near, "dom", 1)
    cot = cotangent[0]
    own, out_mid, agg_mid, d_node_mid, d_nodes1_mid, d_agg_mid = call(
        own_body,
        [rims, mid, mid, mid, shape(*mid.shape, dtype=F32), mid],
        (nodes, msg, adj, cot, w_node),
        flops=2 * rows * rows * width + 2 * square,
        nbytes=8 * unit,
    )
    ends = []
    for is_far, arrived in ((True, far), (False, near)):
        ends.append(
            call(
                functools.partial(rim_body, is_far),
                [edge, edge, edge, shape(*edge.shape, dtype=F32), edge],
                (nodes, own, arrived, cot, w_node),
                flops=square,
                nbytes=2 * unit,
            )
        )
    out_rim, agg_rim, d_node_rim, d_nodes1_rim, d_agg_rim = zip(*ends[::-1])
    far = swapped_across(d_agg_rim[1], "dom")
    near = swapped(d_agg_rim[0], "dom", 1)
    tiled = ndp == 2 and ndom == 16

    node_part = call(
        functools.partial(grad_node_body, scale),
        [shape(2 * width, width // 2, dtype=F32), shape(2 * width, width // 2)]
        if tiled
        else [shape(2 * width, width, dtype=F32)],
        (nodes, agg_mid, *agg_rim, d_node_mid, *d_node_rim),
        flops=2 * square,
        nbytes=3 * unit,
    )
    if tiled:
        node_part = (node_part[0], swapped(node_part[1], "dp", 1))
    node_out, d_msg, slope = call(
        behind_body,
        [tall, tall_f, tall_f],
        (nodes, adj, w_edge, out_mid, *out_rim, d_agg_mid, *d_agg_rim),
        flops=2 * rows * rows * width + square,
        nbytes=8 * unit,
    )
    back, edge_part = call(
        functools.partial(edge_body, scale),
        [tall, shape(width, width, dtype=F32)],
        (nodes, adj, near, far, d_msg, slope, d_nodes1_mid, *d_nodes1_rim, w_edge),
        scratch=[
            pltpu.VMEM((rows, width), BF16),
            pltpu.VMEM((rows, width), BF16),
            pltpu.SemaphoreType.DMA((rows // rim,)),
        ],
        out_specs=[ANY, VMEM],
        flops=2 * square + 4 * rim * rows * width,
        nbytes=8 * unit,
    )
    if tiled:
        back, node_in = lax.optimization_barrier((back, node_part[1]))
        keep, send = cut_grads(edge_part, (node_part[0], node_in))
    back = lax.all_to_all(
        back.reshape(ndom, per_peer, width), "dom", split_axis=0, concat_axis=0, tiled=True
    ).reshape(rows, width)
    if tiled:
        grad_edge, grad_node, grad_brick = joined(keep, send, back, send_order, width)
    else:
        grad_edge, grad_node = (lax.psum(part, ("dp", "dom")) for part in (edge_part, node_part[0]))
        grad_brick = placed(send_order, back)
    return (node_out[None], grad_brick[None], grad_edge, grad_node)


def solution(mesh):
    in_specs = (
        P("dp", "dom", None),
        P("dom", None),
        P("dom"),
        P("dom", None),
        P("dom", None, None, None),
        P(),
        P(),
        P("dp", "dom", None),
    )
    out_specs = (P("dp", "dom", None), P("dp", "dom", None), P(), P())
    return jax.shard_map(shards, mesh=mesh, in_specs=in_specs, out_specs=out_specs, check_vma=False)
```

```python
import functools
import math

import jax
import jax.numpy as jnp
from jax import lax
from jax.experimental import pallas as pl
from jax.experimental.pallas import tpu as pltpu
from jax.sharding import PartitionSpec as P

ROWS = 128
RIM = 2
ANY = pl.BlockSpec(memory_space=pl.ANY)
VMEM = pl.BlockSpec(memory_space=pltpu.VMEM)
SMEM = pl.BlockSpec(memory_space=pltpu.SMEM)
BF16 = jnp.bfloat16
F32 = jnp.float32
MIB = 1024 * 1024
CORE, ALONG_Y, ALONG_Z = 1, 2, 4


def swapped(x, axis, mask):
    peers = lax.axis_size(axis)
    return lax.ppermute(x, axis, [(i, i ^ mask) for i in range(peers)])


def swapped_across(x, axis):
    peers = lax.axis_size(axis)
    return lax.ppermute(x, axis, [(i, (i + 1 if i % 2 else i - 1) % peers) for i in range(peers)])


def dot(a, b, contract=((1,), (0,))):
    return lax.dot_general(a, b, (contract, ((), ())), preferred_element_type=F32)


def shape(*dims, dtype=BF16):
    return jax.ShapeDtypeStruct(dims, dtype)


def call(body, outs, args, specs=None, scratch=(), flops=0, nbytes=0, limit=24 * MIB, out_specs=None):
    return pl.pallas_call(
        body,
        out_shape=outs,
        in_specs=specs or [VMEM] * len(args),
        out_specs=out_specs or [VMEM] * len(outs),
        scratch_shapes=list(scratch),
        cost_estimate=pl.CostEstimate(flops=flops, bytes_accessed=nbytes, transcendentals=0),
        compiler_params=pltpu.CompilerParams(vmem_limit_bytes=limit),
    )(*args)


def pick_body(order_hbm, feat_hbm, out_hbm, order_ref, feat_ref, hot_ref, out_ref, order_sem, feat_sem, out_sems):
    rows = feat_ref.shape[0]
    early = hot_ref.shape[0] // ROWS
    load_order = pltpu.make_async_copy(order_hbm, order_ref, order_sem)
    load_feat = pltpu.make_async_copy(feat_hbm, feat_ref, feat_sem)
    load_order.start()
    load_feat.start()
    lane = lax.broadcasted_iota(jnp.int32, (ROWS, ROWS), 1).astype(F32)
    zero = jnp.zeros((ROWS, ROWS), BF16)
    load_order.wait()

    def column(row):
        return jnp.transpose(jnp.broadcast_to(row.astype(F32), (ROWS, ROWS)))

    def hot_rows(k):
        row = order_ref[:, k * ROWS : (k + 1) * ROWS]
        high = column(row // ROWS).astype(BF16)
        low = jnp.where(column(row % ROWS) == lane, 1.0, 0.0).astype(BF16)
        return jnp.concatenate([jnp.where(high == b, low, zero) for b in range(rows // ROWS)], axis=1)

    for k in range(early):
        hot_ref[k * ROWS : (k + 1) * ROWS, :] = hot_rows(k)
    load_feat.wait()
    feat = feat_ref[...]
    puts = []
    for k in range(rows // ROWS):
        mine = slice(k * ROWS, (k + 1) * ROWS)
        hot = hot_ref[mine, :] if k < early else hot_rows(k)
        out_ref[mine, :] = dot(hot, feat).astype(BF16)
        puts.append(pltpu.make_async_copy(out_ref.at[pl.ds(k * ROWS, ROWS)], out_hbm.at[pl.ds(k * ROWS, ROWS)], out_sems.at[k]))
        puts[k].start()
    for put in puts:
        put.wait()


def build_body(cnt_ref, tgt_ref, vals_ref, w_edge_ref, rim_ref, both_ref, a_ref):
    blocks, slots = vals_ref.shape[:2]
    spare = blocks + 2 * RIM
    a_ref[...] = jnp.zeros_like(a_ref)
    both_ref[...] = jnp.zeros_like(both_ref)
    for c in range(blocks):
        mine = slice(c * ROWS, (c + 1) * ROWS)
        for s in range(slots):
            w = tgt_ref[c, s]
            at = jnp.where(w < blocks, w + RIM, jnp.where(w < 2 * blocks, w - blocks, w - blocks + RIM))
            at = jnp.where(s < cnt_ref[c], at, spare)
            value = vals_ref[c, s].astype(F32)
            a_ref[at, :, mine] = (a_ref[at, :, mine].astype(F32) + value).astype(BF16)
            lanes = pl.ds(pl.multiple_of(at * ROWS, ROWS), ROWS)
            both_ref[mine, lanes] = (both_ref[mine, lanes].astype(F32) + jnp.transpose(value)).astype(BF16)
    width = w_edge_ref.shape[0]
    rim_ref[: 2 * RIM * ROWS, :] = a_ref[blocks:spare].reshape(2 * RIM * ROWS, blocks * ROWS)
    rim_ref[2 * RIM * ROWS :, :width] = w_edge_ref[...]
    both_ref[:, (spare + 1) * ROWS :] = a_ref[:blocks].reshape(blocks * ROWS, blocks * ROWS)


def chosen(first, second):
    odd = lax.rem(lax.axis_index("dom"), 2) == 1
    return jnp.where(odd, first, second), jnp.where(odd, second, first)


def message_body(nodes_ref, a_ref, far_ref, msg_ref):
    rows, width = nodes_ref.shape
    rim = RIM * ROWS
    w_edge = a_ref[2 * rim :, :width]
    for k in range(rows // rim):
        mine = slice(k * rim, (k + 1) * rim)
        pre = dot(nodes_ref[mine, :], w_edge)
        msg_ref[mine, :] = (pre * jax.nn.sigmoid(pre)).astype(BF16)
    far_ref[...] = dot(a_ref[end_of(True, rim), :], msg_ref[...]).astype(BF16)


def end_of(far, start):
    odd = lax.rem(lax.axis_index("dom"), 2)
    return pl.ds(pl.multiple_of((odd if far else 1 - odd) * start, ROWS), RIM * ROWS)


def node_step(nodes, agg, gout, w_node):
    width = nodes.shape[1]
    pre = dot(nodes, w_node[:width]) + dot(agg, w_node[width:])
    sig = jax.nn.sigmoid(pre)
    out = (nodes.astype(F32) + pre * sig).astype(BF16)
    gout = gout.astype(F32)
    d_node = (gout * (sig * (1.0 + pre * (1.0 - sig)))).astype(BF16)
    back = dot(d_node, w_node, ((1,), (1,)))
    return out, d_node, gout + back[:, :width], back[:, width:].astype(BF16)


def own_body(
    nodes_ref, msg_ref, adj_ref, rims_ref, cot_ref, w_node_ref,
    near_ref, own_ref, out_ref, agg_ref, d_node_ref, d_nodes1_ref, d_agg_ref,
):
    rows, width = nodes_ref.shape
    rim = RIM * ROWS
    msg = msg_ref[...]
    near_ref[...] = dot(rims_ref[end_of(False, rim), :], msg).astype(BF16)
    first = adj_ref.shape[1] - rows
    for k in range(rows // rim):
        mine = slice(k * rim, (k + 1) * rim)
        window = dot(adj_ref[mine, first:], msg).astype(BF16)
        if k == 0:
            own_ref[:rim, :] = window
        elif k == rows // rim - 1:
            own_ref[rim:, :] = window
        else:
            here = slice((k - 1) * rim, k * rim)
            agg_ref[here, :] = window
            out, d_node, d_nodes1, d_agg = node_step(nodes_ref[mine, :], window, cot_ref[mine, :], w_node_ref[...])
            out_ref[here, :] = out
            d_node_ref[here, :] = d_node
            d_nodes1_ref[here, :] = d_nodes1
            d_agg_ref[here, :] = d_agg


def rim_body(
    far, nodes_ref, own_ref, in_ref, cot_ref, w_node_ref,
    out_ref, agg_ref, d_node_ref, d_nodes1_ref, d_agg_ref,
):
    rim = RIM * ROWS
    mine = end_of(far, nodes_ref.shape[0] - rim)
    agg = (own_ref[end_of(far, rim), :].astype(F32) + in_ref[...].astype(F32)).astype(BF16)
    agg_ref[...] = agg
    out, d_node, d_nodes1, d_agg = node_step(nodes_ref[mine, :], agg, cot_ref[mine, :], w_node_ref[...])
    out_ref[...] = out
    d_node_ref[...] = d_node
    d_nodes1_ref[...] = d_nodes1
    d_agg_ref[...] = d_agg


def in_order(mid_ref, near_ref, far_ref):
    first, last = chosen(near_ref[...], far_ref[...])
    return jnp.concatenate([first, mid_ref[...], last], axis=0)


def grad_node_body(scale, nodes_ref, *refs):
    width = nodes_ref.shape[1]
    out_refs = refs[6:]
    agg = in_order(*refs[:3])
    d_node = in_order(*refs[3:6])
    first = lax.axis_index("dp") == 0
    for k, left in enumerate((nodes_ref[...], agg)):
        mine = slice(k * width, (k + 1) * width)
        grad = dot(left, d_node, ((0,), (0,))) * scale
        if len(out_refs) == 1:
            out_refs[0][mine, :] = grad
            continue
        half = width // 2
        out_refs[0][mine, :] = jnp.where(first, grad[:, :half], grad[:, half:])
        out_refs[1][mine, :] = jnp.where(first, grad[:, half:], grad[:, :half]).astype(BF16)


def behind_body(
    nodes_ref, at_ref, w_edge_ref, out_mid_ref, out_near_ref, out_far_ref,
    d_agg_mid_ref, d_agg_near_ref, d_agg_far_ref, out_ref, d_msg_ref, slope_ref,
):
    rows = nodes_ref.shape[0]
    rim = RIM * ROWS
    out_ref[...] = in_order(out_mid_ref, out_near_ref, out_far_ref)
    d_agg = in_order(d_agg_mid_ref, d_agg_near_ref, d_agg_far_ref)
    for k in range(rows // rim):
        mine = slice(k * rim, (k + 1) * rim)
        d_msg_ref[mine, :] = dot(at_ref[mine, :rows], d_agg)
        pre = dot(nodes_ref[mine, :], w_edge_ref[...])
        sig = jax.nn.sigmoid(pre)
        slope_ref[mine, :] = sig * (1.0 + pre * (1.0 - sig))


def edge_body(
    scale, nodes_ref, at_ref, near_ref, far_ref, d_msg_ref, slope_ref, mid_ref, near1_ref, far1_ref, w_edge_ref,
    back_hbm, g_edge_ref, d_edge_ref, back_ref, sems,
):
    rows, width = nodes_ref.shape
    rim = RIM * ROWS
    prev, after = chosen(near_ref[...], far_ref[...])
    rims = jnp.concatenate([prev, after], axis=0)
    ends = chosen(near1_ref[...], far1_ref[...])
    w_edge = w_edge_ref[...]
    puts = []
    for k in range(rows // rim):
        mine = slice(k * rim, (k + 1) * rim)
        d_msg = d_msg_ref[mine, :] + dot(at_ref[mine, rows : rows + 2 * rim], rims)
        d_edge = (d_msg.astype(BF16).astype(F32) * slope_ref[mine, :]).astype(BF16)
        d_edge_ref[mine, :] = d_edge
        if k == 0:
            d_nodes1 = ends[0]
        elif k == rows // rim - 1:
            d_nodes1 = ends[1]
        else:
            d_nodes1 = mid_ref[(k - 1) * rim : k * rim, :]
        back_ref[mine, :] = (d_nodes1 + dot(d_edge, w_edge, ((1,), (1,)))).astype(BF16)
        part = pl.ds(k * rim, rim)
        puts.append(pltpu.make_async_copy(back_ref.at[part], back_hbm.at[part], sems.at[k]))
        puts[k].start()
    g_edge_ref[...] = dot(nodes_ref[...], d_edge_ref[...], ((0,), (0,))) * scale
    for put in puts:
        put.wait()


def bit_of(mask):
    return lax.rem(lax.div(lax.axis_index("dom"), mask), 2)


def cut_rows(total_ref, mask, keep_ref, send_ref):
    size = keep_ref.shape[0]
    bit = bit_of(mask)
    keep_ref[...] = total_ref[pl.ds(pl.multiple_of(bit * size, 16), size), :]
    send_ref[...] = total_ref[pl.ds(pl.multiple_of((1 - bit) * size, 16), size), :].astype(BF16)


def first_cut_body(mask, edge_ref, node_ref, node_in_ref, keep_ref, send_ref, total_ref):
    half = node_ref.shape[1]
    few, more = edge_ref.shape[0] // 4, node_ref.shape[0] // 4
    for q in range(4):
        row = q * (2 * few + more)
        mine = slice(q * more, (q + 1) * more)
        total_ref[row : row + more, :] = node_ref[mine, :] + node_in_ref[mine, :].astype(F32)
        row += more
        mine = slice(q * few, (q + 1) * few)
        total_ref[row : row + few, :] = edge_ref[mine, :half]
        total_ref[row + few : row + 2 * few, :] = edge_ref[mine, half:]
    cut_rows(total_ref, mask, keep_ref, send_ref)


def next_cut_body(mask, mine_ref, in_ref, keep_ref, send_ref, total_ref):
    total_ref[...] = mine_ref[...] + in_ref[...].astype(F32)
    cut_rows(total_ref, mask, keep_ref, send_ref)


def sum_body(mine_ref, in_ref, out_ref):
    out_ref[...] = (mine_ref[...].astype(F32) + in_ref[...].astype(F32)).astype(BF16)


def join_body(mask, mine_ref, dp_ref, y_ref, both_ref, out_ref):
    size, half = mine_ref.shape
    more = size // 2
    few = more // 2
    first = lax.axis_index("dp") == 0
    low = bit_of(mask) == 0
    mine = [ref[...] for ref in (mine_ref, dp_ref)]
    other = [ref[...] for ref in (y_ref, both_ref)]
    for side in range(2):
        a, b = (jnp.where(low, x, y) if side == 0 else jnp.where(low, y, x) for x, y in zip(mine, other))
        row = side * (few + more)
        total = (a[more:].astype(F32) + b[more:].astype(F32)).astype(BF16)
        out_ref[row : row + few, :half] = total[:few]
        out_ref[row : row + few, half:] = total[few:]
        row += few
        out_ref[row : row + more, :half] = jnp.where(first, a[:more], b[:more])
        out_ref[row : row + more, half:] = jnp.where(first, b[:more], a[:more])


def finish_body(own, *refs):
    part_ref = refs[0]
    edge_hbm, node_hbm, edge_ref, node_ref, sems = refs[-5:]
    few, more = edge_ref.shape[0] // 2, node_ref.shape[0] // 2
    for k in range(2):
        row = k * (few + more)
        edge_ref[k * few : (k + 1) * few, :] = part_ref[row : row + few, :].astype(F32)
        node_ref[k * more : (k + 1) * more, :] = part_ref[row + few : row + few + more, :].astype(F32)
    side = bit_of(CORE) if own else 1 - bit_of(CORE)
    puts = []
    for k, (ref, hbm) in enumerate(((edge_ref, edge_hbm), (node_ref, node_hbm))):
        size = ref.shape[0]
        to = hbm.at[pl.ds(pl.multiple_of(side * size, 8), size), :]
        puts.append(pltpu.make_async_copy(ref, to, sems.at[k]))
        puts[k].start()
    for put in puts:
        put.wait()


def finished(own, part, grads, width):
    outs = [shape(width, width, dtype=F32), shape(2 * width, width, dtype=F32)]
    return pl.pallas_call(
        functools.partial(finish_body, own),
        out_shape=outs,
        in_specs=[VMEM] + [ANY] * len(grads),
        out_specs=[ANY, ANY],
        scratch_shapes=[
            pltpu.VMEM((width // 2, width), F32),
            pltpu.VMEM((width, width), F32),
            pltpu.SemaphoreType.DMA((2,)),
        ],
        input_output_aliases={1: 0, 2: 1} if grads else {},
        cost_estimate=pl.CostEstimate(flops=0, bytes_accessed=3 * width * width * 4, transcendentals=0),
        compiler_params=pltpu.CompilerParams(vmem_limit_bytes=24 * MIB),
    )(part, *grads)


def swapped_both(x, mask):
    peers = lax.axis_size("dom")
    total = 2 * peers
    return lax.ppermute(x, ("dp", "dom"), [(i, (i + peers) % total ^ mask) for i in range(total)])


def cut_grads(edge_part, node_part):
    half = node_part[0].shape[1]
    size = node_part[0].shape[0] + 2 * edge_part.shape[0]

    def cut(body, mask, args, size):
        return call(
            functools.partial(body, mask),
            [shape(size // 2, half, dtype=F32), shape(size // 2, half)],
            args,
            scratch=[pltpu.VMEM((size, half), F32)],
        )

    keep, send = cut(first_cut_body, CORE, (edge_part, *node_part), size)
    return cut(next_cut_body, ALONG_Y, (keep, swapped(send, "dom", CORE)), size // 2)


def joined(keep, send, back, send_order, width):
    out = [shape(*send.shape)]
    (mine,) = call(sum_body, out, (keep, swapped(send, "dom", ALONG_Y)))
    for mask in (ALONG_Z, 2 * ALONG_Z):
        (mine,) = call(sum_body, out, (mine, swapped(mine, "dom", mask)))
    others = swapped(mine, "dp", 1), swapped(mine, "dom", ALONG_Y), swapped_both(mine, ALONG_Y)
    grad_brick = placed(send_order, back)
    mine, grad_brick = lax.optimization_barrier((mine, grad_brick))
    (mine,) = call(functools.partial(join_body, ALONG_Y), [shape(6 * (width // 4), width)], (mine, *others))
    grads = finished(True, mine, (), width)
    return *finished(False, swapped(mine, "dom", CORE), grads, width), grad_brick


def placed(send_order, back):
    rows, width = back.shape
    return call(
        place_body,
        [shape(rows, width)],
        (send_order, back),
        flops=2 * rows * rows * width,
        nbytes=4 * rows * width,
    )[0]


def place_body(order_ref, back_ref, out_ref):
    rows = back_ref.shape[0]
    back = back_ref[...]
    order = order_ref[...]
    high = jnp.broadcast_to((order // ROWS).astype(F32), (ROWS, rows)).astype(BF16)
    row = lax.broadcasted_iota(jnp.int32, (ROWS, rows), 0)
    low = jnp.where(jnp.broadcast_to(order % ROWS, (ROWS, rows)) == row, 1.0, 0.0).astype(BF16)
    zero = jnp.zeros((ROWS, rows), BF16)
    for k in range(rows // ROWS):
        mine = slice(k * ROWS, (k + 1) * ROWS)
        hot = jnp.where(high == k, low, zero)
        out_ref[mine, :] = dot(hot, back).astype(BF16)


def shards(features, send_order, adj_count, adj_target, adj_vals, w_edge, w_node, cotangent):
    ndp = lax.axis_size("dp")
    ndom = lax.axis_size("dom")
    rows, width = features.shape[1:]
    per_peer = rows // ndom
    blocks, slots = adj_vals.shape[:2]
    rim = RIM * ROWS
    scale = 1.0 / math.sqrt(float(ndp * rows * ndom))
    tall = shape(rows, width)
    tall_f = shape(rows, width, dtype=F32)
    edge = shape(rim, width)
    rims = shape(2 * rim, width)
    mid = shape(rows - 2 * rim, width)
    unit = rows * width * 2
    square = 2 * rows * width * width

    (picked,) = call(
        pick_body,
        [tall],
        (send_order, features[0]),
        [ANY, ANY],
        [
            pltpu.VMEM((1, rows), jnp.int32),
            pltpu.VMEM((rows, width), BF16),
            pltpu.VMEM((2 * ROWS, rows), BF16),
            pltpu.VMEM((rows, width), BF16),
            pltpu.SemaphoreType.DMA,
            pltpu.SemaphoreType.DMA,
            pltpu.SemaphoreType.DMA((blocks,)),
        ],
        flops=2 * rows * rows * width,
        nbytes=2 * unit,
        out_specs=[ANY],
        limit=56 * MIB,
    )
    nodes = lax.all_to_all(
        picked.reshape(ndom, per_peer, width), "dom", split_axis=0, concat_axis=0, tiled=True
    ).reshape(rows, width)
    spots = blocks + 2 * RIM + 1
    adj_rim, adj = call(
        build_body,
        [shape(2 * rim + width, rows), shape(rows, spots * ROWS + rows)],
        (adj_count, adj_target, adj_vals, w_edge),
        [SMEM, SMEM, VMEM, VMEM],
        [pltpu.VMEM((spots, ROWS, rows), BF16)],
        nbytes=16 * unit,
    )
    far, msg = call(
        message_body, [edge, tall], (nodes, adj_rim), flops=square + 2 * rim * rows * width, nbytes=4 * unit
    )
    far = swapped_across(far, "dom")
    cot = cotangent[0]
    near, own, out_mid, agg_mid, d_node_mid, d_nodes1_mid, d_agg_mid = call(
        own_body,
        [edge, rims, mid, mid, mid, shape(*mid.shape, dtype=F32), mid],
        (nodes, msg, adj, adj_rim, cot, w_node),
        flops=2 * rows * rows * width + 2 * square,
        nbytes=8 * unit,
    )
    near = swapped(near, "dom", 1)
    ends = []
    for is_far, arrived in ((True, far), (False, near)):
        if not is_far:
            arrived, ends[0] = lax.optimization_barrier((arrived, ends[0]))
        ends.append(
            call(
                functools.partial(rim_body, is_far),
                [edge, edge, edge, shape(*edge.shape, dtype=F32), edge],
                (nodes, own, arrived, cot, w_node),
                flops=square,
                nbytes=2 * unit,
            )
        )
    out_rim, agg_rim, d_node_rim, d_nodes1_rim, d_agg_rim = zip(*ends[::-1])
    far = swapped_across(d_agg_rim[1], "dom")
    near = swapped(d_agg_rim[0], "dom", 1)
    tiled = ndp == 2 and ndom == 16

    node_part = call(
        functools.partial(grad_node_body, scale),
        [shape(2 * width, width // 2, dtype=F32), shape(2 * width, width // 2)]
        if tiled
        else [shape(2 * width, width, dtype=F32)],
        (nodes, agg_mid, *agg_rim, d_node_mid, *d_node_rim),
        flops=2 * square,
        nbytes=3 * unit,
    )
    if tiled:
        node_part = (node_part[0], swapped(node_part[1], "dp", 1))
    node_out, d_msg, slope = call(
        behind_body,
        [tall, tall_f, tall_f],
        (nodes, adj, w_edge, out_mid, *out_rim, d_agg_mid, *d_agg_rim),
        flops=2 * rows * rows * width + square,
        nbytes=8 * unit,
    )
    back, edge_part = call(
        functools.partial(edge_body, scale),
        [tall, shape(width, width, dtype=F32)],
        (nodes, adj, near, far, d_msg, slope, d_nodes1_mid, *d_nodes1_rim, w_edge),
        scratch=[
            pltpu.VMEM((rows, width), BF16),
            pltpu.VMEM((rows, width), BF16),
            pltpu.SemaphoreType.DMA((rows // rim,)),
        ],
        out_specs=[ANY, VMEM],
        flops=2 * square + 4 * rim * rows * width,
        nbytes=8 * unit,
    )
    if tiled:
        back, node_in = lax.optimization_barrier((back, node_part[1]))
        keep, send = cut_grads(edge_part, (node_part[0], node_in))
    back = lax.all_to_all(
        back.reshape(ndom, per_peer, width), "dom", split_axis=0, concat_axis=0, tiled=True
    ).reshape(rows, width)
    if tiled:
        grad_edge, grad_node, grad_brick = joined(keep, send, back, send_order, width)
    else:
        grad_edge, grad_node = (lax.psum(part, ("dp", "dom")) for part in (edge_part, node_part[0]))
        grad_brick = placed(send_order, back)
    return (node_out[None], grad_brick[None], grad_edge, grad_node)


def solution(mesh):
    in_specs = (
        P("dp", "dom", None),
        P("dom", None),
        P("dom"),
        P("dom", None),
        P("dom", None, None, None),
        P(),
        P(),
        P("dp", "dom", None),
    )
    out_specs = (P("dp", "dom", None), P("dp", "dom", None), P(), P())
    return jax.shard_map(shards, mesh=mesh, in_specs=in_specs, out_specs=out_specs, check_vma=False)
```

```python
import functools
import math

import jax
import jax.numpy as jnp
from jax import lax
from jax.experimental import pallas as pl
from jax.experimental.pallas import tpu as pltpu
from jax.sharding import PartitionSpec as P

ROWS = 128
RIM = 2
ANY = pl.BlockSpec(memory_space=pl.ANY)
VMEM = pl.BlockSpec(memory_space=pltpu.VMEM)
SMEM = pl.BlockSpec(memory_space=pltpu.SMEM)
BF16 = jnp.bfloat16
F32 = jnp.float32
MIB = 1024 * 1024
CORE, ALONG_Y, ALONG_Z = 1, 2, 4


def swapped(x, axis, mask):
    peers = lax.axis_size(axis)
    return lax.ppermute(x, axis, [(i, i ^ mask) for i in range(peers)])


def swapped_across(x, axis):
    peers = lax.axis_size(axis)
    return lax.ppermute(x, axis, [(i, (i + 1 if i % 2 else i - 1) % peers) for i in range(peers)])


def dot(a, b, contract=((1,), (0,))):
    return lax.dot_general(a, b, (contract, ((), ())), preferred_element_type=F32)


def shape(*dims, dtype=BF16):
    return jax.ShapeDtypeStruct(dims, dtype)


def call(body, outs, args, specs=None, scratch=(), flops=0, nbytes=0, limit=24 * MIB, out_specs=None):
    return pl.pallas_call(
        body,
        out_shape=outs,
        in_specs=specs or [VMEM] * len(args),
        out_specs=out_specs or [VMEM] * len(outs),
        scratch_shapes=list(scratch),
        cost_estimate=pl.CostEstimate(flops=flops, bytes_accessed=nbytes, transcendentals=0),
        compiler_params=pltpu.CompilerParams(vmem_limit_bytes=limit),
    )(*args)


def pick_body(order_hbm, feat_hbm, out_hbm, order_ref, feat_ref, hot_ref, out_ref, order_sem, feat_sem, out_sems):
    rows = feat_ref.shape[0]
    early = hot_ref.shape[0] // ROWS
    load_order = pltpu.make_async_copy(order_hbm, order_ref, order_sem)
    load_feat = pltpu.make_async_copy(feat_hbm, feat_ref, feat_sem)
    load_order.start()
    load_feat.start()
    lane = lax.broadcasted_iota(jnp.int32, (ROWS, ROWS), 1).astype(F32)
    zero = jnp.zeros((ROWS, ROWS), BF16)
    load_order.wait()

    def column(row):
        return jnp.transpose(jnp.broadcast_to(row.astype(F32), (ROWS, ROWS)))

    def hot_rows(k):
        row = order_ref[:, k * ROWS : (k + 1) * ROWS]
        high = column(row // ROWS).astype(BF16)
        low = jnp.where(column(row % ROWS) == lane, 1.0, 0.0).astype(BF16)
        return jnp.concatenate([jnp.where(high == b, low, zero) for b in range(rows // ROWS)], axis=1)

    for k in range(early):
        hot_ref[k * ROWS : (k + 1) * ROWS, :] = hot_rows(k)
    load_feat.wait()
    feat = feat_ref[...]
    puts = []
    for k in range(rows // ROWS):
        mine = slice(k * ROWS, (k + 1) * ROWS)
        hot = hot_ref[mine, :] if k < early else hot_rows(k)
        out_ref[mine, :] = dot(hot, feat).astype(BF16)
        puts.append(pltpu.make_async_copy(out_ref.at[pl.ds(k * ROWS, ROWS)], out_hbm.at[pl.ds(k * ROWS, ROWS)], out_sems.at[k]))
        puts[k].start()
    for put in puts:
        put.wait()


def build_body(cnt_ref, tgt_ref, vals_ref, w_edge_ref, rim_ref, both_ref, a_ref):
    blocks, slots = vals_ref.shape[:2]
    spare = blocks + 2 * RIM
    a_ref[...] = jnp.zeros_like(a_ref)
    both_ref[...] = jnp.zeros_like(both_ref)
    for c in range(blocks):
        mine = slice(c * ROWS, (c + 1) * ROWS)
        for s in range(slots):
            w = tgt_ref[c, s]
            at = jnp.where(w < blocks, w + RIM, jnp.where(w < 2 * blocks, w - blocks, w - blocks + RIM))
            at = jnp.where(s < cnt_ref[c], at, spare)
            value = vals_ref[c, s].astype(F32)
            a_ref[at, :, mine] = (a_ref[at, :, mine].astype(F32) + value).astype(BF16)
            lanes = pl.ds(pl.multiple_of(at * ROWS, ROWS), ROWS)
            both_ref[mine, lanes] = (both_ref[mine, lanes].astype(F32) + jnp.transpose(value)).astype(BF16)
    width = w_edge_ref.shape[0]
    rim_ref[: 2 * RIM * ROWS, :] = a_ref[blocks:spare].reshape(2 * RIM * ROWS, blocks * ROWS)
    rim_ref[2 * RIM * ROWS :, :width] = w_edge_ref[...]
    both_ref[:, (spare + 1) * ROWS :] = a_ref[:blocks].reshape(blocks * ROWS, blocks * ROWS)


def chosen(first, second):
    odd = lax.rem(lax.axis_index("dom"), 2) == 1
    return jnp.where(odd, first, second), jnp.where(odd, second, first)


def message_body(nodes_ref, a_ref, near_ref, far_ref, msg_ref):
    rows, width = nodes_ref.shape
    rim = RIM * ROWS
    w_edge = a_ref[2 * rim :, :width]
    for k in range(rows // rim):
        mine = slice(k * rim, (k + 1) * rim)
        pre = dot(nodes_ref[mine, :], w_edge)
        msg_ref[mine, :] = (pre * jax.nn.sigmoid(pre)).astype(BF16)
    sums = dot(a_ref[: 2 * rim, :], msg_ref[...])
    near, far = chosen(sums[:rim], sums[rim:])
    near_ref[...] = near.astype(BF16)
    far_ref[...] = far.astype(BF16)


def node_step(nodes, agg, gout, w_node):
    width = nodes.shape[1]
    pre = dot(nodes, w_node[:width]) + dot(agg, w_node[width:])
    sig = jax.nn.sigmoid(pre)
    out = (nodes.astype(F32) + pre * sig).astype(BF16)
    gout = gout.astype(F32)
    d_node = (gout * (sig * (1.0 + pre * (1.0 - sig)))).astype(BF16)
    back = dot(d_node, w_node, ((1,), (1,)))
    return out, d_node, gout + back[:, :width], back[:, width:].astype(BF16)


def own_body(
    nodes_ref, msg_ref, adj_ref, cot_ref, w_node_ref,
    own_ref, out_ref, agg_ref, d_node_ref, d_nodes1_ref, d_agg_ref,
):
    rows, width = nodes_ref.shape
    rim = RIM * ROWS
    msg = msg_ref[...]
    first = adj_ref.shape[1] - rows
    for k in range(rows // rim):
        mine = slice(k * rim, (k + 1) * rim)
        window = dot(adj_ref[mine, first:], msg).astype(BF16)
        if k == 0:
            own_ref[:rim, :] = window
        elif k == rows // rim - 1:
            own_ref[rim:, :] = window
        else:
            here = slice((k - 1) * rim, k * rim)
            agg_ref[here, :] = window
            out, d_node, d_nodes1, d_agg = node_step(nodes_ref[mine, :], window, cot_ref[mine, :], w_node_ref[...])
            out_ref[here, :] = out
            d_node_ref[here, :] = d_node
            d_nodes1_ref[here, :] = d_nodes1
            d_agg_ref[here, :] = d_agg


def rim_body(
    nodes_ref, own_ref, near_in_ref, far_in_ref, cot_ref, w_node_ref,
    near_ref, far_ref, out_ref, agg_ref, d_node_ref, d_nodes1_ref, d_agg_ref,
):
    rows = nodes_ref.shape[0]
    rim = RIM * ROWS
    arrived = chosen(near_in_ref[...].astype(F32), far_in_ref[...].astype(F32))
    rims = []
    for k in range(2):
        mine = slice(k * (rows - rim), k * (rows - rim) + rim)
        here = slice(k * rim, (k + 1) * rim)
        agg = (own_ref[here, :].astype(F32) + arrived[k]).astype(BF16)
        agg_ref[here, :] = agg
        out, d_node, d_nodes1, d_agg = node_step(nodes_ref[mine, :], agg, cot_ref[mine, :], w_node_ref[...])
        out_ref[here, :] = out
        d_node_ref[here, :] = d_node
        d_nodes1_ref[here, :] = d_nodes1
        d_agg_ref[here, :] = d_agg
        rims.append(d_agg)
    near_ref[...], far_ref[...] = chosen(rims[0], rims[1])


def in_order(mid_ref, rim_ref):
    rim = RIM * ROWS
    return jnp.concatenate([rim_ref[:rim, :], mid_ref[...], rim_ref[rim:, :]], axis=0)


def grad_node_body(scale, nodes_ref, agg_mid_ref, agg_rim_ref, d_node_mid_ref, d_node_rim_ref, *out_refs):
    width = nodes_ref.shape[1]
    d_node = in_order(d_node_mid_ref, d_node_rim_ref)
    agg = in_order(agg_mid_ref, agg_rim_ref)
    first = lax.axis_index("dp") == 0
    for k, left in enumerate((nodes_ref[...], agg)):
        mine = slice(k * width, (k + 1) * width)
        grad = dot(left, d_node, ((0,), (0,))) * scale
        if len(out_refs) == 1:
            out_refs[0][mine, :] = grad
            continue
        half = width // 2
        out_refs[0][mine, :] = jnp.where(first, grad[:, :half], grad[:, half:])
        out_refs[1][mine, :] = jnp.where(first, grad[:, half:], grad[:, :half]).astype(BF16)


def behind_body(
    nodes_ref, at_ref, w_edge_ref, out_mid_ref, out_rim_ref, d_agg_mid_ref, d_agg_rim_ref,
    out_ref, d_msg_ref, slope_ref,
):
    rows = nodes_ref.shape[0]
    rim = RIM * ROWS
    out_ref[...] = in_order(out_mid_ref, out_rim_ref)
    d_agg = in_order(d_agg_mid_ref, d_agg_rim_ref)
    for k in range(rows // rim):
        mine = slice(k * rim, (k + 1) * rim)
        d_msg_ref[mine, :] = dot(at_ref[mine, :rows], d_agg)
        pre = dot(nodes_ref[mine, :], w_edge_ref[...])
        sig = jax.nn.sigmoid(pre)
        slope_ref[mine, :] = sig * (1.0 + pre * (1.0 - sig))


def edge_body(
    scale, nodes_ref, at_ref, near_ref, far_ref, d_msg_ref, slope_ref, mid_ref, rim_ref, w_edge_ref,
    back_hbm, g_edge_ref, d_edge_ref, back_ref, sems,
):
    rows, width = nodes_ref.shape
    rim = RIM * ROWS
    prev, after = chosen(near_ref[...], far_ref[...])
    rims = jnp.concatenate([prev, after], axis=0)
    w_edge = w_edge_ref[...]
    puts = []
    for k in range(rows // rim):
        mine = slice(k * rim, (k + 1) * rim)
        d_msg = d_msg_ref[mine, :] + dot(at_ref[mine, rows : rows + 2 * rim], rims)
        d_edge = (d_msg.astype(BF16).astype(F32) * slope_ref[mine, :]).astype(BF16)
        d_edge_ref[mine, :] = d_edge
        if k == 0:
            d_nodes1 = rim_ref[:rim, :]
        elif k == rows // rim - 1:
            d_nodes1 = rim_ref[rim:, :]
        else:
            d_nodes1 = mid_ref[(k - 1) * rim : k * rim, :]
        back_ref[mine, :] = (d_nodes1 + dot(d_edge, w_edge, ((1,), (1,)))).astype(BF16)
        part = pl.ds(k * rim, rim)
        puts.append(pltpu.make_async_copy(back_ref.at[part], back_hbm.at[part], sems.at[k]))
        puts[k].start()
    g_edge_ref[...] = dot(nodes_ref[...], d_edge_ref[...], ((0,), (0,))) * scale
    for put in puts:
        put.wait()


def bit_of(mask):
    return lax.rem(lax.div(lax.axis_index("dom"), mask), 2)


def cut_rows(total_ref, mask, keep_ref, send_ref):
    size = keep_ref.shape[0]
    bit = bit_of(mask)
    keep_ref[...] = total_ref[pl.ds(pl.multiple_of(bit * size, 16), size), :]
    send_ref[...] = total_ref[pl.ds(pl.multiple_of((1 - bit) * size, 16), size), :].astype(BF16)


def first_cut_body(mask, edge_ref, node_ref, node_in_ref, keep_ref, send_ref, total_ref):
    half = node_ref.shape[1]
    few, more = edge_ref.shape[0] // 4, node_ref.shape[0] // 4
    for q in range(4):
        row = q * (2 * few + more)
        mine = slice(q * more, (q + 1) * more)
        total_ref[row : row + more, :] = node_ref[mine, :] + node_in_ref[mine, :].astype(F32)
        row += more
        mine = slice(q * few, (q + 1) * few)
        total_ref[row : row + few, :] = edge_ref[mine, :half]
        total_ref[row + few : row + 2 * few, :] = edge_ref[mine, half:]
    cut_rows(total_ref, mask, keep_ref, send_ref)


def next_cut_body(mask, mine_ref, in_ref, keep_ref, send_ref, total_ref):
    total_ref[...] = mine_ref[...] + in_ref[...].astype(F32)
    cut_rows(total_ref, mask, keep_ref, send_ref)


def sum_body(mine_ref, in_ref, out_ref):
    out_ref[...] = (mine_ref[...].astype(F32) + in_ref[...].astype(F32)).astype(BF16)


def join_body(mask, mine_ref, dp_ref, y_ref, both_ref, out_ref):
    size, half = mine_ref.shape
    more = size // 2
    few = more // 2
    first = lax.axis_index("dp") == 0
    low = bit_of(mask) == 0
    mine = [ref[...] for ref in (mine_ref, dp_ref)]
    other = [ref[...] for ref in (y_ref, both_ref)]
    for side in range(2):
        a, b = (jnp.where(low, x, y) if side == 0 else jnp.where(low, y, x) for x, y in zip(mine, other))
        row = side * (few + more)
        total = (a[more:].astype(F32) + b[more:].astype(F32)).astype(BF16)
        out_ref[row : row + few, :half] = total[:few]
        out_ref[row : row + few, half:] = total[few:]
        row += few
        out_ref[row : row + more, :half] = jnp.where(first, a[:more], b[:more])
        out_ref[row : row + more, half:] = jnp.where(first, b[:more], a[:more])


def finish_body(own, *refs):
    part_ref = refs[0]
    edge_hbm, node_hbm, edge_ref, node_ref, sems = refs[-5:]
    few, more = edge_ref.shape[0] // 2, node_ref.shape[0] // 2
    for k in range(2):
        row = k * (few + more)
        edge_ref[k * few : (k + 1) * few, :] = part_ref[row : row + few, :].astype(F32)
        node_ref[k * more : (k + 1) * more, :] = part_ref[row + few : row + few + more, :].astype(F32)
    side = bit_of(CORE) if own else 1 - bit_of(CORE)
    puts = []
    for k, (ref, hbm) in enumerate(((edge_ref, edge_hbm), (node_ref, node_hbm))):
        size = ref.shape[0]
        to = hbm.at[pl.ds(pl.multiple_of(side * size, 8), size), :]
        puts.append(pltpu.make_async_copy(ref, to, sems.at[k]))
        puts[k].start()
    for put in puts:
        put.wait()


def finished(own, part, grads, width):
    outs = [shape(width, width, dtype=F32), shape(2 * width, width, dtype=F32)]
    return pl.pallas_call(
        functools.partial(finish_body, own),
        out_shape=outs,
        in_specs=[VMEM] + [ANY] * len(grads),
        out_specs=[ANY, ANY],
        scratch_shapes=[
            pltpu.VMEM((width // 2, width), F32),
            pltpu.VMEM((width, width), F32),
            pltpu.SemaphoreType.DMA((2,)),
        ],
        input_output_aliases={1: 0, 2: 1} if grads else {},
        cost_estimate=pl.CostEstimate(flops=0, bytes_accessed=3 * width * width * 4, transcendentals=0),
        compiler_params=pltpu.CompilerParams(vmem_limit_bytes=24 * MIB),
    )(part, *grads)


def swapped_both(x, mask):
    peers = lax.axis_size("dom")
    total = 2 * peers
    return lax.ppermute(x, ("dp", "dom"), [(i, (i + peers) % total ^ mask) for i in range(total)])


def cut_grads(edge_part, node_part):
    half = node_part[0].shape[1]
    size = node_part[0].shape[0] + 2 * edge_part.shape[0]

    def cut(body, mask, args, size):
        return call(
            functools.partial(body, mask),
            [shape(size // 2, half, dtype=F32), shape(size // 2, half)],
            args,
            scratch=[pltpu.VMEM((size, half), F32)],
        )

    keep, send = cut(first_cut_body, CORE, (edge_part, *node_part), size)
    return cut(next_cut_body, ALONG_Y, (keep, swapped(send, "dom", CORE)), size // 2)


def joined(keep, send, back, send_order, width):
    out = [shape(*send.shape)]
    (mine,) = call(sum_body, out, (keep, swapped(send, "dom", ALONG_Y)))
    for mask in (ALONG_Z, 2 * ALONG_Z):
        (mine,) = call(sum_body, out, (mine, swapped(mine, "dom", mask)))
    others = swapped(mine, "dp", 1), swapped(mine, "dom", ALONG_Y), swapped_both(mine, ALONG_Y)
    grad_brick = placed(send_order, back)
    mine, grad_brick = lax.optimization_barrier((mine, grad_brick))
    (mine,) = call(functools.partial(join_body, ALONG_Y), [shape(6 * (width // 4), width)], (mine, *others))
    grads = finished(True, mine, (), width)
    return *finished(False, swapped(mine, "dom", CORE), grads, width), grad_brick


def placed(send_order, back):
    rows, width = back.shape
    return call(
        place_body,
        [shape(rows, width)],
        (send_order, back),
        flops=2 * rows * rows * width,
        nbytes=4 * rows * width,
    )[0]


def place_body(order_ref, back_ref, out_ref):
    rows = back_ref.shape[0]
    back = back_ref[...]
    order = order_ref[...]
    high = jnp.broadcast_to((order // ROWS).astype(F32), (ROWS, rows)).astype(BF16)
    row = lax.broadcasted_iota(jnp.int32, (ROWS, rows), 0)
    low = jnp.where(jnp.broadcast_to(order % ROWS, (ROWS, rows)) == row, 1.0, 0.0).astype(BF16)
    zero = jnp.zeros((ROWS, rows), BF16)
    for k in range(rows // ROWS):
        mine = slice(k * ROWS, (k + 1) * ROWS)
        hot = jnp.where(high == k, low, zero)
        out_ref[mine, :] = dot(hot, back).astype(BF16)


def shards(features, send_order, adj_count, adj_target, adj_vals, w_edge, w_node, cotangent):
    ndp = lax.axis_size("dp")
    ndom = lax.axis_size("dom")
    rows, width = features.shape[1:]
    per_peer = rows // ndom
    blocks, slots = adj_vals.shape[:2]
    rim = RIM * ROWS
    scale = 1.0 / math.sqrt(float(ndp * rows * ndom))
    tall = shape(rows, width)
    tall_f = shape(rows, width, dtype=F32)
    edge = shape(rim, width)
    rims = shape(2 * rim, width)
    mid = shape(rows - 2 * rim, width)
    unit = rows * width * 2
    square = 2 * rows * width * width

    (picked,) = call(
        pick_body,
        [tall],
        (send_order, features[0]),
        [ANY, ANY],
        [
            pltpu.VMEM((1, rows), jnp.int32),
            pltpu.VMEM((rows, width), BF16),
            pltpu.VMEM((4 * ROWS, rows), BF16),
            pltpu.VMEM((rows, width), BF16),
            pltpu.SemaphoreType.DMA,
            pltpu.SemaphoreType.DMA,
            pltpu.SemaphoreType.DMA((blocks,)),
        ],
        flops=2 * rows * rows * width,
        nbytes=2 * unit,
        out_specs=[ANY],
        limit=56 * MIB,
    )
    nodes = lax.all_to_all(
        picked.reshape(ndom, per_peer, width), "dom", split_axis=0, concat_axis=0, tiled=True
    ).reshape(rows, width)
    spots = blocks + 2 * RIM + 1
    adj_rim, adj = call(
        build_body,
        [shape(2 * rim + width, rows), shape(rows, spots * ROWS + rows)],
        (adj_count, adj_target, adj_vals, w_edge),
        [SMEM, SMEM, VMEM, VMEM],
        [pltpu.VMEM((spots, ROWS, rows), BF16)],
        nbytes=16 * unit,
    )
    near, far, msg = call(
        message_body, [edge, edge, tall], (nodes, adj_rim), flops=square + 4 * rim * rows * width, nbytes=4 * unit
    )
    far = swapped_across(far, "dom")
    near = swapped(near, "dom", 1)
    cot = cotangent[0]
    own, out_mid, agg_mid, d_node_mid, d_nodes1_mid, d_agg_mid = call(
        own_body,
        [rims, mid, mid, mid, shape(*mid.shape, dtype=F32), mid],
        (nodes, msg, adj, cot, w_node),
        flops=2 * rows * rows * width + 2 * square,
        nbytes=8 * unit,
    )
    near, far, out_rim, agg_rim, d_node_rim, d_nodes1_rim, d_agg_rim = call(
        rim_body,
        [edge, edge, rims, rims, rims, shape(*rims.shape, dtype=F32), rims],
        (nodes, own, near, far, cot, w_node),
        flops=2 * square,
        nbytes=4 * unit,
    )
    far = swapped_across(far, "dom")
    near = swapped(near, "dom", 1)
    tiled = ndp == 2 and ndom == 16

    node_part = call(
        functools.partial(grad_node_body, scale),
        [shape(2 * width, width // 2, dtype=F32), shape(2 * width, width // 2)]
        if tiled
        else [shape(2 * width, width, dtype=F32)],
        (nodes, agg_mid, agg_rim, d_node_mid, d_node_rim),
        flops=2 * square,
        nbytes=3 * unit,
    )
    if tiled:
        node_part = (node_part[0], swapped(node_part[1], "dp", 1))
    node_out, d_msg, slope = call(
        behind_body,
        [tall, tall_f, tall_f],
        (nodes, adj, w_edge, out_mid, out_rim, d_agg_mid, d_agg_rim),
        flops=2 * rows * rows * width + square,
        nbytes=8 * unit,
    )
    back, edge_part = call(
        functools.partial(edge_body, scale),
        [tall, shape(width, width, dtype=F32)],
        (nodes, adj, near, far, d_msg, slope, d_nodes1_mid, d_nodes1_rim, w_edge),
        scratch=[
            pltpu.VMEM((rows, width), BF16),
            pltpu.VMEM((rows, width), BF16),
            pltpu.SemaphoreType.DMA((rows // rim,)),
        ],
        out_specs=[ANY, VMEM],
        flops=2 * square + 4 * rim * rows * width,
        nbytes=8 * unit,
    )
    if tiled:
        back, node_in = lax.optimization_barrier((back, node_part[1]))
        keep, send = cut_grads(edge_part, (node_part[0], node_in))
    back = lax.all_to_all(
        back.reshape(ndom, per_peer, width), "dom", split_axis=0, concat_axis=0, tiled=True
    ).reshape(rows, width)
    if tiled:
        grad_edge, grad_node, grad_brick = joined(keep, send, back, send_order, width)
    else:
        grad_edge, grad_node = (lax.psum(part, ("dp", "dom")) for part in (edge_part, node_part[0]))
        grad_brick = placed(send_order, back)
    return (node_out[None], grad_brick[None], grad_edge, grad_node)


def solution(mesh):
    in_specs = (
        P("dp", "dom", None),
        P("dom", None),
        P("dom"),
        P("dom", None),
        P("dom", None, None, None),
        P(),
        P(),
        P("dp", "dom", None),
    )
    out_specs = (P("dp", "dom", None), P("dp", "dom", None), P(), P())
    return jax.shard_map(shards, mesh=mesh, in_specs=in_specs, out_specs=out_specs, check_vma=False)
```
